32 devices in a mesh: dp: 4 (over y, x), mp: 8 (over z, core).
Axes of the slice: x: 2, y: 2, z: 4, core: 2. Of those that a mesh axis runs over, the one named last changes fastest.
Arguments:
- image: bfloat16 [4, 32, 128, 1024], P('dp', 'mp'), may hold values from -24 to 24
- embedding: bfloat16 [4, 1024], P('dp'), may hold values from -6 to 6
- extents: int32 [4, 2], P('dp'), may hold values from 8 to 64, as said below
- gain_first: float32 [1024], replicated, may hold values from 0.1 to 1.9
- conv_first: bfloat16 [9, 1024, 1024], P(None, 'mp'), may hold values from -0.0625 to 0.0625
- gain_second: float32 [1024], replicated, may hold values from 0.1 to 1.9
- conv_second: bfloat16 [9, 1024, 1024], P(None, 'mp'), may hold values from -0.0625 to 0.0625
- shift_weight: bfloat16 [1024, 1024], P(None, 'mp'), may hold values from -0.1875 to 0.1875
- down_weight: bfloat16 [4, 1024, 2048], P(None, 'mp'), may hold values from -0.09375 to 0.09375
- ada_weight: bfloat16 [1024, 8192], P(None, 'mp'), may hold values from -0.09375 to 0.09375
- qkv_weight: bfloat16 [3, 2048, 2048], P(None, None, 'mp'), may hold values from -0.125 to 0.125
- out_weight: bfloat16 [2048, 2048], P('mp'), may hold values from -1 to 1
- up_weight: bfloat16 [2048, 8192], P(None, 'mp'), may hold values from -0.125 to 0.125
- proj_weight: bfloat16 [8192, 2048], P('mp'), may hold values from -0.0625 to 0.0625
- cotangent: bfloat16 [4, 16, 64, 2048], P('dp', 'mp'), may hold values from -6 to 6
Outputs:
- output: bfloat16 [4, 16, 64, 2048], P('dp', 'mp')
- image_grad: bfloat16 [4, 32, 128, 1024], P('dp', 'mp')
- embedding_grad: float32 [4, 1024], P('dp')
- gain_first_grad: float32 [1024], P(('dp', 'mp'))
- conv_first_grad: float32 [9, 1024, 1024], P(None, 'dp', 'mp')
- gain_second_grad: float32 [1024], P(('dp', 'mp'))
- conv_second_grad: float32 [9, 1024, 1024], P(None, 'dp', 'mp')
- shift_weight_grad: float32 [1024, 1024], P('dp', 'mp')
- down_weight_grad: float32 [4, 1024, 2048], P(None, 'dp', 'mp')
- ada_weight_grad: float32 [1024, 8192], P('dp', 'mp')
- qkv_weight_grad: float32 [3, 2048, 2048], P(None, 'dp', 'mp')
- out_weight_grad: float32 [2048, 2048], P('mp', 'dp')
- up_weight_grad: float32 [2048, 8192], P('dp', 'mp')
- proj_weight_grad: float32 [8192, 2048], P('mp', 'dp')
The draws below stay inside these ranges and needn't reach their ends.
Inputs may be any that keep to these rules, and one draw needn't show every extreme that they name: extents[b, 0] is the height and extents[b, 1] the width, in tokens, of the valid top-left part of image b; heights are 8 or more and widths 64 // 4 or more; in every draw one image is valid everywhere.
All inputs are finite; a program needn't handle non-finite values.
Results may differ from the reference program's by a relative error of at most 0.028.
Values may be sent and summed in bfloat16 or wider, within the bound.
A program may use at most 448 MiB of HBM per device.

```python
import math
from functools import partial
import jax
import jax.numpy as jnp
from jax import lax

CHANNELS = 1024
WIDTH = 2048
HEADS = 16
HEAD_DIM = 128
MLP_HIDDEN = 8192
EMBED = 1024
GROUPS = 32
COLS = 128
ROWS = 32
TOKEN_ROWS = 16
TOKEN_COLS = 64
SEQUENCE = 1024
IMAGES = 4


def draw_image(key, part):
    key_base, key_scale, key_offset = jax.random.split(key, 3)
    row_place = jnp.arange(ROWS, dtype=jnp.float32)[None, :, None, None] / ROWS
    channel_scale = jnp.exp(jax.random.uniform(key_scale, (1, 1, 1, CHANNELS), minval=-0.69, maxval=0.69))
    offsets = jnp.clip(jax.random.normal(key_offset, (1, 1, 1, CHANNELS)), -3.0, 3.0)
    noise = jnp.clip(jax.random.normal(key_base, (IMAGES, ROWS, COLS, CHANNELS)), -4.0, 4.0)
    values = noise * (0.6 + 2.0 * row_place) * channel_scale + 0.5 * row_place * offsets
    return values.astype(jnp.bfloat16)


def draw_extents(key, part):
    key_height, key_width, key_chosen = jax.random.split(key, 3)
    heights = jax.random.randint(key_height, (IMAGES,), TOKEN_ROWS // 2, TOKEN_ROWS + 1)
    widths = jax.random.randint(key_width, (IMAGES,), TOKEN_COLS // 4, TOKEN_COLS + 1)
    chosen = jax.random.randint(key_chosen, (), 0, IMAGES)
    filled = jnp.arange(IMAGES) == chosen
    heights = jnp.where(filled, TOKEN_ROWS, heights)
    widths = jnp.where(filled, TOKEN_COLS, widths)
    return jnp.stack([heights, widths], axis=1).astype(jnp.int32)


def steps_of(key, dims, shards, least, largest):
    def one(dim, parts):
        draws = jax.random.uniform(jax.random.fold_in(jax.random.fold_in(key, 6), dim), (parts,), jnp.float32, least / len(shards), largest / len(shards))
        return jnp.repeat(jnp.exp(draws), dims[dim] // parts).reshape((-1,) + (1,) * (len(dims) - dim - 1))

    factor_of = one(*shards[0])
    for cut in shards[1:]:
        factor_of = factor_of * one(*cut)
    return factor_of


def centred(key, dims, scale, most, cuts=(), kind=jnp.bfloat16):
    drawn = jax.random.normal(key, dims, jnp.float32) * scale
    if len(cuts) > 0:
        drawn = steps_of(key, dims, cuts, -0.22, 0.18) * drawn
    return jnp.clip(drawn, min=-most, max=most).astype(kind)


def setup_inputs(seed: int = 0) -> dict:
    key_list = jax.random.split(jax.random.key(seed), 16)
    return {
        "image": draw_image(jax.random.fold_in(key_list[15], 71), 0),
        "embedding": centred(key_list[1], (IMAGES, EMBED), 1.0, 6.0, ((0, 4),)),
        "extents": draw_extents(jax.random.fold_in(key_list[15], 71), 0),
        "gain_first": jnp.clip(1.0 + 0.18 * jax.random.normal(key_list[3], (CHANNELS,), jnp.float32), 0.1, 1.9),
        "conv_first": centred(key_list[4], (9, CHANNELS, CHANNELS), (9 * CHANNELS) ** -0.5, 0.0625, ((1, 8),)),
        "gain_second": jnp.clip(1.0 + 0.18 * jax.random.normal(key_list[5], (CHANNELS,), jnp.float32), 0.1, 1.9),
        "conv_second": centred(key_list[6], (9, CHANNELS, CHANNELS), (9 * CHANNELS) ** -0.5, 0.0625, ((1, 8),)),
        "shift_weight": centred(key_list[7], (EMBED, CHANNELS), EMBED ** -0.5, 0.1875, ((1, 8),)),
        "down_weight": centred(key_list[8], (4, CHANNELS, WIDTH), (4 * CHANNELS) ** -0.5, 0.09375, ((1, 8),)),
        "ada_weight": centred(key_list[9], (EMBED, 4 * WIDTH), (4 * EMBED) ** -0.5, 0.09375, ((1, 8),)),
        "qkv_weight": centred(key_list[10], (3, WIDTH, WIDTH), WIDTH ** -0.5, 0.125, ((2, 8),)),
        "out_weight": centred(key_list[11], (WIDTH, WIDTH), (max(1, 16 * WIDTH // SEQUENCE)) ** -0.5, 1.0, ((0, 8),)),
        "up_weight": centred(key_list[12], (WIDTH, MLP_HIDDEN), WIDTH ** -0.5, 0.125, ((1, 8),)),
        "proj_weight": centred(key_list[13], (MLP_HIDDEN, WIDTH), MLP_HIDDEN ** -0.5, 0.0625, ((0, 8),)),
        "cotangent": centred(key_list[14], (IMAGES, TOKEN_ROWS, TOKEN_COLS, WIDTH), 1.0, 6.0, ((0, 4), (1, 8))),
    }


@jax.custom_vjp
def low(v):
    return lax.optimization_barrier(v.astype(jnp.bfloat16)).astype(jnp.float32)

@jax.custom_vjp
def low_back(v):
    return v

def low_keep(v):
    return (low(v), None)

def low_pass(kept, grad):
    return (grad,)

def back_keep(v):
    return (v, None)

def back_low(kept, grad):
    return (low(grad),)
low.defvjp(low_keep, low_pass)
low_back.defvjp(back_keep, back_low)
GROUP_EPSILON = 1e-05
LAYER_EPSILON = 1e-06
MASKED_SCORE = -1000000000.0
PRECISE = lax.Precision.HIGHEST

def group_norm(values, gain_vec):
    height, breadth, channel_count = values.shape
    grouped = values.reshape(height * breadth, GROUPS, channel_count // GROUPS)
    centre = grouped - lax.optimization_barrier(jnp.mean(grouped, axis=(0, 2), keepdims=True))
    spread = lax.optimization_barrier(jnp.mean(centre * centre, axis=(0, 2), keepdims=True))
    normed = centre * lax.rsqrt(spread + GROUP_EPSILON)
    return normed.reshape(height, breadth, channel_count) * gain_vec

def conv_three(source, kernel):
    height, breadth, channel_count = source.shape
    padded = jnp.pad(source, ((1, 1), (1, 1), (0, 0)))
    total = jnp.zeros((height * breadth, kernel.shape[2]), source.dtype)
    for tap_index in range(9):
        row_off, col_off = divmod(tap_index, 3)
        window = padded[row_off:row_off + height, col_off:col_off + breadth].reshape(height * breadth, channel_count)
        total = total + jnp.dot(window, kernel[tap_index], precision=PRECISE)
    return total.reshape(height, breadth, kernel.shape[2])

def layer_norm(stream):
    centre = stream - lax.optimization_barrier(jnp.mean(stream, axis=-1, keepdims=True))
    spread = lax.optimization_barrier(jnp.mean(centre * centre, axis=-1, keepdims=True))
    return centre * lax.rsqrt(spread + LAYER_EPSILON)

def attention(queries, key_rows, value_rows, key_valid):
    block_rows = min(512, SEQUENCE)
    score_scale = 1.0 / math.sqrt(HEAD_DIM)

    def one_block(query_block):
        raw_scores = low_back(jnp.einsum('qhd,khd->hqk', query_block, key_rows, precision=PRECISE))
        logits = jnp.where(key_valid[None, None, :], raw_scores * score_scale, MASKED_SCORE)
        mix_weights = jax.nn.softmax(logits, axis=-1)
        return jnp.einsum('hqk,khd->qhd', low(mix_weights), value_rows, precision=PRECISE)
    blocks = queries.reshape(SEQUENCE // block_rows, block_rows, HEADS, HEAD_DIM)
    mixed_heads = lax.map(jax.checkpoint(one_block), blocks)
    return mixed_heads.reshape(SEQUENCE, WIDTH)

def image_forward(weights, inputs):
    gain_first, conv_first, gain_second, conv_second, shift_weight, down_weight, ada_weight, qkv_weight, out_weight, up_weight, proj_weight = weights
    pixels, embed_row, extent_row = inputs
    shift_vector = jnp.dot(embed_row, shift_weight, precision=PRECISE)
    modulation = jnp.dot(embed_row, ada_weight, precision=PRECISE)
    scale_attend = modulation[:WIDTH]
    shift_attend = modulation[WIDTH:2 * WIDTH]
    scale_mlp = modulation[2 * WIDTH:3 * WIDTH]
    shift_mlp = modulation[3 * WIDTH:]
    hidden_first = low(jax.nn.silu(group_norm(pixels, gain_first)))
    conv_output = low_back(conv_three(hidden_first, conv_first)) + shift_vector
    hidden_second = low(jax.nn.silu(group_norm(conv_output, gain_second)))
    residual = pixels + low_back(conv_three(hidden_second, conv_second))
    tap_grid = low(residual).reshape(TOKEN_ROWS, 2, TOKEN_COLS, 2, CHANNELS)
    stream = jnp.einsum('iajbc,abce->ije', tap_grid, down_weight.reshape(2, 2, CHANNELS, WIDTH), precision=PRECISE)
    stream = low_back(stream).reshape(SEQUENCE, WIDTH)
    normed_attend = low(layer_norm(stream) * (1.0 + scale_attend) + shift_attend)
    projected = [low(low_back(jnp.dot(normed_attend, qkv_weight[proj_index], precision=PRECISE))).reshape(SEQUENCE, HEADS, HEAD_DIM) for proj_index in range(3)]
    token_index = jnp.arange(SEQUENCE)
    key_valid = (token_index // TOKEN_COLS < extent_row[0]) & (token_index % TOKEN_COLS < extent_row[1])
    mixed_heads = low(low_back(attention(projected[0], projected[1], projected[2], key_valid)))
    stream_mid = stream + low_back(jnp.dot(mixed_heads, out_weight, precision=PRECISE))
    normed_mlp = low(layer_norm(stream_mid) * (1.0 + scale_mlp) + shift_mlp)
    upper_proj = low_back(jnp.dot(normed_mlp, up_weight, precision=PRECISE))
    activated = low(jax.nn.gelu(upper_proj, approximate=True))
    final_stream = stream_mid + low_back(jnp.dot(activated, proj_weight, precision=PRECISE))
    return final_stream.reshape(TOKEN_ROWS, TOKEN_COLS, WIDTH)

def reference(image, embedding, extents, gain_first, conv_first, gain_second, conv_second, shift_weight, down_weight, ada_weight, qkv_weight, out_weight, up_weight, proj_weight, cotangent):

    def forward(image_float, embed_float, weights):
        stepper = jax.checkpoint(partial(image_forward, weights))
        return lax.map(stepper, (image_float, embed_float, extents))
    weights = tuple((array_in.astype(jnp.float32) for array_in in (gain_first, conv_first, gain_second, conv_second, shift_weight, down_weight, ada_weight, qkv_weight, out_weight, up_weight, proj_weight)))
    output, pullback = jax.vjp(forward, image.astype(jnp.float32), embedding.astype(jnp.float32), weights)
    image_grad, embed_grad, weight_grads = pullback(cotangent.astype(jnp.float32))
    return (output.astype(jnp.bfloat16), image_grad.astype(jnp.bfloat16), embed_grad, weight_grads[0], weight_grads[1], weight_grads[2], weight_grads[3], weight_grads[4], weight_grads[5], weight_grads[6], weight_grads[7], weight_grads[8], weight_grads[9], weight_grads[10])
```

```python
from functools import partial
import math

import jax
import jax.numpy as jnp
from jax import lax
from jax.experimental import pallas as pl
from jax.experimental.pallas import tpu as pltpu
from jax.sharding import PartitionSpec as P

HEAD_DIM = 128
GROUPS = 32


GROUP_EPSILON = 1e-05
LAYER_EPSILON = 1e-06
MASKED_SCORE = -1000000000.0
PRECISE = lax.Precision.HIGHEST


def group_spread(per_channel, size):
    grouped = jnp.sum(per_channel.reshape(-1, size), axis=1)
    return jnp.repeat(grouped, size)


def group_forward(values, size):
    counted = values.shape[0] * size
    average = group_spread(jnp.sum(values, axis=0), size) / counted
    centre = values - average
    inverse = lax.rsqrt(
        group_spread(jnp.sum(centre * centre, axis=0), size) / counted + GROUP_EPSILON
    )
    return (centre * inverse, inverse)


def group_backward(incoming, normed, inverse, gain_vec, size):
    pre_act = normed * gain_vec
    sigmoid_part = jax.nn.sigmoid(pre_act)
    through = incoming * sigmoid_part * (1.0 + pre_act * (1.0 - sigmoid_part))
    counted = normed.shape[0] * size
    gain_part = jnp.sum(through * normed, axis=0)
    plain_part = jnp.sum(through, axis=0)
    first_mean = group_spread(plain_part * gain_vec, size) / counted
    second_mean = group_spread(gain_part * gain_vec, size) / counted
    outgoing = inverse * (through * gain_vec - first_mean - normed * second_mean)
    return (outgoing, gain_part)


def windows(planes, flipped):
    row_count, col_count, depth = planes.shape
    padded = jnp.pad(planes, ((1, 1), (1, 1), (0, 0)))
    pieces = []
    for tap_index in range(9):
        row_off, col_off = divmod(tap_index, 3)
        if flipped:
            row_off, col_off = (2 - row_off, 2 - col_off)
        pieces.append(padded[row_off : row_off + row_count, col_off : col_off + col_count])
    return jnp.stack(pieces, axis=2).reshape(row_count * col_count, 9, depth)


def gather_rows(rows):
    return lax.all_gather(rows, "mp", axis=0, tiled=True)


def scatter_rows(rows):
    return lax.psum_scatter(
        rows.astype(jnp.bfloat16), "mp", scatter_dimension=0, tiled=True
    ).astype(jnp.float32)


def conv_scatter(hidden, kernel, n):
    patch = windows(hidden, False)
    depth = kernel.shape[2] // n
    total = jnp.einsum("ptc,tcd->pd", patch, kernel, preferred_element_type=jnp.float32)
    parts = total.astype(jnp.bfloat16).reshape(-1, n, depth).transpose(1, 0, 2)
    return lax.psum_scatter(parts, "mp", scatter_dimension=0, tiled=False).astype(jnp.float32)


def conv_backward(grad_low, hidden, kernel, n):
    row_count, col_count, depth = hidden.shape
    gathered = lax.all_gather(grad_low, "mp", axis=1, tiled=True)
    padded = jnp.pad(gathered, ((col_count, col_count), (0, 0)))
    taps = kernel.reshape(3, 3 * depth, kernel.shape[2])
    acc = sum(
        jnp.einsum(
            "pd,td->pt",
            padded[(2 - i) * col_count : (2 - i) * col_count + row_count * col_count],
            taps[i],
            preferred_element_type=jnp.float32,
        )
        for i in range(3)
    )
    grad_kernel = jnp.einsum(
        "ptc,pd->tcd", windows(hidden, False), gathered, preferred_element_type=jnp.float32
    )
    return (join_columns(acc, col_count), grad_kernel)


def dp_rows(grad, dim):
    return lax.psum_scatter(
        grad.astype(jnp.bfloat16), "dp", scatter_dimension=dim, tiled=True
    ).astype(jnp.float32)


def by_images(grad, m):
    taps, own, outs = grad.shape
    return grad.astype(jnp.bfloat16).reshape(taps * own, m, outs // m).transpose(1, 0, 2)


def turn_kernel(parts, taps, m, n):
    own = parts.shape[1] // taps
    outs = parts.shape[2] * m
    mine = lax.psum_scatter(parts, "dp", scatter_dimension=0, tiled=False)
    ratio = n // m
    pieces = mine.reshape(taps, own, ratio, outs // n)
    me = lax.axis_index("mp") % ratio
    result = jnp.zeros((taps, ratio, own, outs // n), jnp.bfloat16)
    for shift in range(ratio):
        route = []
        for i in range(m):
            for j in range(n):
                target = (j // ratio) * n + ratio * i + (j % ratio + shift) % ratio
                route.append((i * n + j, target))
        half = lax.dynamic_index_in_dim(pieces, (me + shift) % ratio, axis=2, keepdims=False)
        moved = lax.ppermute(half, ("dp", "mp"), route)
        place = (me - shift + ratio) % ratio
        result = lax.dynamic_update_slice(result, moved[:, None], (0, place, 0, 0))
    return result.reshape(taps, ratio * own, outs // n).astype(jnp.float32)


def layer_forward(stream):
    centre = stream - jnp.mean(stream, axis=1, keepdims=True)
    inverse = lax.rsqrt(jnp.mean(centre * centre, axis=1, keepdims=True) + LAYER_EPSILON)
    return (centre * inverse, inverse)


def layer_backward(incoming, normed, inverse, scale_vec):
    through = incoming * (1.0 + scale_vec)
    outgoing = inverse * (
        through
        - jnp.mean(through, axis=1, keepdims=True)
        - normed * jnp.mean(through * normed, axis=1, keepdims=True)
    )
    return (outgoing, jnp.sum(incoming * normed, axis=0), jnp.sum(incoming, axis=0))


def attend_forward(queries, key_rows, value_rows, key_valid, block_rows):
    score_scale = 1.0 / math.sqrt(queries.shape[-1])

    def one_block(query_block):
        raw_scores = jnp.einsum(
            "qhd,khd->hqk", query_block, key_rows, preferred_element_type=jnp.float32
        )
        logits = jnp.where(key_valid[None, None, :], raw_scores * score_scale, MASKED_SCORE)
        peak_score = jnp.max(logits, axis=-1, keepdims=True)
        exponent = jnp.exp(logits - peak_score)
        totals = jnp.sum(exponent, axis=-1, keepdims=True)
        mix_weights = (exponent / totals).astype(jnp.bfloat16)
        mixed_heads = jnp.einsum(
            "hqk,khd->qhd", mix_weights, value_rows, preferred_element_type=jnp.float32
        )
        return (mixed_heads, (peak_score + jnp.log(totals))[..., 0])

    blocks = queries.reshape(-1, block_rows, queries.shape[1], queries.shape[2])
    mixed_heads, log_totals = lax.map(one_block, blocks)
    return (mixed_heads.reshape(queries.shape), log_totals)


def attend_backward(queries, key_rows, value_rows, key_valid, log_totals, grad_mixed, block_rows):
    score_scale = 1.0 / math.sqrt(queries.shape[-1])
    block_shape = (-1, block_rows, queries.shape[1], queries.shape[2])

    def one_block(running, inputs):
        grad_keys, grad_values = running
        query_block, grad_block, log_block = inputs
        raw_scores = jnp.einsum(
            "qhd,khd->hqk", query_block, key_rows, preferred_element_type=jnp.float32
        )
        logits = jnp.where(key_valid[None, None, :], raw_scores * score_scale, MASKED_SCORE)
        mix_weights = jnp.exp(logits - log_block[..., None])
        grad_weights = jnp.einsum(
            "qhd,khd->hqk", grad_block, value_rows, preferred_element_type=jnp.float32
        )
        inner_sum = jnp.sum(mix_weights * grad_weights, axis=-1, keepdims=True)
        grad_scores = (mix_weights * (grad_weights - inner_sum) * score_scale).astype(jnp.bfloat16)
        grad_query = jnp.einsum(
            "hqk,khd->qhd", grad_scores, key_rows, preferred_element_type=jnp.float32
        )
        grad_keys = grad_keys + jnp.einsum(
            "hqk,qhd->khd", grad_scores, query_block, preferred_element_type=jnp.float32
        )
        grad_values = grad_values + jnp.einsum(
            "hqk,qhd->khd",
            mix_weights.astype(jnp.bfloat16),
            grad_block,
            preferred_element_type=jnp.float32,
        )
        return ((grad_keys, grad_values), grad_query)

    zero_rows = jnp.zeros(key_rows.shape, jnp.float32)
    (grad_keys, grad_values), grad_query = lax.scan(
        one_block,
        (zero_rows, zero_rows),
        (queries.reshape(block_shape), grad_mixed.reshape(block_shape), log_totals),
    )
    return (grad_query.reshape(queries.shape), grad_keys, grad_values)


MESH = pl.DeviceIdType.MESH
CONV_PARTS = 4
TOKEN_PARTS = 4
VMEM_BYTES = 60 * 1024 * 1024


class Line:
    def __init__(self, chips):
        self.chips = chips
        self.dp = lax.axis_index("dp")
        self.mp = lax.axis_index("mp")
        self.z = self.mp // 2
        self.c = self.mp % 2
        self.has_up = self.z < chips - 1
        self.has_down = self.z > 0
        self.up = (self.dp, self.mp + 2)
        self.down = (self.dp, self.mp - 2)
        self.sibling = (self.dp, 2 * self.z + 1 - self.c)

    def barrier(self):
        bar = pltpu.get_barrier_semaphore()
        pl.semaphore_signal(bar, inc=1, device_id=self.sibling, device_id_type=MESH)

        @pl.when(self.has_up)
        def _():
            pl.semaphore_signal(bar, inc=1, device_id=self.up, device_id_type=MESH)

        @pl.when(self.has_down)
        def _():
            pl.semaphore_signal(bar, inc=1, device_id=self.down, device_id_type=MESH)

        middle = jnp.logical_and(self.has_up, self.has_down)

        @pl.when(middle)
        def _():
            pl.semaphore_wait(bar, 3)

        @pl.when(jnp.logical_not(middle))
        def _():
            pl.semaphore_wait(bar, 2)


def remote(src, dst, send, recv, target):
    return pltpu.make_async_remote_copy(
        src_ref=src,
        dst_ref=dst,
        send_sem=send,
        recv_sem=recv,
        device_id=target,
        device_id_type=MESH,
    )


def gather_sems(chips):
    return [pltpu.SemaphoreType.DMA((3, 2, chips)), pltpu.SemaphoreType.DMA((3, 2, chips))]


def line_gather(line, x_ref, slot, send, recv, on_own, on_pair):
    chips = line.chips
    z, c = line.z, line.c
    line.barrier()

    def hop(stream, step, src, block, target):
        return remote(src, slot(block), send.at[stream, 0, step], recv.at[stream, 0, step], target)

    def across(way, step, src, block):
        return remote(src, slot(block), send.at[2, way, step], recv.at[2, way, step], line.sibling)

    @pl.when(line.has_up)
    def _():
        hop(0, 1, x_ref, line.mp, line.up).start()

    @pl.when(line.has_down)
    def _():
        hop(1, 1, x_ref, line.mp, line.down).start()

    across(0, 0, x_ref, line.mp).start()
    slot(line.mp)[...] = x_ref[...]
    on_own()
    across(0, 0, x_ref, line.mp).wait_recv()
    on_pair(z)
    for step in range(1, chips):
        below, above = z - step, z + step

        @pl.when(below >= 0)
        def _():
            block = 2 * below + c
            hop(0, step, slot(block), block, line.up).wait_recv()
            if step + 1 < chips:

                @pl.when(line.has_up)
                def _():
                    hop(0, step + 1, slot(block), block, line.up).start()

            across(0, step, slot(block), block).start()

        @pl.when(above < chips)
        def _():
            block = 2 * above + c
            hop(1, step, slot(block), block, line.down).wait_recv()
            if step + 1 < chips:

                @pl.when(line.has_down)
                def _():
                    hop(1, step + 1, slot(block), block, line.down).start()

            across(1, step, slot(block), block).start()

        @pl.when(below >= 0)
        def _():
            across(0, step, slot(2 * below + c), 2 * below + c).wait_recv()
            on_pair(below)

        @pl.when(above < chips)
        def _():
            across(1, step, slot(2 * above + c), 2 * above + c).wait_recv()
            on_pair(above)

    @pl.when(line.has_up)
    def _():
        hop(0, 1, x_ref, line.mp, line.up).wait_send()

    @pl.when(line.has_down)
    def _():
        hop(1, 1, x_ref, line.mp, line.down).wait_send()

    across(0, 0, x_ref, line.mp).wait_send()
    for step in range(1, chips):
        below, above = z - step, z + step

        @pl.when(below >= 0)
        def _():
            block = 2 * below + c
            if step + 1 < chips:

                @pl.when(line.has_up)
                def _():
                    hop(0, step + 1, slot(block), block, line.up).wait_send()

            across(0, step, slot(block), block).wait_send()

        @pl.when(above < chips)
        def _():
            block = 2 * above + c
            if step + 1 < chips:

                @pl.when(line.has_down)
                def _():
                    hop(1, step + 1, slot(block), block, line.down).wait_send()

            across(1, step, slot(block), block).wait_send()


def scatter_scratch(chips, rows, cols, parts):
    block = (chips, rows, cols)
    return [
        pltpu.VMEM(block, jnp.float32),
        pltpu.VMEM(block, jnp.bfloat16),
        pltpu.VMEM(block, jnp.bfloat16),
        pltpu.VMEM((2,) + block, jnp.bfloat16),
        pltpu.SemaphoreType.DMA((2, 3, chips, parts)),
    ]


def line_scatter(line, scratch, parts, produce, finish, tile):
    chips = line.chips
    z = line.z
    kept, out_ref, in_ref, moving, sems = scratch
    count = kept.shape[1] // parts
    line.barrier()

    def span(part):
        return pl.ds(part * count, count)

    def across(chip, part):
        return remote(
            out_ref.at[chip, span(part)],
            in_ref.at[chip, span(part)],
            sems.at[0, 0, chip, part],
            sems.at[1, 0, chip, part],
            line.sibling,
        )

    def hop(way, chip, part):
        target = line.up if way == 0 else line.down
        ref = moving.at[way, chip, span(part)]
        return remote(
            ref, ref, sems.at[0, 1 + way, chip, part], sems.at[1, 1 + way, chip, part], target
        )

    items = []
    for step in range(chips - 1):
        for part in range(parts):
            items.append((0, chips - 1 - step + z, part, step >= z))
            items.append((1, step - (chips - 1 - z), part, step >= chips - 1 - z))
    for part in range(parts):
        items.append((2, z, part, None))

    def run(active, body):
        if active is None:
            body()
        else:
            pl.when(active)(body)

    def start(item):
        way, chip, part, active = item

        def body():
            produce(chip, part, count, kept.at[chip], out_ref.at[chip])
            across(chip, part).start()

        run(active, body)

    def tiles(part, body):
        @pl.loop(0, count // tile)
        def _(index):
            body(pl.ds(pl.multiple_of(part * count + index * tile, tile), tile))

    def close(item):
        way, chip, part, active = item

        def body():
            across(chip, part).wait_recv()
            if way < 2:
                later = line.has_down if way == 0 else line.has_up

                @pl.when(later)
                def _():
                    hop(way, chip, part).wait_recv()

                    def add(rows):
                        moving[way, chip, rows] = (
                            kept[chip, rows]
                            + in_ref[chip, rows].astype(jnp.float32)
                            + moving[way, chip, rows].astype(jnp.float32)
                        ).astype(jnp.bfloat16)

                    tiles(part, add)

                @pl.when(jnp.logical_not(later))
                def _():
                    def add(rows):
                        moving[way, chip, rows] = (
                            kept[chip, rows] + in_ref[chip, rows].astype(jnp.float32)
                        ).astype(jnp.bfloat16)

                    tiles(part, add)

                hop(way, chip, part).start()
            else:

                def total(rows):
                    return kept[chip, rows] + in_ref[chip, rows].astype(jnp.float32)

                def from_side(side, rows):
                    return moving[side, chip, rows].astype(jnp.float32)

                both = jnp.logical_and(line.has_down, line.has_up)

                @pl.when(both)
                def _():
                    hop(0, chip, part).wait_recv()
                    hop(1, chip, part).wait_recv()
                    tiles(
                        part,
                        lambda rows: finish(
                            part, rows, total(rows) + from_side(0, rows) + from_side(1, rows)
                        ),
                    )

                for side, present in ((0, line.has_down), (1, line.has_up)):

                    @pl.when(jnp.logical_and(present, jnp.logical_not(both)))
                    def _():
                        hop(side, chip, part).wait_recv()
                        tiles(
                            part,
                            lambda rows: finish(part, rows, total(rows) + from_side(side, rows)),
                        )

        run(active, body)

    lag = 2
    for index, item in enumerate(items):
        start(item)
        if index >= lag:
            close(items[index - lag])
    for item in items[-lag:]:
        close(item)
    for way, chip, part, active in items:

        def body():
            across(chip, part).wait_send()
            if way < 2:
                hop(way, chip, part).wait_send()

        run(active, body)


def whole(count):
    return [pl.BlockSpec(memory_space=pltpu.VMEM)] * count


def comm_params(number):
    return pltpu.CompilerParams(
        collective_id=number, has_side_effects=True, vmem_limit_bytes=VMEM_BYTES
    )


def pick(c, low, high):
    return jnp.where(c == 0, low, high), jnp.where(c == 0, high, low)


def conv_scatter_kernel(chips, breadth, x_ref, w_ref, o_ref, *scratch):
    line = Line(chips)
    pixels, own = o_ref.shape
    tile = 512

    def produce(chip, part, count, mine, other):
        columns = pl.ds(pl.multiple_of(chip * 2 * own, 2 * own), 2 * own)

        @pl.loop(0, count // tile)
        def _(index):
            base = pl.multiple_of(part * count + index * tile, tile)
            total = jnp.zeros((tile, 2 * own), jnp.float32)
            for i in range(3):
                total += jnp.dot(
                    x_ref[pl.ds(base + i * breadth, tile)],
                    w_ref[i, :, columns],
                    preferred_element_type=jnp.float32,
                )
            first, second = pick(line.c, total[:, :own], total[:, own:])
            mine[pl.ds(base, tile)] = first
            other[pl.ds(base, tile)] = second.astype(jnp.bfloat16)

    def finish(part, rows, total):
        o_ref[rows] = total

    line_scatter(line, scratch, CONV_PARTS, produce, finish, tile)


def side_by_side(hidden):
    rows, cols, depth = hidden.shape
    padded = jnp.pad(hidden, ((1, 1), (1, 1), (0, 0)))
    return jnp.concatenate([padded[:, j : j + cols] for j in range(3)], axis=2).reshape(
        (rows + 2) * cols, 3 * depth
    )


def conv_scatter_fused(spread, kernel, cols, n, number):
    own = kernel.shape[2] // n
    depth = kernel.shape[1]
    pixels = spread.shape[0] - 2 * cols
    chips = n // 2
    return pl.pallas_call(
        partial(conv_scatter_kernel, chips, cols),
        out_shape=jax.ShapeDtypeStruct((pixels, own), jnp.float32),
        in_specs=whole(2),
        out_specs=whole(1)[0],
        scratch_shapes=scatter_scratch(chips, pixels, own, CONV_PARTS),
        compiler_params=comm_params(number),
    )(spread, kernel.reshape(3, 3 * depth, kernel.shape[2]))


def conv_back_kernel(chips, breadth, g_ref, w_ref, xt_ref, acc_ref, wg_ref, held, sums, send, recv):
    line = Line(chips)
    pixels, own = g_ref.shape
    wide = w_ref.shape[1]
    tile = 512
    zero = jnp.zeros((breadth, own), jnp.bfloat16)
    for block in range(2 * chips):
        held[block, pl.ds(0, breadth)] = zero
        held[block, pl.ds(breadth + pixels, breadth)] = zero

    def slot(block):
        return held.at[block, pl.ds(breadth, pixels)]

    def pair(chip, rows):
        return jnp.concatenate([held[2 * chip, rows], held[2 * chip + 1, rows]], axis=1)

    def on_own():
        @pl.loop(0, pixels // tile)
        def _(index):
            acc_ref[pl.ds(pl.multiple_of(index * tile, tile), tile)] = jnp.zeros(
                (tile, wide), jnp.float32
            )

    def on_pair(chip):
        columns = pl.ds(pl.multiple_of(chip * 2 * own, 2 * own), 2 * own)

        @pl.loop(0, pixels // tile)
        def _(index):
            base = pl.multiple_of(index * tile, tile)
            total = acc_ref[pl.ds(base, tile)]
            for i in range(3):
                total += lax.dot_general(
                    pair(chip, pl.ds(base + (2 - i) * breadth, tile)),
                    w_ref[i, :, columns],
                    (((1,), (1,)), ((), ())),
                    preferred_element_type=jnp.float32,
                )
            acc_ref[pl.ds(base, tile)] = total

        for i in range(3):
            sums[...] = jnp.zeros_like(sums)

            @pl.loop(0, pixels // tile)
            def _(index):
                base = pl.multiple_of(index * tile, tile)
                sums[...] += jnp.dot(
                    xt_ref[:, pl.ds(base + i * breadth, tile)],
                    pair(chip, pl.ds(base + breadth, tile)),
                    preferred_element_type=jnp.float32,
                )

            wg_ref[chip, i] = sums[...].astype(jnp.bfloat16)

    line_gather(line, g_ref, slot, send, recv, on_own, on_pair)


def conv_back_fused(grad_low, spread_turned, kernel, cols, n, number):
    pixels, own = grad_low.shape
    depth = kernel.shape[1]
    chips = n // 2
    return pl.pallas_call(
        partial(conv_back_kernel, chips, cols),
        out_shape=(
            jax.ShapeDtypeStruct((pixels, 3 * depth), jnp.float32),
            jax.ShapeDtypeStruct((chips, 3, 3 * depth, 2 * own), jnp.bfloat16),
        ),
        in_specs=whole(3),
        out_specs=tuple(whole(2)),
        scratch_shapes=[
            pltpu.VMEM((n, pixels + 2 * cols, own), jnp.bfloat16),
            pltpu.VMEM((3 * depth, 2 * own), jnp.float32),
        ]
        + gather_sems(chips),
        compiler_params=comm_params(number),
    )(grad_low, kernel.reshape(3, 3 * depth, kernel.shape[2]), spread_turned)


def join_columns(acc, cols):
    pixels, wide = acc.shape
    depth = wide // 3
    planes = acc.reshape(-1, cols, wide)
    none = jnp.zeros_like(planes[:, :1, :depth])
    left = jnp.concatenate([planes[:, 1:, :depth], none], axis=1)
    right = jnp.concatenate([none, planes[:, :-1, 2 * depth :]], axis=1)
    return (left + planes[:, :, depth : 2 * depth] + right).reshape(pixels, depth)


def product(x, w, turned):
    return lax.dot_general(
        x, w, (((1,), (1 if turned else 0,)), ((), ())), preferred_element_type=jnp.float32
    )


def tokens_scatter_kernel(chips, turned, x_ref, w_ref, o_ref, *scratch):
    line = Line(chips)
    tokens, width = o_ref.shape
    cut = width // TOKEN_PARTS
    depth = x_ref.shape[1] // w_ref.shape[0]

    def produce(chip, part, count, mine, other):
        rows = pl.ds(pl.multiple_of(chip * 2 * tokens, 2 * tokens), 2 * tokens)
        columns = pl.ds(part * cut, cut)
        total = None
        for j in range(w_ref.shape[0]):
            w = w_ref[j, columns] if turned else w_ref[j, :, columns]
            term = product(x_ref[rows, pl.ds(j * depth, depth)], w, turned)
            total = term if total is None else total + term
        first, second = pick(line.c, total[:tokens], total[tokens:])
        mine[pl.ds(part * count, count)] = first
        other[pl.ds(part * count, count)] = second.astype(jnp.bfloat16)

    def finish(part, rows, total):
        o_ref[:, pl.ds(part * cut, cut)] = total

    line_scatter(line, scratch, TOKEN_PARTS, produce, finish, tokens)


def tokens_scatter(x, w, turned, n, number):
    tokens = x.shape[0] // n
    width = w.shape[1] if turned else w.shape[2]
    chips = n // 2
    return pl.pallas_call(
        partial(tokens_scatter_kernel, chips, turned),
        out_shape=jax.ShapeDtypeStruct((tokens, width), jnp.float32),
        in_specs=whole(2),
        out_specs=whole(1)[0],
        scratch_shapes=scatter_scratch(chips, TOKEN_PARTS * tokens, width // TOKEN_PARTS, TOKEN_PARTS),
        compiler_params=comm_params(number),
    )(x, w)


def tokens_gather_kernel(chips, turned, shape_out, outs, x_ref, w_ref, *refs):
    line = Line(chips)
    held = refs[0]
    results = refs[1 : 1 + outs]
    send, recv = refs[1 + outs :]
    tokens = x_ref.shape[0]
    across = w_ref.shape[1 if turned else 2]
    cut = min(across, 512)

    def slot(block):
        return held.at[pl.ds(pl.multiple_of(block * tokens, tokens), tokens)]

    def on_pair(chip):
        rows = pl.ds(pl.multiple_of(chip * 2 * tokens, 2 * tokens), 2 * tokens)
        for j in range(w_ref.shape[0]):
            for start in range(0, across, cut):
                w = w_ref[j, pl.ds(start, cut)] if turned else w_ref[j, :, pl.ds(start, cut)]
                values = shape_out(product(held[rows], w, turned))
                for ref, value in zip(results, values):
                    ref[rows, pl.ds(j * across + start, cut)] = value.astype(ref.dtype)

    line_gather(line, x_ref, slot, send, recv, lambda: None, on_pair)


def tokens_gather(x, w, turned, kinds, shape_out, n, number):
    tokens, width = x.shape
    across = w.shape[0] * w.shape[1 if turned else 2]
    chips = n // 2
    return pl.pallas_call(
        partial(tokens_gather_kernel, chips, turned, shape_out, len(kinds)),
        out_shape=(jax.ShapeDtypeStruct((tokens * n, width), x.dtype),)
        + tuple(jax.ShapeDtypeStruct((tokens * n, across), kind) for kind in kinds),
        in_specs=whole(2),
        out_specs=tuple(whole(1 + len(kinds))),
        scratch_shapes=gather_sems(chips),
        compiler_params=comm_params(number),
    )(x, w)


def local(
    image,
    embedding,
    extents,
    gain_first,
    conv_first,
    gain_second,
    conv_second,
    shift_weight,
    down_weight,
    ada_weight,
    qkv_weight,
    out_weight,
    up_weight,
    proj_weight,
    cotangent,
):
    strip_rows, canvas_cols, channel_count = (image.shape[1], image.shape[2], image.shape[3])
    width_all = out_weight.shape[1]
    n = lax.axis_size("mp")
    m = lax.axis_size("dp")
    me_mp = lax.axis_index("mp")
    me_dp = lax.axis_index("dp")
    rows_all = strip_rows * n
    pixel_total = rows_all * canvas_cols
    own = channel_count // n
    size = channel_count // GROUPS
    token_rows = strip_rows // 2
    token_cols = canvas_cols // 2
    local_tokens = token_rows * token_cols
    token_total = local_tokens * n
    block_rows = min(512, token_total)
    local_width = out_weight.shape[0]
    head_count = local_width // HEAD_DIM

    shift_vector = jnp.dot(embedding, shift_weight, preferred_element_type=jnp.float32)[0]
    modulation = lax.all_gather(
        jnp.dot(embedding, ada_weight, preferred_element_type=jnp.float32), "mp", axis=1, tiled=True
    )
    scale_attend = modulation[0, :width_all]
    shift_attend = modulation[0, width_all : 2 * width_all]
    scale_mlp = modulation[0, 2 * width_all : 3 * width_all]
    shift_mlp = modulation[0, 3 * width_all :]
    own_first = lax.dynamic_slice_in_dim(gain_first, me_mp * own, own)
    own_second = lax.dynamic_slice_in_dim(gain_second, me_mp * own, own)

    pixels_low = lax.all_to_all(image[0], "mp", 2, 0, tiled=True)
    pixels = pixels_low.astype(jnp.float32).reshape(pixel_total, own)
    normed_first, inverse_first = group_forward(pixels, size)
    hidden_first = (
        jax.nn.silu(normed_first * own_first)
        .astype(jnp.bfloat16)
        .reshape(rows_all, canvas_cols, own)
    )
    fused = own % 128 == 0 and n == 2 * m
    spread_first = side_by_side(hidden_first)
    if fused:
        conv_output = conv_scatter_fused(spread_first, conv_first, canvas_cols, n, 0)
    else:
        conv_output = conv_scatter(hidden_first, conv_first, n)
    conv_output = conv_output + shift_vector
    normed_second, inverse_second = group_forward(conv_output, size)
    hidden_second = (
        jax.nn.silu(normed_second * own_second)
        .astype(jnp.bfloat16)
        .reshape(rows_all, canvas_cols, own)
    )
    spread_second = side_by_side(hidden_second)
    if fused:
        conv_again = conv_scatter_fused(spread_second, conv_second, canvas_cols, n, 1)
    else:
        conv_again = conv_scatter(hidden_second, conv_second, n)
    residual = pixels + conv_again
    down_patch = (
        residual.astype(jnp.bfloat16)
        .reshape(rows_all // 2, 2, token_cols, 2, own)
        .transpose(0, 2, 1, 3, 4)
        .reshape(token_total, 4 * own)
    )
    down_matrix = down_weight.reshape(4 * own, width_all)
    stream = tokens_scatter(down_patch, down_matrix[None], False, n, 2)
    normed_attend, inverse_attend = layer_forward(stream)
    input_attend = (normed_attend * (1.0 + scale_attend) + shift_attend).astype(jnp.bfloat16)
    all_attend, qkv_rows = tokens_gather(
        input_attend, qkv_weight, False, (jnp.bfloat16,), lambda value: (value,), n, 3
    )
    qkv_rows = qkv_rows.reshape(token_total, 3, head_count, HEAD_DIM)
    queries = qkv_rows[:, 0]
    key_rows = qkv_rows[:, 1]
    value_rows = qkv_rows[:, 2]
    token_index = jnp.arange(token_total, dtype=jnp.int32)
    key_valid = (token_index // token_cols < extents[0, 0]) & (
        token_index % token_cols < extents[0, 1]
    )
    mixed_heads, log_totals = attend_forward(queries, key_rows, value_rows, key_valid, block_rows)
    mixed_low = mixed_heads.reshape(token_total, local_width).astype(jnp.bfloat16)
    stream_mid = stream + tokens_scatter(mixed_low, out_weight[None], False, n, 4)
    normed_mlp, inverse_mlp = layer_forward(stream_mid)
    input_mlp = (normed_mlp * (1.0 + scale_mlp) + shift_mlp).astype(jnp.bfloat16)
    all_mlp, upper_proj, activated = tokens_gather(
        input_mlp,
        up_weight[None],
        False,
        (jnp.float32, jnp.bfloat16),
        lambda value: (value, jax.nn.gelu(value, approximate=True)),
        n,
        5,
    )
    final_stream = stream_mid + scatter_rows(
        jnp.dot(activated, proj_weight, preferred_element_type=jnp.float32)
    )
    output = final_stream.astype(jnp.bfloat16).reshape(1, token_rows, token_cols, width_all)

    grad_final_low = cotangent[0].reshape(local_tokens, width_all)
    grad_final = grad_final_low.astype(jnp.float32)
    all_final = gather_rows(grad_final_low)
    grad_act = jnp.einsum("le,fe->lf", all_final, proj_weight, preferred_element_type=jnp.float32)
    gelu_pull = jax.vjp(partial(jax.nn.gelu, approximate=True), upper_proj)[1]
    grad_upper = gelu_pull(grad_act)[0].astype(jnp.bfloat16)
    grad_normed_mlp = tokens_scatter(grad_upper, up_weight[None], True, n, 6)
    grad_proj = jnp.einsum("lf,le->fe", activated, all_final, preferred_element_type=jnp.float32)
    grad_up = jnp.einsum("le,lf->ef", all_mlp, grad_upper, preferred_element_type=jnp.float32)
    grad_mid_norm, grad_scale_mlp, grad_shift_mlp = layer_backward(
        grad_normed_mlp, normed_mlp, inverse_mlp, scale_mlp
    )
    grad_mid = grad_final + grad_mid_norm
    all_mid, grad_mixed_low = tokens_gather(
        grad_mid.astype(jnp.bfloat16),
        out_weight[None],
        True,
        (jnp.bfloat16,),
        lambda value: (value,),
        n,
        7,
    )
    grad_mixed_low = grad_mixed_low.reshape(token_total, head_count, HEAD_DIM)
    grad_out = jnp.einsum("lh,le->he", mixed_low, all_mid, preferred_element_type=jnp.float32)
    grad_query, grad_keys, grad_values = attend_backward(
        queries, key_rows, value_rows, key_valid, log_totals, grad_mixed_low, block_rows
    )
    grad_qkv = (
        jnp.stack([grad_query, grad_keys, grad_values], axis=1)
        .astype(jnp.bfloat16)
        .reshape(token_total, 3, local_width)
    )
    grad_normed_attend = tokens_scatter(
        grad_qkv.reshape(token_total, 3 * local_width), qkv_weight, True, n, 8
    )
    grad_qkv_weight = jnp.einsum(
        "le,ljf->jef", all_attend, grad_qkv, preferred_element_type=jnp.float32
    )
    grad_stream_norm, grad_scale_attend, grad_shift_attend = layer_backward(
        grad_normed_attend, normed_attend, inverse_attend, scale_attend
    )
    grad_stream = grad_mid + grad_stream_norm
    all_stream, grad_tap_patch = tokens_gather(
        grad_stream.astype(jnp.bfloat16),
        down_matrix[None],
        True,
        (jnp.float32,),
        lambda value: (value,),
        n,
        9,
    )
    grad_down = jnp.einsum(
        "lk,le->ke", down_patch, all_stream, preferred_element_type=jnp.float32
    ).reshape(4, own, width_all)
    grad_residual = (
        grad_tap_patch.reshape(rows_all // 2, token_cols, 2, 2, own)
        .transpose(0, 2, 1, 3, 4)
        .reshape(pixel_total, own)
    )
    def back(grad_low, hidden, spread, kernel, number):
        if fused:
            acc, parts = conv_back_fused(grad_low, spread.T, kernel, canvas_cols, n, number)
            return join_columns(acc, canvas_cols), parts.reshape(m, 9 * own, -1)
        grad_hidden, grad_kernel = conv_backward(grad_low, hidden, kernel, n)
        return grad_hidden, by_images(grad_kernel, m)

    grad_hidden_second, parts_second = back(
        grad_residual.astype(jnp.bfloat16), hidden_second, spread_second, conv_second, 10
    )
    grad_conv_output, grad_gain_second = group_backward(
        grad_hidden_second, normed_second, inverse_second, own_second, size
    )
    grad_shift = jnp.sum(grad_conv_output, axis=0)
    grad_hidden_first, parts_first = back(
        grad_conv_output.astype(jnp.bfloat16), hidden_first, spread_first, conv_first, 11
    )
    grad_base, grad_gain_first = group_backward(
        grad_hidden_first, normed_first, inverse_first, own_first, size
    )
    image_turned = (grad_residual + grad_base).astype(jnp.bfloat16)
    image_grad = lax.all_to_all(
        image_turned.reshape(rows_all, canvas_cols, own), "mp", 0, 2, tiled=True
    )[None]

    grad_modulation = jnp.concatenate(
        [grad_scale_attend, grad_shift_attend, grad_scale_mlp, grad_shift_mlp]
    )
    ada_columns = lax.psum_scatter(
        grad_modulation[None].astype(jnp.bfloat16), "mp", scatter_dimension=1, tiled=True
    ).astype(jnp.float32)
    embed_float = embedding.astype(jnp.float32)
    embed_term = jnp.dot(
        grad_shift[None], shift_weight.astype(jnp.float32).T, precision=PRECISE
    ) + jnp.dot(ada_columns, ada_weight.astype(jnp.float32).T, precision=PRECISE)
    embedding_grad = lax.psum(embed_term, "mp")
    packed = jnp.concatenate([embed_float[0], grad_shift, ada_columns[0]])
    every = lax.all_gather(packed, "dp", axis=0)
    embed_count = embedding.shape[1]
    embed_rows = lax.dynamic_slice_in_dim(
        every[:, :embed_count], me_dp * (embed_count // m), embed_count // m, axis=1
    )
    grad_shift_weight = jnp.dot(
        embed_rows.T, every[:, embed_count : embed_count + own], precision=PRECISE
    )
    grad_ada_weight = jnp.dot(embed_rows.T, every[:, embed_count + own :], precision=PRECISE)
    gains = lax.all_gather(jnp.stack([grad_gain_first, grad_gain_second]), ("dp", "mp"), axis=0)
    gains = jnp.sum(gains.reshape(m, n, 2, own), axis=0).transpose(1, 0, 2).reshape(2, -1)
    piece = channel_count // (m * n)
    gains = lax.dynamic_slice_in_dim(gains, (me_dp * n + me_mp) * piece, piece, axis=1)
    return (
        output,
        image_grad,
        embedding_grad,
        gains[0],
        turn_kernel(parts_first, 9, m, n),
        gains[1],
        turn_kernel(parts_second, 9, m, n),
        grad_shift_weight,
        turn_kernel(by_images(grad_down, m), 4, m, n),
        grad_ada_weight,
        dp_rows(grad_qkv_weight, 1),
        dp_rows(grad_out, 1),
        dp_rows(grad_up, 0),
        dp_rows(grad_proj, 1),
    )


def solution(mesh):
    placed = (
        P("dp", "mp", None, None),
        P("dp", None),
        P("dp", None),
        P(),
        P(None, "mp", None),
        P(),
        P(None, "mp", None),
        P(None, "mp"),
        P(None, "mp", None),
        P(None, "mp"),
        P(None, None, "mp"),
        P("mp", None),
        P(None, "mp"),
        P("mp", None),
        P("dp", "mp", None, None),
    )
    return jax.shard_map(
        local,
        mesh=mesh,
        in_specs=placed,
        out_specs=(
            P("dp", "mp", None, None),
            P("dp", "mp", None, None),
            P("dp", None),
            P(("dp", "mp")),
            P(None, "dp", "mp"),
            P(("dp", "mp")),
            P(None, "dp", "mp"),
            P("dp", "mp"),
            P(None, "dp", "mp"),
            P("dp", "mp"),
            P(None, "dp", "mp"),
            P("mp", "dp"),
            P("dp", "mp"),
            P("mp", "dp"),
        ),
        check_vma=False,
    )
```

```python
from functools import partial
import math

import jax
import jax.numpy as jnp
from jax import lax
from jax.experimental import pallas as pl
from jax.experimental.pallas import tpu as pltpu
from jax.sharding import PartitionSpec as P

HEAD_DIM = 128
GROUPS = 32


GROUP_EPSILON = 1e-05
LAYER_EPSILON = 1e-06
MASKED_SCORE = -1000000000.0
PRECISE = lax.Precision.HIGHEST


def group_spread(per_channel, size):
    grouped = jnp.sum(per_channel.reshape(-1, size), axis=1)
    return jnp.repeat(grouped, size)


def group_forward(values, size):
    counted = values.shape[0] * size
    average = group_spread(jnp.sum(values, axis=0), size) / counted
    centre = values - average
    inverse = lax.rsqrt(
        group_spread(jnp.sum(centre * centre, axis=0), size) / counted + GROUP_EPSILON
    )
    return (centre * inverse, inverse)


def group_backward(incoming, normed, inverse, gain_vec, size):
    pre_act = normed * gain_vec
    sigmoid_part = jax.nn.sigmoid(pre_act)
    through = incoming * sigmoid_part * (1.0 + pre_act * (1.0 - sigmoid_part))
    counted = normed.shape[0] * size
    gain_part = jnp.sum(through * normed, axis=0)
    plain_part = jnp.sum(through, axis=0)
    first_mean = group_spread(plain_part * gain_vec, size) / counted
    second_mean = group_spread(gain_part * gain_vec, size) / counted
    outgoing = inverse * (through * gain_vec - first_mean - normed * second_mean)
    return (outgoing, gain_part)


def windows(planes, flipped):
    row_count, col_count, depth = planes.shape
    padded = jnp.pad(planes, ((1, 1), (1, 1), (0, 0)))
    pieces = []
    for tap_index in range(9):
        row_off, col_off = divmod(tap_index, 3)
        if flipped:
            row_off, col_off = (2 - row_off, 2 - col_off)
        pieces.append(padded[row_off : row_off + row_count, col_off : col_off + col_count])
    return jnp.stack(pieces, axis=2).reshape(row_count * col_count, 9, depth)


def gather_rows(rows):
    return lax.all_gather(rows, "mp", axis=0, tiled=True)


def scatter_rows(rows):
    return lax.psum_scatter(
        rows.astype(jnp.bfloat16), "mp", scatter_dimension=0, tiled=True
    ).astype(jnp.float32)


def conv_scatter(hidden, kernel, n):
    patch = windows(hidden, False)
    depth = kernel.shape[2] // n
    total = jnp.einsum("ptc,tcd->pd", patch, kernel, preferred_element_type=jnp.float32)
    parts = total.astype(jnp.bfloat16).reshape(-1, n, depth).transpose(1, 0, 2)
    return lax.psum_scatter(parts, "mp", scatter_dimension=0, tiled=False).astype(jnp.float32)


def conv_backward(grad_low, hidden, kernel, n):
    row_count, col_count, depth = hidden.shape
    gathered = lax.all_gather(grad_low, "mp", axis=1, tiled=True)
    padded = jnp.pad(gathered, ((col_count, col_count), (0, 0)))
    taps = kernel.reshape(3, 3 * depth, kernel.shape[2])
    acc = sum(
        jnp.einsum(
            "pd,td->pt",
            padded[(2 - i) * col_count : (2 - i) * col_count + row_count * col_count],
            taps[i],
            preferred_element_type=jnp.float32,
        )
        for i in range(3)
    )
    grad_kernel = jnp.einsum(
        "ptc,pd->tcd", windows(hidden, False), gathered, preferred_element_type=jnp.float32
    )
    return (join_columns(acc, col_count), grad_kernel)


def by_images(grad, m):
    taps, own, outs = grad.shape
    return grad.astype(jnp.bfloat16).reshape(taps * own, m, outs // m).transpose(1, 0, 2)


def turn_kernel(mine, taps, m, n):
    own = mine.shape[0] // taps
    outs = mine.shape[1] * m
    ratio = n // m
    pieces = mine.astype(jnp.bfloat16).reshape(taps, own, ratio, outs // n)
    me = lax.axis_index("mp") % ratio
    result = jnp.zeros((taps, ratio, own, outs // n), jnp.bfloat16)
    for shift in range(ratio):
        route = []
        for i in range(m):
            for j in range(n):
                target = (j // ratio) * n + ratio * i + (j % ratio + shift) % ratio
                route.append((i * n + j, target))
        half = lax.dynamic_index_in_dim(pieces, (me + shift) % ratio, axis=2, keepdims=False)
        moved = lax.ppermute(half, ("dp", "mp"), route)
        place = (me - shift + ratio) % ratio
        result = lax.dynamic_update_slice(result, moved[:, None], (0, place, 0, 0))
    return result.reshape(taps, ratio * own, outs // n).astype(jnp.float32)


def added(received):
    return jnp.sum(received.astype(jnp.float32), axis=0)


def layer_forward(stream):
    centre = stream - jnp.mean(stream, axis=1, keepdims=True)
    inverse = lax.rsqrt(jnp.mean(centre * centre, axis=1, keepdims=True) + LAYER_EPSILON)
    return (centre * inverse, inverse)


def layer_backward(incoming, normed, inverse, scale_vec):
    through = incoming * (1.0 + scale_vec)
    outgoing = inverse * (
        through
        - jnp.mean(through, axis=1, keepdims=True)
        - normed * jnp.mean(through * normed, axis=1, keepdims=True)
    )
    return (outgoing, jnp.sum(incoming * normed, axis=0), jnp.sum(incoming, axis=0))


def attend_forward(queries, key_rows, value_rows, key_valid, block_rows):
    score_scale = 1.0 / math.sqrt(queries.shape[-1])

    def one_block(query_block):
        raw_scores = jnp.einsum(
            "qhd,khd->hqk", query_block, key_rows, preferred_element_type=jnp.float32
        )
        logits = jnp.where(key_valid[None, None, :], raw_scores * score_scale, MASKED_SCORE)
        peak_score = jnp.max(logits, axis=-1, keepdims=True)
        exponent = jnp.exp(logits - peak_score)
        totals = jnp.sum(exponent, axis=-1, keepdims=True)
        mix_weights = (exponent / totals).astype(jnp.bfloat16)
        mixed_heads = jnp.einsum(
            "hqk,khd->qhd", mix_weights, value_rows, preferred_element_type=jnp.float32
        )
        return (mixed_heads, (peak_score + jnp.log(totals))[..., 0])

    blocks = queries.reshape(-1, block_rows, queries.shape[1], queries.shape[2])
    mixed_heads, log_totals = lax.map(one_block, blocks)
    return (mixed_heads.reshape(queries.shape), log_totals)


def attend_backward(queries, key_rows, value_rows, key_valid, log_totals, grad_mixed, block_rows):
    score_scale = 1.0 / math.sqrt(queries.shape[-1])
    block_shape = (-1, block_rows, queries.shape[1], queries.shape[2])

    def one_block(running, inputs):
        grad_keys, grad_values = running
        query_block, grad_block, log_block = inputs
        raw_scores = jnp.einsum(
            "qhd,khd->hqk", query_block, key_rows, preferred_element_type=jnp.float32
        )
        logits = jnp.where(key_valid[None, None, :], raw_scores * score_scale, MASKED_SCORE)
        mix_weights = jnp.exp(logits - log_block[..., None])
        grad_weights = jnp.einsum(
            "qhd,khd->hqk", grad_block, value_rows, preferred_element_type=jnp.float32
        )
        inner_sum = jnp.sum(mix_weights * grad_weights, axis=-1, keepdims=True)
        grad_scores = (mix_weights * (grad_weights - inner_sum) * score_scale).astype(jnp.bfloat16)
        grad_query = jnp.einsum(
            "hqk,khd->qhd", grad_scores, key_rows, preferred_element_type=jnp.float32
        )
        grad_keys = grad_keys + jnp.einsum(
            "hqk,qhd->khd", grad_scores, query_block, preferred_element_type=jnp.float32
        )
        grad_values = grad_values + jnp.einsum(
            "hqk,qhd->khd",
            mix_weights.astype(jnp.bfloat16),
            grad_block,
            preferred_element_type=jnp.float32,
        )
        return ((grad_keys, grad_values), grad_query)

    zero_rows = jnp.zeros(key_rows.shape, jnp.float32)
    (grad_keys, grad_values), grad_query = lax.scan(
        one_block,
        (zero_rows, zero_rows),
        (queries.reshape(block_shape), grad_mixed.reshape(block_shape), log_totals),
    )
    return (grad_query.reshape(queries.shape), grad_keys, grad_values)


MESH = pl.DeviceIdType.MESH
CONV_PARTS = 4
TOKEN_PARTS = 4
VMEM_BYTES = 60 * 1024 * 1024


class Line:
    def __init__(self, chips, images):
        self.chips = chips
        self.images = images
        self.dp = lax.axis_index("dp")
        self.mp = lax.axis_index("mp")
        self.z = self.mp // 2
        self.c = self.mp % 2
        self.has_up = self.z < chips - 1
        self.has_down = self.z > 0
        self.up = (self.dp, self.mp + 2)
        self.down = (self.dp, self.mp - 2)
        self.sibling = (self.dp, 2 * self.z + 1 - self.c)

    def count(self, axis):
        return {"dp": self.images, "mp": 2 * self.chips, "all": 2 * self.chips * self.images}[axis]

    def index(self, axis):
        return {"dp": self.dp, "mp": self.mp, "all": self.dp * 2 * self.chips + self.mp}[axis]

    def place(self, axis, index):
        if axis == "dp":
            return (index, self.mp)
        if axis == "mp":
            return (self.dp, index)
        return (index // (2 * self.chips), index % (2 * self.chips))

    def peer(self, axis, step):
        return lax.rem(self.index(axis) + step, self.count(axis))

    def barrier(self, axes, neighbours):
        bar = pltpu.get_barrier_semaphore()
        if "all" in axes:
            axes = ("all",)
        steady = 0
        for axis in axes:
            for step in range(1, self.count(axis)):
                target = self.place(axis, self.peer(axis, step))
                pl.semaphore_signal(bar, inc=1, device_id=target, device_id_type=MESH)
            steady += self.count(axis) - 1
        if "all" in axes or "mp" in axes or not neighbours:
            pl.semaphore_wait(bar, steady)
            return
        pl.semaphore_signal(bar, inc=1, device_id=self.sibling, device_id_type=MESH)

        @pl.when(self.has_up)
        def _():
            pl.semaphore_signal(bar, inc=1, device_id=self.up, device_id_type=MESH)

        @pl.when(self.has_down)
        def _():
            pl.semaphore_signal(bar, inc=1, device_id=self.down, device_id_type=MESH)

        middle = jnp.logical_and(self.has_up, self.has_down)

        @pl.when(middle)
        def _():
            pl.semaphore_wait(bar, steady + 3)

        @pl.when(jnp.logical_not(middle))
        def _():
            pl.semaphore_wait(bar, steady + 2)


class Rider:
    def __init__(self, axis, array, cut=None):
        self.axis = axis
        self.array = array
        self.cut = cut

    def result(self, count):
        shape = list(self.array.shape)
        if self.cut is not None:
            shape[self.cut] //= count
        return jax.ShapeDtypeStruct((count,) + tuple(shape), self.array.dtype)

    def piece(self, ref, index, count):
        if self.cut is None:
            return ref
        size = self.array.shape[self.cut] // count
        where = [slice(None)] * len(self.array.shape)
        where[self.cut] = pl.ds(pl.multiple_of(index * size, size), size)
        return ref.at[tuple(where)]

    def copies(self, line, src, dst, send, recv):
        count, me = line.count(self.axis), line.index(self.axis)
        made = [pltpu.make_async_copy(self.piece(src, me, count), dst.at[me], send.at[0])]
        for step in range(1, count):
            peer = line.peer(self.axis, step)
            made.append(
                remote(
                    self.piece(src, peer, count),
                    dst.at[me],
                    send.at[step],
                    recv.at[step],
                    line.place(self.axis, peer),
                )
            )
        return made


def comm_call(kernel, inputs, out_shapes, scratch, riders, n, m, number, neighbours=True):
    chips = n // 2
    sizes = {"dp": m, "mp": n, "all": m * n}
    counts = [sizes[rider.axis] for rider in riders]
    ride_shapes = tuple(rider.result(count) for rider, count in zip(riders, counts))
    any_spec = pl.BlockSpec(memory_space=pl.ANY)
    ni, nr, no = len(inputs), len(riders), len(out_shapes)

    def body(*refs):
        main_in, ride_in = refs[:ni], refs[ni : ni + nr]
        rest = refs[ni + nr :]
        main_out, ride_out = rest[:no], rest[no : no + nr]
        rest = rest[no + nr :]
        main_scratch, sems = rest[: len(scratch)], rest[len(scratch) :]
        line = Line(chips, m)
        line.barrier(sorted(set(rider.axis for rider in riders)), neighbours)
        copies = []
        for index, rider in enumerate(riders):
            copies += rider.copies(
                line, ride_in[index], ride_out[index], sems[2 * index], sems[2 * index + 1]
            )
        for copy in copies:
            copy.start()
        kernel(line, *main_in, *main_out, *main_scratch)
        for copy in copies:
            copy.wait()

    ride_sems = []
    for count in counts:
        ride_sems += [pltpu.SemaphoreType.DMA((count,)), pltpu.SemaphoreType.DMA((count,))]
    return pl.pallas_call(
        body,
        out_shape=tuple(out_shapes) + ride_shapes,
        in_specs=whole(ni) + [any_spec] * nr,
        out_specs=tuple(whole(no) + [any_spec] * nr),
        scratch_shapes=list(scratch) + ride_sems,
        compiler_params=comm_params(number),
    )(*inputs, *[rider.array for rider in riders])


def remote(src, dst, send, recv, target):
    return pltpu.make_async_remote_copy(
        src_ref=src,
        dst_ref=dst,
        send_sem=send,
        recv_sem=recv,
        device_id=target,
        device_id_type=MESH,
    )


def gather_sems(chips):
    return [pltpu.SemaphoreType.DMA((3, 2, chips)), pltpu.SemaphoreType.DMA((3, 2, chips))]


def line_gather(line, x_ref, slot, send, recv, on_own, on_pair):
    chips = line.chips
    z, c = line.z, line.c

    def hop(stream, step, src, block, target):
        return remote(src, slot(block), send.at[stream, 0, step], recv.at[stream, 0, step], target)

    def across(way, step, src, block):
        return remote(src, slot(block), send.at[2, way, step], recv.at[2, way, step], line.sibling)

    @pl.when(line.has_up)
    def _():
        hop(0, 1, x_ref, line.mp, line.up).start()

    @pl.when(line.has_down)
    def _():
        hop(1, 1, x_ref, line.mp, line.down).start()

    across(0, 0, x_ref, line.mp).start()
    slot(line.mp)[...] = x_ref[...]
    on_own()
    across(0, 0, x_ref, line.mp).wait_recv()
    on_pair(z)
    for step in range(1, chips):
        below, above = z - step, z + step

        @pl.when(below >= 0)
        def _():
            block = 2 * below + c
            hop(0, step, slot(block), block, line.up).wait_recv()
            if step + 1 < chips:

                @pl.when(line.has_up)
                def _():
                    hop(0, step + 1, slot(block), block, line.up).start()

            across(0, step, slot(block), block).start()

        @pl.when(above < chips)
        def _():
            block = 2 * above + c
            hop(1, step, slot(block), block, line.down).wait_recv()
            if step + 1 < chips:

                @pl.when(line.has_down)
                def _():
                    hop(1, step + 1, slot(block), block, line.down).start()

            across(1, step, slot(block), block).start()

        @pl.when(below >= 0)
        def _():
            across(0, step, slot(2 * below + c), 2 * below + c).wait_recv()
            on_pair(below)

        @pl.when(above < chips)
        def _():
            across(1, step, slot(2 * above + c), 2 * above + c).wait_recv()
            on_pair(above)

    @pl.when(line.has_up)
    def _():
        hop(0, 1, x_ref, line.mp, line.up).wait_send()

    @pl.when(line.has_down)
    def _():
        hop(1, 1, x_ref, line.mp, line.down).wait_send()

    across(0, 0, x_ref, line.mp).wait_send()
    for step in range(1, chips):
        below, above = z - step, z + step

        @pl.when(below >= 0)
        def _():
            block = 2 * below + c
            if step + 1 < chips:

                @pl.when(line.has_up)
                def _():
                    hop(0, step + 1, slot(block), block, line.up).wait_send()

            across(0, step, slot(block), block).wait_send()

        @pl.when(above < chips)
        def _():
            block = 2 * above + c
            if step + 1 < chips:

                @pl.when(line.has_down)
                def _():
                    hop(1, step + 1, slot(block), block, line.down).wait_send()

            across(1, step, slot(block), block).wait_send()


def scatter_scratch(chips, rows, cols, parts):
    block = (chips, rows, cols)
    return [
        pltpu.VMEM(block, jnp.float32),
        pltpu.VMEM(block, jnp.bfloat16),
        pltpu.VMEM(block, jnp.bfloat16),
        pltpu.VMEM((2,) + block, jnp.bfloat16),
        pltpu.SemaphoreType.DMA((2, 3, chips, parts)),
    ]


def line_scatter(line, scratch, parts, produce, finish, tile):
    chips = line.chips
    z = line.z
    kept, out_ref, in_ref, moving, sems = scratch
    count = kept.shape[1] // parts

    def span(part):
        return pl.ds(part * count, count)

    def across(chip, part):
        return remote(
            out_ref.at[chip, span(part)],
            in_ref.at[chip, span(part)],
            sems.at[0, 0, chip, part],
            sems.at[1, 0, chip, part],
            line.sibling,
        )

    def hop(way, chip, part):
        target = line.up if way == 0 else line.down
        ref = moving.at[way, chip, span(part)]
        return remote(
            ref, ref, sems.at[0, 1 + way, chip, part], sems.at[1, 1 + way, chip, part], target
        )

    items = []
    for step in range(chips - 1):
        for part in range(parts):
            items.append((0, chips - 1 - step + z, part, step >= z))
            items.append((1, step - (chips - 1 - z), part, step >= chips - 1 - z))
    for part in range(parts):
        items.append((2, z, part, None))

    def run(active, body):
        if active is None:
            body()
        else:
            pl.when(active)(body)

    def start(item):
        way, chip, part, active = item

        def body():
            produce(chip, part, count, kept.at[chip], out_ref.at[chip])
            across(chip, part).start()

        run(active, body)

    def tiles(part, body):
        @pl.loop(0, count // tile)
        def _(index):
            body(pl.ds(pl.multiple_of(part * count + index * tile, tile), tile))

    def close(item):
        way, chip, part, active = item

        def body():
            across(chip, part).wait_recv()
            if way < 2:
                later = line.has_down if way == 0 else line.has_up

                @pl.when(later)
                def _():
                    hop(way, chip, part).wait_recv()

                    def add(rows):
                        moving[way, chip, rows] = (
                            kept[chip, rows]
                            + in_ref[chip, rows].astype(jnp.float32)
                            + moving[way, chip, rows].astype(jnp.float32)
                        ).astype(jnp.bfloat16)

                    tiles(part, add)

                @pl.when(jnp.logical_not(later))
                def _():
                    def add(rows):
                        moving[way, chip, rows] = (
                            kept[chip, rows] + in_ref[chip, rows].astype(jnp.float32)
                        ).astype(jnp.bfloat16)

                    tiles(part, add)

                hop(way, chip, part).start()
            else:

                def total(rows):
                    return kept[chip, rows] + in_ref[chip, rows].astype(jnp.float32)

                def from_side(side, rows):
                    return moving[side, chip, rows].astype(jnp.float32)

                both = jnp.logical_and(line.has_down, line.has_up)

                @pl.when(both)
                def _():
                    hop(0, chip, part).wait_recv()
                    hop(1, chip, part).wait_recv()
                    tiles(
                        part,
                        lambda rows: finish(
                            part, rows, total(rows) + from_side(0, rows) + from_side(1, rows)
                        ),
                    )

                for side, present in ((0, line.has_down), (1, line.has_up)):

                    @pl.when(jnp.logical_and(present, jnp.logical_not(both)))
                    def _():
                        hop(side, chip, part).wait_recv()
                        tiles(
                            part,
                            lambda rows: finish(part, rows, total(rows) + from_side(side, rows)),
                        )

        run(active, body)

    lag = 2
    for index, item in enumerate(items):
        start(item)
        if index >= lag:
            close(items[index - lag])
    for item in items[-lag:]:
        close(item)
    for way, chip, part, active in items:

        def body():
            across(chip, part).wait_send()
            if way < 2:
                hop(way, chip, part).wait_send()

        run(active, body)


def whole(count):
    return [pl.BlockSpec(memory_space=pltpu.VMEM)] * count


def comm_params(number):
    return pltpu.CompilerParams(
        collective_id=number, has_side_effects=True, vmem_limit_bytes=VMEM_BYTES
    )


def pick(c, low, high):
    return jnp.where(c == 0, low, high), jnp.where(c == 0, high, low)


def conv_scatter_kernel(breadth, line, x_ref, w_ref, o_ref, *scratch):
    pixels, own = o_ref.shape
    tile = 512

    def produce(chip, part, count, mine, other):
        columns = pl.ds(pl.multiple_of(chip * 2 * own, 2 * own), 2 * own)

        @pl.loop(0, count // tile)
        def _(index):
            base = pl.multiple_of(part * count + index * tile, tile)
            total = jnp.zeros((tile, 2 * own), jnp.float32)
            for i in range(3):
                total += jnp.dot(
                    x_ref[pl.ds(base + i * breadth, tile)],
                    w_ref[i, :, columns],
                    preferred_element_type=jnp.float32,
                )
            first, second = pick(line.c, total[:, :own], total[:, own:])
            mine[pl.ds(base, tile)] = first
            other[pl.ds(base, tile)] = second.astype(jnp.bfloat16)

    def finish(part, rows, total):
        o_ref[rows] = total

    line_scatter(line, scratch, CONV_PARTS, produce, finish, tile)


def side_by_side(hidden):
    rows, cols, depth = hidden.shape
    padded = jnp.pad(hidden, ((1, 1), (1, 1), (0, 0)))
    return jnp.concatenate([padded[:, j : j + cols] for j in range(3)], axis=2).reshape(
        (rows + 2) * cols, 3 * depth
    )


def conv_scatter_fused(spread, kernel, cols, n, m, number, riders=()):
    own = kernel.shape[2] // n
    depth = kernel.shape[1]
    pixels = spread.shape[0] - 2 * cols
    return comm_call(
        partial(conv_scatter_kernel, cols),
        (spread, kernel.reshape(3, 3 * depth, kernel.shape[2])),
        (jax.ShapeDtypeStruct((pixels, own), jnp.float32),),
        scatter_scratch(n // 2, pixels, own, CONV_PARTS),
        riders,
        n,
        m,
        number,
    )


def conv_back_kernel(breadth, line, g_ref, w_ref, xt_ref, acc_ref, wg_ref, held, sums, send, recv):
    chips = line.chips
    pixels, own = g_ref.shape
    wide = w_ref.shape[1]
    tile = 512
    zero = jnp.zeros((breadth, own), jnp.bfloat16)
    for block in range(2 * chips):
        held[block, pl.ds(0, breadth)] = zero
        held[block, pl.ds(breadth + pixels, breadth)] = zero

    def slot(block):
        return held.at[block, pl.ds(breadth, pixels)]

    def pair(chip, rows):
        return jnp.concatenate([held[2 * chip, rows], held[2 * chip + 1, rows]], axis=1)

    def on_own():
        @pl.loop(0, pixels // tile)
        def _(index):
            acc_ref[pl.ds(pl.multiple_of(index * tile, tile), tile)] = jnp.zeros(
                (tile, wide), jnp.float32
            )

    def on_pair(chip):
        columns = pl.ds(pl.multiple_of(chip * 2 * own, 2 * own), 2 * own)

        @pl.loop(0, pixels // tile)
        def _(index):
            base = pl.multiple_of(index * tile, tile)
            total = acc_ref[pl.ds(base, tile)]
            for i in range(3):
                total += lax.dot_general(
                    pair(chip, pl.ds(base + (2 - i) * breadth, tile)),
                    w_ref[i, :, columns],
                    (((1,), (1,)), ((), ())),
                    preferred_element_type=jnp.float32,
                )
            acc_ref[pl.ds(base, tile)] = total

        for i in range(3):
            sums[...] = jnp.zeros_like(sums)

            @pl.loop(0, pixels // tile)
            def _(index):
                base = pl.multiple_of(index * tile, tile)
                sums[...] += jnp.dot(
                    xt_ref[:, pl.ds(base + i * breadth, tile)],
                    pair(chip, pl.ds(base + breadth, tile)),
                    preferred_element_type=jnp.float32,
                )

            wg_ref[chip, i] = sums[...].astype(jnp.bfloat16)

    line_gather(line, g_ref, slot, send, recv, on_own, on_pair)


def conv_back_fused(grad_low, spread_turned, kernel, cols, n, m, number, riders=()):
    pixels, own = grad_low.shape
    depth = kernel.shape[1]
    chips = n // 2
    return comm_call(
        partial(conv_back_kernel, cols),
        (grad_low, kernel.reshape(3, 3 * depth, kernel.shape[2]), spread_turned),
        (
            jax.ShapeDtypeStruct((pixels, 3 * depth), jnp.float32),
            jax.ShapeDtypeStruct((chips, 3, 3 * depth, 2 * own), jnp.bfloat16),
        ),
        [
            pltpu.VMEM((n, pixels + 2 * cols, own), jnp.bfloat16),
            pltpu.VMEM((3 * depth, 2 * own), jnp.float32),
        ]
        + gather_sems(chips),
        riders,
        n,
        m,
        number,
    )


def join_columns(acc, cols):
    pixels, wide = acc.shape
    depth = wide // 3
    planes = acc.reshape(-1, cols, wide)
    none = jnp.zeros_like(planes[:, :1, :depth])
    left = jnp.concatenate([planes[:, 1:, :depth], none], axis=1)
    right = jnp.concatenate([none, planes[:, :-1, 2 * depth :]], axis=1)
    return (left + planes[:, :, depth : 2 * depth] + right).reshape(pixels, depth)


def product(x, w, turned):
    return lax.dot_general(
        x, w, (((1,), (1 if turned else 0,)), ((), ())), preferred_element_type=jnp.float32
    )


def tokens_scatter_kernel(turned, line, x_ref, w_ref, o_ref, *scratch):
    tokens, width = o_ref.shape
    cut = width // TOKEN_PARTS
    depth = x_ref.shape[1] // w_ref.shape[0]

    def produce(chip, part, count, mine, other):
        rows = pl.ds(pl.multiple_of(chip * 2 * tokens, 2 * tokens), 2 * tokens)
        columns = pl.ds(part * cut, cut)
        total = None
        for j in range(w_ref.shape[0]):
            w = w_ref[j, columns] if turned else w_ref[j, :, columns]
            term = product(x_ref[rows, pl.ds(j * depth, depth)], w, turned)
            total = term if total is None else total + term
        first, second = pick(line.c, total[:tokens], total[tokens:])
        mine[pl.ds(part * count, count)] = first
        other[pl.ds(part * count, count)] = second.astype(jnp.bfloat16)

    def finish(part, rows, total):
        o_ref[:, pl.ds(part * cut, cut)] = total

    line_scatter(line, scratch, TOKEN_PARTS, produce, finish, tokens)


def tokens_scatter(x, w, turned, n, m, number, riders=()):
    tokens = x.shape[0] // n
    width = w.shape[1] if turned else w.shape[2]
    return comm_call(
        partial(tokens_scatter_kernel, turned),
        (x, w),
        (jax.ShapeDtypeStruct((tokens, width), jnp.float32),),
        scatter_scratch(n // 2, TOKEN_PARTS * tokens, width // TOKEN_PARTS, TOKEN_PARTS),
        riders,
        n,
        m,
        number,
    )


def tokens_gather_kernel(turned, shape_out, outs, line, x_ref, w_ref, *refs):
    held = refs[0]
    results = refs[1 : 1 + outs]
    send, recv = refs[1 + outs :]
    tokens = x_ref.shape[0]
    across = w_ref.shape[1 if turned else 2]
    cut = min(across, 512)

    def slot(block):
        return held.at[pl.ds(pl.multiple_of(block * tokens, tokens), tokens)]

    def on_pair(chip):
        rows = pl.ds(pl.multiple_of(chip * 2 * tokens, 2 * tokens), 2 * tokens)
        for j in range(w_ref.shape[0]):
            for start in range(0, across, cut):
                w = w_ref[j, pl.ds(start, cut)] if turned else w_ref[j, :, pl.ds(start, cut)]
                values = shape_out(product(held[rows], w, turned))
                for ref, value in zip(results, values):
                    ref[rows, pl.ds(j * across + start, cut)] = value.astype(ref.dtype)

    line_gather(line, x_ref, slot, send, recv, lambda: None, on_pair)


def tokens_gather(x, w, turned, kinds, shape_out, n, m, number, riders=()):
    tokens, width = x.shape
    across = w.shape[0] * w.shape[1 if turned else 2]
    return comm_call(
        partial(tokens_gather_kernel, turned, shape_out, len(kinds)),
        (x, w),
        (jax.ShapeDtypeStruct((tokens * n, width), x.dtype),)
        + tuple(jax.ShapeDtypeStruct((tokens * n, across), kind) for kind in kinds),
        gather_sems(n // 2),
        riders,
        n,
        m,
        number,
    )


def exchange(riders, n, m, number):
    return comm_call(lambda line: None, (), (), [], riders, n, m, number, neighbours=False)


def tiled_up(vector):
    count = -(-vector.shape[0] // 1024) * 1024
    return jnp.pad(vector.astype(jnp.float32), (0, count - vector.shape[0])).reshape(-1, 128)


def local(
    image,
    embedding,
    extents,
    gain_first,
    conv_first,
    gain_second,
    conv_second,
    shift_weight,
    down_weight,
    ada_weight,
    qkv_weight,
    out_weight,
    up_weight,
    proj_weight,
    cotangent,
):
    strip_rows, canvas_cols, channel_count = (image.shape[1], image.shape[2], image.shape[3])
    width_all = out_weight.shape[1]
    n = lax.axis_size("mp")
    m = lax.axis_size("dp")
    me_mp = lax.axis_index("mp")
    me_dp = lax.axis_index("dp")
    rows_all = strip_rows * n
    pixel_total = rows_all * canvas_cols
    own = channel_count // n
    size = channel_count // GROUPS
    token_rows = strip_rows // 2
    token_cols = canvas_cols // 2
    local_tokens = token_rows * token_cols
    token_total = local_tokens * n
    block_rows = min(512, token_total)
    local_width = out_weight.shape[0]
    head_count = local_width // HEAD_DIM

    fused = own % 128 == 0 and n == 2 * m
    shift_vector = jnp.dot(embedding, shift_weight, preferred_element_type=jnp.float32)[0]
    columns = jnp.dot(embedding, ada_weight, preferred_element_type=jnp.float32)[0]
    riders = (Rider("mp", tiled_up(columns)),)
    if fused:
        modulation, pixels_low = exchange(
            riders + (Rider("mp", image[0].reshape(-1, channel_count), 1),), n, m, 12
        )
    else:
        (modulation,) = exchange(riders, n, m, 12)
        pixels_low = lax.all_to_all(image[0], "mp", 2, 0, tiled=True)
    modulation = modulation.reshape(n, -1)[:, : columns.shape[0]].reshape(-1)
    scale_attend = modulation[:width_all]
    shift_attend = modulation[width_all : 2 * width_all]
    scale_mlp = modulation[2 * width_all : 3 * width_all]
    shift_mlp = modulation[3 * width_all :]
    own_first = lax.dynamic_slice_in_dim(gain_first, me_mp * own, own)
    own_second = lax.dynamic_slice_in_dim(gain_second, me_mp * own, own)

    pixels = pixels_low.astype(jnp.float32).reshape(pixel_total, own)
    normed_first, inverse_first = group_forward(pixels, size)
    hidden_first = (
        jax.nn.silu(normed_first * own_first)
        .astype(jnp.bfloat16)
        .reshape(rows_all, canvas_cols, own)
    )
    spread_first = side_by_side(hidden_first)
    if fused:
        (conv_output,) = conv_scatter_fused(spread_first, conv_first, canvas_cols, n, m, 0)
    else:
        conv_output = conv_scatter(hidden_first, conv_first, n)
    conv_output = conv_output + shift_vector
    normed_second, inverse_second = group_forward(conv_output, size)
    hidden_second = (
        jax.nn.silu(normed_second * own_second)
        .astype(jnp.bfloat16)
        .reshape(rows_all, canvas_cols, own)
    )
    spread_second = side_by_side(hidden_second)
    if fused:
        (conv_again,) = conv_scatter_fused(spread_second, conv_second, canvas_cols, n, m, 1)
    else:
        conv_again = conv_scatter(hidden_second, conv_second, n)
    residual = pixels + conv_again
    down_patch = (
        residual.astype(jnp.bfloat16)
        .reshape(rows_all // 2, 2, token_cols, 2, own)
        .transpose(0, 2, 1, 3, 4)
        .reshape(token_total, 4 * own)
    )
    down_matrix = down_weight.reshape(4 * own, width_all)
    (stream,) = tokens_scatter(down_patch, down_matrix[None], False, n, m, 2)
    normed_attend, inverse_attend = layer_forward(stream)
    input_attend = (normed_attend * (1.0 + scale_attend) + shift_attend).astype(jnp.bfloat16)
    all_attend, qkv_rows = tokens_gather(
        input_attend, qkv_weight, False, (jnp.bfloat16,), lambda value: (value,), n, m, 3
    )
    qkv_rows = qkv_rows.reshape(token_total, 3, head_count, HEAD_DIM)
    queries = qkv_rows[:, 0]
    key_rows = qkv_rows[:, 1]
    value_rows = qkv_rows[:, 2]
    token_index = jnp.arange(token_total, dtype=jnp.int32)
    key_valid = (token_index // token_cols < extents[0, 0]) & (
        token_index % token_cols < extents[0, 1]
    )
    mixed_heads, log_totals = attend_forward(queries, key_rows, value_rows, key_valid, block_rows)
    mixed_low = mixed_heads.reshape(token_total, local_width).astype(jnp.bfloat16)
    (attended,) = tokens_scatter(mixed_low, out_weight[None], False, n, m, 4)
    stream_mid = stream + attended
    normed_mlp, inverse_mlp = layer_forward(stream_mid)
    input_mlp = (normed_mlp * (1.0 + scale_mlp) + shift_mlp).astype(jnp.bfloat16)
    all_mlp, upper_proj, activated = tokens_gather(
        input_mlp,
        up_weight[None],
        False,
        (jnp.float32, jnp.bfloat16),
        lambda value: (value, jax.nn.gelu(value, approximate=True)),
        n,
        m,
        5,
    )
    final_stream = stream_mid + scatter_rows(
        jnp.dot(activated, proj_weight, preferred_element_type=jnp.float32)
    )
    output = final_stream.astype(jnp.bfloat16).reshape(1, token_rows, token_cols, width_all)

    grad_final_low = cotangent[0].reshape(local_tokens, width_all)
    grad_final = grad_final_low.astype(jnp.float32)
    all_final = gather_rows(grad_final_low)
    grad_act = jnp.einsum("le,fe->lf", all_final, proj_weight, preferred_element_type=jnp.float32)
    gelu_pull = jax.vjp(partial(jax.nn.gelu, approximate=True), upper_proj)[1]
    grad_upper = gelu_pull(grad_act)[0].astype(jnp.bfloat16)
    grad_proj = jnp.einsum("lf,le->fe", activated, all_final, preferred_element_type=jnp.float32)
    grad_normed_mlp, sums_proj = tokens_scatter(
        grad_upper,
        up_weight[None],
        True,
        n,
        m,
        6,
        (Rider("dp", grad_proj.astype(jnp.bfloat16), 1),),
    )
    grad_up = jnp.einsum("le,lf->ef", all_mlp, grad_upper, preferred_element_type=jnp.float32)
    grad_mid_norm, grad_scale_mlp, grad_shift_mlp = layer_backward(
        grad_normed_mlp, normed_mlp, inverse_mlp, scale_mlp
    )
    grad_mid = grad_final + grad_mid_norm
    all_mid, grad_mixed_low, sums_up = tokens_gather(
        grad_mid.astype(jnp.bfloat16),
        out_weight[None],
        True,
        (jnp.bfloat16,),
        lambda value: (value,),
        n,
        m,
        7,
        (Rider("dp", grad_up.astype(jnp.bfloat16), 0),),
    )
    grad_mixed_low = grad_mixed_low.reshape(token_total, head_count, HEAD_DIM)
    grad_out = jnp.einsum("lh,le->he", mixed_low, all_mid, preferred_element_type=jnp.float32)
    grad_query, grad_keys, grad_values = attend_backward(
        queries, key_rows, value_rows, key_valid, log_totals, grad_mixed_low, block_rows
    )
    grad_qkv = (
        jnp.stack([grad_query, grad_keys, grad_values], axis=1)
        .astype(jnp.bfloat16)
        .reshape(token_total, 3, local_width)
    )
    grad_qkv = grad_qkv.reshape(token_total, 3 * local_width)
    grad_normed_attend, sums_out = tokens_scatter(
        grad_qkv, qkv_weight, True, n, m, 8, (Rider("dp", grad_out.astype(jnp.bfloat16), 1),)
    )
    grad_qkv_weight = jnp.einsum(
        "le,lf->ef", all_attend, grad_qkv, preferred_element_type=jnp.float32
    )
    grad_stream_norm, grad_scale_attend, grad_shift_attend = layer_backward(
        grad_normed_attend, normed_attend, inverse_attend, scale_attend
    )
    grad_stream = grad_mid + grad_stream_norm
    grad_modulation = jnp.concatenate(
        [
            tiled_up(piece)
            for piece in jnp.concatenate(
                [grad_scale_attend, grad_shift_attend, grad_scale_mlp, grad_shift_mlp]
            ).reshape(n, -1)
        ]
    )
    all_stream, grad_tap_patch, sums_qkv, ada_columns = tokens_gather(
        grad_stream.astype(jnp.bfloat16),
        down_matrix[None],
        True,
        (jnp.float32,),
        lambda value: (value,),
        n,
        m,
        9,
        (
            Rider("dp", grad_qkv_weight.astype(jnp.bfloat16), 0),
            Rider("mp", grad_modulation, 0),
        ),
    )
    grad_down = jnp.einsum(
        "lk,le->ke", down_patch, all_stream, preferred_element_type=jnp.float32
    )
    ada_columns = added(ada_columns).reshape(-1)[: columns.shape[0]]
    grad_residual = (
        grad_tap_patch.reshape(rows_all // 2, token_cols, 2, 2, own)
        .transpose(0, 2, 1, 3, 4)
        .reshape(pixel_total, own)
    )
    def back(grad_low, hidden, spread, kernel, number, riders):
        if fused:
            acc, parts, *ridden = conv_back_fused(
                grad_low, spread.T, kernel, canvas_cols, n, m, number, riders
            )
            return join_columns(acc, canvas_cols), parts.reshape(m, 9 * own, -1), ridden
        grad_hidden, grad_kernel = conv_backward(grad_low, hidden, kernel, n)
        return grad_hidden, by_images(grad_kernel, m), exchange(riders, n, m, number)

    grad_hidden_second, parts_second, (sums_down, every_small) = back(
        grad_residual.astype(jnp.bfloat16),
        hidden_second,
        spread_second,
        conv_second,
        10,
        (
            Rider("dp", grad_down.astype(jnp.bfloat16), 1),
            Rider("dp", jnp.concatenate([tiled_up(embedding[0]), tiled_up(ada_columns)])),
        ),
    )
    grad_conv_output, grad_gain_second = group_backward(
        grad_hidden_second, normed_second, inverse_second, own_second, size
    )
    grad_shift = jnp.sum(grad_conv_output, axis=0)
    grad_hidden_first, parts_first, (sums_second, every_shift) = back(
        grad_conv_output.astype(jnp.bfloat16),
        hidden_first,
        spread_first,
        conv_first,
        11,
        (Rider("dp", parts_second, 0), Rider("dp", tiled_up(grad_shift))),
    )
    grad_base, grad_gain_first = group_backward(
        grad_hidden_first, normed_first, inverse_first, own_first, size
    )
    image_turned = (grad_residual + grad_base).astype(jnp.bfloat16)
    embed_term = jnp.dot(
        grad_shift[None], shift_weight.astype(jnp.float32).T, precision=PRECISE
    ) + jnp.dot(ada_columns[None], ada_weight.astype(jnp.float32).T, precision=PRECISE)
    small = jnp.concatenate(
        [tiled_up(embed_term[0]), tiled_up(jnp.concatenate([grad_gain_first, grad_gain_second]))]
    )
    riders = (Rider("dp", parts_first, 0), Rider("all", small))
    if fused:
        sums_first, small, image_turned = exchange(
            riders + (Rider("mp", image_turned, 0),), n, m, 13
        )
        image_grad = image_turned.transpose(1, 0, 2).reshape(image.shape)
    else:
        sums_first, small = exchange(riders, n, m, 13)
        image_grad = lax.all_to_all(
            image_turned.reshape(rows_all, canvas_cols, own), "mp", 0, 2, tiled=True
        )[None]

    small = small.reshape(m, n, -1)
    embed_count = embedding.shape[1]
    embedding_grad = jnp.sum(
        lax.dynamic_index_in_dim(small, me_dp, axis=0, keepdims=False)[:, :embed_count], axis=0
    )[None]
    gain_start = -(-embed_count // 1024) * 1024
    gains = jnp.sum(small[:, :, gain_start : gain_start + 2 * own], axis=0)
    gains = gains.reshape(n, 2, own).transpose(1, 0, 2).reshape(2, -1)
    piece = channel_count // (m * n)
    gains = lax.dynamic_slice_in_dim(gains, (me_dp * n + me_mp) * piece, piece, axis=1)
    every_small = every_small.reshape(m, -1)
    embed_rows = lax.dynamic_slice_in_dim(
        every_small[:, :embed_count], me_dp * (embed_count // m), embed_count // m, axis=1
    )
    grad_shift_weight = jnp.dot(
        embed_rows.T, every_shift.reshape(m, -1)[:, :own], precision=PRECISE
    )
    grad_ada_weight = jnp.dot(
        embed_rows.T,
        every_small[:, gain_start : gain_start + columns.shape[0]],
        precision=PRECISE,
    )
    qkv_grad = added(sums_qkv).reshape(-1, 3, local_width).transpose(1, 0, 2)
    return (
        output,
        image_grad,
        embedding_grad,
        gains[0],
        turn_kernel(added(sums_first)[0], 9, m, n),
        gains[1],
        turn_kernel(added(sums_second)[0], 9, m, n),
        grad_shift_weight,
        turn_kernel(added(sums_down), 4, m, n),
        grad_ada_weight,
        qkv_grad,
        added(sums_out),
        added(sums_up),
        added(sums_proj),
    )


def solution(mesh):
    placed = (
        P("dp", "mp", None, None),
        P("dp", None),
        P("dp", None),
        P(),
        P(None, "mp", None),
        P(),
        P(None, "mp", None),
        P(None, "mp"),
        P(None, "mp", None),
        P(None, "mp"),
        P(None, None, "mp"),
        P("mp", None),
        P(None, "mp"),
        P("mp", None),
        P("dp", "mp", None, None),
    )
    return jax.shard_map(
        local,
        mesh=mesh,
        in_specs=placed,
        out_specs=(
            P("dp", "mp", None, None),
            P("dp", "mp", None, None),
            P("dp", None),
            P(("dp", "mp")),
            P(None, "dp", "mp"),
            P(("dp", "mp")),
            P(None, "dp", "mp"),
            P("dp", "mp"),
            P(None, "dp", "mp"),
            P("dp", "mp"),
            P(None, "dp", "mp"),
            P("mp", "dp"),
            P("dp", "mp"),
            P("mp", "dp"),
        ),
        check_vma=False,
    )
```

```python
from functools import partial
import math

import jax
import jax.numpy as jnp
from jax import lax
from jax.experimental import pallas as pl
from jax.experimental.pallas import tpu as pltpu
from jax.sharding import PartitionSpec as P

HEAD_DIM = 128
GROUPS = 32


GROUP_EPSILON = 1e-05
LAYER_EPSILON = 1e-06
MASKED_SCORE = -1000000000.0
PRECISE = lax.Precision.HIGHEST


def group_spread(per_channel, size):
    grouped = jnp.sum(per_channel.reshape(-1, size), axis=1)
    return jnp.repeat(grouped, size)


def group_forward(values, size):
    counted = values.shape[0] * size
    average = group_spread(jnp.sum(values, axis=0), size) / counted
    centre = values - average
    inverse = lax.rsqrt(
        group_spread(jnp.sum(centre * centre, axis=0), size) / counted + GROUP_EPSILON
    )
    return (centre * inverse, inverse)


def group_backward(incoming, normed, inverse, gain_vec, size):
    pre_act = normed * gain_vec
    sigmoid_part = jax.nn.sigmoid(pre_act)
    through = incoming * sigmoid_part * (1.0 + pre_act * (1.0 - sigmoid_part))
    counted = normed.shape[0] * size
    gain_part = jnp.sum(through * normed, axis=0)
    plain_part = jnp.sum(through, axis=0)
    first_mean = group_spread(plain_part * gain_vec, size) / counted
    second_mean = group_spread(gain_part * gain_vec, size) / counted
    outgoing = inverse * (through * gain_vec - first_mean - normed * second_mean)
    return (outgoing, gain_part)


def windows(planes, flipped):
    row_count, col_count, depth = planes.shape
    padded = jnp.pad(planes, ((1, 1), (1, 1), (0, 0)))
    pieces = []
    for tap_index in range(9):
        row_off, col_off = divmod(tap_index, 3)
        if flipped:
            row_off, col_off = (2 - row_off, 2 - col_off)
        pieces.append(padded[row_off : row_off + row_count, col_off : col_off + col_count])
    return jnp.stack(pieces, axis=2).reshape(row_count * col_count, 9, depth)


def gather_rows(rows):
    return lax.all_gather(rows, "mp", axis=0, tiled=True)


def scatter_rows(rows):
    return lax.psum_scatter(
        rows.astype(jnp.bfloat16), "mp", scatter_dimension=0, tiled=True
    ).astype(jnp.float32)


def conv_scatter(hidden, kernel, n):
    patch = windows(hidden, False)
    depth = kernel.shape[2] // n
    total = jnp.einsum("ptc,tcd->pd", patch, kernel, preferred_element_type=jnp.float32)
    parts = total.astype(jnp.bfloat16).reshape(-1, n, depth).transpose(1, 0, 2)
    return lax.psum_scatter(parts, "mp", scatter_dimension=0, tiled=False).astype(jnp.float32)


def conv_backward(grad_low, hidden, kernel, n):
    row_count, col_count, depth = hidden.shape
    gathered = lax.all_gather(grad_low, "mp", axis=1, tiled=True)
    padded = jnp.pad(gathered, ((col_count, col_count), (0, 0)))
    taps = kernel.reshape(3, 3 * depth, kernel.shape[2])
    acc = sum(
        jnp.einsum(
            "pd,td->pt",
            padded[(2 - i) * col_count : (2 - i) * col_count + row_count * col_count],
            taps[i],
            preferred_element_type=jnp.float32,
        )
        for i in range(3)
    )
    grad_kernel = jnp.einsum(
        "ptc,pd->tcd", windows(hidden, False), gathered, preferred_element_type=jnp.float32
    )
    return (join_columns(acc, col_count), grad_kernel)


def by_images(grad, m):
    taps, own, outs = grad.shape
    return grad.astype(jnp.bfloat16).reshape(taps * own, m, outs // m).transpose(1, 0, 2)


def turn_kernel(mine, taps, m, n):
    own = mine.shape[0] // taps
    outs = mine.shape[1] * m
    ratio = n // m
    pieces = mine.astype(jnp.bfloat16).reshape(taps, own, ratio, outs // n)
    me = lax.axis_index("mp") % ratio
    result = jnp.zeros((taps, ratio, own, outs // n), jnp.bfloat16)
    for shift in range(ratio):
        route = []
        for i in range(m):
            for j in range(n):
                target = (j // ratio) * n + ratio * i + (j % ratio + shift) % ratio
                route.append((i * n + j, target))
        half = lax.dynamic_index_in_dim(pieces, (me + shift) % ratio, axis=2, keepdims=False)
        moved = lax.ppermute(half, ("dp", "mp"), route)
        place = (me - shift + ratio) % ratio
        result = lax.dynamic_update_slice(result, moved[:, None], (0, place, 0, 0))
    return result.reshape(taps, ratio * own, outs // n).astype(jnp.float32)


def added(received):
    return jnp.sum(received.astype(jnp.float32), axis=0)


def layer_forward(stream):
    centre = stream - jnp.mean(stream, axis=1, keepdims=True)
    inverse = lax.rsqrt(jnp.mean(centre * centre, axis=1, keepdims=True) + LAYER_EPSILON)
    return (centre * inverse, inverse)


def layer_backward(incoming, normed, inverse, scale_vec):
    through = incoming * (1.0 + scale_vec)
    outgoing = inverse * (
        through
        - jnp.mean(through, axis=1, keepdims=True)
        - normed * jnp.mean(through * normed, axis=1, keepdims=True)
    )
    return (outgoing, jnp.sum(incoming * normed, axis=0), jnp.sum(incoming, axis=0))


MESH = pl.DeviceIdType.MESH
CONV_PARTS = 4
TOKEN_PARTS = 4
VMEM_BYTES = 60 * 1024 * 1024


class Line:
    def __init__(self, chips, images):
        self.chips = chips
        self.images = images
        self.dp = lax.axis_index("dp")
        self.mp = lax.axis_index("mp")
        self.z = self.mp // 2
        self.c = self.mp % 2
        self.has_up = self.z < chips - 1
        self.has_down = self.z > 0
        self.up = (self.dp, self.mp + 2)
        self.down = (self.dp, self.mp - 2)
        self.sibling = (self.dp, 2 * self.z + 1 - self.c)

    def count(self, axis):
        return {"dp": self.images, "mp": 2 * self.chips, "all": 2 * self.chips * self.images}[axis]

    def index(self, axis):
        return {"dp": self.dp, "mp": self.mp, "all": self.dp * 2 * self.chips + self.mp}[axis]

    def place(self, axis, index):
        if axis == "dp":
            return (index, self.mp)
        if axis == "mp":
            return (self.dp, index)
        return (index // (2 * self.chips), index % (2 * self.chips))

    def peer(self, axis, step):
        return lax.rem(self.index(axis) + step, self.count(axis))

    def barrier(self, axes, neighbours):
        bar = pltpu.get_barrier_semaphore()
        if "all" in axes:
            axes = ("all",)
        steady = 0
        for axis in axes:
            for step in range(1, self.count(axis)):
                target = self.place(axis, self.peer(axis, step))
                pl.semaphore_signal(bar, inc=1, device_id=target, device_id_type=MESH)
            steady += self.count(axis) - 1
        if "all" in axes or "mp" in axes or not neighbours:
            pl.semaphore_wait(bar, steady)
            return
        pl.semaphore_signal(bar, inc=1, device_id=self.sibling, device_id_type=MESH)

        @pl.when(self.has_up)
        def _():
            pl.semaphore_signal(bar, inc=1, device_id=self.up, device_id_type=MESH)

        @pl.when(self.has_down)
        def _():
            pl.semaphore_signal(bar, inc=1, device_id=self.down, device_id_type=MESH)

        middle = jnp.logical_and(self.has_up, self.has_down)

        @pl.when(middle)
        def _():
            pl.semaphore_wait(bar, steady + 3)

        @pl.when(jnp.logical_not(middle))
        def _():
            pl.semaphore_wait(bar, steady + 2)


class Rider:
    def __init__(self, axis, array, cut=None):
        self.axis = axis
        self.array = array
        self.cut = cut

    def result(self, count):
        shape = list(self.array.shape)
        if self.cut is not None:
            shape[self.cut] //= count
        return jax.ShapeDtypeStruct((count,) + tuple(shape), self.array.dtype)

    def piece(self, ref, index, count):
        if self.cut is None:
            return ref
        size = self.array.shape[self.cut] // count
        where = [slice(None)] * len(self.array.shape)
        where[self.cut] = pl.ds(pl.multiple_of(index * size, size), size)
        return ref.at[tuple(where)]

    def copies(self, line, src, dst, send, recv):
        count, me = line.count(self.axis), line.index(self.axis)
        made = [pltpu.make_async_copy(self.piece(src, me, count), dst.at[me], send.at[0])]
        for step in range(1, count):
            peer = line.peer(self.axis, step)
            made.append(
                remote(
                    self.piece(src, peer, count),
                    dst.at[me],
                    send.at[step],
                    recv.at[step],
                    line.place(self.axis, peer),
                )
            )
        return made


def comm_call(kernel, inputs, out_shapes, scratch, riders, n, m, number, neighbours=True):
    chips = n // 2
    sizes = {"dp": m, "mp": n, "all": m * n}
    counts = [sizes[rider.axis] for rider in riders]
    ride_shapes = tuple(rider.result(count) for rider, count in zip(riders, counts))
    any_spec = pl.BlockSpec(memory_space=pl.ANY)
    ni, nr, no = len(inputs), len(riders), len(out_shapes)

    def body(*refs):
        main_in, ride_in = refs[:ni], refs[ni : ni + nr]
        rest = refs[ni + nr :]
        main_out, ride_out = rest[:no], rest[no : no + nr]
        rest = rest[no + nr :]
        main_scratch, sems = rest[: len(scratch)], rest[len(scratch) :]
        line = Line(chips, m)
        line.barrier(sorted(set(rider.axis for rider in riders)), neighbours)
        copies = []
        for index, rider in enumerate(riders):
            copies += rider.copies(
                line, ride_in[index], ride_out[index], sems[2 * index], sems[2 * index + 1]
            )
        for copy in copies:
            copy.start()
        kernel(line, *main_in, *main_out, *main_scratch)
        for copy in copies:
            copy.wait()

    ride_sems = []
    for count in counts:
        ride_sems += [pltpu.SemaphoreType.DMA((count,)), pltpu.SemaphoreType.DMA((count,))]
    return pl.pallas_call(
        body,
        out_shape=tuple(out_shapes) + ride_shapes,
        in_specs=whole(ni) + [any_spec] * nr,
        out_specs=tuple(whole(no) + [any_spec] * nr),
        scratch_shapes=list(scratch) + ride_sems,
        compiler_params=comm_params(number),
    )(*inputs, *[rider.array for rider in riders])


def remote(src, dst, send, recv, target):
    return pltpu.make_async_remote_copy(
        src_ref=src,
        dst_ref=dst,
        send_sem=send,
        recv_sem=recv,
        device_id=target,
        device_id_type=MESH,
    )


def gather_sems(chips):
    return [pltpu.SemaphoreType.DMA((3, 2, chips)), pltpu.SemaphoreType.DMA((3, 2, chips))]


def line_gather(line, x_ref, slot, send, recv, on_own, on_pair):
    chips = line.chips
    z, c = line.z, line.c

    def hop(stream, step, src, block, target):
        return remote(src, slot(block), send.at[stream, 0, step], recv.at[stream, 0, step], target)

    def across(way, step, src, block):
        return remote(src, slot(block), send.at[2, way, step], recv.at[2, way, step], line.sibling)

    @pl.when(line.has_up)
    def _():
        hop(0, 1, x_ref, line.mp, line.up).start()

    @pl.when(line.has_down)
    def _():
        hop(1, 1, x_ref, line.mp, line.down).start()

    across(0, 0, x_ref, line.mp).start()
    slot(line.mp)[...] = x_ref[...]
    on_own()
    across(0, 0, x_ref, line.mp).wait_recv()
    on_pair(z)
    for step in range(1, chips):
        below, above = z - step, z + step

        @pl.when(below >= 0)
        def _():
            block = 2 * below + c
            hop(0, step, slot(block), block, line.up).wait_recv()
            if step + 1 < chips:

                @pl.when(line.has_up)
                def _():
                    hop(0, step + 1, slot(block), block, line.up).start()

            across(0, step, slot(block), block).start()

        @pl.when(above < chips)
        def _():
            block = 2 * above + c
            hop(1, step, slot(block), block, line.down).wait_recv()
            if step + 1 < chips:

                @pl.when(line.has_down)
                def _():
                    hop(1, step + 1, slot(block), block, line.down).start()

            across(1, step, slot(block), block).start()

        @pl.when(below >= 0)
        def _():
            across(0, step, slot(2 * below + c), 2 * below + c).wait_recv()
            on_pair(below)

        @pl.when(above < chips)
        def _():
            across(1, step, slot(2 * above + c), 2 * above + c).wait_recv()
            on_pair(above)

    @pl.when(line.has_up)
    def _():
        hop(0, 1, x_ref, line.mp, line.up).wait_send()

    @pl.when(line.has_down)
    def _():
        hop(1, 1, x_ref, line.mp, line.down).wait_send()

    across(0, 0, x_ref, line.mp).wait_send()
    for step in range(1, chips):
        below, above = z - step, z + step

        @pl.when(below >= 0)
        def _():
            block = 2 * below + c
            if step + 1 < chips:

                @pl.when(line.has_up)
                def _():
                    hop(0, step + 1, slot(block), block, line.up).wait_send()

            across(0, step, slot(block), block).wait_send()

        @pl.when(above < chips)
        def _():
            block = 2 * above + c
            if step + 1 < chips:

                @pl.when(line.has_down)
                def _():
                    hop(1, step + 1, slot(block), block, line.down).wait_send()

            across(1, step, slot(block), block).wait_send()


def scatter_scratch(chips, rows, cols, parts):
    block = (chips, rows, cols)
    return [
        pltpu.VMEM(block, jnp.float32),
        pltpu.VMEM(block, jnp.bfloat16),
        pltpu.VMEM(block, jnp.bfloat16),
        pltpu.VMEM((2,) + block, jnp.bfloat16),
        pltpu.SemaphoreType.DMA((2, 3, chips, parts)),
    ]


def line_scatter(line, scratch, parts, produce, finish, tile):
    chips = line.chips
    z = line.z
    kept, out_ref, in_ref, moving, sems = scratch
    count = kept.shape[1] // parts

    def span(part):
        return pl.ds(part * count, count)

    def across(chip, part):
        return remote(
            out_ref.at[chip, span(part)],
            in_ref.at[chip, span(part)],
            sems.at[0, 0, chip, part],
            sems.at[1, 0, chip, part],
            line.sibling,
        )

    def hop(way, chip, part):
        target = line.up if way == 0 else line.down
        ref = moving.at[way, chip, span(part)]
        return remote(
            ref, ref, sems.at[0, 1 + way, chip, part], sems.at[1, 1 + way, chip, part], target
        )

    items = []
    for step in range(chips - 1):
        for part in range(parts):
            items.append((0, chips - 1 - step + z, part, step >= z))
            items.append((1, step - (chips - 1 - z), part, step >= chips - 1 - z))
    for part in range(parts):
        items.append((2, z, part, None))

    def run(active, body):
        if active is None:
            body()
        else:
            pl.when(active)(body)

    def start(item):
        way, chip, part, active = item

        def body():
            produce(chip, part, count, kept.at[chip], out_ref.at[chip])
            across(chip, part).start()

        run(active, body)

    def tiles(part, body):
        @pl.loop(0, count // tile)
        def _(index):
            body(pl.ds(pl.multiple_of(part * count + index * tile, tile), tile))

    def close(item):
        way, chip, part, active = item

        def body():
            across(chip, part).wait_recv()
            if way < 2:
                later = line.has_down if way == 0 else line.has_up

                @pl.when(later)
                def _():
                    hop(way, chip, part).wait_recv()

                    def add(rows):
                        moving[way, chip, rows] = (
                            kept[chip, rows]
                            + in_ref[chip, rows].astype(jnp.float32)
                            + moving[way, chip, rows].astype(jnp.float32)
                        ).astype(jnp.bfloat16)

                    tiles(part, add)

                @pl.when(jnp.logical_not(later))
                def _():
                    def add(rows):
                        moving[way, chip, rows] = (
                            kept[chip, rows] + in_ref[chip, rows].astype(jnp.float32)
                        ).astype(jnp.bfloat16)

                    tiles(part, add)

                hop(way, chip, part).start()
            else:

                def total(rows):
                    return kept[chip, rows] + in_ref[chip, rows].astype(jnp.float32)

                def from_side(side, rows):
                    return moving[side, chip, rows].astype(jnp.float32)

                both = jnp.logical_and(line.has_down, line.has_up)

                @pl.when(both)
                def _():
                    hop(0, chip, part).wait_recv()
                    hop(1, chip, part).wait_recv()
                    tiles(
                        part,
                        lambda rows: finish(
                            part, rows, total(rows) + from_side(0, rows) + from_side(1, rows)
                        ),
                    )

                for side, present in ((0, line.has_down), (1, line.has_up)):

                    @pl.when(jnp.logical_and(present, jnp.logical_not(both)))
                    def _():
                        hop(side, chip, part).wait_recv()
                        tiles(
                            part,
                            lambda rows: finish(part, rows, total(rows) + from_side(side, rows)),
                        )

        run(active, body)

    lag = 2
    for index, item in enumerate(items):
        start(item)
        if index >= lag:
            close(items[index - lag])
    for item in items[-lag:]:
        close(item)
    for way, chip, part, active in items:

        def body():
            across(chip, part).wait_send()
            if way < 2:
                hop(way, chip, part).wait_send()

        run(active, body)


def whole(count):
    return [pl.BlockSpec(memory_space=pltpu.VMEM)] * count


def comm_params(number):
    return pltpu.CompilerParams(
        collective_id=number, has_side_effects=True, vmem_limit_bytes=VMEM_BYTES
    )


def pick(c, low, high):
    return jnp.where(c == 0, low, high), jnp.where(c == 0, high, low)


def conv_scatter_kernel(breadth, line, x_ref, w_ref, o_ref, *scratch):
    pixels, own = o_ref.shape
    tile = 512

    def produce(chip, part, count, mine, other):
        columns = pl.ds(pl.multiple_of(chip * 2 * own, 2 * own), 2 * own)

        @pl.loop(0, count // tile)
        def _(index):
            base = pl.multiple_of(part * count + index * tile, tile)
            total = jnp.zeros((tile, 2 * own), jnp.float32)
            for i in range(3):
                total += jnp.dot(
                    x_ref[pl.ds(base + i * breadth, tile)],
                    w_ref[i, :, columns],
                    preferred_element_type=jnp.float32,
                )
            first, second = pick(line.c, total[:, :own], total[:, own:])
            mine[pl.ds(base, tile)] = first
            other[pl.ds(base, tile)] = second.astype(jnp.bfloat16)

    def finish(part, rows, total):
        o_ref[rows] = total

    line_scatter(line, scratch, CONV_PARTS, produce, finish, tile)


def side_by_side(hidden):
    rows, cols, depth = hidden.shape
    padded = jnp.pad(hidden, ((1, 1), (1, 1), (0, 0)))
    return jnp.concatenate([padded[:, j : j + cols] for j in range(3)], axis=2).reshape(
        (rows + 2) * cols, 3 * depth
    )


def conv_scatter_fused(spread, kernel, cols, n, m, number, riders=()):
    own = kernel.shape[2] // n
    depth = kernel.shape[1]
    pixels = spread.shape[0] - 2 * cols
    return comm_call(
        partial(conv_scatter_kernel, cols),
        (spread, kernel.reshape(3, 3 * depth, kernel.shape[2])),
        (jax.ShapeDtypeStruct((pixels, own), jnp.float32),),
        scatter_scratch(n // 2, pixels, own, CONV_PARTS),
        riders,
        n,
        m,
        number,
    )


def conv_back_kernel(breadth, line, g_ref, w_ref, x_ref, acc_ref, wg_ref, held, sums, send, recv):
    chips = line.chips
    pixels, own = g_ref.shape
    wide = w_ref.shape[1]
    tile = 512
    zero = jnp.zeros((breadth, own), jnp.bfloat16)
    for block in range(2 * chips):
        held[block, pl.ds(0, breadth)] = zero
        held[block, pl.ds(breadth + pixels, breadth)] = zero

    def slot(block):
        return held.at[block, pl.ds(breadth, pixels)]

    def pair(chip, rows):
        return jnp.concatenate([held[2 * chip, rows], held[2 * chip + 1, rows]], axis=1)

    def on_own():
        @pl.loop(0, pixels // tile)
        def _(index):
            acc_ref[pl.ds(pl.multiple_of(index * tile, tile), tile)] = jnp.zeros(
                (tile, wide), jnp.float32
            )

    def on_pair(chip):
        columns = pl.ds(pl.multiple_of(chip * 2 * own, 2 * own), 2 * own)

        @pl.loop(0, pixels // tile)
        def _(index):
            base = pl.multiple_of(index * tile, tile)
            total = acc_ref[pl.ds(base, tile)]
            for i in range(3):
                total += lax.dot_general(
                    pair(chip, pl.ds(base + (2 - i) * breadth, tile)),
                    w_ref[i, :, columns],
                    (((1,), (1,)), ((), ())),
                    preferred_element_type=jnp.float32,
                )
            acc_ref[pl.ds(base, tile)] = total

        for i in range(3):
            sums[...] = jnp.zeros_like(sums)

            @pl.loop(0, pixels // tile)
            def _(index):
                base = pl.multiple_of(index * tile, tile)
                sums[...] += lax.dot_general(
                    x_ref[pl.ds(base + i * breadth, tile)],
                    pair(chip, pl.ds(base + breadth, tile)),
                    (((0,), (0,)), ((), ())),
                    preferred_element_type=jnp.float32,
                )

            wg_ref[chip, i] = sums[...].astype(jnp.bfloat16)

    line_gather(line, g_ref, slot, send, recv, on_own, on_pair)


def conv_back_fused(grad_low, spread, kernel, cols, n, m, number, riders=()):
    pixels, own = grad_low.shape
    depth = kernel.shape[1]
    chips = n // 2
    return comm_call(
        partial(conv_back_kernel, cols),
        (grad_low, kernel.reshape(3, 3 * depth, kernel.shape[2]), spread),
        (
            jax.ShapeDtypeStruct((pixels, 3 * depth), jnp.float32),
            jax.ShapeDtypeStruct((chips, 3, 3 * depth, 2 * own), jnp.bfloat16),
        ),
        [
            pltpu.VMEM((n, pixels + 2 * cols, own), jnp.bfloat16),
            pltpu.VMEM((3 * depth, 2 * own), jnp.float32),
        ]
        + gather_sems(chips),
        riders,
        n,
        m,
        number,
    )


def join_columns(acc, cols):
    pixels, wide = acc.shape
    depth = wide // 3
    planes = acc.reshape(-1, cols, wide)
    none = jnp.zeros_like(planes[:, :1, :depth])
    left = jnp.concatenate([planes[:, 1:, :depth], none], axis=1)
    right = jnp.concatenate([none, planes[:, :-1, 2 * depth :]], axis=1)
    return (left + planes[:, :, depth : 2 * depth] + right).reshape(pixels, depth)


def product(x, w, turned):
    return lax.dot_general(
        x, w, (((1,), (1 if turned else 0,)), ((), ())), preferred_element_type=jnp.float32
    )


def tokens_scatter_kernel(turned, line, x_ref, w_ref, o_ref, *scratch):
    tokens, width = o_ref.shape
    cut = width // TOKEN_PARTS
    depth = x_ref.shape[1] // w_ref.shape[0]

    def produce(chip, part, count, mine, other):
        rows = pl.ds(pl.multiple_of(chip * 2 * tokens, 2 * tokens), 2 * tokens)
        columns = pl.ds(part * cut, cut)
        total = None
        for j in range(w_ref.shape[0]):
            w = w_ref[j, columns] if turned else w_ref[j, :, columns]
            term = product(x_ref[rows, pl.ds(j * depth, depth)], w, turned)
            total = term if total is None else total + term
        first, second = pick(line.c, total[:tokens], total[tokens:])
        mine[pl.ds(part * count, count)] = first
        other[pl.ds(part * count, count)] = second.astype(jnp.bfloat16)

    def finish(part, rows, total):
        o_ref[:, pl.ds(part * cut, cut)] = total

    line_scatter(line, scratch, TOKEN_PARTS, produce, finish, tokens)


def tokens_scatter(x, w, turned, n, m, number, riders=()):
    tokens = x.shape[0] // n
    width = w.shape[1] if turned else w.shape[2]
    return comm_call(
        partial(tokens_scatter_kernel, turned),
        (x, w),
        (jax.ShapeDtypeStruct((tokens, width), jnp.float32),),
        scatter_scratch(n // 2, TOKEN_PARTS * tokens, width // TOKEN_PARTS, TOKEN_PARTS),
        riders,
        n,
        m,
        number,
    )


def tokens_gather_kernel(turned, shape_out, outs, line, x_ref, w_ref, *refs):
    held = refs[0]
    results = refs[1 : 1 + outs]
    send, recv = refs[1 + outs :]
    tokens = x_ref.shape[0]
    across = w_ref.shape[1 if turned else 2]
    cut = min(across, 512)

    def slot(block):
        return held.at[pl.ds(pl.multiple_of(block * tokens, tokens), tokens)]

    def on_pair(chip):
        rows = pl.ds(pl.multiple_of(chip * 2 * tokens, 2 * tokens), 2 * tokens)
        for j in range(w_ref.shape[0]):
            for start in range(0, across, cut):
                w = w_ref[j, pl.ds(start, cut)] if turned else w_ref[j, :, pl.ds(start, cut)]
                values = shape_out(product(held[rows], w, turned))
                for ref, value in zip(results, values):
                    ref[rows, pl.ds(j * across + start, cut)] = value.astype(ref.dtype)

    line_gather(line, x_ref, slot, send, recv, lambda: None, on_pair)


def tokens_gather(x, w, turned, kinds, shape_out, n, m, number, riders=()):
    tokens, width = x.shape
    across = w.shape[0] * w.shape[1 if turned else 2]
    return comm_call(
        partial(tokens_gather_kernel, turned, shape_out, len(kinds)),
        (x, w),
        (jax.ShapeDtypeStruct((tokens * n, width), x.dtype),)
        + tuple(jax.ShapeDtypeStruct((tokens * n, across), kind) for kind in kinds),
        gather_sems(n // 2),
        riders,
        n,
        m,
        number,
    )


def exchange(riders, n, m, number):
    return comm_call(lambda line: None, (), (), [], riders, n, m, number, neighbours=False)


def tiled_up(vector):
    count = -(-vector.shape[0] // 1024) * 1024
    return jnp.pad(vector.astype(jnp.float32), (0, count - vector.shape[0])).reshape(-1, 128)


def attend_scatter_kernel(line, x_ref, valid_ref, w_ref, o_ref, mixed_ref, *scratch):
    tokens, width = o_ref.shape
    wide = mixed_ref.shape[1]
    cut = width // TOKEN_PARTS
    scale = 1.0 / math.sqrt(HEAD_DIM)

    def attend(rows):
        for head in range(wide // HEAD_DIM):
            where = [pl.ds(j * wide + head * HEAD_DIM, HEAD_DIM) for j in range(3)]
            scores = product(x_ref[rows, where[0]], x_ref[:, where[1]], True) * scale
            scores = jnp.where(valid_ref[0:1] > 0.5, scores, MASKED_SCORE)
            exponent = jnp.exp(scores - jnp.max(scores, axis=1, keepdims=True))
            inverse = 1.0 / jnp.sum(exponent, axis=1, keepdims=True)
            mixed_ref[rows, pl.ds(head * HEAD_DIM, HEAD_DIM)] = product(
                (exponent * inverse).astype(jnp.bfloat16), x_ref[:, where[2]], False
            ).astype(jnp.bfloat16)

    def produce(chip, part, count, mine, other):
        rows = pl.ds(pl.multiple_of(chip * 2 * tokens, 2 * tokens), 2 * tokens)
        if part == 0:
            attend(rows)
        total = product(mixed_ref[rows], w_ref[:, pl.ds(part * cut, cut)], False)
        first, second = pick(line.c, total[:tokens], total[tokens:])
        mine[pl.ds(part * count, count)] = first
        other[pl.ds(part * count, count)] = second.astype(jnp.bfloat16)

    def finish(part, rows, total):
        o_ref[:, pl.ds(part * cut, cut)] = total

    line_scatter(line, scratch, TOKEN_PARTS, produce, finish, tokens)


def attend_scatter(qkv_rows, valid, out_weight, n, m, number):
    total = qkv_rows.shape[0]
    tokens = total // n
    width = out_weight.shape[1]
    return comm_call(
        attend_scatter_kernel,
        (qkv_rows, jnp.broadcast_to(valid[None], (8, total)), out_weight),
        (
            jax.ShapeDtypeStruct((tokens, width), jnp.float32),
            jax.ShapeDtypeStruct((total, out_weight.shape[0]), jnp.bfloat16),
        ),
        scatter_scratch(n // 2, TOKEN_PARTS * tokens, width // TOKEN_PARTS, TOKEN_PARTS),
        (),
        n,
        m,
        number,
    )


def attend_gather_kernel(
    line, g_ref, w_ref, x_ref, kt_ref, valid_ref, held, grad_ref, keys_sum, values_sum, send, recv
):
    tokens = g_ref.shape[0]
    wide = w_ref.shape[0]
    heads = wide // HEAD_DIM
    scale = 1.0 / math.sqrt(HEAD_DIM)

    def slot(block):
        return held.at[pl.ds(pl.multiple_of(block * tokens, tokens), tokens)]

    def on_own():
        keys_sum[...] = jnp.zeros_like(keys_sum)
        values_sum[...] = jnp.zeros_like(values_sum)

    def on_pair(chip):
        rows = pl.ds(pl.multiple_of(chip * 2 * tokens, 2 * tokens), 2 * tokens)
        for head in range(heads):
            place = pl.ds(head * HEAD_DIM, HEAD_DIM)
            where = [pl.ds(j * wide + head * HEAD_DIM, HEAD_DIM) for j in range(3)]
            grad = product(held[rows], w_ref[place], True).astype(jnp.bfloat16)
            query = x_ref[rows, where[0]]
            scores = product(x_ref[:, where[1]], query, True) * scale
            scores = jnp.where(valid_ref[:, 0:1] > 0.5, scores, MASKED_SCORE)
            exponent = jnp.exp(scores - jnp.max(scores, axis=0, keepdims=True))
            probs = exponent * (1.0 / jnp.sum(exponent, axis=0, keepdims=True))
            values_sum[:, place] += product(probs.astype(jnp.bfloat16), grad, False)
            grad_probs = product(x_ref[:, where[2]], grad, True)
            inner = jnp.sum(probs * grad_probs, axis=0, keepdims=True)
            grad_scores = (probs * (grad_probs - inner) * scale).astype(jnp.bfloat16)
            keys_sum[:, place] += product(grad_scores, query, False)
            grad_ref[rows, where[0]] = product(kt_ref[place], grad_scores, False).T.astype(
                jnp.bfloat16
            )

    line_gather(line, g_ref, slot, send, recv, on_own, on_pair)
    grad_ref[:, pl.ds(wide, wide)] = keys_sum[...].astype(jnp.bfloat16)
    grad_ref[:, pl.ds(2 * wide, wide)] = values_sum[...].astype(jnp.bfloat16)


def attend_gather(grad_mid, out_weight, qkv_rows, valid, n, m, number, riders):
    tokens, width = grad_mid.shape
    total = tokens * n
    wide = out_weight.shape[0]
    return comm_call(
        attend_gather_kernel,
        (
            grad_mid,
            out_weight,
            qkv_rows,
            qkv_rows[:, wide : 2 * wide].T,
            jnp.broadcast_to(valid[:, None], (total, 128)),
        ),
        (
            jax.ShapeDtypeStruct((total, width), jnp.bfloat16),
            jax.ShapeDtypeStruct((total, 3 * wide), jnp.bfloat16),
        ),
        [pltpu.VMEM((total, wide), jnp.float32), pltpu.VMEM((total, wide), jnp.float32)]
        + gather_sems(n // 2),
        riders,
        n,
        m,
        number,
    )


def local(
    image,
    embedding,
    extents,
    gain_first,
    conv_first,
    gain_second,
    conv_second,
    shift_weight,
    down_weight,
    ada_weight,
    qkv_weight,
    out_weight,
    up_weight,
    proj_weight,
    cotangent,
):
    strip_rows, canvas_cols, channel_count = (image.shape[1], image.shape[2], image.shape[3])
    width_all = out_weight.shape[1]
    n = lax.axis_size("mp")
    m = lax.axis_size("dp")
    me_mp = lax.axis_index("mp")
    me_dp = lax.axis_index("dp")
    rows_all = strip_rows * n
    pixel_total = rows_all * canvas_cols
    own = channel_count // n
    size = channel_count // GROUPS
    token_rows = strip_rows // 2
    token_cols = canvas_cols // 2
    local_tokens = token_rows * token_cols
    token_total = local_tokens * n
    local_width = out_weight.shape[0]

    fused = own % 128 == 0 and n == 2 * m
    shift_vector = jnp.dot(embedding, shift_weight, preferred_element_type=jnp.float32)[0]
    columns = jnp.dot(embedding, ada_weight, preferred_element_type=jnp.float32)[0]
    riders = (Rider("mp", tiled_up(columns)),)
    if fused:
        modulation, pixels_low = exchange(
            riders + (Rider("mp", image[0].reshape(-1, channel_count), 1),), n, m, 12
        )
    else:
        (modulation,) = exchange(riders, n, m, 12)
        pixels_low = lax.all_to_all(image[0], "mp", 2, 0, tiled=True)
    modulation = modulation.reshape(n, -1)[:, : columns.shape[0]].reshape(-1)
    scale_attend = modulation[:width_all]
    shift_attend = modulation[width_all : 2 * width_all]
    scale_mlp = modulation[2 * width_all : 3 * width_all]
    shift_mlp = modulation[3 * width_all :]
    own_first = lax.dynamic_slice_in_dim(gain_first, me_mp * own, own)
    own_second = lax.dynamic_slice_in_dim(gain_second, me_mp * own, own)

    pixels = pixels_low.astype(jnp.float32).reshape(pixel_total, own)
    normed_first, inverse_first = group_forward(pixels, size)
    hidden_first = (
        jax.nn.silu(normed_first * own_first)
        .astype(jnp.bfloat16)
        .reshape(rows_all, canvas_cols, own)
    )
    spread_first = side_by_side(hidden_first)
    if fused:
        (conv_output,) = conv_scatter_fused(spread_first, conv_first, canvas_cols, n, m, 0)
    else:
        conv_output = conv_scatter(hidden_first, conv_first, n)
    conv_output = conv_output + shift_vector
    normed_second, inverse_second = group_forward(conv_output, size)
    hidden_second = (
        jax.nn.silu(normed_second * own_second)
        .astype(jnp.bfloat16)
        .reshape(rows_all, canvas_cols, own)
    )
    spread_second = side_by_side(hidden_second)
    if fused:
        (conv_again,) = conv_scatter_fused(spread_second, conv_second, canvas_cols, n, m, 1)
    else:
        conv_again = conv_scatter(hidden_second, conv_second, n)
    residual = pixels + conv_again
    down_patch = (
        residual.astype(jnp.bfloat16)
        .reshape(rows_all // 2, 2, token_cols, 2, own)
        .transpose(0, 2, 1, 3, 4)
        .reshape(token_total, 4 * own)
    )
    down_matrix = down_weight.reshape(4 * own, width_all)
    (stream,) = tokens_scatter(down_patch, down_matrix[None], False, n, m, 2)
    normed_attend, inverse_attend = layer_forward(stream)
    input_attend = (normed_attend * (1.0 + scale_attend) + shift_attend).astype(jnp.bfloat16)
    all_attend, qkv_rows = tokens_gather(
        input_attend, qkv_weight, False, (jnp.bfloat16,), lambda value: (value,), n, m, 3
    )
    token_index = jnp.arange(token_total, dtype=jnp.int32)
    key_valid = (token_index // token_cols < extents[0, 0]) & (
        token_index % token_cols < extents[0, 1]
    )
    valid = key_valid.astype(jnp.float32)
    attended, mixed_low = attend_scatter(qkv_rows, valid, out_weight, n, m, 4)
    stream_mid = stream + attended
    normed_mlp, inverse_mlp = layer_forward(stream_mid)
    input_mlp = (normed_mlp * (1.0 + scale_mlp) + shift_mlp).astype(jnp.bfloat16)
    all_mlp, upper_proj, activated = tokens_gather(
        input_mlp,
        up_weight[None],
        False,
        (jnp.float32, jnp.bfloat16),
        lambda value: (value, jax.nn.gelu(value, approximate=True)),
        n,
        m,
        5,
    )
    final_stream = stream_mid + scatter_rows(
        jnp.dot(activated, proj_weight, preferred_element_type=jnp.float32)
    )
    output = final_stream.astype(jnp.bfloat16).reshape(1, token_rows, token_cols, width_all)

    grad_final_low = cotangent[0].reshape(local_tokens, width_all)
    grad_final = grad_final_low.astype(jnp.float32)
    all_final = gather_rows(lax.optimization_barrier((grad_final_low, qkv_rows))[0])
    grad_act = jnp.einsum("le,fe->lf", all_final, proj_weight, preferred_element_type=jnp.float32)
    gelu_pull = jax.vjp(partial(jax.nn.gelu, approximate=True), upper_proj)[1]
    grad_upper = gelu_pull(grad_act)[0].astype(jnp.bfloat16)
    grad_proj = jnp.einsum("lf,le->fe", activated, all_final, preferred_element_type=jnp.float32)
    grad_normed_mlp, sums_proj = tokens_scatter(
        grad_upper,
        up_weight[None],
        True,
        n,
        m,
        6,
        (Rider("dp", grad_proj.astype(jnp.bfloat16), 1),),
    )
    grad_up = jnp.einsum("le,lf->ef", all_mlp, grad_upper, preferred_element_type=jnp.float32)
    grad_mid_norm, grad_scale_mlp, grad_shift_mlp = layer_backward(
        grad_normed_mlp, normed_mlp, inverse_mlp, scale_mlp
    )
    grad_mid = grad_final + grad_mid_norm
    all_mid, grad_qkv, sums_up = attend_gather(
        grad_mid.astype(jnp.bfloat16),
        out_weight,
        qkv_rows,
        valid,
        n,
        m,
        7,
        (Rider("dp", grad_up.astype(jnp.bfloat16), 0),),
    )
    grad_out = jnp.einsum("lh,le->he", mixed_low, all_mid, preferred_element_type=jnp.float32)
    grad_normed_attend, sums_out = tokens_scatter(
        grad_qkv, qkv_weight, True, n, m, 8, (Rider("dp", grad_out.astype(jnp.bfloat16), 1),)
    )
    grad_qkv_weight = jnp.einsum(
        "le,lf->ef", all_attend, grad_qkv, preferred_element_type=jnp.float32
    )
    grad_stream_norm, grad_scale_attend, grad_shift_attend = layer_backward(
        grad_normed_attend, normed_attend, inverse_attend, scale_attend
    )
    grad_stream = grad_mid + grad_stream_norm
    grad_modulation = jnp.concatenate(
        [
            tiled_up(piece)
            for piece in jnp.concatenate(
                [grad_scale_attend, grad_shift_attend, grad_scale_mlp, grad_shift_mlp]
            ).reshape(n, -1)
        ]
    )
    all_stream, grad_tap_patch, sums_qkv, ada_columns = tokens_gather(
        grad_stream.astype(jnp.bfloat16),
        down_matrix[None],
        True,
        (jnp.float32,),
        lambda value: (value,),
        n,
        m,
        9,
        (
            Rider("dp", grad_qkv_weight.astype(jnp.bfloat16), 0),
            Rider("mp", grad_modulation, 0),
        ),
    )
    grad_down = jnp.einsum(
        "lk,le->ke", down_patch, all_stream, preferred_element_type=jnp.float32
    )
    ada_columns = added(ada_columns).reshape(-1)[: columns.shape[0]]
    grad_residual = (
        grad_tap_patch.reshape(rows_all // 2, token_cols, 2, 2, own)
        .transpose(0, 2, 1, 3, 4)
        .reshape(pixel_total, own)
    )
    def back(grad_low, hidden, spread, kernel, number, riders):
        if fused:
            acc, parts, *ridden = conv_back_fused(
                grad_low, spread, kernel, canvas_cols, n, m, number, riders
            )
            return join_columns(acc, canvas_cols), parts.reshape(m, 9 * own, -1), ridden
        grad_hidden, grad_kernel = conv_backward(grad_low, hidden, kernel, n)
        return grad_hidden, by_images(grad_kernel, m), exchange(riders, n, m, number)

    grad_hidden_second, parts_second, (sums_down, every_small) = back(
        grad_residual.astype(jnp.bfloat16),
        hidden_second,
        spread_second,
        conv_second,
        10,
        (
            Rider("dp", grad_down.astype(jnp.bfloat16), 1),
            Rider("dp", jnp.concatenate([tiled_up(embedding[0]), tiled_up(ada_columns)])),
        ),
    )
    grad_conv_output, grad_gain_second = group_backward(
        grad_hidden_second, normed_second, inverse_second, own_second, size
    )
    grad_shift = jnp.sum(grad_conv_output, axis=0)
    grad_hidden_first, parts_first, (sums_second, every_shift) = back(
        grad_conv_output.astype(jnp.bfloat16),
        hidden_first,
        spread_first,
        conv_first,
        11,
        (Rider("dp", parts_second, 0), Rider("dp", tiled_up(grad_shift))),
    )
    grad_base, grad_gain_first = group_backward(
        grad_hidden_first, normed_first, inverse_first, own_first, size
    )
    image_turned = (grad_residual + grad_base).astype(jnp.bfloat16)
    embed_term = jnp.dot(
        grad_shift[None], shift_weight.astype(jnp.float32).T, precision=PRECISE
    ) + jnp.dot(ada_columns[None], ada_weight.astype(jnp.float32).T, precision=PRECISE)
    small = jnp.concatenate(
        [tiled_up(embed_term[0]), tiled_up(jnp.concatenate([grad_gain_first, grad_gain_second]))]
    )
    riders = (Rider("dp", parts_first, 0), Rider("all", small))
    if fused:
        sums_first, small, image_turned = exchange(
            riders + (Rider("mp", image_turned, 0),), n, m, 13
        )
        image_grad = image_turned.transpose(1, 0, 2).reshape(image.shape)
    else:
        sums_first, small = exchange(riders, n, m, 13)
        image_grad = lax.all_to_all(
            image_turned.reshape(rows_all, canvas_cols, own), "mp", 0, 2, tiled=True
        )[None]

    small = small.reshape(m, n, -1)
    embed_count = embedding.shape[1]
    embedding_grad = jnp.sum(
        lax.dynamic_index_in_dim(small, me_dp, axis=0, keepdims=False)[:, :embed_count], axis=0
    )[None]
    gain_start = -(-embed_count // 1024) * 1024
    gains = jnp.sum(small[:, :, gain_start : gain_start + 2 * own], axis=0)
    gains = gains.reshape(n, 2, own).transpose(1, 0, 2).reshape(2, -1)
    piece = channel_count // (m * n)
    gains = lax.dynamic_slice_in_dim(gains, (me_dp * n + me_mp) * piece, piece, axis=1)
    every_small = every_small.reshape(m, -1)
    embed_rows = lax.dynamic_slice_in_dim(
        every_small[:, :embed_count], me_dp * (embed_count // m), embed_count // m, axis=1
    )
    grad_shift_weight = jnp.dot(
        embed_rows.T, every_shift.reshape(m, -1)[:, :own], precision=PRECISE
    )
    grad_ada_weight = jnp.dot(
        embed_rows.T,
        every_small[:, gain_start : gain_start + columns.shape[0]],
        precision=PRECISE,
    )
    qkv_grad = added(sums_qkv).reshape(-1, 3, local_width).transpose(1, 0, 2)
    return (
        output,
        image_grad,
        embedding_grad,
        gains[0],
        turn_kernel(added(sums_first)[0], 9, m, n),
        gains[1],
        turn_kernel(added(sums_second)[0], 9, m, n),
        grad_shift_weight,
        turn_kernel(added(sums_down), 4, m, n),
        grad_ada_weight,
        qkv_grad,
        added(sums_out),
        added(sums_up),
        added(sums_proj),
    )


def solution(mesh):
    placed = (
        P("dp", "mp", None, None),
        P("dp", None),
        P("dp", None),
        P(),
        P(None, "mp", None),
        P(),
        P(None, "mp", None),
        P(None, "mp"),
        P(None, "mp", None),
        P(None, "mp"),
        P(None, None, "mp"),
        P("mp", None),
        P(None, "mp"),
        P("mp", None),
        P("dp", "mp", None, None),
    )
    return jax.shard_map(
        local,
        mesh=mesh,
        in_specs=placed,
        out_specs=(
            P("dp", "mp", None, None),
            P("dp", "mp", None, None),
            P("dp", None),
            P(("dp", "mp")),
            P(None, "dp", "mp"),
            P(("dp", "mp")),
            P(None, "dp", "mp"),
            P("dp", "mp"),
            P(None, "dp", "mp"),
            P("dp", "mp"),
            P(None, "dp", "mp"),
            P("mp", "dp"),
            P("dp", "mp"),
            P("mp", "dp"),
        ),
        check_vma=False,
    )
```

```python
from functools import partial
import math

import jax
import jax.numpy as jnp
from jax import lax
from jax.experimental import pallas as pl
from jax.experimental.pallas import tpu as pltpu
from jax.sharding import PartitionSpec as P

HEAD_DIM = 128
GROUPS = 32


GROUP_EPSILON = 1e-05
LAYER_EPSILON = 1e-06
MASKED_SCORE = -1000000000.0
PRECISE = lax.Precision.HIGHEST


def group_spread(per_channel, size):
    grouped = jnp.sum(per_channel.reshape(-1, size), axis=1)
    return jnp.repeat(grouped, size)


def group_forward(values, size):
    counted = values.shape[0] * size
    average = group_spread(jnp.sum(values, axis=0), size) / counted
    centre = values - average
    inverse = lax.rsqrt(
        group_spread(jnp.sum(centre * centre, axis=0), size) / counted + GROUP_EPSILON
    )
    return (centre * inverse, inverse)


def group_backward(incoming, normed, inverse, gain_vec, size):
    pre_act = normed * gain_vec
    sigmoid_part = jax.nn.sigmoid(pre_act)
    through = incoming * sigmoid_part * (1.0 + pre_act * (1.0 - sigmoid_part))
    counted = normed.shape[0] * size
    gain_part = jnp.sum(through * normed, axis=0)
    plain_part = jnp.sum(through, axis=0)
    first_mean = group_spread(plain_part * gain_vec, size) / counted
    second_mean = group_spread(gain_part * gain_vec, size) / counted
    outgoing = inverse * (through * gain_vec - first_mean - normed * second_mean)
    return (outgoing, gain_part)


def windows(planes, flipped):
    row_count, col_count, depth = planes.shape
    padded = jnp.pad(planes, ((1, 1), (1, 1), (0, 0)))
    pieces = []
    for tap_index in range(9):
        row_off, col_off = divmod(tap_index, 3)
        if flipped:
            row_off, col_off = (2 - row_off, 2 - col_off)
        pieces.append(padded[row_off : row_off + row_count, col_off : col_off + col_count])
    return jnp.stack(pieces, axis=2).reshape(row_count * col_count, 9, depth)


def gather_rows(rows):
    return lax.all_gather(rows, "mp", axis=0, tiled=True)


def scatter_rows(rows):
    return lax.psum_scatter(
        rows.astype(jnp.bfloat16), "mp", scatter_dimension=0, tiled=True
    ).astype(jnp.float32)


def conv_scatter(hidden, kernel, n):
    patch = windows(hidden, False)
    depth = kernel.shape[2] // n
    total = jnp.einsum("ptc,tcd->pd", patch, kernel, preferred_element_type=jnp.float32)
    parts = total.astype(jnp.bfloat16).reshape(-1, n, depth).transpose(1, 0, 2)
    return lax.psum_scatter(parts, "mp", scatter_dimension=0, tiled=False).astype(jnp.float32)


def conv_backward(grad_low, hidden, kernel, n):
    row_count, col_count, depth = hidden.shape
    gathered = lax.all_gather(grad_low, "mp", axis=1, tiled=True)
    padded = jnp.pad(gathered, ((col_count, col_count), (0, 0)))
    taps = kernel.reshape(3, 3 * depth, kernel.shape[2])
    acc = sum(
        jnp.einsum(
            "pd,td->pt",
            padded[(2 - i) * col_count : (2 - i) * col_count + row_count * col_count],
            taps[i],
            preferred_element_type=jnp.float32,
        )
        for i in range(3)
    )
    grad_kernel = jnp.einsum(
        "ptc,pd->tcd", windows(hidden, False), gathered, preferred_element_type=jnp.float32
    )
    return (join_columns(acc, col_count), grad_kernel)


def by_images(grad, m):
    taps, own, outs = grad.shape
    return grad.astype(jnp.bfloat16).reshape(taps * own, outs).T.reshape(m, outs // m, taps * own)


def unturned(halves, taps):
    count, outs, _ = halves.shape
    return (
        halves.astype(jnp.float32)
        .reshape(count, outs, taps, -1)
        .transpose(2, 0, 3, 1)
        .reshape(taps, -1, outs)
    )


def added(received):
    return jnp.sum(received.astype(jnp.float32), axis=0)


def layer_forward(stream):
    centre = stream - jnp.mean(stream, axis=1, keepdims=True)
    inverse = lax.rsqrt(jnp.mean(centre * centre, axis=1, keepdims=True) + LAYER_EPSILON)
    return (centre * inverse, inverse)


def layer_backward(incoming, normed, inverse, scale_vec):
    through = incoming * (1.0 + scale_vec)
    outgoing = inverse * (
        through
        - jnp.mean(through, axis=1, keepdims=True)
        - normed * jnp.mean(through * normed, axis=1, keepdims=True)
    )
    return (outgoing, jnp.sum(incoming * normed, axis=0), jnp.sum(incoming, axis=0))


MESH = pl.DeviceIdType.MESH
CONV_PARTS = 4
TOKEN_PARTS = 4
VMEM_BYTES = 60 * 1024 * 1024


class Line:
    def __init__(self, chips, images):
        self.chips = chips
        self.images = images
        self.dp = lax.axis_index("dp")
        self.mp = lax.axis_index("mp")
        self.z = self.mp // 2
        self.c = self.mp % 2
        self.has_up = self.z < chips - 1
        self.has_down = self.z > 0
        self.up = (self.dp, self.mp + 2)
        self.down = (self.dp, self.mp - 2)
        self.sibling = (self.dp, 2 * self.z + 1 - self.c)

    def count(self, axis):
        return {"dp": self.images, "mp": 2 * self.chips, "all": 2 * self.chips * self.images}[axis]

    def index(self, axis):
        return {"dp": self.dp, "mp": self.mp, "all": self.dp * 2 * self.chips + self.mp}[axis]

    def place(self, axis, index):
        if axis == "dp":
            return (index, self.mp)
        if axis == "mp":
            return (self.dp, index)
        return (index // (2 * self.chips), index % (2 * self.chips))

    def peer(self, axis, step):
        return lax.rem(self.index(axis) + step, self.count(axis))

    def turned(self, half):
        ratio = 2 * self.chips // self.images
        return (self.mp // ratio, ratio * self.dp + half)

    def stays(self, half):
        ratio = 2 * self.chips // self.images
        return jnp.logical_and(self.dp == self.mp // ratio, self.mp % ratio == half)

    def barrier(self, axes, neighbours):
        bar = pltpu.get_barrier_semaphore()
        turn = "turn" in axes and "all" not in axes
        axes = ("all",) if "all" in axes else tuple(axis for axis in axes if axis != "turn")
        steady = 0
        for axis in axes:
            for step in range(1, self.count(axis)):
                target = self.place(axis, self.peer(axis, step))
                pl.semaphore_signal(bar, inc=1, device_id=target, device_id_type=MESH)
            steady += self.count(axis) - 1
        cases = [(steady, None)]
        if neighbours and not ("all" in axes or "mp" in axes):
            pl.semaphore_signal(bar, inc=1, device_id=self.sibling, device_id_type=MESH)

            @pl.when(self.has_up)
            def _():
                pl.semaphore_signal(bar, inc=1, device_id=self.up, device_id_type=MESH)

            @pl.when(self.has_down)
            def _():
                pl.semaphore_signal(bar, inc=1, device_id=self.down, device_id_type=MESH)

            middle = jnp.logical_and(self.has_up, self.has_down)
            cases = [(steady + 3, middle), (steady + 2, jnp.logical_not(middle))]
        if turn:
            ratio = 2 * self.chips // self.images
            for half in range(ratio):

                @pl.when(jnp.logical_not(self.stays(half)))
                def _():
                    pl.semaphore_signal(
                        bar, inc=1, device_id=self.turned(half), device_id_type=MESH
                    )

            same = self.dp == self.mp // ratio
            cases = [
                (count + ratio - less, here if when is None else jnp.logical_and(when, here))
                for count, when in cases
                for less, here in ((1, same), (0, jnp.logical_not(same)))
            ]
        for count, when in cases:
            if when is None:
                pl.semaphore_wait(bar, count)
            else:

                @pl.when(when)
                def _():
                    pl.semaphore_wait(bar, count)


class Rider:
    def __init__(self, axis, array, cut=None, beside=False):
        self.axes = (axis,)
        self.axis = axis
        self.array = array
        self.cut = cut
        self.beside = beside

    def result(self, sizes):
        count = sizes[self.axis]
        shape = list(self.array.shape)
        if self.cut is not None:
            shape[self.cut] //= count
        self.columns = shape[-1]
        if self.beside:
            shape[-1] *= count
        else:
            shape = [count] + shape
        return jax.ShapeDtypeStruct(tuple(shape), self.array.dtype)

    def scratch(self, sizes):
        count = sizes[self.axis]
        return [pltpu.SemaphoreType.DMA((count,)), pltpu.SemaphoreType.DMA((count,))]

    def piece(self, ref, index, count):
        if self.cut is None:
            return ref
        size = self.array.shape[self.cut] // count
        where = [slice(None)] * len(self.array.shape)
        where[self.cut] = pl.ds(pl.multiple_of(index * size, size), size)
        return ref.at[tuple(where)]

    def copies(self, line, src, dst, send, recv):
        count, me = line.count(self.axis), line.index(self.axis)
        if self.beside:
            land = dst.at[:, pl.ds(pl.multiple_of(me * self.columns, self.columns), self.columns)]
        else:
            land = dst.at[me]
        made = [pltpu.make_async_copy(self.piece(src, me, count), land, send.at[0])]
        for step in range(1, count):
            peer = line.peer(self.axis, step)
            made.append(
                remote(
                    self.piece(src, peer, count),
                    land,
                    send.at[step],
                    recv.at[step],
                    line.place(self.axis, peer),
                )
            )
        return made

    def start(self, line, src, dst, send, recv):
        for copy in self.copies(line, src, dst, send, recv):
            copy.start()

    def middle(self, line, src, dst, send, recv):
        pass

    def finish(self, line, src, dst, send, recv):
        for copy in self.copies(line, src, dst, send, recv):
            copy.wait()


class Turn:
    def __init__(self, array):
        self.axes = ("turn",)
        self.array = array

    def result(self, sizes):
        self.ratio = sizes["mp"] // sizes["dp"]
        rows, columns = self.array.shape[-2:]
        return jax.ShapeDtypeStruct((self.ratio, rows // self.ratio, columns), self.array.dtype)

    def scratch(self, sizes):
        ratio = sizes["mp"] // sizes["dp"]
        return [pltpu.SemaphoreType.DMA((ratio,)), pltpu.SemaphoreType.DMA((ratio,))]

    def leave(self, line, src, dst, send, recv, half):
        size = dst.shape[1]
        piece = src.at[pl.ds(half * size, size)]
        mine = line.mp % self.ratio
        away = remote(piece, dst.at[mine], send.at[half], recv.at[mine], line.turned(half))
        return away, pltpu.make_async_copy(piece, dst.at[half], send.at[half])

    def start(self, line, src, dst, send, recv):
        for half in range(self.ratio):
            away, here = self.leave(line, src, dst, send, recv, half)

            @pl.when(line.stays(half))
            def _():
                here.start()

            @pl.when(jnp.logical_not(line.stays(half)))
            def _():
                away.start()

    def middle(self, line, src, dst, send, recv):
        pass

    def finish(self, line, src, dst, send, recv):
        for half in range(self.ratio):
            away, here = self.leave(line, src, dst, send, recv, half)

            @pl.when(line.stays(half))
            def _():
                here.wait()

            @pl.when(jnp.logical_not(line.stays(half)))
            def _():
                away.wait_send()
                remote(
                    dst.at[half], dst.at[half], send.at[half], recv.at[half], line.turned(half)
                ).wait_recv()


class SumTurn:
    def __init__(self, array):
        self.axes = ("dp", "turn")
        self.first = Rider("dp", array, 0)
        self.second = Turn(array)
        self.array = array

    def result(self, sizes):
        self.first.result(sizes)
        return self.second.result(sizes)

    def scratch(self, sizes):
        shape = self.array.shape
        return (
            [
                pltpu.VMEM((shape[0], 1) + shape[1:], self.array.dtype),
                pltpu.VMEM(shape[1:], self.array.dtype),
            ]
            + self.first.scratch(sizes)
            + self.second.scratch(sizes)
        )

    def start(self, line, src, dst, got, total, *sems):
        self.first.start(line, src, got, *sems[:2])

    def middle(self, line, src, dst, got, total, *sems):
        self.first.finish(line, src, got, *sems[:2])
        rows = total.shape[0]
        tile = 32

        @pl.loop(0, rows // tile)
        def _(index):
            where = pl.ds(pl.multiple_of(index * tile, tile), tile)
            added_up = got[0, 0, where].astype(jnp.float32)
            for image in range(1, got.shape[0]):
                added_up += got[image, 0, where].astype(jnp.float32)
            total[where] = added_up.astype(total.dtype)

        self.second.start(line, total, dst, *sems[2:])

    def finish(self, line, src, dst, got, total, *sems):
        self.second.finish(line, total, dst, *sems[2:])


def comm_call(kernel, inputs, out_shapes, scratch, riders, n, m, number, neighbours=True):
    chips = n // 2
    sizes = {"dp": m, "mp": n, "all": m * n}
    ride_shapes = tuple(rider.result(sizes) for rider in riders)
    ride_scratch = [rider.scratch(sizes) for rider in riders]
    any_spec = pl.BlockSpec(memory_space=pl.ANY)
    ni, nr, no = len(inputs), len(riders), len(out_shapes)

    def body(*refs):
        main_in, ride_in = refs[:ni], refs[ni : ni + nr]
        rest = refs[ni + nr :]
        main_out, ride_out = rest[:no], rest[no : no + nr]
        rest = rest[no + nr :]
        main_scratch, rest = rest[: len(scratch)], rest[len(scratch) :]
        line = Line(chips, m)
        line.barrier(sorted(set(axis for rider in riders for axis in rider.axes)), neighbours)
        riding = []
        for rider, src, dst, needs in zip(riders, ride_in, ride_out, ride_scratch):
            riding.append((rider, (line, src, dst) + tuple(rest[: len(needs)])))
            rest = rest[len(needs) :]
        for rider, refs_in in riding:
            rider.start(*refs_in)
        kernel(line, *main_in, *main_out, *main_scratch)
        for rider, refs_in in riding:
            rider.middle(*refs_in)
        for rider, refs_in in riding:
            rider.finish(*refs_in)

    return pl.pallas_call(
        body,
        out_shape=tuple(out_shapes) + ride_shapes,
        in_specs=whole(ni) + [any_spec] * nr,
        out_specs=tuple(whole(no) + [any_spec] * nr),
        scratch_shapes=list(scratch) + [ref for needs in ride_scratch for ref in needs],
        compiler_params=comm_params(number),
    )(*inputs, *[rider.array for rider in riders])


def remote(src, dst, send, recv, target):
    return pltpu.make_async_remote_copy(
        src_ref=src,
        dst_ref=dst,
        send_sem=send,
        recv_sem=recv,
        device_id=target,
        device_id_type=MESH,
    )


def gather_sems(chips):
    return [pltpu.SemaphoreType.DMA((3, 2, chips)), pltpu.SemaphoreType.DMA((3, 2, chips))]


def line_gather(line, x_ref, slot, send, recv, on_own, on_pair):
    chips = line.chips
    z, c = line.z, line.c

    def hop(stream, step, src, block, target):
        return remote(src, slot(block), send.at[stream, 0, step], recv.at[stream, 0, step], target)

    def across(way, step, src, block):
        return remote(src, slot(block), send.at[2, way, step], recv.at[2, way, step], line.sibling)

    @pl.when(line.has_up)
    def _():
        hop(0, 1, x_ref, line.mp, line.up).start()

    @pl.when(line.has_down)
    def _():
        hop(1, 1, x_ref, line.mp, line.down).start()

    across(0, 0, x_ref, line.mp).start()
    slot(line.mp)[...] = x_ref[...]
    on_own()
    across(0, 0, x_ref, line.mp).wait_recv()
    on_pair(z)
    for step in range(1, chips):
        below, above = z - step, z + step

        @pl.when(below >= 0)
        def _():
            block = 2 * below + c
            hop(0, step, slot(block), block, line.up).wait_recv()
            if step + 1 < chips:

                @pl.when(line.has_up)
                def _():
                    hop(0, step + 1, slot(block), block, line.up).start()

            across(0, step, slot(block), block).start()

        @pl.when(above < chips)
        def _():
            block = 2 * above + c
            hop(1, step, slot(block), block, line.down).wait_recv()
            if step + 1 < chips:

                @pl.when(line.has_down)
                def _():
                    hop(1, step + 1, slot(block), block, line.down).start()

            across(1, step, slot(block), block).start()

        @pl.when(below >= 0)
        def _():
            across(0, step, slot(2 * below + c), 2 * below + c).wait_recv()
            on_pair(below)

        @pl.when(above < chips)
        def _():
            across(1, step, slot(2 * above + c), 2 * above + c).wait_recv()
            on_pair(above)

    @pl.when(line.has_up)
    def _():
        hop(0, 1, x_ref, line.mp, line.up).wait_send()

    @pl.when(line.has_down)
    def _():
        hop(1, 1, x_ref, line.mp, line.down).wait_send()

    across(0, 0, x_ref, line.mp).wait_send()
    for step in range(1, chips):
        below, above = z - step, z + step

        @pl.when(below >= 0)
        def _():
            block = 2 * below + c
            if step + 1 < chips:

                @pl.when(line.has_up)
                def _():
                    hop(0, step + 1, slot(block), block, line.up).wait_send()

            across(0, step, slot(block), block).wait_send()

        @pl.when(above < chips)
        def _():
            block = 2 * above + c
            if step + 1 < chips:

                @pl.when(line.has_down)
                def _():
                    hop(1, step + 1, slot(block), block, line.down).wait_send()

            across(1, step, slot(block), block).wait_send()


def scatter_scratch(chips, rows, cols, parts):
    block = (chips, rows, cols)
    return [
        pltpu.VMEM(block, jnp.float32),
        pltpu.VMEM(block, jnp.bfloat16),
        pltpu.VMEM(block, jnp.bfloat16),
        pltpu.VMEM((2,) + block, jnp.bfloat16),
        pltpu.SemaphoreType.DMA((2, 3, chips, parts)),
    ]


def line_scatter(line, scratch, parts, produce, finish, tile):
    chips = line.chips
    z = line.z
    kept, out_ref, in_ref, moving, sems = scratch
    count = kept.shape[1] // parts

    def span(part):
        return pl.ds(part * count, count)

    def across(chip, part):
        return remote(
            out_ref.at[chip, span(part)],
            in_ref.at[chip, span(part)],
            sems.at[0, 0, chip, part],
            sems.at[1, 0, chip, part],
            line.sibling,
        )

    def hop(way, chip, part):
        target = line.up if way == 0 else line.down
        ref = moving.at[way, chip, span(part)]
        return remote(
            ref, ref, sems.at[0, 1 + way, chip, part], sems.at[1, 1 + way, chip, part], target
        )

    items = []
    for step in range(chips - 1):
        for part in range(parts):
            items.append((0, chips - 1 - step + z, part, step >= z))
            items.append((1, step - (chips - 1 - z), part, step >= chips - 1 - z))
    for part in range(parts):
        items.append((2, z, part, None))

    def run(active, body):
        if active is None:
            body()
        else:
            pl.when(active)(body)

    def start(item):
        way, chip, part, active = item

        def body():
            produce(chip, part, count, kept.at[chip], out_ref.at[chip])
            across(chip, part).start()

        run(active, body)

    def tiles(part, body):
        @pl.loop(0, count // tile)
        def _(index):
            body(pl.ds(pl.multiple_of(part * count + index * tile, tile), tile))

    def close(item):
        way, chip, part, active = item

        def body():
            across(chip, part).wait_recv()
            if way < 2:
                later = line.has_down if way == 0 else line.has_up

                @pl.when(later)
                def _():
                    hop(way, chip, part).wait_recv()

                    def add(rows):
                        moving[way, chip, rows] = (
                            kept[chip, rows]
                            + in_ref[chip, rows].astype(jnp.float32)
                            + moving[way, chip, rows].astype(jnp.float32)
                        ).astype(jnp.bfloat16)

                    tiles(part, add)

                @pl.when(jnp.logical_not(later))
                def _():
                    def add(rows):
                        moving[way, chip, rows] = (
                            kept[chip, rows] + in_ref[chip, rows].astype(jnp.float32)
                        ).astype(jnp.bfloat16)

                    tiles(part, add)

                hop(way, chip, part).start()
            else:

                def total(rows):
                    return kept[chip, rows] + in_ref[chip, rows].astype(jnp.float32)

                def from_side(side, rows):
                    return moving[side, chip, rows].astype(jnp.float32)

                both = jnp.logical_and(line.has_down, line.has_up)

                @pl.when(both)
                def _():
                    hop(0, chip, part).wait_recv()
                    hop(1, chip, part).wait_recv()
                    tiles(
                        part,
                        lambda rows: finish(
                            part, rows, total(rows) + from_side(0, rows) + from_side(1, rows)
                        ),
                    )

                for side, present in ((0, line.has_down), (1, line.has_up)):

                    @pl.when(jnp.logical_and(present, jnp.logical_not(both)))
                    def _():
                        hop(side, chip, part).wait_recv()
                        tiles(
                            part,
                            lambda rows: finish(part, rows, total(rows) + from_side(side, rows)),
                        )

        run(active, body)

    lag = 2
    for index, item in enumerate(items):
        start(item)
        if index >= lag:
            close(items[index - lag])
    for item in items[-lag:]:
        close(item)
    for way, chip, part, active in items:

        def body():
            across(chip, part).wait_send()
            if way < 2:
                hop(way, chip, part).wait_send()

        run(active, body)


def whole(count):
    return [pl.BlockSpec(memory_space=pltpu.VMEM)] * count


def comm_params(number):
    return pltpu.CompilerParams(
        collective_id=number, has_side_effects=True, vmem_limit_bytes=VMEM_BYTES
    )


def pick(c, low, high):
    return jnp.where(c == 0, low, high), jnp.where(c == 0, high, low)


def conv_scatter_kernel(breadth, line, x_ref, w_ref, o_ref, *scratch):
    pixels, own = o_ref.shape
    tile = 512

    def produce(chip, part, count, mine, other):
        columns = pl.ds(pl.multiple_of(chip * 2 * own, 2 * own), 2 * own)

        @pl.loop(0, count // tile)
        def _(index):
            base = pl.multiple_of(part * count + index * tile, tile)
            total = jnp.zeros((tile, 2 * own), jnp.float32)
            for i in range(3):
                total += jnp.dot(
                    x_ref[pl.ds(base + i * breadth, tile)],
                    w_ref[i, :, columns],
                    preferred_element_type=jnp.float32,
                )
            first, second = pick(line.c, total[:, :own], total[:, own:])
            mine[pl.ds(base, tile)] = first
            other[pl.ds(base, tile)] = second.astype(jnp.bfloat16)

    def finish(part, rows, total):
        o_ref[rows] = total

    line_scatter(line, scratch, CONV_PARTS, produce, finish, tile)


def side_by_side(hidden):
    rows, cols, depth = hidden.shape
    padded = jnp.pad(hidden, ((1, 1), (1, 1), (0, 0)))
    return jnp.concatenate([padded[:, j : j + cols] for j in range(3)], axis=2).reshape(
        (rows + 2) * cols, 3 * depth
    )


def conv_scatter_fused(spread, kernel, cols, n, m, number, riders=()):
    own = kernel.shape[2] // n
    depth = kernel.shape[1]
    pixels = spread.shape[0] - 2 * cols
    return comm_call(
        partial(conv_scatter_kernel, cols),
        (spread, kernel.reshape(3, 3 * depth, kernel.shape[2])),
        (jax.ShapeDtypeStruct((pixels, own), jnp.float32),),
        scatter_scratch(n // 2, pixels, own, CONV_PARTS),
        riders,
        n,
        m,
        number,
    )


def conv_back_kernel(breadth, line, g_ref, w_ref, x_ref, acc_ref, wg_ref, held, sums, send, recv):
    chips = line.chips
    pixels, own = g_ref.shape
    wide = w_ref.shape[1]
    tile, long = 512, 1024
    zero = jnp.zeros((breadth, own), jnp.bfloat16)
    for block in range(2 * chips):
        held[block, pl.ds(0, breadth)] = zero
        held[block, pl.ds(breadth + pixels, breadth)] = zero

    def slot(block):
        return held.at[block, pl.ds(breadth, pixels)]

    def beside(base, count, chip):
        rows = pl.ds(base, count)
        return [held[2 * chip, rows], held[2 * chip + 1, rows]]

    def on_own():
        @pl.loop(0, pixels // tile)
        def _(index):
            acc_ref[pl.ds(pl.multiple_of(index * tile, tile), tile)] = jnp.zeros(
                (tile, wide), jnp.float32
            )

    def on_pair(chip):
        columns = pl.ds(pl.multiple_of(chip * 2 * own, 2 * own), 2 * own)

        @pl.loop(0, pixels // tile)
        def _(index):
            base = pl.multiple_of(index * tile, tile)
            shifted = []
            for i in range(3):
                shifted += beside(base + (2 - i) * breadth, tile, chip)
            acc_ref[pl.ds(base, tile)] += product(
                jnp.concatenate(shifted, axis=1),
                jnp.concatenate([w_ref[i, :, columns] for i in range(3)], axis=1),
                True,
            )

        sums[...] = jnp.zeros_like(sums)

        @pl.loop(0, pixels // long)
        def _(index):
            base = pl.multiple_of(index * long, long)
            sums[...] += lax.dot_general(
                jnp.concatenate(beside(base + breadth, long, chip), axis=1),
                jnp.concatenate(
                    [x_ref[pl.ds(base + i * breadth, long)] for i in range(3)], axis=1
                ),
                (((0,), (0,)), ((), ())),
                preferred_element_type=jnp.float32,
            )

        wg_ref[chip] = sums[...].astype(jnp.bfloat16)

    line_gather(line, g_ref, slot, send, recv, on_own, on_pair)


def conv_back_fused(grad_low, spread, kernel, cols, n, m, number, riders=()):
    pixels, own = grad_low.shape
    depth = kernel.shape[1]
    chips = n // 2
    return comm_call(
        partial(conv_back_kernel, cols),
        (grad_low, kernel.reshape(3, 3 * depth, kernel.shape[2]), spread),
        (
            jax.ShapeDtypeStruct((pixels, 3 * depth), jnp.float32),
            jax.ShapeDtypeStruct((chips, 2 * own, 9 * depth), jnp.bfloat16),
        ),
        [
            pltpu.VMEM((n, pixels + 2 * cols, own), jnp.bfloat16),
            pltpu.VMEM((2 * own, 9 * depth), jnp.float32),
        ]
        + gather_sems(chips),
        riders,
        n,
        m,
        number,
    )


def join_columns(acc, cols):
    pixels, wide = acc.shape
    depth = wide // 3
    planes = acc.reshape(-1, cols, wide)
    none = jnp.zeros_like(planes[:, :1, :depth])
    left = jnp.concatenate([planes[:, 1:, :depth], none], axis=1)
    right = jnp.concatenate([none, planes[:, :-1, 2 * depth :]], axis=1)
    return (left + planes[:, :, depth : 2 * depth] + right).reshape(pixels, depth)


def product(x, w, turned):
    return lax.dot_general(
        x, w, (((1,), (1 if turned else 0,)), ((), ())), preferred_element_type=jnp.float32
    )


def tokens_scatter_kernel(turned, line, x_ref, w_ref, o_ref, *scratch):
    tokens, width = o_ref.shape
    cut = width // TOKEN_PARTS
    depth = x_ref.shape[1] // w_ref.shape[0]

    def produce(chip, part, count, mine, other):
        rows = pl.ds(pl.multiple_of(chip * 2 * tokens, 2 * tokens), 2 * tokens)
        columns = pl.ds(part * cut, cut)
        total = None
        for j in range(w_ref.shape[0]):
            w = w_ref[j, columns] if turned else w_ref[j, :, columns]
            term = product(x_ref[rows, pl.ds(j * depth, depth)], w, turned)
            total = term if total is None else total + term
        first, second = pick(line.c, total[:tokens], total[tokens:])
        mine[pl.ds(part * count, count)] = first
        other[pl.ds(part * count, count)] = second.astype(jnp.bfloat16)

    def finish(part, rows, total):
        o_ref[:, pl.ds(part * cut, cut)] = total

    line_scatter(line, scratch, TOKEN_PARTS, produce, finish, tokens)


def tokens_scatter(x, w, turned, n, m, number, riders=()):
    tokens = x.shape[0] // n
    width = w.shape[1] if turned else w.shape[2]
    return comm_call(
        partial(tokens_scatter_kernel, turned),
        (x, w),
        (jax.ShapeDtypeStruct((tokens, width), jnp.float32),),
        scatter_scratch(n // 2, TOKEN_PARTS * tokens, width // TOKEN_PARTS, TOKEN_PARTS),
        riders,
        n,
        m,
        number,
    )


def tokens_gather_kernel(turned, shape_out, outs, line, x_ref, w_ref, *refs):
    held = refs[0]
    results = refs[1 : 1 + outs]
    send, recv = refs[1 + outs :]
    tokens = x_ref.shape[0]
    across = w_ref.shape[1 if turned else 2]
    cut = min(across, 512)

    def slot(block):
        return held.at[pl.ds(pl.multiple_of(block * tokens, tokens), tokens)]

    def on_pair(chip):
        rows = pl.ds(pl.multiple_of(chip * 2 * tokens, 2 * tokens), 2 * tokens)
        for j in range(w_ref.shape[0]):
            for start in range(0, across, cut):
                w = w_ref[j, pl.ds(start, cut)] if turned else w_ref[j, :, pl.ds(start, cut)]
                values = shape_out(product(held[rows], w, turned))
                for ref, value in zip(results, values):
                    ref[rows, pl.ds(j * across + start, cut)] = value.astype(ref.dtype)

    line_gather(line, x_ref, slot, send, recv, lambda: None, on_pair)


def tokens_gather(x, w, turned, kinds, shape_out, n, m, number, riders=()):
    tokens, width = x.shape
    across = w.shape[0] * w.shape[1 if turned else 2]
    return comm_call(
        partial(tokens_gather_kernel, turned, shape_out, len(kinds)),
        (x, w),
        (jax.ShapeDtypeStruct((tokens * n, width), x.dtype),)
        + tuple(jax.ShapeDtypeStruct((tokens * n, across), kind) for kind in kinds),
        gather_sems(n // 2),
        riders,
        n,
        m,
        number,
    )


def exchange(riders, n, m, number):
    return comm_call(lambda line: None, (), (), [], riders, n, m, number, neighbours=False)


def tiled_up(vector):
    count = -(-vector.shape[0] // 1024) * 1024
    return jnp.pad(vector.astype(jnp.float32), (0, count - vector.shape[0])).reshape(-1, 128)


def attend_scatter_kernel(line, x_ref, valid_ref, w_ref, o_ref, mixed_ref, *scratch):
    tokens, width = o_ref.shape
    wide = mixed_ref.shape[1]
    cut = width // TOKEN_PARTS
    scale = 1.0 / math.sqrt(HEAD_DIM)

    def attend(rows):
        for head in range(wide // HEAD_DIM):
            where = [pl.ds(j * wide + head * HEAD_DIM, HEAD_DIM) for j in range(3)]
            scores = product(x_ref[rows, where[0]], x_ref[:, where[1]], True) * scale
            scores = jnp.where(valid_ref[0:1] > 0.5, scores, MASKED_SCORE)
            exponent = jnp.exp(scores - jnp.max(scores, axis=1, keepdims=True))
            inverse = 1.0 / jnp.sum(exponent, axis=1, keepdims=True)
            mixed_ref[rows, pl.ds(head * HEAD_DIM, HEAD_DIM)] = product(
                (exponent * inverse).astype(jnp.bfloat16), x_ref[:, where[2]], False
            ).astype(jnp.bfloat16)

    def produce(chip, part, count, mine, other):
        rows = pl.ds(pl.multiple_of(chip * 2 * tokens, 2 * tokens), 2 * tokens)
        if part == 0:
            attend(rows)
        total = product(mixed_ref[rows], w_ref[:, pl.ds(part * cut, cut)], False)
        first, second = pick(line.c, total[:tokens], total[tokens:])
        mine[pl.ds(part * count, count)] = first
        other[pl.ds(part * count, count)] = second.astype(jnp.bfloat16)

    def finish(part, rows, total):
        o_ref[:, pl.ds(part * cut, cut)] = total

    line_scatter(line, scratch, TOKEN_PARTS, produce, finish, tokens)


def attend_scatter(qkv_rows, valid, out_weight, n, m, number):
    total = qkv_rows.shape[0]
    tokens = total // n
    width = out_weight.shape[1]
    return comm_call(
        attend_scatter_kernel,
        (qkv_rows, jnp.broadcast_to(valid[None], (8, total)), out_weight),
        (
            jax.ShapeDtypeStruct((tokens, width), jnp.float32),
            jax.ShapeDtypeStruct((total, out_weight.shape[0]), jnp.bfloat16),
        ),
        scatter_scratch(n // 2, TOKEN_PARTS * tokens, width // TOKEN_PARTS, TOKEN_PARTS),
        (),
        n,
        m,
        number,
    )


def attend_gather_kernel(
    line, g_ref, w_ref, x_ref, kt_ref, valid_ref, held, grad_ref, keys_sum, values_sum, send, recv
):
    tokens = g_ref.shape[0]
    wide = w_ref.shape[0]
    heads = wide // HEAD_DIM
    scale = 1.0 / math.sqrt(HEAD_DIM)

    def slot(block):
        return held.at[pl.ds(pl.multiple_of(block * tokens, tokens), tokens)]

    def on_own():
        keys_sum[...] = jnp.zeros_like(keys_sum)
        values_sum[...] = jnp.zeros_like(values_sum)

    def on_pair(chip):
        rows = pl.ds(pl.multiple_of(chip * 2 * tokens, 2 * tokens), 2 * tokens)
        for head in range(heads):
            place = pl.ds(head * HEAD_DIM, HEAD_DIM)
            where = [pl.ds(j * wide + head * HEAD_DIM, HEAD_DIM) for j in range(3)]
            grad = product(held[rows], w_ref[place], True).astype(jnp.bfloat16)
            query = x_ref[rows, where[0]]
            scores = product(x_ref[:, where[1]], query, True) * scale
            scores = jnp.where(valid_ref[:, 0:1] > 0.5, scores, MASKED_SCORE)
            exponent = jnp.exp(scores - jnp.max(scores, axis=0, keepdims=True))
            probs = exponent * (1.0 / jnp.sum(exponent, axis=0, keepdims=True))
            values_sum[:, place] += product(probs.astype(jnp.bfloat16), grad, False)
            grad_probs = product(x_ref[:, where[2]], grad, True)
            inner = jnp.sum(probs * grad_probs, axis=0, keepdims=True)
            grad_scores = (probs * (grad_probs - inner) * scale).astype(jnp.bfloat16)
            keys_sum[:, place] += product(grad_scores, query, False)
            grad_ref[rows, where[0]] = product(kt_ref[place], grad_scores, False).T.astype(
                jnp.bfloat16
            )

    line_gather(line, g_ref, slot, send, recv, on_own, on_pair)
    grad_ref[:, pl.ds(wide, wide)] = keys_sum[...].astype(jnp.bfloat16)
    grad_ref[:, pl.ds(2 * wide, wide)] = values_sum[...].astype(jnp.bfloat16)


def attend_gather(grad_mid, out_weight, qkv_rows, valid, n, m, number, riders):
    tokens, width = grad_mid.shape
    total = tokens * n
    wide = out_weight.shape[0]
    return comm_call(
        attend_gather_kernel,
        (
            grad_mid,
            out_weight,
            qkv_rows,
            qkv_rows[:, wide : 2 * wide].T,
            jnp.broadcast_to(valid[:, None], (total, 128)),
        ),
        (
            jax.ShapeDtypeStruct((total, width), jnp.bfloat16),
            jax.ShapeDtypeStruct((total, 3 * wide), jnp.bfloat16),
        ),
        [pltpu.VMEM((total, wide), jnp.float32), pltpu.VMEM((total, wide), jnp.float32)]
        + gather_sems(n // 2),
        riders,
        n,
        m,
        number,
    )


def local(
    image,
    embedding,
    extents,
    gain_first,
    conv_first,
    gain_second,
    conv_second,
    shift_weight,
    down_weight,
    ada_weight,
    qkv_weight,
    out_weight,
    up_weight,
    proj_weight,
    cotangent,
):
    strip_rows, canvas_cols, channel_count = (image.shape[1], image.shape[2], image.shape[3])
    width_all = out_weight.shape[1]
    n = lax.axis_size("mp")
    m = lax.axis_size("dp")
    me_mp = lax.axis_index("mp")
    me_dp = lax.axis_index("dp")
    rows_all = strip_rows * n
    pixel_total = rows_all * canvas_cols
    own = channel_count // n
    size = channel_count // GROUPS
    token_rows = strip_rows // 2
    token_cols = canvas_cols // 2
    local_tokens = token_rows * token_cols
    token_total = local_tokens * n
    local_width = out_weight.shape[0]

    fused = own % 128 == 0 and n == 2 * m
    shift_vector = jnp.dot(embedding, shift_weight, preferred_element_type=jnp.float32)[0]
    columns = jnp.dot(embedding, ada_weight, preferred_element_type=jnp.float32)[0]
    riders = (Rider("mp", tiled_up(columns)),)
    if fused:
        modulation, pixels_low = exchange(
            riders + (Rider("mp", image[0].reshape(-1, channel_count), 1),), n, m, 12
        )
    else:
        (modulation,) = exchange(riders, n, m, 12)
        pixels_low = lax.all_to_all(image[0], "mp", 2, 0, tiled=True)
    modulation = modulation.reshape(n, -1)[:, : columns.shape[0]].reshape(-1)
    scale_attend = modulation[:width_all]
    shift_attend = modulation[width_all : 2 * width_all]
    scale_mlp = modulation[2 * width_all : 3 * width_all]
    shift_mlp = modulation[3 * width_all :]
    own_first = lax.dynamic_slice_in_dim(gain_first, me_mp * own, own)
    own_second = lax.dynamic_slice_in_dim(gain_second, me_mp * own, own)

    pixels = pixels_low.astype(jnp.float32).reshape(pixel_total, own)
    normed_first, inverse_first = group_forward(pixels, size)
    hidden_first = (
        jax.nn.silu(normed_first * own_first)
        .astype(jnp.bfloat16)
        .reshape(rows_all, canvas_cols, own)
    )
    spread_first = side_by_side(hidden_first)
    if fused:
        (conv_output,) = conv_scatter_fused(spread_first, conv_first, canvas_cols, n, m, 0)
    else:
        conv_output = conv_scatter(hidden_first, conv_first, n)
    conv_output = conv_output + shift_vector
    normed_second, inverse_second = group_forward(conv_output, size)
    hidden_second = (
        jax.nn.silu(normed_second * own_second)
        .astype(jnp.bfloat16)
        .reshape(rows_all, canvas_cols, own)
    )
    spread_second = side_by_side(hidden_second)
    if fused:
        (conv_again,) = conv_scatter_fused(spread_second, conv_second, canvas_cols, n, m, 1)
    else:
        conv_again = conv_scatter(hidden_second, conv_second, n)
    residual = pixels + conv_again
    down_patch = (
        residual.astype(jnp.bfloat16)
        .reshape(rows_all // 2, 2, token_cols, 2, own)
        .transpose(0, 2, 1, 3, 4)
        .reshape(token_total, 4 * own)
    )
    down_matrix = down_weight.reshape(4 * own, width_all)
    (stream,) = tokens_scatter(down_patch, down_matrix[None], False, n, m, 2)
    normed_attend, inverse_attend = layer_forward(stream)
    input_attend = (normed_attend * (1.0 + scale_attend) + shift_attend).astype(jnp.bfloat16)
    all_attend, qkv_rows = tokens_gather(
        input_attend, qkv_weight, False, (jnp.bfloat16,), lambda value: (value,), n, m, 3
    )
    token_index = jnp.arange(token_total, dtype=jnp.int32)
    key_valid = (token_index // token_cols < extents[0, 0]) & (
        token_index % token_cols < extents[0, 1]
    )
    valid = key_valid.astype(jnp.float32)
    attended, mixed_low = attend_scatter(qkv_rows, valid, out_weight, n, m, 4)
    stream_mid = stream + attended
    normed_mlp, inverse_mlp = layer_forward(stream_mid)
    input_mlp = (normed_mlp * (1.0 + scale_mlp) + shift_mlp).astype(jnp.bfloat16)
    all_mlp, upper_proj, activated = tokens_gather(
        input_mlp,
        up_weight[None],
        False,
        (jnp.float32, jnp.bfloat16),
        lambda value: (value, jax.nn.gelu(value, approximate=True)),
        n,
        m,
        5,
    )
    final_stream = stream_mid + scatter_rows(
        jnp.dot(activated, proj_weight, preferred_element_type=jnp.float32)
    )
    output = final_stream.astype(jnp.bfloat16).reshape(1, token_rows, token_cols, width_all)

    grad_final_low = cotangent[0].reshape(local_tokens, width_all)
    grad_final = grad_final_low.astype(jnp.float32)
    all_final = gather_rows(lax.optimization_barrier((grad_final_low, qkv_rows))[0])
    grad_act = jnp.einsum("le,fe->lf", all_final, proj_weight, preferred_element_type=jnp.float32)
    gelu_pull = jax.vjp(partial(jax.nn.gelu, approximate=True), upper_proj)[1]
    grad_upper = gelu_pull(grad_act)[0].astype(jnp.bfloat16)
    grad_proj = jnp.einsum("lf,le->fe", activated, all_final, preferred_element_type=jnp.float32)
    grad_normed_mlp, sums_proj = tokens_scatter(
        grad_upper,
        up_weight[None],
        True,
        n,
        m,
        6,
        (Rider("dp", grad_proj.astype(jnp.bfloat16), 1),),
    )
    grad_up = jnp.einsum("le,lf->ef", all_mlp, grad_upper, preferred_element_type=jnp.float32)
    grad_mid_norm, grad_scale_mlp, grad_shift_mlp = layer_backward(
        grad_normed_mlp, normed_mlp, inverse_mlp, scale_mlp
    )
    grad_mid = grad_final + grad_mid_norm
    all_mid, grad_qkv, sums_up = attend_gather(
        grad_mid.astype(jnp.bfloat16),
        out_weight,
        qkv_rows,
        valid,
        n,
        m,
        7,
        (Rider("dp", grad_up.astype(jnp.bfloat16), 0),),
    )
    grad_out = jnp.einsum("lh,le->he", mixed_low, all_mid, preferred_element_type=jnp.float32)
    grad_normed_attend, sums_out = tokens_scatter(
        grad_qkv, qkv_weight, True, n, m, 8, (Rider("dp", grad_out.astype(jnp.bfloat16), 1),)
    )
    grad_qkv_weight = jnp.einsum(
        "le,lf->ef", all_attend, grad_qkv, preferred_element_type=jnp.float32
    )
    grad_stream_norm, grad_scale_attend, grad_shift_attend = layer_backward(
        grad_normed_attend, normed_attend, inverse_attend, scale_attend
    )
    grad_stream = grad_mid + grad_stream_norm
    grad_modulation = jnp.concatenate(
        [
            tiled_up(piece)
            for piece in jnp.concatenate(
                [grad_scale_attend, grad_shift_attend, grad_scale_mlp, grad_shift_mlp]
            ).reshape(n, -1)
        ]
    )
    all_stream, grad_tap_patch, sums_qkv, ada_columns = tokens_gather(
        grad_stream.astype(jnp.bfloat16),
        down_matrix[None],
        True,
        (jnp.float32,),
        lambda value: (value,),
        n,
        m,
        9,
        (
            Rider("dp", grad_qkv_weight.astype(jnp.bfloat16), 0),
            Rider("mp", grad_modulation, 0),
        ),
    )
    grad_down = jnp.einsum(
        "le,lk->ek", all_stream, down_patch, preferred_element_type=jnp.float32
    )
    ada_columns = added(ada_columns).reshape(-1)[: columns.shape[0]]
    grad_residual = (
        grad_tap_patch.reshape(rows_all // 2, token_cols, 2, 2, own)
        .transpose(0, 2, 1, 3, 4)
        .reshape(pixel_total, own)
    )
    def back(grad_low, hidden, spread, kernel, number, riders):
        if fused:
            acc, parts, *ridden = conv_back_fused(
                grad_low, spread, kernel, canvas_cols, n, m, number, riders
            )
            return join_columns(acc, canvas_cols), parts, ridden
        grad_hidden, grad_kernel = conv_backward(grad_low, hidden, kernel, n)
        return grad_hidden, by_images(grad_kernel, m), exchange(riders, n, m, number)

    grad_hidden_second, parts_second, (sums_down, every_small) = back(
        grad_residual.astype(jnp.bfloat16),
        hidden_second,
        spread_second,
        conv_second,
        10,
        (
            Rider("dp", grad_down.astype(jnp.bfloat16), 0),
            Rider("dp", jnp.concatenate([tiled_up(embedding[0]), tiled_up(ada_columns)])),
        ),
    )
    grad_conv_output, grad_gain_second = group_backward(
        grad_hidden_second, normed_second, inverse_second, own_second, size
    )
    grad_shift = jnp.sum(grad_conv_output, axis=0)
    grad_hidden_first, parts_first, (sums_second, every_shift, turned_down) = back(
        grad_conv_output.astype(jnp.bfloat16),
        hidden_first,
        spread_first,
        conv_first,
        11,
        (
            Rider("dp", parts_second, 0),
            Rider("dp", tiled_up(grad_shift)),
            Turn(added(sums_down).astype(jnp.bfloat16)),
        ),
    )
    grad_base, grad_gain_first = group_backward(
        grad_hidden_first, normed_first, inverse_first, own_first, size
    )
    image_turned = (grad_residual + grad_base).astype(jnp.bfloat16)
    embed_term = jnp.dot(
        grad_shift[None], shift_weight.astype(jnp.float32).T, precision=PRECISE
    ) + jnp.dot(ada_columns[None], ada_weight.astype(jnp.float32).T, precision=PRECISE)
    small = jnp.concatenate(
        [tiled_up(embed_term[0]), tiled_up(jnp.concatenate([grad_gain_first, grad_gain_second]))]
    )
    riders = (
        SumTurn(parts_first),
        Rider("all", small),
        Turn(added(sums_second)[0].astype(jnp.bfloat16)),
    )
    if fused:
        turned_first, small, turned_second, image_turned = exchange(
            riders + (Rider("mp", image_turned, 0, True),), n, m, 13
        )
        image_grad = image_turned.reshape(image.shape)
    else:
        turned_first, small, turned_second = exchange(riders, n, m, 13)
        image_grad = lax.all_to_all(
            image_turned.reshape(rows_all, canvas_cols, own), "mp", 0, 2, tiled=True
        )[None]

    small = small.reshape(m, n, -1)
    embed_count = embedding.shape[1]
    embedding_grad = jnp.sum(
        lax.dynamic_index_in_dim(small, me_dp, axis=0, keepdims=False)[:, :embed_count], axis=0
    )[None]
    gain_start = -(-embed_count // 1024) * 1024
    gains = jnp.sum(small[:, :, gain_start : gain_start + 2 * own], axis=0)
    gains = gains.reshape(n, 2, own).transpose(1, 0, 2).reshape(2, -1)
    piece = channel_count // (m * n)
    gains = lax.dynamic_slice_in_dim(gains, (me_dp * n + me_mp) * piece, piece, axis=1)
    every_small = every_small.reshape(m, -1)
    embed_rows = lax.dynamic_slice_in_dim(
        every_small[:, :embed_count], me_dp * (embed_count // m), embed_count // m, axis=1
    )
    grad_shift_weight = jnp.dot(
        embed_rows.T, every_shift.reshape(m, -1)[:, :own], precision=PRECISE
    )
    grad_ada_weight = jnp.dot(
        embed_rows.T,
        every_small[:, gain_start : gain_start + columns.shape[0]],
        precision=PRECISE,
    )
    qkv_grad = jnp.stack(
        [added(sums_qkv[:, :, j * local_width : (j + 1) * local_width]) for j in range(3)]
    )
    return (
        output,
        image_grad,
        embedding_grad,
        gains[0],
        unturned(turned_first, 9),
        gains[1],
        unturned(turned_second, 9),
        grad_shift_weight,
        unturned(turned_down, 4),
        grad_ada_weight,
        qkv_grad,
        added(sums_out),
        added(sums_up),
        added(sums_proj),
    )


def solution(mesh):
    placed = (
        P("dp", "mp", None, None),
        P("dp", None),
        P("dp", None),
        P(),
        P(None, "mp", None),
        P(),
        P(None, "mp", None),
        P(None, "mp"),
        P(None, "mp", None),
        P(None, "mp"),
        P(None, None, "mp"),
        P("mp", None),
        P(None, "mp"),
        P("mp", None),
        P("dp", "mp", None, None),
    )
    return jax.shard_map(
        local,
        mesh=mesh,
        in_specs=placed,
        out_specs=(
            P("dp", "mp", None, None),
            P("dp", "mp", None, None),
            P("dp", None),
            P(("dp", "mp")),
            P(None, "dp", "mp"),
            P(("dp", "mp")),
            P(None, "dp", "mp"),
            P("dp", "mp"),
            P(None, "dp", "mp"),
            P("dp", "mp"),
            P(None, "dp", "mp"),
            P("mp", "dp"),
            P("dp", "mp"),
            P("mp", "dp"),
        ),
        check_vma=False,
    )
```

```python
from functools import partial
import math

import jax
import jax.numpy as jnp
from jax import lax
from jax.experimental import pallas as pl
from jax.experimental.pallas import tpu as pltpu
from jax.sharding import PartitionSpec as P

HEAD_DIM = 128
GROUPS = 32


GROUP_EPSILON = 1e-05
LAYER_EPSILON = 1e-06
MASKED_SCORE = -1000000000.0
PRECISE = lax.Precision.HIGHEST


def group_spread(per_channel, size):
    grouped = jnp.sum(per_channel.reshape(-1, size), axis=1)
    return jnp.repeat(grouped, size)


def group_forward(values, size):
    counted = values.shape[0] * size
    average = group_spread(jnp.sum(values, axis=0), size) / counted
    centre = values - average
    inverse = lax.rsqrt(
        group_spread(jnp.sum(centre * centre, axis=0), size) / counted + GROUP_EPSILON
    )
    return (centre * inverse, inverse)


def group_backward(incoming, normed, inverse, gain_vec, size):
    pre_act = normed * gain_vec
    sigmoid_part = jax.nn.sigmoid(pre_act)
    through = incoming * sigmoid_part * (1.0 + pre_act * (1.0 - sigmoid_part))
    counted = normed.shape[0] * size
    gain_part = jnp.sum(through * normed, axis=0)
    plain_part = jnp.sum(through, axis=0)
    first_mean = group_spread(plain_part * gain_vec, size) / counted
    second_mean = group_spread(gain_part * gain_vec, size) / counted
    outgoing = inverse * (through * gain_vec - first_mean - normed * second_mean)
    return (outgoing, gain_part)


def windows(planes, flipped):
    row_count, col_count, depth = planes.shape
    padded = jnp.pad(planes, ((1, 1), (1, 1), (0, 0)))
    pieces = []
    for tap_index in range(9):
        row_off, col_off = divmod(tap_index, 3)
        if flipped:
            row_off, col_off = (2 - row_off, 2 - col_off)
        pieces.append(padded[row_off : row_off + row_count, col_off : col_off + col_count])
    return jnp.stack(pieces, axis=2).reshape(row_count * col_count, 9, depth)


def gather_rows(rows):
    return lax.all_gather(rows, "mp", axis=0, tiled=True)


def scatter_rows(rows):
    return lax.psum_scatter(
        rows.astype(jnp.bfloat16), "mp", scatter_dimension=0, tiled=True
    ).astype(jnp.float32)


def conv_scatter(hidden, kernel, n):
    patch = windows(hidden, False)
    depth = kernel.shape[2] // n
    total = jnp.einsum("ptc,tcd->pd", patch, kernel, preferred_element_type=jnp.float32)
    parts = total.astype(jnp.bfloat16).reshape(-1, n, depth).transpose(1, 0, 2)
    return lax.psum_scatter(parts, "mp", scatter_dimension=0, tiled=False).astype(jnp.float32)


def conv_backward(grad_low, hidden, kernel, n):
    row_count, col_count, depth = hidden.shape
    gathered = lax.all_gather(grad_low, "mp", axis=1, tiled=True)
    padded = jnp.pad(gathered, ((col_count, col_count), (0, 0)))
    taps = kernel.reshape(3, 3 * depth, kernel.shape[2])
    acc = sum(
        jnp.einsum(
            "pd,td->pt",
            padded[(2 - i) * col_count : (2 - i) * col_count + row_count * col_count],
            taps[i],
            preferred_element_type=jnp.float32,
        )
        for i in range(3)
    )
    grad_kernel = jnp.einsum(
        "ptc,pd->tcd", windows(hidden, False), gathered, preferred_element_type=jnp.float32
    )
    return (join_columns(acc, col_count), grad_kernel)


def unsettled(parts, m, n):
    return parts.reshape(n, m, -1, parts.shape[-1])


def settled(pieces, taps):
    m, count, outs, _ = pieces.shape
    return (
        pieces.astype(jnp.float32)
        .reshape(m, count, outs, taps, -1)
        .transpose(3, 1, 4, 0, 2)
        .reshape(taps, -1, m * outs)
    )


def added(received):
    return jnp.sum(received.astype(jnp.float32), axis=0)


def layer_forward(stream):
    centre = stream - jnp.mean(stream, axis=1, keepdims=True)
    inverse = lax.rsqrt(jnp.mean(centre * centre, axis=1, keepdims=True) + LAYER_EPSILON)
    return (centre * inverse, inverse)


def layer_backward(incoming, normed, inverse, scale_vec):
    through = incoming * (1.0 + scale_vec)
    outgoing = inverse * (
        through
        - jnp.mean(through, axis=1, keepdims=True)
        - normed * jnp.mean(through * normed, axis=1, keepdims=True)
    )
    return (outgoing, jnp.sum(incoming * normed, axis=0), jnp.sum(incoming, axis=0))


MESH = pl.DeviceIdType.MESH
CONV_PARTS = 4
TOKEN_PARTS = 4
VMEM_BYTES = 60 * 1024 * 1024


class Line:
    def __init__(self, chips, images):
        self.chips = chips
        self.images = images
        self.dp = lax.axis_index("dp")
        self.mp = lax.axis_index("mp")
        self.z = self.mp // 2
        self.c = self.mp % 2
        self.has_up = self.z < chips - 1
        self.has_down = self.z > 0
        self.up = (self.dp, self.mp + 2)
        self.down = (self.dp, self.mp - 2)
        self.sibling = (self.dp, 2 * self.z + 1 - self.c)

    def count(self, axis):
        return {"dp": self.images, "mp": 2 * self.chips, "all": 2 * self.chips * self.images}[axis]

    def index(self, axis):
        return {"dp": self.dp, "mp": self.mp, "all": self.dp * 2 * self.chips + self.mp}[axis]

    def place(self, axis, index):
        if axis == "dp":
            return (index, self.mp)
        if axis == "mp":
            return (self.dp, index)
        return (index // (2 * self.chips), index % (2 * self.chips))

    def peer(self, axis, step):
        return lax.rem(self.index(axis) + step, self.count(axis))

    def barrier(self, axes, neighbours):
        bar = pltpu.get_barrier_semaphore()
        axes = ("all",) if "all" in axes else axes
        steady = 0
        for axis in axes:
            for step in range(1, self.count(axis)):
                target = self.place(axis, self.peer(axis, step))
                pl.semaphore_signal(bar, inc=1, device_id=target, device_id_type=MESH)
            steady += self.count(axis) - 1
        cases = [(steady, None)]
        if neighbours and not ("all" in axes or "mp" in axes):
            pl.semaphore_signal(bar, inc=1, device_id=self.sibling, device_id_type=MESH)

            @pl.when(self.has_up)
            def _():
                pl.semaphore_signal(bar, inc=1, device_id=self.up, device_id_type=MESH)

            @pl.when(self.has_down)
            def _():
                pl.semaphore_signal(bar, inc=1, device_id=self.down, device_id_type=MESH)

            middle = jnp.logical_and(self.has_up, self.has_down)
            cases = [(steady + 3, middle), (steady + 2, jnp.logical_not(middle))]
        for count, when in cases:
            if when is None:
                pl.semaphore_wait(bar, count)
            else:

                @pl.when(when)
                def _():
                    pl.semaphore_wait(bar, count)


class Rider:
    def __init__(self, axis, array, cut=None, beside=False):
        self.axes = (axis,)
        self.axis = axis
        self.array = array
        self.cut = cut
        self.beside = beside

    def result(self, sizes):
        count = sizes[self.axis]
        shape = list(self.array.shape)
        if self.cut is not None:
            shape[self.cut] //= count
        self.columns = shape[-1]
        if self.beside:
            shape[-1] *= count
        else:
            shape = [count] + shape
        return jax.ShapeDtypeStruct(tuple(shape), self.array.dtype)

    def scratch(self, sizes):
        count = sizes[self.axis]
        return [pltpu.SemaphoreType.DMA((count,)), pltpu.SemaphoreType.DMA((count,))]

    def piece(self, ref, index, count):
        if self.cut is None:
            return ref
        size = self.array.shape[self.cut] // count
        where = [slice(None)] * len(self.array.shape)
        where[self.cut] = pl.ds(pl.multiple_of(index * size, size), size)
        return ref.at[tuple(where)]

    def copies(self, line, src, dst, send, recv):
        count, me = line.count(self.axis), line.index(self.axis)
        if self.beside:
            land = dst.at[:, pl.ds(pl.multiple_of(me * self.columns, self.columns), self.columns)]
        else:
            land = dst.at[me]
        made = [pltpu.make_async_copy(self.piece(src, me, count), land, send.at[0])]
        for step in range(1, count):
            peer = line.peer(self.axis, step)
            made.append(
                remote(
                    self.piece(src, peer, count),
                    land,
                    send.at[step],
                    recv.at[step],
                    line.place(self.axis, peer),
                )
            )
        return made

    def start(self, line, src, dst, send, recv):
        for copy in self.copies(line, src, dst, send, recv):
            copy.start()

    def middle(self, phase, *refs):
        pass

    def finish(self, line, src, dst, send, recv):
        for copy in self.copies(line, src, dst, send, recv):
            copy.wait()


class Settle:
    def __init__(self, array, summed):
        self.axes = ("dp", "mp")
        self.array = array
        self.summed = summed

    def result(self, sizes):
        n, m = sizes["mp"], sizes["dp"]
        self.ratio = n // m
        self.tail = tuple(self.array.shape[-2:])
        self.total = jax.ShapeDtypeStruct((n,) + self.tail, self.array.dtype)
        self.out = jax.ShapeDtypeStruct((m, self.ratio) + self.tail, self.array.dtype)
        self.add = Rider("dp", self.array, None if self.summed else 1)
        self.outward = Rider("mp", self.total, 0)
        self.inward = Rider("dp", self.total, 0)
        return self.out

    def scratch(self, sizes):
        n, m = sizes["mp"], sizes["dp"]
        dtype = self.array.dtype
        refs = [pltpu.VMEM((n, 1) + self.tail, dtype)]
        if not self.summed:
            refs += [pltpu.VMEM((m, n, 1) + self.tail, dtype), pltpu.VMEM((n,) + self.tail, dtype)]
            refs += self.add.scratch(sizes)
        return refs + self.outward.scratch(sizes) + self.inward.scratch(sizes)

    def copies(self, step, line, src, dst, stage, *rest):
        if not self.summed:
            got, total = rest[:2]
            if step == 0:
                return self.add.copies(line, src, got, *rest[2:4])
            src, rest = total, rest[4:]
            step -= 1
        if step == 0:
            return self.outward.copies(line, src, stage, *rest[:2])
        return self.inward.copies(line, stage.at[:, 0], dst, *rest[2:4])

    def start(self, *refs):
        for copy in self.copies(0, *refs):
            copy.start()

    def middle(self, phase, line, src, dst, stage, *rest):
        if phase > (0 if self.summed else 1):
            return
        refs = (line, src, dst, stage) + rest
        for copy in self.copies(phase, *refs):
            copy.wait()
        if not self.summed and phase == 0:
            got, total = rest[:2]

            @pl.loop(0, total.shape[0])
            def _(index):
                added_up = got[0, index, 0].astype(jnp.float32)
                for image in range(1, got.shape[0]):
                    added_up += got[image, index, 0].astype(jnp.float32)
                total[index] = added_up.astype(total.dtype)

        for copy in self.copies(phase + 1, *refs):
            copy.start()

    def finish(self, *refs):
        for copy in self.copies(1 if self.summed else 2, *refs):
            copy.wait()


def comm_call(kernel, inputs, out_shapes, scratch, riders, n, m, number, neighbours=True):
    chips = n // 2
    sizes = {"dp": m, "mp": n, "all": m * n}
    ride_shapes = tuple(rider.result(sizes) for rider in riders)
    ride_scratch = [rider.scratch(sizes) for rider in riders]
    any_spec = pl.BlockSpec(memory_space=pl.ANY)
    ni, nr, no = len(inputs), len(riders), len(out_shapes)

    def body(*refs):
        main_in, ride_in = refs[:ni], refs[ni : ni + nr]
        rest = refs[ni + nr :]
        main_out, ride_out = rest[:no], rest[no : no + nr]
        rest = rest[no + nr :]
        main_scratch, rest = rest[: len(scratch)], rest[len(scratch) :]
        line = Line(chips, m)
        line.barrier(sorted(set(axis for rider in riders for axis in rider.axes)), neighbours)
        riding = []
        for rider, src, dst, needs in zip(riders, ride_in, ride_out, ride_scratch):
            riding.append((rider, (line, src, dst) + tuple(rest[: len(needs)])))
            rest = rest[len(needs) :]
        for rider, refs_in in riding:
            rider.start(*refs_in)
        kernel(line, *main_in, *main_out, *main_scratch)
        for phase in range(2):
            for rider, refs_in in riding:
                rider.middle(phase, *refs_in)
        for rider, refs_in in riding:
            rider.finish(*refs_in)

    return pl.pallas_call(
        body,
        out_shape=tuple(out_shapes) + ride_shapes,
        in_specs=whole(ni) + [any_spec] * nr,
        out_specs=tuple(whole(no) + [any_spec] * nr),
        scratch_shapes=list(scratch) + [ref for needs in ride_scratch for ref in needs],
        compiler_params=comm_params(number),
    )(*inputs, *[rider.array for rider in riders])


def remote(src, dst, send, recv, target):
    return pltpu.make_async_remote_copy(
        src_ref=src,
        dst_ref=dst,
        send_sem=send,
        recv_sem=recv,
        device_id=target,
        device_id_type=MESH,
    )


def gather_sems(chips):
    return [pltpu.SemaphoreType.DMA((3, 2, chips)), pltpu.SemaphoreType.DMA((3, 2, chips))]


def line_gather(line, x_ref, slot, send, recv, on_own, on_pair):
    chips = line.chips
    z, c = line.z, line.c

    def hop(stream, step, src, block, target):
        return remote(src, slot(block), send.at[stream, 0, step], recv.at[stream, 0, step], target)

    def across(way, step, src, block):
        return remote(src, slot(block), send.at[2, way, step], recv.at[2, way, step], line.sibling)

    @pl.when(line.has_up)
    def _():
        hop(0, 1, x_ref, line.mp, line.up).start()

    @pl.when(line.has_down)
    def _():
        hop(1, 1, x_ref, line.mp, line.down).start()

    across(0, 0, x_ref, line.mp).start()
    slot(line.mp)[...] = x_ref[...]
    on_own()
    across(0, 0, x_ref, line.mp).wait_recv()
    on_pair(z)
    for step in range(1, chips):
        below, above = z - step, z + step

        @pl.when(below >= 0)
        def _():
            block = 2 * below + c
            hop(0, step, slot(block), block, line.up).wait_recv()
            if step + 1 < chips:

                @pl.when(line.has_up)
                def _():
                    hop(0, step + 1, slot(block), block, line.up).start()

            across(0, step, slot(block), block).start()

        @pl.when(above < chips)
        def _():
            block = 2 * above + c
            hop(1, step, slot(block), block, line.down).wait_recv()
            if step + 1 < chips:

                @pl.when(line.has_down)
                def _():
                    hop(1, step + 1, slot(block), block, line.down).start()

            across(1, step, slot(block), block).start()

        @pl.when(below >= 0)
        def _():
            across(0, step, slot(2 * below + c), 2 * below + c).wait_recv()
            on_pair(below)

        @pl.when(above < chips)
        def _():
            across(1, step, slot(2 * above + c), 2 * above + c).wait_recv()
            on_pair(above)

    @pl.when(line.has_up)
    def _():
        hop(0, 1, x_ref, line.mp, line.up).wait_send()

    @pl.when(line.has_down)
    def _():
        hop(1, 1, x_ref, line.mp, line.down).wait_send()

    across(0, 0, x_ref, line.mp).wait_send()
    for step in range(1, chips):
        below, above = z - step, z + step

        @pl.when(below >= 0)
        def _():
            block = 2 * below + c
            if step + 1 < chips:

                @pl.when(line.has_up)
                def _():
                    hop(0, step + 1, slot(block), block, line.up).wait_send()

            across(0, step, slot(block), block).wait_send()

        @pl.when(above < chips)
        def _():
            block = 2 * above + c
            if step + 1 < chips:

                @pl.when(line.has_down)
                def _():
                    hop(1, step + 1, slot(block), block, line.down).wait_send()

            across(1, step, slot(block), block).wait_send()


def scatter_scratch(chips, rows, cols, parts):
    block = (chips, rows, cols)
    return [
        pltpu.VMEM(block, jnp.float32),
        pltpu.VMEM(block, jnp.bfloat16),
        pltpu.VMEM(block, jnp.bfloat16),
        pltpu.VMEM((2,) + block, jnp.bfloat16),
        pltpu.SemaphoreType.DMA((2, 3, chips, parts)),
    ]


def line_scatter(line, scratch, parts, produce, finish, tile):
    chips = line.chips
    z = line.z
    kept, out_ref, in_ref, moving, sems = scratch
    count = kept.shape[1] // parts

    def span(part):
        return pl.ds(part * count, count)

    def across(chip, part):
        return remote(
            out_ref.at[chip, span(part)],
            in_ref.at[chip, span(part)],
            sems.at[0, 0, chip, part],
            sems.at[1, 0, chip, part],
            line.sibling,
        )

    def hop(way, chip, part):
        target = line.up if way == 0 else line.down
        ref = moving.at[way, chip, span(part)]
        return remote(
            ref, ref, sems.at[0, 1 + way, chip, part], sems.at[1, 1 + way, chip, part], target
        )

    items = []
    for step in range(chips - 1):
        for part in range(parts):
            items.append((0, chips - 1 - step + z, part, step >= z))
            items.append((1, step - (chips - 1 - z), part, step >= chips - 1 - z))
    for part in range(parts):
        items.append((2, z, part, None))

    def run(active, body):
        if active is None:
            body()
        else:
            pl.when(active)(body)

    def start(item):
        way, chip, part, active = item

        def body():
            produce(chip, part, count, kept.at[chip], out_ref.at[chip])
            across(chip, part).start()

        run(active, body)

    def tiles(part, body):
        @pl.loop(0, count // tile)
        def _(index):
            body(pl.ds(pl.multiple_of(part * count + index * tile, tile), tile))

    def close(item):
        way, chip, part, active = item

        def body():
            across(chip, part).wait_recv()
            if way < 2:
                later = line.has_down if way == 0 else line.has_up

                @pl.when(later)
                def _():
                    hop(way, chip, part).wait_recv()

                    def add(rows):
                        moving[way, chip, rows] = (
                            kept[chip, rows]
                            + in_ref[chip, rows].astype(jnp.float32)
                            + moving[way, chip, rows].astype(jnp.float32)
                        ).astype(jnp.bfloat16)

                    tiles(part, add)

                @pl.when(jnp.logical_not(later))
                def _():
                    def add(rows):
                        moving[way, chip, rows] = (
                            kept[chip, rows] + in_ref[chip, rows].astype(jnp.float32)
                        ).astype(jnp.bfloat16)

                    tiles(part, add)

                hop(way, chip, part).start()
            else:

                def total(rows):
                    return kept[chip, rows] + in_ref[chip, rows].astype(jnp.float32)

                def from_side(side, rows):
                    return moving[side, chip, rows].astype(jnp.float32)

                both = jnp.logical_and(line.has_down, line.has_up)

                @pl.when(both)
                def _():
                    hop(0, chip, part).wait_recv()
                    hop(1, chip, part).wait_recv()
                    tiles(
                        part,
                        lambda rows: finish(
                            part, rows, total(rows) + from_side(0, rows) + from_side(1, rows)
                        ),
                    )

                for side, present in ((0, line.has_down), (1, line.has_up)):

                    @pl.when(jnp.logical_and(present, jnp.logical_not(both)))
                    def _():
                        hop(side, chip, part).wait_recv()
                        tiles(
                            part,
                            lambda rows: finish(part, rows, total(rows) + from_side(side, rows)),
                        )

        run(active, body)

    lag = 2
    for index, item in enumerate(items):
        start(item)
        if index >= lag:
            close(items[index - lag])
    for item in items[-lag:]:
        close(item)
    for way, chip, part, active in items:

        def body():
            across(chip, part).wait_send()
            if way < 2:
                hop(way, chip, part).wait_send()

        run(active, body)


def whole(count):
    return [pl.BlockSpec(memory_space=pltpu.VMEM)] * count


def comm_params(number):
    return pltpu.CompilerParams(
        collective_id=number, has_side_effects=True, vmem_limit_bytes=VMEM_BYTES
    )


def pick(c, low, high):
    return jnp.where(c == 0, low, high), jnp.where(c == 0, high, low)


def conv_scatter_kernel(breadth, line, x_ref, w_ref, o_ref, *scratch):
    pixels, own = o_ref.shape
    tile = 512

    def produce(chip, part, count, mine, other):
        columns = pl.ds(pl.multiple_of(chip * 2 * own, 2 * own), 2 * own)

        @pl.loop(0, count // tile)
        def _(index):
            base = pl.multiple_of(part * count + index * tile, tile)
            total = jnp.zeros((tile, 2 * own), jnp.float32)
            for i in range(3):
                total += jnp.dot(
                    x_ref[pl.ds(base + i * breadth, tile)],
                    w_ref[i, :, columns],
                    preferred_element_type=jnp.float32,
                )
            first, second = pick(line.c, total[:, :own], total[:, own:])
            mine[pl.ds(base, tile)] = first
            other[pl.ds(base, tile)] = second.astype(jnp.bfloat16)

    def finish(part, rows, total):
        o_ref[rows] = total

    line_scatter(line, scratch, CONV_PARTS, produce, finish, tile)


def side_by_side(hidden):
    rows, cols, depth = hidden.shape
    padded = jnp.pad(hidden, ((1, 1), (1, 1), (0, 0)))
    return jnp.concatenate([padded[:, j : j + cols] for j in range(3)], axis=2).reshape(
        (rows + 2) * cols, 3 * depth
    )


def conv_scatter_fused(spread, kernel, cols, n, m, number, riders=()):
    own = kernel.shape[2] // n
    depth = kernel.shape[1]
    pixels = spread.shape[0] - 2 * cols
    return comm_call(
        partial(conv_scatter_kernel, cols),
        (spread, kernel.reshape(3, 3 * depth, kernel.shape[2])),
        (jax.ShapeDtypeStruct((pixels, own), jnp.float32),),
        scatter_scratch(n // 2, pixels, own, CONV_PARTS),
        riders,
        n,
        m,
        number,
    )


def conv_back_kernel(breadth, line, g_ref, w_ref, x_ref, acc_ref, wg_ref, held, sums, send, recv):
    chips = line.chips
    pixels, own = g_ref.shape
    wide = w_ref.shape[1]
    tile, long = 512, 1024
    zero = jnp.zeros((breadth, own), jnp.bfloat16)
    for block in range(2 * chips):
        held[block, pl.ds(0, breadth)] = zero
        held[block, pl.ds(breadth + pixels, breadth)] = zero

    def slot(block):
        return held.at[block, pl.ds(breadth, pixels)]

    def beside(base, count, chip):
        rows = pl.ds(base, count)
        return [held[2 * chip, rows], held[2 * chip + 1, rows]]

    def on_own():
        @pl.loop(0, pixels // tile)
        def _(index):
            acc_ref[pl.ds(pl.multiple_of(index * tile, tile), tile)] = jnp.zeros(
                (tile, wide), jnp.float32
            )

    def on_pair(chip):
        columns = pl.ds(pl.multiple_of(chip * 2 * own, 2 * own), 2 * own)

        @pl.loop(0, pixels // tile)
        def _(index):
            base = pl.multiple_of(index * tile, tile)
            shifted = []
            for i in range(3):
                shifted += beside(base + (2 - i) * breadth, tile, chip)
            acc_ref[pl.ds(base, tile)] += product(
                jnp.concatenate(shifted, axis=1),
                jnp.concatenate([w_ref[i, :, columns] for i in range(3)], axis=1),
                True,
            )

        sums[...] = jnp.zeros_like(sums)

        @pl.loop(0, pixels // long)
        def _(index):
            base = pl.multiple_of(index * long, long)
            sums[...] += lax.dot_general(
                jnp.concatenate(beside(base + breadth, long, chip), axis=1),
                jnp.concatenate(
                    [x_ref[pl.ds(base + i * breadth, long)] for i in range(3)], axis=1
                ),
                (((0,), (0,)), ((), ())),
                preferred_element_type=jnp.float32,
            )

        wg_ref[chip] = sums[...].astype(jnp.bfloat16)

    line_gather(line, g_ref, slot, send, recv, on_own, on_pair)


def conv_back_fused(grad_low, spread, kernel, cols, n, m, number, riders=()):
    pixels, own = grad_low.shape
    depth = kernel.shape[1]
    chips = n // 2
    return comm_call(
        partial(conv_back_kernel, cols),
        (grad_low, kernel.reshape(3, 3 * depth, kernel.shape[2]), spread),
        (
            jax.ShapeDtypeStruct((pixels, 3 * depth), jnp.float32),
            jax.ShapeDtypeStruct((chips, 2 * own, 9 * depth), jnp.bfloat16),
        ),
        [
            pltpu.VMEM((n, pixels + 2 * cols, own), jnp.bfloat16),
            pltpu.VMEM((2 * own, 9 * depth), jnp.float32),
        ]
        + gather_sems(chips),
        riders,
        n,
        m,
        number,
    )


def join_columns(acc, cols):
    pixels, wide = acc.shape
    depth = wide // 3
    planes = acc.reshape(-1, cols, wide)
    none = jnp.zeros_like(planes[:, :1, :depth])
    left = jnp.concatenate([planes[:, 1:, :depth], none], axis=1)
    right = jnp.concatenate([none, planes[:, :-1, 2 * depth :]], axis=1)
    return (left + planes[:, :, depth : 2 * depth] + right).reshape(pixels, depth)


def product(x, w, turned):
    return lax.dot_general(
        x, w, (((1,), (1 if turned else 0,)), ((), ())), preferred_element_type=jnp.float32
    )


def tokens_scatter_kernel(turned, line, x_ref, w_ref, o_ref, *scratch):
    tokens, width = o_ref.shape
    cut = width // TOKEN_PARTS
    depth = x_ref.shape[1] // w_ref.shape[0]

    def produce(chip, part, count, mine, other):
        rows = pl.ds(pl.multiple_of(chip * 2 * tokens, 2 * tokens), 2 * tokens)
        columns = pl.ds(part * cut, cut)
        total = None
        for j in range(w_ref.shape[0]):
            w = w_ref[j, columns] if turned else w_ref[j, :, columns]
            term = product(x_ref[rows, pl.ds(j * depth, depth)], w, turned)
            total = term if total is None else total + term
        first, second = pick(line.c, total[:tokens], total[tokens:])
        mine[pl.ds(part * count, count)] = first
        other[pl.ds(part * count, count)] = second.astype(jnp.bfloat16)

    def finish(part, rows, total):
        o_ref[:, pl.ds(part * cut, cut)] = total

    line_scatter(line, scratch, TOKEN_PARTS, produce, finish, tokens)


def tokens_scatter(x, w, turned, n, m, number, riders=()):
    tokens = x.shape[0] // n
    width = w.shape[1] if turned else w.shape[2]
    return comm_call(
        partial(tokens_scatter_kernel, turned),
        (x, w),
        (jax.ShapeDtypeStruct((tokens, width), jnp.float32),),
        scatter_scratch(n // 2, TOKEN_PARTS * tokens, width // TOKEN_PARTS, TOKEN_PARTS),
        riders,
        n,
        m,
        number,
    )


def add_outer(total, left, right, rows):
    cut = min(left.shape[1], 512)
    for start in range(0, left.shape[1], cut):
        total[pl.ds(start, cut)] += lax.dot_general(
            left[rows, pl.ds(start, cut)],
            right[rows],
            (((0,), (0,)), ((), ())),
            preferred_element_type=jnp.float32,
        )


def tokens_gather_kernel(turned, shape_out, outs, side, line, x_ref, w_ref, *refs):
    if side:
        left, refs = refs[0], refs[1:]
    held = refs[0]
    results = refs[1 : 1 + outs]
    refs = refs[1 + outs :]
    if side:
        grad, total, refs = refs[0], refs[1], refs[2:]
    send, recv = refs
    tokens = x_ref.shape[0]
    across = w_ref.shape[1 if turned else 2]
    cut = min(across, 512)

    def slot(block):
        return held.at[pl.ds(pl.multiple_of(block * tokens, tokens), tokens)]

    def on_pair(chip):
        rows = pl.ds(pl.multiple_of(chip * 2 * tokens, 2 * tokens), 2 * tokens)
        for j in range(w_ref.shape[0]):
            for start in range(0, across, cut):
                w = w_ref[j, pl.ds(start, cut)] if turned else w_ref[j, :, pl.ds(start, cut)]
                values = shape_out(product(held[rows], w, turned))
                for ref, value in zip(results, values):
                    ref[rows, pl.ds(j * across + start, cut)] = value.astype(ref.dtype)
        if side:
            add_outer(total, held, left, rows)

    def on_own():
        if side:
            total[...] = jnp.zeros_like(total)

    line_gather(line, x_ref, slot, send, recv, on_own, on_pair)
    if side:
        grad[...] = total[...].astype(grad.dtype)


def tokens_gather(x, w, turned, kinds, shape_out, n, m, number, riders=(), left=None):
    tokens, width = x.shape
    across = w.shape[0] * w.shape[1 if turned else 2]
    side = left is not None
    grads = ((width, left.shape[1]),) if side else ()
    return comm_call(
        partial(tokens_gather_kernel, turned, shape_out, len(kinds), side),
        (x, w) + ((left,) if side else ()),
        (jax.ShapeDtypeStruct((tokens * n, width), x.dtype),)
        + tuple(jax.ShapeDtypeStruct((tokens * n, across), kind) for kind in kinds)
        + tuple(jax.ShapeDtypeStruct(shape, jnp.bfloat16) for shape in grads),
        [pltpu.VMEM(shape, jnp.float32) for shape in grads] + gather_sems(n // 2),
        riders,
        n,
        m,
        number,
    )


def exchange(riders, n, m, number):
    return comm_call(lambda line: None, (), (), [], riders, n, m, number, neighbours=False)


def tiled_up(vector):
    count = -(-vector.shape[0] // 1024) * 1024
    return jnp.pad(vector.astype(jnp.float32), (0, count - vector.shape[0])).reshape(-1, 128)


def attend_scatter_kernel(line, x_ref, valid_ref, w_ref, o_ref, mixed_ref, *scratch):
    tokens, width = o_ref.shape
    wide = mixed_ref.shape[1]
    cut = width // TOKEN_PARTS
    scale = 1.0 / math.sqrt(HEAD_DIM)

    def attend(rows):
        for head in range(wide // HEAD_DIM):
            where = [pl.ds(j * wide + head * HEAD_DIM, HEAD_DIM) for j in range(3)]
            scores = product(x_ref[rows, where[0]], x_ref[:, where[1]], True) * scale
            scores = jnp.where(valid_ref[0:1] > 0.5, scores, MASKED_SCORE)
            exponent = jnp.exp(scores - jnp.max(scores, axis=1, keepdims=True))
            inverse = 1.0 / jnp.sum(exponent, axis=1, keepdims=True)
            mixed_ref[rows, pl.ds(head * HEAD_DIM, HEAD_DIM)] = product(
                (exponent * inverse).astype(jnp.bfloat16), x_ref[:, where[2]], False
            ).astype(jnp.bfloat16)

    def produce(chip, part, count, mine, other):
        rows = pl.ds(pl.multiple_of(chip * 2 * tokens, 2 * tokens), 2 * tokens)
        if part == 0:
            attend(rows)
        total = product(mixed_ref[rows], w_ref[:, pl.ds(part * cut, cut)], False)
        first, second = pick(line.c, total[:tokens], total[tokens:])
        mine[pl.ds(part * count, count)] = first
        other[pl.ds(part * count, count)] = second.astype(jnp.bfloat16)

    def finish(part, rows, total):
        o_ref[:, pl.ds(part * cut, cut)] = total

    line_scatter(line, scratch, TOKEN_PARTS, produce, finish, tokens)


def attend_scatter(qkv_rows, valid, out_weight, n, m, number):
    total = qkv_rows.shape[0]
    tokens = total // n
    width = out_weight.shape[1]
    return comm_call(
        attend_scatter_kernel,
        (qkv_rows, jnp.broadcast_to(valid[None], (8, total)), out_weight),
        (
            jax.ShapeDtypeStruct((tokens, width), jnp.float32),
            jax.ShapeDtypeStruct((total, out_weight.shape[0]), jnp.bfloat16),
        ),
        scatter_scratch(n // 2, TOKEN_PARTS * tokens, width // TOKEN_PARTS, TOKEN_PARTS),
        (),
        n,
        m,
        number,
    )


def attend_gather_kernel(
    line,
    g_ref,
    w_ref,
    x_ref,
    kt_ref,
    valid_ref,
    mixed_ref,
    held,
    grad_ref,
    out_ref,
    keys_sum,
    values_sum,
    out_sum,
    send,
    recv,
):
    tokens = g_ref.shape[0]
    wide = w_ref.shape[0]
    heads = wide // HEAD_DIM
    scale = 1.0 / math.sqrt(HEAD_DIM)

    def slot(block):
        return held.at[pl.ds(pl.multiple_of(block * tokens, tokens), tokens)]

    def on_own():
        keys_sum[...] = jnp.zeros_like(keys_sum)
        values_sum[...] = jnp.zeros_like(values_sum)
        out_sum[...] = jnp.zeros_like(out_sum)

    def on_pair(chip):
        rows = pl.ds(pl.multiple_of(chip * 2 * tokens, 2 * tokens), 2 * tokens)
        for head in range(heads):
            place = pl.ds(head * HEAD_DIM, HEAD_DIM)
            where = [pl.ds(j * wide + head * HEAD_DIM, HEAD_DIM) for j in range(3)]
            grad = product(held[rows], w_ref[place], True).astype(jnp.bfloat16)
            query = x_ref[rows, where[0]]
            scores = product(x_ref[:, where[1]], query, True) * scale
            scores = jnp.where(valid_ref[:, 0:1] > 0.5, scores, MASKED_SCORE)
            exponent = jnp.exp(scores - jnp.max(scores, axis=0, keepdims=True))
            probs = exponent * (1.0 / jnp.sum(exponent, axis=0, keepdims=True))
            values_sum[:, place] += product(probs.astype(jnp.bfloat16), grad, False)
            grad_probs = product(x_ref[:, where[2]], grad, True)
            inner = jnp.sum(probs * grad_probs, axis=0, keepdims=True)
            grad_scores = (probs * (grad_probs - inner) * scale).astype(jnp.bfloat16)
            keys_sum[:, place] += product(grad_scores, query, False)
            grad_ref[rows, where[0]] = product(kt_ref[place], grad_scores, False).T.astype(
                jnp.bfloat16
            )
        add_outer(out_sum, mixed_ref, held, rows)

    line_gather(line, g_ref, slot, send, recv, on_own, on_pair)
    grad_ref[:, pl.ds(wide, wide)] = keys_sum[...].astype(jnp.bfloat16)
    grad_ref[:, pl.ds(2 * wide, wide)] = values_sum[...].astype(jnp.bfloat16)
    out_ref[...] = out_sum[...].astype(jnp.bfloat16)


def attend_gather(grad_mid, out_weight, qkv_rows, valid, mixed_low, n, m, number, riders):
    tokens, width = grad_mid.shape
    total = tokens * n
    wide = out_weight.shape[0]
    return comm_call(
        attend_gather_kernel,
        (
            grad_mid,
            out_weight,
            qkv_rows,
            qkv_rows[:, wide : 2 * wide].T,
            jnp.broadcast_to(valid[:, None], (total, 128)),
            mixed_low,
        ),
        (
            jax.ShapeDtypeStruct((total, width), jnp.bfloat16),
            jax.ShapeDtypeStruct((total, 3 * wide), jnp.bfloat16),
            jax.ShapeDtypeStruct((wide, width), jnp.bfloat16),
        ),
        [
            pltpu.VMEM((total, wide), jnp.float32),
            pltpu.VMEM((total, wide), jnp.float32),
            pltpu.VMEM((wide, width), jnp.float32),
        ]
        + gather_sems(n // 2),
        riders,
        n,
        m,
        number,
    )


def local(
    image,
    embedding,
    extents,
    gain_first,
    conv_first,
    gain_second,
    conv_second,
    shift_weight,
    down_weight,
    ada_weight,
    qkv_weight,
    out_weight,
    up_weight,
    proj_weight,
    cotangent,
):
    strip_rows, canvas_cols, channel_count = (image.shape[1], image.shape[2], image.shape[3])
    width_all = out_weight.shape[1]
    n = lax.axis_size("mp")
    m = lax.axis_size("dp")
    me_mp = lax.axis_index("mp")
    me_dp = lax.axis_index("dp")
    rows_all = strip_rows * n
    pixel_total = rows_all * canvas_cols
    own = channel_count // n
    size = channel_count // GROUPS
    token_rows = strip_rows // 2
    token_cols = canvas_cols // 2
    local_tokens = token_rows * token_cols
    token_total = local_tokens * n
    local_width = out_weight.shape[0]

    fused = own % 128 == 0 and n == 2 * m
    shift_vector = jnp.dot(embedding, shift_weight, preferred_element_type=jnp.float32)[0]
    columns = jnp.dot(embedding, ada_weight, preferred_element_type=jnp.float32)[0]
    riders = (Rider("mp", tiled_up(columns)),)
    if fused:
        modulation, pixels_low = exchange(
            riders + (Rider("mp", image[0].reshape(-1, channel_count), 1),), n, m, 12
        )
    else:
        (modulation,) = exchange(riders, n, m, 12)
        pixels_low = lax.all_to_all(image[0], "mp", 2, 0, tiled=True)
    modulation = modulation.reshape(n, -1)[:, : columns.shape[0]].reshape(-1)
    scale_attend = modulation[:width_all]
    shift_attend = modulation[width_all : 2 * width_all]
    scale_mlp = modulation[2 * width_all : 3 * width_all]
    shift_mlp = modulation[3 * width_all :]
    own_first = lax.dynamic_slice_in_dim(gain_first, me_mp * own, own)
    own_second = lax.dynamic_slice_in_dim(gain_second, me_mp * own, own)

    pixels = pixels_low.astype(jnp.float32).reshape(pixel_total, own)
    normed_first, inverse_first = group_forward(pixels, size)
    hidden_first = (
        jax.nn.silu(normed_first * own_first)
        .astype(jnp.bfloat16)
        .reshape(rows_all, canvas_cols, own)
    )
    spread_first = side_by_side(hidden_first)
    if fused:
        (conv_output,) = conv_scatter_fused(spread_first, conv_first, canvas_cols, n, m, 0)
    else:
        conv_output = conv_scatter(hidden_first, conv_first, n)
    conv_output = conv_output + shift_vector
    normed_second, inverse_second = group_forward(conv_output, size)
    hidden_second = (
        jax.nn.silu(normed_second * own_second)
        .astype(jnp.bfloat16)
        .reshape(rows_all, canvas_cols, own)
    )
    spread_second = side_by_side(hidden_second)
    if fused:
        (conv_again,) = conv_scatter_fused(spread_second, conv_second, canvas_cols, n, m, 1)
    else:
        conv_again = conv_scatter(hidden_second, conv_second, n)
    residual = pixels + conv_again
    down_patch = (
        residual.astype(jnp.bfloat16)
        .reshape(rows_all // 2, 2, token_cols, 2, own)
        .transpose(0, 2, 1, 3, 4)
        .reshape(token_total, 4 * own)
    )
    down_matrix = down_weight.reshape(4 * own, width_all)
    (stream,) = tokens_scatter(down_patch, down_matrix[None], False, n, m, 2)
    normed_attend, inverse_attend = layer_forward(stream)
    input_attend = (normed_attend * (1.0 + scale_attend) + shift_attend).astype(jnp.bfloat16)
    all_attend, qkv_rows = tokens_gather(
        input_attend, qkv_weight, False, (jnp.bfloat16,), lambda value: (value,), n, m, 3
    )
    token_index = jnp.arange(token_total, dtype=jnp.int32)
    key_valid = (token_index // token_cols < extents[0, 0]) & (
        token_index % token_cols < extents[0, 1]
    )
    valid = key_valid.astype(jnp.float32)
    attended, mixed_low = attend_scatter(qkv_rows, valid, out_weight, n, m, 4)
    stream_mid = stream + attended
    normed_mlp, inverse_mlp = layer_forward(stream_mid)
    input_mlp = (normed_mlp * (1.0 + scale_mlp) + shift_mlp).astype(jnp.bfloat16)
    all_mlp, upper_proj, activated = tokens_gather(
        input_mlp,
        up_weight[None],
        False,
        (jnp.float32, jnp.bfloat16),
        lambda value: (value, jax.nn.gelu(value, approximate=True)),
        n,
        m,
        5,
    )
    final_stream = stream_mid + scatter_rows(
        jnp.dot(activated, proj_weight, preferred_element_type=jnp.float32)
    )
    output = final_stream.astype(jnp.bfloat16).reshape(1, token_rows, token_cols, width_all)

    grad_final_low = cotangent[0].reshape(local_tokens, width_all)
    grad_final = grad_final_low.astype(jnp.float32)
    all_final = gather_rows(lax.optimization_barrier((grad_final_low, qkv_rows))[0])
    grad_act = jnp.einsum("le,fe->lf", all_final, proj_weight, preferred_element_type=jnp.float32)
    gelu_pull = jax.vjp(partial(jax.nn.gelu, approximate=True), upper_proj)[1]
    grad_upper = gelu_pull(grad_act)[0].astype(jnp.bfloat16)
    grad_proj = jnp.einsum("lf,le->fe", activated, all_final, preferred_element_type=jnp.float32)
    grad_normed_mlp, sums_proj = tokens_scatter(
        grad_upper,
        up_weight[None],
        True,
        n,
        m,
        6,
        (Rider("dp", grad_proj.astype(jnp.bfloat16), 1),),
    )
    grad_up = jnp.einsum("le,lf->ef", all_mlp, grad_upper, preferred_element_type=jnp.float32)
    grad_mid_norm, grad_scale_mlp, grad_shift_mlp = layer_backward(
        grad_normed_mlp, normed_mlp, inverse_mlp, scale_mlp
    )
    grad_mid = grad_final + grad_mid_norm
    all_mid, grad_qkv, grad_out, sums_up = attend_gather(
        grad_mid.astype(jnp.bfloat16),
        out_weight,
        qkv_rows,
        valid,
        mixed_low,
        n,
        m,
        7,
        (Rider("dp", grad_up.astype(jnp.bfloat16), 0),),
    )
    grad_normed_attend, sums_out = tokens_scatter(
        grad_qkv, qkv_weight, True, n, m, 8, (Rider("dp", grad_out, 1),)
    )
    grad_qkv_weight = jnp.einsum(
        "le,lf->ef", all_attend, grad_qkv, preferred_element_type=jnp.float32
    )
    grad_stream_norm, grad_scale_attend, grad_shift_attend = layer_backward(
        grad_normed_attend, normed_attend, inverse_attend, scale_attend
    )
    grad_stream = grad_mid + grad_stream_norm
    grad_modulation = jnp.concatenate(
        [
            tiled_up(piece)
            for piece in jnp.concatenate(
                [grad_scale_attend, grad_shift_attend, grad_scale_mlp, grad_shift_mlp]
            ).reshape(n, -1)
        ]
    )
    all_stream, grad_tap_patch, grad_down, sums_qkv, ada_columns = tokens_gather(
        grad_stream.astype(jnp.bfloat16),
        down_matrix[None],
        True,
        (jnp.float32,),
        lambda value: (value,),
        n,
        m,
        9,
        (
            Rider("dp", grad_qkv_weight.astype(jnp.bfloat16), 0),
            Rider("mp", grad_modulation, 0),
        ),
        down_patch,
    )
    ada_columns = added(ada_columns).reshape(-1)[: columns.shape[0]]
    grad_residual = (
        grad_tap_patch.reshape(rows_all // 2, token_cols, 2, 2, own)
        .transpose(0, 2, 1, 3, 4)
        .reshape(pixel_total, own)
    )
    def back(grad_low, hidden, spread, kernel, number, riders):
        if fused:
            acc, parts, *ridden = conv_back_fused(
                grad_low, spread, kernel, canvas_cols, n, m, number, riders
            )
            return join_columns(acc, canvas_cols), parts, ridden
        grad_hidden, grad_kernel = conv_backward(grad_low, hidden, kernel, n)
        parts = grad_kernel.astype(jnp.bfloat16).reshape(9 * own, -1).T
        return grad_hidden, parts, exchange(riders, n, m, number)

    grad_hidden_second, parts_second, (sums_down, every_small) = back(
        grad_residual.astype(jnp.bfloat16),
        hidden_second,
        spread_second,
        conv_second,
        10,
        (
            Rider("dp", unsettled(grad_down, m, n), 1),
            Rider("dp", jnp.concatenate([tiled_up(embedding[0]), tiled_up(ada_columns)])),
        ),
    )
    grad_conv_output, grad_gain_second = group_backward(
        grad_hidden_second, normed_second, inverse_second, own_second, size
    )
    grad_shift = jnp.sum(grad_conv_output, axis=0)
    grad_hidden_first, parts_first, (sums_second, every_shift, pieces_down) = back(
        grad_conv_output.astype(jnp.bfloat16),
        hidden_first,
        spread_first,
        conv_first,
        11,
        (
            Rider("dp", unsettled(parts_second, m, n), 1),
            Rider("dp", tiled_up(grad_shift)),
            Settle(added(sums_down)[:, 0].astype(jnp.bfloat16), True),
        ),
    )
    grad_base, grad_gain_first = group_backward(
        grad_hidden_first, normed_first, inverse_first, own_first, size
    )
    image_turned = (grad_residual + grad_base).astype(jnp.bfloat16)
    embed_term = jnp.dot(
        grad_shift[None], shift_weight.astype(jnp.float32).T, precision=PRECISE
    ) + jnp.dot(ada_columns[None], ada_weight.astype(jnp.float32).T, precision=PRECISE)
    small = jnp.concatenate(
        [tiled_up(embed_term[0]), tiled_up(jnp.concatenate([grad_gain_first, grad_gain_second]))]
    )
    riders = (
        Settle(unsettled(parts_first, m, n), False),
        Rider("all", small),
        Settle(added(sums_second)[:, 0].astype(jnp.bfloat16), True),
    )
    if fused:
        pieces_first, small, pieces_second, image_turned = exchange(
            riders + (Rider("mp", image_turned, 0, True),), n, m, 13
        )
        image_grad = image_turned.reshape(image.shape)
    else:
        pieces_first, small, pieces_second = exchange(riders, n, m, 13)
        image_grad = lax.all_to_all(
            image_turned.reshape(rows_all, canvas_cols, own), "mp", 0, 2, tiled=True
        )[None]

    small = small.reshape(m, n, -1)
    embed_count = embedding.shape[1]
    embedding_grad = jnp.sum(
        lax.dynamic_index_in_dim(small, me_dp, axis=0, keepdims=False)[:, :embed_count], axis=0
    )[None]
    gain_start = -(-embed_count // 1024) * 1024
    gains = jnp.sum(small[:, :, gain_start : gain_start + 2 * own], axis=0)
    gains = gains.reshape(n, 2, own).transpose(1, 0, 2).reshape(2, -1)
    piece = channel_count // (m * n)
    gains = lax.dynamic_slice_in_dim(gains, (me_dp * n + me_mp) * piece, piece, axis=1)
    every_small = every_small.reshape(m, -1)
    embed_rows = lax.dynamic_slice_in_dim(
        every_small[:, :embed_count], me_dp * (embed_count // m), embed_count // m, axis=1
    )
    grad_shift_weight = jnp.dot(
        embed_rows.T, every_shift.reshape(m, -1)[:, :own], precision=PRECISE
    )
    grad_ada_weight = jnp.dot(
        embed_rows.T,
        every_small[:, gain_start : gain_start + columns.shape[0]],
        precision=PRECISE,
    )
    qkv_grad = jnp.stack(
        [added(sums_qkv[:, :, j * local_width : (j + 1) * local_width]) for j in range(3)]
    )
    return (
        output,
        image_grad,
        embedding_grad,
        gains[0],
        settled(pieces_first, 9),
        gains[1],
        settled(pieces_second, 9),
        grad_shift_weight,
        settled(pieces_down, 4),
        grad_ada_weight,
        qkv_grad,
        added(sums_out),
        added(sums_up),
        added(sums_proj),
    )


def solution(mesh):
    placed = (
        P("dp", "mp", None, None),
        P("dp", None),
        P("dp", None),
        P(),
        P(None, "mp", None),
        P(),
        P(None, "mp", None),
        P(None, "mp"),
        P(None, "mp", None),
        P(None, "mp"),
        P(None, None, "mp"),
        P("mp", None),
        P(None, "mp"),
        P("mp", None),
        P("dp", "mp", None, None),
    )
    return jax.shard_map(
        local,
        mesh=mesh,
        in_specs=placed,
        out_specs=(
            P("dp", "mp", None, None),
            P("dp", "mp", None, None),
            P("dp", None),
            P(("dp", "mp")),
            P(None, "dp", "mp"),
            P(("dp", "mp")),
            P(None, "dp", "mp"),
            P("dp", "mp"),
            P(None, "dp", "mp"),
            P("dp", "mp"),
            P(None, "dp", "mp"),
            P("mp", "dp"),
            P("dp", "mp"),
            P("mp", "dp"),
        ),
        check_vma=False,
    )
```

```python
from functools import partial
import math

import jax
import jax.numpy as jnp
from jax import lax
from jax.experimental import pallas as pl
from jax.experimental.pallas import tpu as pltpu
from jax.sharding import PartitionSpec as P

HEAD_DIM = 128
GROUPS = 32


GROUP_EPSILON = 1e-05
LAYER_EPSILON = 1e-06
MASKED_SCORE = -1000000000.0
PRECISE = lax.Precision.HIGHEST


def group_spread(per_channel, size):
    grouped = jnp.sum(per_channel.reshape(-1, size), axis=1)
    return jnp.repeat(grouped, size)


def group_forward(values, size):
    counted = values.shape[0] * size
    average = group_spread(jnp.sum(values, axis=0), size) / counted
    centre = values - average
    inverse = lax.rsqrt(
        group_spread(jnp.sum(centre * centre, axis=0), size) / counted + GROUP_EPSILON
    )
    return (centre * inverse, inverse)


def group_backward(incoming, normed, inverse, gain_vec, size):
    pre_act = normed * gain_vec
    sigmoid_part = jax.nn.sigmoid(pre_act)
    through = incoming * sigmoid_part * (1.0 + pre_act * (1.0 - sigmoid_part))
    counted = normed.shape[0] * size
    gain_part = jnp.sum(through * normed, axis=0)
    plain_part = jnp.sum(through, axis=0)
    first_mean = group_spread(plain_part * gain_vec, size) / counted
    second_mean = group_spread(gain_part * gain_vec, size) / counted
    outgoing = inverse * (through * gain_vec - first_mean - normed * second_mean)
    return (outgoing, gain_part)


def windows(planes, flipped):
    row_count, col_count, depth = planes.shape
    padded = jnp.pad(planes, ((1, 1), (1, 1), (0, 0)))
    pieces = []
    for tap_index in range(9):
        row_off, col_off = divmod(tap_index, 3)
        if flipped:
            row_off, col_off = (2 - row_off, 2 - col_off)
        pieces.append(padded[row_off : row_off + row_count, col_off : col_off + col_count])
    return jnp.stack(pieces, axis=2).reshape(row_count * col_count, 9, depth)


def gather_rows(rows):
    return lax.all_gather(rows, "mp", axis=0, tiled=True)


def scatter_rows(rows):
    return lax.psum_scatter(
        rows.astype(jnp.bfloat16), "mp", scatter_dimension=0, tiled=True
    ).astype(jnp.float32)


def conv_scatter(hidden, kernel, n):
    patch = windows(hidden, False)
    depth = kernel.shape[2] // n
    total = jnp.einsum("ptc,tcd->pd", patch, kernel, preferred_element_type=jnp.float32)
    parts = total.astype(jnp.bfloat16).reshape(-1, n, depth).transpose(1, 0, 2)
    return lax.psum_scatter(parts, "mp", scatter_dimension=0, tiled=False).astype(jnp.float32)


def conv_backward(grad_low, hidden, kernel, n):
    row_count, col_count, depth = hidden.shape
    gathered = lax.all_gather(grad_low, "mp", axis=1, tiled=True)
    padded = jnp.pad(gathered, ((col_count, col_count), (0, 0)))
    taps = kernel.reshape(3, 3 * depth, kernel.shape[2])
    acc = sum(
        jnp.einsum(
            "pd,td->pt",
            padded[(2 - i) * col_count : (2 - i) * col_count + row_count * col_count],
            taps[i],
            preferred_element_type=jnp.float32,
        )
        for i in range(3)
    )
    grad_kernel = jnp.einsum(
        "ptc,pd->tcd", windows(hidden, False), gathered, preferred_element_type=jnp.float32
    )
    return (join_columns(acc, col_count), grad_kernel)


def unsettled(parts, m, n):
    return parts.reshape(n, m, -1, parts.shape[-1])


def settled(pieces, taps):
    if pieces.ndim == 3:
        return pieces
    m, count, outs, _ = pieces.shape
    return (
        pieces.astype(jnp.float32)
        .reshape(m, count, outs, taps, -1)
        .transpose(3, 1, 4, 0, 2)
        .reshape(taps, -1, m * outs)
    )


def added(received):
    return jnp.sum(received.astype(jnp.float32), axis=0)


def layer_forward(stream):
    centre = stream - jnp.mean(stream, axis=1, keepdims=True)
    inverse = lax.rsqrt(jnp.mean(centre * centre, axis=1, keepdims=True) + LAYER_EPSILON)
    return (centre * inverse, inverse)


def layer_backward(incoming, normed, inverse, scale_vec):
    through = incoming * (1.0 + scale_vec)
    outgoing = inverse * (
        through
        - jnp.mean(through, axis=1, keepdims=True)
        - normed * jnp.mean(through * normed, axis=1, keepdims=True)
    )
    return (outgoing, jnp.sum(incoming * normed, axis=0), jnp.sum(incoming, axis=0))


MESH = pl.DeviceIdType.MESH
CONV_PARTS = 4
TOKEN_PARTS = 4
VMEM_BYTES = 60 * 1024 * 1024


class Line:
    def __init__(self, chips, images):
        self.chips = chips
        self.images = images
        self.dp = lax.axis_index("dp")
        self.mp = lax.axis_index("mp")
        self.z = self.mp // 2
        self.c = self.mp % 2
        self.has_up = self.z < chips - 1
        self.has_down = self.z > 0
        self.up = (self.dp, self.mp + 2)
        self.down = (self.dp, self.mp - 2)
        self.sibling = (self.dp, 2 * self.z + 1 - self.c)

    def count(self, axis):
        return {"dp": self.images, "mp": 2 * self.chips, "all": 2 * self.chips * self.images}[axis]

    def index(self, axis):
        return {"dp": self.dp, "mp": self.mp, "all": self.dp * 2 * self.chips + self.mp}[axis]

    def place(self, axis, index):
        if axis == "dp":
            return (index, self.mp)
        if axis == "mp":
            return (self.dp, index)
        return (index // (2 * self.chips), index % (2 * self.chips))

    def peer(self, axis, step):
        return lax.rem(self.index(axis) + step, self.count(axis))

    def barrier(self, axes, neighbours):
        bar = pltpu.get_barrier_semaphore()
        axes = ("all",) if "all" in axes else axes
        steady = 0
        for axis in axes:
            for step in range(1, self.count(axis)):
                target = self.place(axis, self.peer(axis, step))
                pl.semaphore_signal(bar, inc=1, device_id=target, device_id_type=MESH)
            steady += self.count(axis) - 1
        cases = [(steady, None)]
        if neighbours and not ("all" in axes or "mp" in axes):
            pl.semaphore_signal(bar, inc=1, device_id=self.sibling, device_id_type=MESH)

            @pl.when(self.has_up)
            def _():
                pl.semaphore_signal(bar, inc=1, device_id=self.up, device_id_type=MESH)

            @pl.when(self.has_down)
            def _():
                pl.semaphore_signal(bar, inc=1, device_id=self.down, device_id_type=MESH)

            middle = jnp.logical_and(self.has_up, self.has_down)
            cases = [(steady + 3, middle), (steady + 2, jnp.logical_not(middle))]
        for count, when in cases:
            if when is None:
                pl.semaphore_wait(bar, count)
            else:

                @pl.when(when)
                def _():
                    pl.semaphore_wait(bar, count)


class Rider:
    def __init__(self, axis, array, cut=None, beside=False):
        self.axes = (axis,)
        self.axis = axis
        self.array = array
        self.cut = cut
        self.beside = beside

    def result(self, sizes):
        count = sizes[self.axis]
        shape = list(self.array.shape)
        if self.cut is not None:
            shape[self.cut] //= count
        self.columns = shape[-1]
        if self.beside:
            shape[-1] *= count
        else:
            shape = [count] + shape
        return jax.ShapeDtypeStruct(tuple(shape), self.array.dtype)

    def scratch(self, sizes):
        count = sizes[self.axis]
        return [pltpu.SemaphoreType.DMA((count,)), pltpu.SemaphoreType.DMA((count,))]

    def piece(self, ref, index, count):
        if self.cut is None:
            return ref
        size = self.array.shape[self.cut] // count
        where = [slice(None)] * len(self.array.shape)
        where[self.cut] = pl.ds(pl.multiple_of(index * size, size), size)
        return ref.at[tuple(where)]

    def copies(self, line, src, dst, send, recv):
        count, me = line.count(self.axis), line.index(self.axis)
        if self.beside:
            land = dst.at[:, pl.ds(pl.multiple_of(me * self.columns, self.columns), self.columns)]
        else:
            land = dst.at[me]
        made = [pltpu.make_async_copy(self.piece(src, me, count), land, send.at[0])]
        for step in range(1, count):
            peer = line.peer(self.axis, step)
            made.append(
                remote(
                    self.piece(src, peer, count),
                    land,
                    send.at[step],
                    recv.at[step],
                    line.place(self.axis, peer),
                )
            )
        return made

    def start(self, line, src, dst, send, recv):
        for copy in self.copies(line, src, dst, send, recv):
            copy.start()

    def middle(self, phase, *refs):
        pass

    def finish(self, line, src, dst, send, recv):
        for copy in self.copies(line, src, dst, send, recv):
            copy.wait()


class Settle:
    def __init__(self, array, summed, taps, placed):
        self.axes = ("dp", "mp")
        self.array = array
        self.summed = summed
        self.taps = taps
        self.placed = placed

    def result(self, sizes):
        n, m = sizes["mp"], sizes["dp"]
        self.ratio = n // m
        self.tail = tuple(self.array.shape[-2:])
        self.total = jax.ShapeDtypeStruct((n,) + self.tail, self.array.dtype)
        self.land = (m, self.ratio) + self.tail
        self.add = Rider("dp", self.array, None if self.summed else 1)
        self.outward = Rider("mp", self.total, 0)
        self.inward = Rider("dp", self.total, 0)
        if not self.placed:
            return jax.ShapeDtypeStruct(self.land, self.array.dtype)
        shape = (self.taps, self.ratio * self.tail[1] // self.taps, m * self.tail[0])
        return jax.ShapeDtypeStruct(shape, jnp.float32)

    def scratch(self, sizes):
        n, m = sizes["mp"], sizes["dp"]
        dtype = self.array.dtype
        refs = [pltpu.VMEM(self.land, dtype), pltpu.VMEM((n, 1) + self.tail, dtype)]
        if not self.summed:
            refs += [pltpu.VMEM((m, n, 1) + self.tail, dtype), pltpu.VMEM((n,) + self.tail, dtype)]
            refs += self.add.scratch(sizes)
        return refs + self.outward.scratch(sizes) + self.inward.scratch(sizes)

    def copies(self, step, line, src, dst, land, stage, *rest):
        if not self.summed:
            got, total = rest[:2]
            if step == 0:
                return self.add.copies(line, src, got, *rest[2:4])
            src, rest = total, rest[4:]
            step -= 1
        if step == 0:
            return self.outward.copies(line, src, stage, *rest[:2])
        return self.inward.copies(line, stage.at[:, 0], land, *rest[2:4])

    def start(self, *refs):
        for copy in self.copies(0, *refs):
            copy.start()

    def middle(self, phase, *refs):
        if self.summed and phase == 1:
            self.end(*refs)
            return
        for copy in self.copies(phase, *refs):
            copy.wait()
        if not self.summed and phase == 0:
            got, total = refs[5:7]

            @pl.loop(0, total.shape[0])
            def _(index):
                added_up = got[0, index, 0].astype(jnp.float32)
                for image in range(1, got.shape[0]):
                    added_up += got[image, index, 0].astype(jnp.float32)
                total[index] = added_up.astype(total.dtype)

        for copy in self.copies(phase + 1, *refs):
            copy.start()

    def finish(self, *refs):
        if not self.summed:
            self.end(*refs)

    def end(self, *refs):
        for copy in self.copies(1 if self.summed else 2, *refs):
            copy.wait()
        dst, land = refs[2:4]
        if not self.placed:
            dst[...] = land[...]
            return
        own = self.tail[1] // self.taps
        for half in range(self.ratio):
            for tap in range(self.taps):
                block = jnp.concatenate(
                    [
                        land[image, half, :, pl.ds(tap * own, own)].astype(jnp.float32)
                        for image in range(land.shape[0])
                    ],
                    axis=0,
                )
                dst[tap, pl.ds(half * own, own)] = block.T


def comm_call(kernel, inputs, out_shapes, scratch, riders, n, m, number, neighbours=True):
    chips = n // 2
    sizes = {"dp": m, "mp": n, "all": m * n}
    ride_shapes = tuple(rider.result(sizes) for rider in riders)
    ride_scratch = [rider.scratch(sizes) for rider in riders]
    any_spec = pl.BlockSpec(memory_space=pl.ANY)
    ni, nr, no = len(inputs), len(riders), len(out_shapes)

    def body(*refs):
        main_in, ride_in = refs[:ni], refs[ni : ni + nr]
        rest = refs[ni + nr :]
        main_out, ride_out = rest[:no], rest[no : no + nr]
        rest = rest[no + nr :]
        main_scratch, rest = rest[: len(scratch)], rest[len(scratch) :]
        line = Line(chips, m)
        line.barrier(sorted(set(axis for rider in riders for axis in rider.axes)), neighbours)
        riding = []
        for rider, src, dst, needs in zip(riders, ride_in, ride_out, ride_scratch):
            riding.append((rider, (line, src, dst) + tuple(rest[: len(needs)])))
            rest = rest[len(needs) :]
        for rider, refs_in in riding:
            rider.start(*refs_in)
        kernel(line, *main_in, *main_out, *main_scratch)
        for phase in range(2):
            for rider, refs_in in riding:
                rider.middle(phase, *refs_in)
        for rider, refs_in in riding:
            rider.finish(*refs_in)

    return pl.pallas_call(
        body,
        out_shape=tuple(out_shapes) + ride_shapes,
        in_specs=whole(ni) + [any_spec] * nr,
        out_specs=tuple(
            whole(no)
            + [whole(1)[0] if isinstance(rider, Settle) else any_spec for rider in riders]
        ),
        scratch_shapes=list(scratch) + [ref for needs in ride_scratch for ref in needs],
        compiler_params=comm_params(number),
    )(*inputs, *[rider.array for rider in riders])


def remote(src, dst, send, recv, target):
    return pltpu.make_async_remote_copy(
        src_ref=src,
        dst_ref=dst,
        send_sem=send,
        recv_sem=recv,
        device_id=target,
        device_id_type=MESH,
    )


def gather_sems(chips):
    return [pltpu.SemaphoreType.DMA((3, 2, chips)), pltpu.SemaphoreType.DMA((3, 2, chips))]


def line_gather(line, x_ref, slot, send, recv, on_own, on_pair):
    chips = line.chips
    z, c = line.z, line.c

    def hop(stream, step, src, block, target):
        return remote(src, slot(block), send.at[stream, 0, step], recv.at[stream, 0, step], target)

    def across(way, step, src, block):
        return remote(src, slot(block), send.at[2, way, step], recv.at[2, way, step], line.sibling)

    @pl.when(line.has_up)
    def _():
        hop(0, 1, x_ref, line.mp, line.up).start()

    @pl.when(line.has_down)
    def _():
        hop(1, 1, x_ref, line.mp, line.down).start()

    across(0, 0, x_ref, line.mp).start()
    slot(line.mp)[...] = x_ref[...]
    on_own()
    across(0, 0, x_ref, line.mp).wait_recv()
    on_pair(z)
    for step in range(1, chips):
        below, above = z - step, z + step

        @pl.when(below >= 0)
        def _():
            block = 2 * below + c
            hop(0, step, slot(block), block, line.up).wait_recv()
            if step + 1 < chips:

                @pl.when(line.has_up)
                def _():
                    hop(0, step + 1, slot(block), block, line.up).start()

            across(0, step, slot(block), block).start()

        @pl.when(above < chips)
        def _():
            block = 2 * above + c
            hop(1, step, slot(block), block, line.down).wait_recv()
            if step + 1 < chips:

                @pl.when(line.has_down)
                def _():
                    hop(1, step + 1, slot(block), block, line.down).start()

            across(1, step, slot(block), block).start()

        @pl.when(below >= 0)
        def _():
            across(0, step, slot(2 * below + c), 2 * below + c).wait_recv()
            on_pair(below)

        @pl.when(above < chips)
        def _():
            across(1, step, slot(2 * above + c), 2 * above + c).wait_recv()
            on_pair(above)

    @pl.when(line.has_up)
    def _():
        hop(0, 1, x_ref, line.mp, line.up).wait_send()

    @pl.when(line.has_down)
    def _():
        hop(1, 1, x_ref, line.mp, line.down).wait_send()

    across(0, 0, x_ref, line.mp).wait_send()
    for step in range(1, chips):
        below, above = z - step, z + step

        @pl.when(below >= 0)
        def _():
            block = 2 * below + c
            if step + 1 < chips:

                @pl.when(line.has_up)
                def _():
                    hop(0, step + 1, slot(block), block, line.up).wait_send()

            across(0, step, slot(block), block).wait_send()

        @pl.when(above < chips)
        def _():
            block = 2 * above + c
            if step + 1 < chips:

                @pl.when(line.has_down)
                def _():
                    hop(1, step + 1, slot(block), block, line.down).wait_send()

            across(1, step, slot(block), block).wait_send()


def scatter_scratch(chips, rows, cols, parts):
    block = (chips, rows, cols)
    return [
        pltpu.VMEM(block, jnp.float32),
        pltpu.VMEM(block, jnp.bfloat16),
        pltpu.VMEM(block, jnp.bfloat16),
        pltpu.VMEM((2,) + block, jnp.bfloat16),
        pltpu.SemaphoreType.DMA((2, 3, chips, parts)),
    ]


def line_scatter(line, scratch, parts, produce, finish, tile, side=()):
    chips = line.chips
    z = line.z
    kept, out_ref, in_ref, moving, sems = scratch
    count = kept.shape[1] // parts

    def span(part):
        return pl.ds(part * count, count)

    def across(chip, part):
        return remote(
            out_ref.at[chip, span(part)],
            in_ref.at[chip, span(part)],
            sems.at[0, 0, chip, part],
            sems.at[1, 0, chip, part],
            line.sibling,
        )

    def hop(way, chip, part):
        target = line.up if way == 0 else line.down
        ref = moving.at[way, chip, span(part)]
        return remote(
            ref, ref, sems.at[0, 1 + way, chip, part], sems.at[1, 1 + way, chip, part], target
        )

    items = []
    for step in range(chips - 1):
        for part in range(parts):
            items.append((0, chips - 1 - step + z, part, step >= z))
            items.append((1, step - (chips - 1 - z), part, step >= chips - 1 - z))
    for part in range(parts):
        items.append((2, z, part, None))

    def run(active, body):
        if active is None:
            body()
        else:
            pl.when(active)(body)

    def start(item):
        way, chip, part, active = item

        def body():
            produce(chip, part, count, kept.at[chip], out_ref.at[chip])
            across(chip, part).start()

        run(active, body)

    def tiles(part, body):
        @pl.loop(0, count // tile)
        def _(index):
            body(pl.ds(pl.multiple_of(part * count + index * tile, tile), tile))

    def close(item):
        way, chip, part, active = item

        def body():
            across(chip, part).wait_recv()
            if way < 2:
                later = line.has_down if way == 0 else line.has_up

                @pl.when(later)
                def _():
                    hop(way, chip, part).wait_recv()

                    def add(rows):
                        moving[way, chip, rows] = (
                            kept[chip, rows]
                            + in_ref[chip, rows].astype(jnp.float32)
                            + moving[way, chip, rows].astype(jnp.float32)
                        ).astype(jnp.bfloat16)

                    tiles(part, add)

                @pl.when(jnp.logical_not(later))
                def _():
                    def add(rows):
                        moving[way, chip, rows] = (
                            kept[chip, rows] + in_ref[chip, rows].astype(jnp.float32)
                        ).astype(jnp.bfloat16)

                    tiles(part, add)

                hop(way, chip, part).start()
            else:

                def total(rows):
                    return kept[chip, rows] + in_ref[chip, rows].astype(jnp.float32)

                def from_side(side, rows):
                    return moving[side, chip, rows].astype(jnp.float32)

                both = jnp.logical_and(line.has_down, line.has_up)

                @pl.when(both)
                def _():
                    hop(0, chip, part).wait_recv()
                    hop(1, chip, part).wait_recv()
                    tiles(
                        part,
                        lambda rows: finish(
                            part, rows, total(rows) + from_side(0, rows) + from_side(1, rows)
                        ),
                    )

                for side, present in ((0, line.has_down), (1, line.has_up)):

                    @pl.when(jnp.logical_and(present, jnp.logical_not(both)))
                    def _():
                        hop(side, chip, part).wait_recv()
                        tiles(
                            part,
                            lambda rows: finish(part, rows, total(rows) + from_side(side, rows)),
                        )

        run(active, body)

    lag = 2
    side = list(side)
    for index, item in enumerate(items):
        start(item)
        if index >= lag:
            close(items[index - lag])
            if index % 2 == 0 and side:
                side.pop(0)()
    for step in side:
        step()
    for item in items[-lag:]:
        close(item)
    for way, chip, part, active in items:

        def body():
            across(chip, part).wait_send()
            if way < 2:
                hop(way, chip, part).wait_send()

        run(active, body)


def whole(count):
    return [pl.BlockSpec(memory_space=pltpu.VMEM)] * count


def comm_params(number):
    return pltpu.CompilerParams(
        collective_id=number, has_side_effects=True, vmem_limit_bytes=VMEM_BYTES
    )


def pick(c, low, high):
    return jnp.where(c == 0, low, high), jnp.where(c == 0, high, low)


def conv_scatter_kernel(breadth, line, x_ref, w_ref, o_ref, *scratch):
    pixels, own = o_ref.shape
    tile = 512

    def produce(chip, part, count, mine, other):
        columns = pl.ds(pl.multiple_of(chip * 2 * own, 2 * own), 2 * own)

        @pl.loop(0, count // tile)
        def _(index):
            base = pl.multiple_of(part * count + index * tile, tile)
            total = jnp.zeros((tile, 2 * own), jnp.float32)
            for i in range(3):
                total += jnp.dot(
                    x_ref[pl.ds(base + i * breadth, tile)],
                    w_ref[i, :, columns],
                    preferred_element_type=jnp.float32,
                )
            first, second = pick(line.c, total[:, :own], total[:, own:])
            mine[pl.ds(base, tile)] = first
            other[pl.ds(base, tile)] = second.astype(jnp.bfloat16)

    def finish(part, rows, total):
        o_ref[rows] = total

    line_scatter(line, scratch, CONV_PARTS, produce, finish, tile)


def side_by_side(hidden):
    rows, cols, depth = hidden.shape
    padded = jnp.pad(hidden, ((1, 1), (1, 1), (0, 0)))
    return jnp.concatenate([padded[:, j : j + cols] for j in range(3)], axis=2).reshape(
        (rows + 2) * cols, 3 * depth
    )


def conv_scatter_fused(spread, kernel, cols, n, m, number, riders=()):
    own = kernel.shape[2] // n
    depth = kernel.shape[1]
    pixels = spread.shape[0] - 2 * cols
    return comm_call(
        partial(conv_scatter_kernel, cols),
        (spread, kernel.reshape(3, 3 * depth, kernel.shape[2])),
        (jax.ShapeDtypeStruct((pixels, own), jnp.float32),),
        scatter_scratch(n // 2, pixels, own, CONV_PARTS),
        riders,
        n,
        m,
        number,
    )


def conv_back_kernel(breadth, line, g_ref, w_ref, x_ref, acc_ref, wg_ref, held, sums, send, recv):
    chips = line.chips
    pixels, own = g_ref.shape
    wide = w_ref.shape[1]
    tile, long = 512, 1024
    zero = jnp.zeros((breadth, own), jnp.bfloat16)
    for block in range(2 * chips):
        held[block, pl.ds(0, breadth)] = zero
        held[block, pl.ds(breadth + pixels, breadth)] = zero

    def slot(block):
        return held.at[block, pl.ds(breadth, pixels)]

    def beside(base, count, chip):
        rows = pl.ds(base, count)
        return [held[2 * chip, rows], held[2 * chip + 1, rows]]

    def on_own():
        @pl.loop(0, pixels // tile)
        def _(index):
            acc_ref[pl.ds(pl.multiple_of(index * tile, tile), tile)] = jnp.zeros(
                (tile, wide), jnp.float32
            )

    def on_pair(chip):
        columns = pl.ds(pl.multiple_of(chip * 2 * own, 2 * own), 2 * own)

        @pl.loop(0, pixels // tile)
        def _(index):
            base = pl.multiple_of(index * tile, tile)
            shifted = []
            for i in range(3):
                shifted += beside(base + (2 - i) * breadth, tile, chip)
            acc_ref[pl.ds(base, tile)] += product(
                jnp.concatenate(shifted, axis=1),
                jnp.concatenate([w_ref[i, :, columns] for i in range(3)], axis=1),
                True,
            )

        sums[...] = jnp.zeros_like(sums)

        @pl.loop(0, pixels // long)
        def _(index):
            base = pl.multiple_of(index * long, long)
            sums[...] += lax.dot_general(
                jnp.concatenate(beside(base + breadth, long, chip), axis=1),
                jnp.concatenate(
                    [x_ref[pl.ds(base + i * breadth, long)] for i in range(3)], axis=1
                ),
                (((0,), (0,)), ((), ())),
                preferred_element_type=jnp.float32,
            )

        wg_ref[chip] = sums[...].astype(jnp.bfloat16)

    line_gather(line, g_ref, slot, send, recv, on_own, on_pair)


def conv_back_fused(grad_low, spread, kernel, cols, n, m, number, riders=()):
    pixels, own = grad_low.shape
    depth = kernel.shape[1]
    chips = n // 2
    return comm_call(
        partial(conv_back_kernel, cols),
        (grad_low, kernel.reshape(3, 3 * depth, kernel.shape[2]), spread),
        (
            jax.ShapeDtypeStruct((pixels, 3 * depth), jnp.float32),
            jax.ShapeDtypeStruct((chips, 2 * own, 9 * depth), jnp.bfloat16),
        ),
        [
            pltpu.VMEM((n, pixels + 2 * cols, own), jnp.bfloat16),
            pltpu.VMEM((2 * own, 9 * depth), jnp.float32),
        ]
        + gather_sems(chips),
        riders,
        n,
        m,
        number,
    )


def join_columns(acc, cols):
    pixels, wide = acc.shape
    depth = wide // 3
    planes = acc.reshape(-1, cols, wide)
    none = jnp.zeros_like(planes[:, :1, :depth])
    left = jnp.concatenate([planes[:, 1:, :depth], none], axis=1)
    right = jnp.concatenate([none, planes[:, :-1, 2 * depth :]], axis=1)
    return (left + planes[:, :, depth : 2 * depth] + right).reshape(pixels, depth)


def product(x, w, turned):
    return lax.dot_general(
        x, w, (((1,), (1 if turned else 0,)), ((), ())), preferred_element_type=jnp.float32
    )


def outer_steps(grad, left, right, cut):
    def step(start):
        grad[pl.ds(start, cut)] = lax.dot_general(
            left[:, pl.ds(start, cut)],
            right[...],
            (((0,), (0,)), ((), ())),
            preferred_element_type=jnp.float32,
        ).astype(grad.dtype)

    return [partial(step, start) for start in range(0, left.shape[1], cut)]


def tokens_scatter_kernel(turned, beside, line, x_ref, w_ref, *refs):
    side = ()
    if beside:
        left, right, o_ref, grad, *scratch = refs
        side = outer_steps(grad, left, right, 128)
    else:
        o_ref, *scratch = refs
    tokens, width = o_ref.shape
    cut = width // TOKEN_PARTS
    depth = x_ref.shape[1] // w_ref.shape[0]

    def produce(chip, part, count, mine, other):
        rows = pl.ds(pl.multiple_of(chip * 2 * tokens, 2 * tokens), 2 * tokens)
        columns = pl.ds(part * cut, cut)
        total = None
        for j in range(w_ref.shape[0]):
            w = w_ref[j, columns] if turned else w_ref[j, :, columns]
            term = product(x_ref[rows, pl.ds(j * depth, depth)], w, turned)
            total = term if total is None else total + term
        first, second = pick(line.c, total[:tokens], total[tokens:])
        mine[pl.ds(part * count, count)] = first
        other[pl.ds(part * count, count)] = second.astype(jnp.bfloat16)

    def finish(part, rows, total):
        o_ref[:, pl.ds(part * cut, cut)] = total

    line_scatter(line, scratch, TOKEN_PARTS, produce, finish, tokens, side)


def outer_shapes(outer):
    if not outer:
        return ()
    return (jax.ShapeDtypeStruct((outer[0].shape[1], outer[1].shape[1]), jnp.bfloat16),)


def tokens_scatter(x, w, turned, n, m, number, riders=(), outer=()):
    tokens = x.shape[0] // n
    width = w.shape[1] if turned else w.shape[2]
    return comm_call(
        partial(tokens_scatter_kernel, turned, len(outer) > 0),
        (x, w) + tuple(outer),
        (jax.ShapeDtypeStruct((tokens, width), jnp.float32),) + outer_shapes(outer),
        scatter_scratch(n // 2, TOKEN_PARTS * tokens, width // TOKEN_PARTS, TOKEN_PARTS),
        riders,
        n,
        m,
        number,
    )


def add_outer(total, left, right, rows):
    cut = min(left.shape[1], 512)
    for start in range(0, left.shape[1], cut):
        total[pl.ds(start, cut)] += lax.dot_general(
            left[rows, pl.ds(start, cut)],
            right[rows],
            (((0,), (0,)), ((), ())),
            preferred_element_type=jnp.float32,
        )


def tokens_gather_kernel(turned, shape_out, outs, side, beside, cols, line, x_ref, w_ref, *refs):
    refs = list(refs)
    left = refs.pop(0) if side else None
    outer = (refs.pop(0), refs.pop(0)) if beside else None
    held = refs.pop(0)
    results = [refs.pop(0) for _ in range(outs)]
    grad = refs.pop(0) if side else None
    outer_grad = refs.pop(0) if beside else None
    total = refs.pop(0) if side else None
    send, recv = refs
    tokens = x_ref.shape[0]
    across = w_ref.shape[1 if turned else 2]
    cut = min(across, 512)

    def slot(block):
        return held.at[pl.ds(pl.multiple_of(block * tokens, tokens), tokens)]

    def store_pixels(ref, chip, value):
        depth = value.shape[1] // 4
        base = chip * 8 * tokens
        for row in range(4 * tokens // cols):
            for tap in range(4):
                start = base + (2 * row + tap // 2) * cols + tap % 2
                ref[pl.Slice(start, cols // 2, 2)] = value[
                    row * (cols // 2) : (row + 1) * (cols // 2), tap * depth : (tap + 1) * depth
                ]

    def on_pair(chip):
        rows = pl.ds(pl.multiple_of(chip * 2 * tokens, 2 * tokens), 2 * tokens)
        for j in range(w_ref.shape[0]):
            for start in range(0, across, cut):
                w = w_ref[j, pl.ds(start, cut)] if turned else w_ref[j, :, pl.ds(start, cut)]
                values = shape_out(product(held[rows], w, turned))
                for ref, value in zip(results, values):
                    if cols:
                        store_pixels(ref, chip, value)
                    else:
                        ref[rows, pl.ds(j * across + start, cut)] = value.astype(ref.dtype)
        if side:
            add_outer(total, held, left, rows)

    def on_own():
        if side:
            total[...] = jnp.zeros_like(total)
        if beside:
            for step in outer_steps(outer_grad, *outer, 256):
                step()

    line_gather(line, x_ref, slot, send, recv, on_own, on_pair)
    if side:
        grad[...] = total[...].astype(grad.dtype)


def tokens_gather(
    x, w, turned, kinds, shape_out, n, m, number, riders=(), left=None, outer=(), cols=0
):
    tokens, width = x.shape
    across = w.shape[0] * w.shape[1 if turned else 2]
    side = left is not None
    grads = ((width, left.shape[1]),) if side else ()
    shape = (tokens * n * 4, across // 4) if cols else (tokens * n, across)
    return comm_call(
        partial(
            tokens_gather_kernel, turned, shape_out, len(kinds), side, len(outer) > 0, cols
        ),
        (x, w) + ((left,) if side else ()) + tuple(outer),
        (jax.ShapeDtypeStruct((tokens * n, width), x.dtype),)
        + tuple(jax.ShapeDtypeStruct(shape, kind) for kind in kinds)
        + tuple(jax.ShapeDtypeStruct(grad, jnp.bfloat16) for grad in grads)
        + outer_shapes(outer),
        [pltpu.VMEM(grad, jnp.float32) for grad in grads] + gather_sems(n // 2),
        riders,
        n,
        m,
        number,
    )


def exchange(riders, n, m, number):
    return comm_call(lambda line: None, (), (), [], riders, n, m, number, neighbours=False)


def tiled_up(vector):
    count = -(-vector.shape[0] // 1024) * 1024
    return jnp.pad(vector.astype(jnp.float32), (0, count - vector.shape[0])).reshape(-1, 128)


def attend_scatter_kernel(line, x_ref, valid_ref, w_ref, o_ref, mixed_ref, *scratch):
    tokens, width = o_ref.shape
    wide = mixed_ref.shape[1]
    cut = width // TOKEN_PARTS
    scale = 1.0 / math.sqrt(HEAD_DIM)

    def attend(rows):
        for head in range(wide // HEAD_DIM):
            where = [pl.ds(j * wide + head * HEAD_DIM, HEAD_DIM) for j in range(3)]
            scores = product(x_ref[rows, where[0]], x_ref[:, where[1]], True) * scale
            scores = jnp.where(valid_ref[0:1] > 0.5, scores, MASKED_SCORE)
            exponent = jnp.exp(scores - jnp.max(scores, axis=1, keepdims=True))
            inverse = 1.0 / jnp.sum(exponent, axis=1, keepdims=True)
            mixed_ref[rows, pl.ds(head * HEAD_DIM, HEAD_DIM)] = product(
                (exponent * inverse).astype(jnp.bfloat16), x_ref[:, where[2]], False
            ).astype(jnp.bfloat16)

    def produce(chip, part, count, mine, other):
        rows = pl.ds(pl.multiple_of(chip * 2 * tokens, 2 * tokens), 2 * tokens)
        if part == 0:
            attend(rows)
        total = product(mixed_ref[rows], w_ref[:, pl.ds(part * cut, cut)], False)
        first, second = pick(line.c, total[:tokens], total[tokens:])
        mine[pl.ds(part * count, count)] = first
        other[pl.ds(part * count, count)] = second.astype(jnp.bfloat16)

    def finish(part, rows, total):
        o_ref[:, pl.ds(part * cut, cut)] = total

    line_scatter(line, scratch, TOKEN_PARTS, produce, finish, tokens)


def attend_scatter(qkv_rows, valid, out_weight, n, m, number):
    total = qkv_rows.shape[0]
    tokens = total // n
    width = out_weight.shape[1]
    return comm_call(
        attend_scatter_kernel,
        (qkv_rows, jnp.broadcast_to(valid[None], (8, total)), out_weight),
        (
            jax.ShapeDtypeStruct((tokens, width), jnp.float32),
            jax.ShapeDtypeStruct((total, out_weight.shape[0]), jnp.bfloat16),
        ),
        scatter_scratch(n // 2, TOKEN_PARTS * tokens, width // TOKEN_PARTS, TOKEN_PARTS),
        (),
        n,
        m,
        number,
    )


def attend_gather_kernel(
    line,
    g_ref,
    w_ref,
    x_ref,
    kt_ref,
    valid_ref,
    mixed_ref,
    left,
    right,
    held,
    grad_ref,
    out_ref,
    outer_grad,
    keys_sum,
    values_sum,
    out_sum,
    send,
    recv,
):
    tokens = g_ref.shape[0]
    wide = w_ref.shape[0]
    heads = wide // HEAD_DIM
    scale = 1.0 / math.sqrt(HEAD_DIM)

    def slot(block):
        return held.at[pl.ds(pl.multiple_of(block * tokens, tokens), tokens)]

    def on_own():
        keys_sum[...] = jnp.zeros_like(keys_sum)
        values_sum[...] = jnp.zeros_like(values_sum)
        out_sum[...] = jnp.zeros_like(out_sum)
        for step in outer_steps(outer_grad, left, right, 256):
            step()

    def on_pair(chip):
        rows = pl.ds(pl.multiple_of(chip * 2 * tokens, 2 * tokens), 2 * tokens)
        for head in range(heads):
            place = pl.ds(head * HEAD_DIM, HEAD_DIM)
            where = [pl.ds(j * wide + head * HEAD_DIM, HEAD_DIM) for j in range(3)]
            grad = product(held[rows], w_ref[place], True).astype(jnp.bfloat16)
            query = x_ref[rows, where[0]]
            scores = product(x_ref[:, where[1]], query, True) * scale
            scores = jnp.where(valid_ref[:, 0:1] > 0.5, scores, MASKED_SCORE)
            exponent = jnp.exp(scores - jnp.max(scores, axis=0, keepdims=True))
            probs = exponent * (1.0 / jnp.sum(exponent, axis=0, keepdims=True))
            values_sum[:, place] += product(probs.astype(jnp.bfloat16), grad, False)
            grad_probs = product(x_ref[:, where[2]], grad, True)
            inner = jnp.sum(probs * grad_probs, axis=0, keepdims=True)
            grad_scores = (probs * (grad_probs - inner) * scale).astype(jnp.bfloat16)
            keys_sum[:, place] += product(grad_scores, query, False)
            grad_ref[rows, where[0]] = product(kt_ref[place], grad_scores, False).T.astype(
                jnp.bfloat16
            )
        add_outer(out_sum, mixed_ref, held, rows)

    line_gather(line, g_ref, slot, send, recv, on_own, on_pair)
    grad_ref[:, pl.ds(wide, wide)] = keys_sum[...].astype(jnp.bfloat16)
    grad_ref[:, pl.ds(2 * wide, wide)] = values_sum[...].astype(jnp.bfloat16)
    out_ref[...] = out_sum[...].astype(jnp.bfloat16)


def attend_gather(grad_mid, out_weight, qkv_rows, valid, mixed_low, outer, n, m, number, riders):
    tokens, width = grad_mid.shape
    total = tokens * n
    wide = out_weight.shape[0]
    return comm_call(
        attend_gather_kernel,
        (
            grad_mid,
            out_weight,
            qkv_rows,
            qkv_rows[:, wide : 2 * wide].T,
            jnp.broadcast_to(valid[:, None], (total, 128)),
            mixed_low,
        )
        + tuple(outer),
        (
            jax.ShapeDtypeStruct((total, width), jnp.bfloat16),
            jax.ShapeDtypeStruct((total, 3 * wide), jnp.bfloat16),
            jax.ShapeDtypeStruct((wide, width), jnp.bfloat16),
        )
        + outer_shapes(outer),
        [
            pltpu.VMEM((total, wide), jnp.float32),
            pltpu.VMEM((total, wide), jnp.float32),
            pltpu.VMEM((wide, width), jnp.float32),
        ]
        + gather_sems(n // 2),
        riders,
        n,
        m,
        number,
    )


def local(
    image,
    embedding,
    extents,
    gain_first,
    conv_first,
    gain_second,
    conv_second,
    shift_weight,
    down_weight,
    ada_weight,
    qkv_weight,
    out_weight,
    up_weight,
    proj_weight,
    cotangent,
):
    strip_rows, canvas_cols, channel_count = (image.shape[1], image.shape[2], image.shape[3])
    width_all = out_weight.shape[1]
    n = lax.axis_size("mp")
    m = lax.axis_size("dp")
    me_mp = lax.axis_index("mp")
    me_dp = lax.axis_index("dp")
    rows_all = strip_rows * n
    pixel_total = rows_all * canvas_cols
    own = channel_count // n
    size = channel_count // GROUPS
    token_rows = strip_rows // 2
    token_cols = canvas_cols // 2
    local_tokens = token_rows * token_cols
    token_total = local_tokens * n
    local_width = out_weight.shape[0]

    fused = own % 128 == 0 and n == 2 * m
    shift_vector = jnp.dot(embedding, shift_weight, preferred_element_type=jnp.float32)[0]
    columns = jnp.dot(embedding, ada_weight, preferred_element_type=jnp.float32)[0]
    riders = (Rider("mp", tiled_up(columns)),)
    if fused:
        modulation, pixels_low = exchange(
            riders + (Rider("mp", image[0].reshape(-1, channel_count), 1),), n, m, 12
        )
    else:
        (modulation,) = exchange(riders, n, m, 12)
        pixels_low = lax.all_to_all(image[0], "mp", 2, 0, tiled=True)
    modulation = modulation.reshape(n, -1)[:, : columns.shape[0]].reshape(-1)
    scale_attend = modulation[:width_all]
    shift_attend = modulation[width_all : 2 * width_all]
    scale_mlp = modulation[2 * width_all : 3 * width_all]
    shift_mlp = modulation[3 * width_all :]
    own_first = lax.dynamic_slice_in_dim(gain_first, me_mp * own, own)
    own_second = lax.dynamic_slice_in_dim(gain_second, me_mp * own, own)

    pixels = pixels_low.astype(jnp.float32).reshape(pixel_total, own)
    normed_first, inverse_first = group_forward(pixels, size)
    hidden_first = (
        jax.nn.silu(normed_first * own_first)
        .astype(jnp.bfloat16)
        .reshape(rows_all, canvas_cols, own)
    )
    spread_first = side_by_side(hidden_first)
    if fused:
        (conv_output,) = conv_scatter_fused(spread_first, conv_first, canvas_cols, n, m, 0)
    else:
        conv_output = conv_scatter(hidden_first, conv_first, n)
    conv_output = conv_output + shift_vector
    normed_second, inverse_second = group_forward(conv_output, size)
    hidden_second = (
        jax.nn.silu(normed_second * own_second)
        .astype(jnp.bfloat16)
        .reshape(rows_all, canvas_cols, own)
    )
    spread_second = side_by_side(hidden_second)
    if fused:
        (conv_again,) = conv_scatter_fused(spread_second, conv_second, canvas_cols, n, m, 1)
    else:
        conv_again = conv_scatter(hidden_second, conv_second, n)
    residual = pixels + conv_again
    down_patch = (
        residual.astype(jnp.bfloat16)
        .reshape(rows_all // 2, 2, token_cols, 2, own)
        .transpose(0, 2, 1, 3, 4)
        .reshape(token_total, 4 * own)
    )
    down_matrix = down_weight.reshape(4 * own, width_all)
    (stream,) = tokens_scatter(down_patch, down_matrix[None], False, n, m, 2)
    normed_attend, inverse_attend = layer_forward(stream)
    input_attend = (normed_attend * (1.0 + scale_attend) + shift_attend).astype(jnp.bfloat16)
    all_attend, qkv_rows = tokens_gather(
        input_attend, qkv_weight, False, (jnp.bfloat16,), lambda value: (value,), n, m, 3
    )
    token_index = jnp.arange(token_total, dtype=jnp.int32)
    key_valid = (token_index // token_cols < extents[0, 0]) & (
        token_index % token_cols < extents[0, 1]
    )
    valid = key_valid.astype(jnp.float32)
    attended, mixed_low = attend_scatter(qkv_rows, valid, out_weight, n, m, 4)
    stream_mid = stream + attended
    normed_mlp, inverse_mlp = layer_forward(stream_mid)
    input_mlp = (normed_mlp * (1.0 + scale_mlp) + shift_mlp).astype(jnp.bfloat16)
    all_mlp, upper_proj, activated = tokens_gather(
        input_mlp,
        up_weight[None],
        False,
        (jnp.float32, jnp.bfloat16),
        lambda value: (value, jax.nn.gelu(value, approximate=True)),
        n,
        m,
        5,
    )
    final_stream = stream_mid + scatter_rows(
        jnp.dot(activated, proj_weight, preferred_element_type=jnp.float32)
    )
    output = final_stream.astype(jnp.bfloat16).reshape(1, token_rows, token_cols, width_all)

    grad_final_low = cotangent[0].reshape(local_tokens, width_all)
    grad_final = grad_final_low.astype(jnp.float32)
    all_final = gather_rows(lax.optimization_barrier((grad_final_low, qkv_rows))[0])
    grad_act = jnp.einsum("le,fe->lf", all_final, proj_weight, preferred_element_type=jnp.float32)
    gelu_pull = jax.vjp(partial(jax.nn.gelu, approximate=True), upper_proj)[1]
    grad_upper = gelu_pull(grad_act)[0].astype(jnp.bfloat16)
    grad_normed_mlp, grad_proj = tokens_scatter(
        grad_upper, up_weight[None], True, n, m, 6, (), (activated, all_final)
    )
    grad_mid_norm, grad_scale_mlp, grad_shift_mlp = layer_backward(
        grad_normed_mlp, normed_mlp, inverse_mlp, scale_mlp
    )
    grad_mid = grad_final + grad_mid_norm
    all_mid, grad_qkv, grad_out, grad_up, sums_proj = attend_gather(
        grad_mid.astype(jnp.bfloat16),
        out_weight,
        qkv_rows,
        valid,
        mixed_low,
        (all_mlp, grad_upper),
        n,
        m,
        7,
        (Rider("dp", grad_proj, 1),),
    )
    (grad_normed_attend,) = tokens_scatter(grad_qkv, qkv_weight, True, n, m, 8)
    grad_stream_norm, grad_scale_attend, grad_shift_attend = layer_backward(
        grad_normed_attend, normed_attend, inverse_attend, scale_attend
    )
    grad_stream = grad_mid + grad_stream_norm
    grad_modulation = jnp.concatenate(
        [
            tiled_up(piece)
            for piece in jnp.concatenate(
                [grad_scale_attend, grad_shift_attend, grad_scale_mlp, grad_shift_mlp]
            ).reshape(n, -1)
        ]
    )
    all_stream, grad_residual, grad_down, grad_qkv_weight, sums_up, ada_columns = tokens_gather(
        grad_stream.astype(jnp.bfloat16),
        down_matrix[None],
        True,
        (jnp.float32,),
        lambda value: (value,),
        n,
        m,
        9,
        (
            Rider("dp", grad_up, 0),
            Rider("mp", grad_modulation, 0),
        ),
        down_patch,
        (all_attend, grad_qkv),
        canvas_cols if fused else 0,
    )
    ada_columns = added(ada_columns).reshape(-1)[: columns.shape[0]]
    if not fused:
        grad_residual = (
            grad_residual.reshape(rows_all // 2, token_cols, 2, 2, own)
            .transpose(0, 2, 1, 3, 4)
            .reshape(pixel_total, own)
        )
    def back(grad_low, hidden, spread, kernel, number, riders):
        if fused:
            acc, parts, *ridden = conv_back_fused(
                grad_low, spread, kernel, canvas_cols, n, m, number, riders
            )
            return join_columns(acc, canvas_cols), parts, ridden
        grad_hidden, grad_kernel = conv_backward(grad_low, hidden, kernel, n)
        parts = grad_kernel.astype(jnp.bfloat16).reshape(9 * own, -1).T
        return grad_hidden, parts, exchange(riders, n, m, number)

    grad_hidden_second, parts_second, (sums_down, sums_qkv, sums_out, every_small) = back(
        grad_residual.astype(jnp.bfloat16),
        hidden_second,
        spread_second,
        conv_second,
        10,
        (
            Rider("dp", unsettled(grad_down, m, n), 1),
            Rider("dp", grad_qkv_weight, 0),
            Rider("dp", grad_out, 1),
            Rider("dp", jnp.concatenate([tiled_up(embedding[0]), tiled_up(ada_columns)])),
        ),
    )
    grad_conv_output, grad_gain_second = group_backward(
        grad_hidden_second, normed_second, inverse_second, own_second, size
    )
    grad_shift = jnp.sum(grad_conv_output, axis=0)
    grad_hidden_first, parts_first, (sums_second, every_shift, pieces_down) = back(
        grad_conv_output.astype(jnp.bfloat16),
        hidden_first,
        spread_first,
        conv_first,
        11,
        (
            Rider("dp", unsettled(parts_second, m, n), 1),
            Rider("dp", tiled_up(grad_shift)),
            Settle(added(sums_down)[:, 0].astype(jnp.bfloat16), True, 4, fused),
        ),
    )
    grad_base, grad_gain_first = group_backward(
        grad_hidden_first, normed_first, inverse_first, own_first, size
    )
    image_turned = (grad_residual + grad_base).astype(jnp.bfloat16)
    embed_term = jnp.dot(
        grad_shift[None], shift_weight.astype(jnp.float32).T, precision=PRECISE
    ) + jnp.dot(ada_columns[None], ada_weight.astype(jnp.float32).T, precision=PRECISE)
    small = jnp.concatenate(
        [tiled_up(embed_term[0]), tiled_up(jnp.concatenate([grad_gain_first, grad_gain_second]))]
    )
    riders = (
        Settle(unsettled(parts_first, m, n), False, 9, fused),
        Rider("all", small),
        Settle(added(sums_second)[:, 0].astype(jnp.bfloat16), True, 9, fused),
    )
    if fused:
        pieces_first, small, pieces_second, image_turned = exchange(
            riders + (Rider("mp", image_turned, 0, True),), n, m, 13
        )
        image_grad = image_turned.reshape(image.shape)
    else:
        pieces_first, small, pieces_second = exchange(riders, n, m, 13)
        image_grad = lax.all_to_all(
            image_turned.reshape(rows_all, canvas_cols, own), "mp", 0, 2, tiled=True
        )[None]

    small = small.reshape(m, n, -1)
    embed_count = embedding.shape[1]
    embedding_grad = jnp.sum(
        lax.dynamic_index_in_dim(small, me_dp, axis=0, keepdims=False)[:, :embed_count], axis=0
    )[None]
    gain_start = -(-embed_count // 1024) * 1024
    gains = jnp.sum(small[:, :, gain_start : gain_start + 2 * own], axis=0)
    gains = gains.reshape(n, 2, own).transpose(1, 0, 2).reshape(2, -1)
    piece = channel_count // (m * n)
    gains = lax.dynamic_slice_in_dim(gains, (me_dp * n + me_mp) * piece, piece, axis=1)
    every_small = every_small.reshape(m, -1)
    embed_rows = lax.dynamic_slice_in_dim(
        every_small[:, :embed_count], me_dp * (embed_count // m), embed_count // m, axis=1
    )
    grad_shift_weight = jnp.dot(
        embed_rows.T, every_shift.reshape(m, -1)[:, :own], precision=PRECISE
    )
    grad_ada_weight = jnp.dot(
        embed_rows.T,
        every_small[:, gain_start : gain_start + columns.shape[0]],
        precision=PRECISE,
    )
    qkv_grad = jnp.stack(
        [added(sums_qkv[:, :, j * local_width : (j + 1) * local_width]) for j in range(3)]
    )
    return (
        output,
        image_grad,
        embedding_grad,
        gains[0],
        settled(pieces_first, 9),
        gains[1],
        settled(pieces_second, 9),
        grad_shift_weight,
        settled(pieces_down, 4),
        grad_ada_weight,
        qkv_grad,
        added(sums_out),
        added(sums_up),
        added(sums_proj),
    )


def solution(mesh):
    placed = (
        P("dp", "mp", None, None),
        P("dp", None),
        P("dp", None),
        P(),
        P(None, "mp", None),
        P(),
        P(None, "mp", None),
        P(None, "mp"),
        P(None, "mp", None),
        P(None, "mp"),
        P(None, None, "mp"),
        P("mp", None),
        P(None, "mp"),
        P("mp", None),
        P("dp", "mp", None, None),
    )
    return jax.shard_map(
        local,
        mesh=mesh,
        in_specs=placed,
        out_specs=(
            P("dp", "mp", None, None),
            P("dp", "mp", None, None),
            P("dp", None),
            P(("dp", "mp")),
            P(None, "dp", "mp"),
            P(("dp", "mp")),
            P(None, "dp", "mp"),
            P("dp", "mp"),
            P(None, "dp", "mp"),
            P("dp", "mp"),
            P(None, "dp", "mp"),
            P("mp", "dp"),
            P("dp", "mp"),
            P("mp", "dp"),
        ),
        check_vma=False,
    )
```

```python
from functools import partial
import math

import jax
import jax.numpy as jnp
from jax import lax
from jax.experimental import pallas as pl
from jax.experimental.pallas import tpu as pltpu
from jax.sharding import PartitionSpec as P

HEAD_DIM = 128
GROUPS = 32


GROUP_EPSILON = 1e-05
LAYER_EPSILON = 1e-06
MASKED_SCORE = -1000000000.0
PRECISE = lax.Precision.HIGHEST


def group_spread(per_channel, size):
    grouped = jnp.sum(per_channel.reshape(-1, size), axis=1)
    return jnp.repeat(grouped, size)


def group_forward(values, size):
    counted = values.shape[0] * size
    average = group_spread(jnp.sum(values, axis=0), size) / counted
    centre = values - average
    inverse = lax.rsqrt(
        group_spread(jnp.sum(centre * centre, axis=0), size) / counted + GROUP_EPSILON
    )
    return (centre * inverse, inverse)


def group_backward(incoming, normed, inverse, gain_vec, size):
    pre_act = normed * gain_vec
    sigmoid_part = jax.nn.sigmoid(pre_act)
    through = incoming * sigmoid_part * (1.0 + pre_act * (1.0 - sigmoid_part))
    counted = normed.shape[0] * size
    gain_part = jnp.sum(through * normed, axis=0)
    plain_part = jnp.sum(through, axis=0)
    first_mean = group_spread(plain_part * gain_vec, size) / counted
    second_mean = group_spread(gain_part * gain_vec, size) / counted
    outgoing = inverse * (through * gain_vec - first_mean - normed * second_mean)
    return (outgoing, gain_part)


def windows(planes, flipped):
    row_count, col_count, depth = planes.shape
    padded = jnp.pad(planes, ((1, 1), (1, 1), (0, 0)))
    pieces = []
    for tap_index in range(9):
        row_off, col_off = divmod(tap_index, 3)
        if flipped:
            row_off, col_off = (2 - row_off, 2 - col_off)
        pieces.append(padded[row_off : row_off + row_count, col_off : col_off + col_count])
    return jnp.stack(pieces, axis=2).reshape(row_count * col_count, 9, depth)


def gather_rows(rows):
    return lax.all_gather(rows, "mp", axis=0, tiled=True)


def scatter_rows(rows):
    return lax.psum_scatter(
        rows.astype(jnp.bfloat16), "mp", scatter_dimension=0, tiled=True
    ).astype(jnp.float32)


def conv_scatter(hidden, kernel, n):
    patch = windows(hidden, False)
    depth = kernel.shape[2] // n
    total = jnp.einsum("ptc,tcd->pd", patch, kernel, preferred_element_type=jnp.float32)
    parts = total.astype(jnp.bfloat16).reshape(-1, n, depth).transpose(1, 0, 2)
    return lax.psum_scatter(parts, "mp", scatter_dimension=0, tiled=False).astype(jnp.float32)


def conv_backward(grad_low, hidden, kernel, n):
    row_count, col_count, depth = hidden.shape
    gathered = lax.all_gather(grad_low, "mp", axis=1, tiled=True)
    padded = jnp.pad(gathered, ((col_count, col_count), (0, 0)))
    taps = kernel.reshape(3, 3 * depth, kernel.shape[2])
    acc = sum(
        jnp.einsum(
            "pd,td->pt",
            padded[(2 - i) * col_count : (2 - i) * col_count + row_count * col_count],
            taps[i],
            preferred_element_type=jnp.float32,
        )
        for i in range(3)
    )
    grad_kernel = jnp.einsum(
        "ptc,pd->tcd", windows(hidden, False), gathered, preferred_element_type=jnp.float32
    )
    return (join_columns(acc, col_count), grad_kernel)


def unsettled(parts, m, n):
    return parts.reshape(n, m, -1, parts.shape[-1])


def settled(pieces, taps):
    if pieces.ndim == 3:
        return pieces
    m, count, outs, _ = pieces.shape
    return (
        pieces.astype(jnp.float32)
        .reshape(m, count, outs, taps, -1)
        .transpose(3, 1, 4, 0, 2)
        .reshape(taps, -1, m * outs)
    )


def added(received):
    return jnp.sum(received.astype(jnp.float32), axis=0)


def layer_forward(stream):
    centre = stream - jnp.mean(stream, axis=1, keepdims=True)
    inverse = lax.rsqrt(jnp.mean(centre * centre, axis=1, keepdims=True) + LAYER_EPSILON)
    return (centre * inverse, inverse)


def layer_backward(incoming, normed, inverse, scale_vec):
    through = incoming * (1.0 + scale_vec)
    outgoing = inverse * (
        through
        - jnp.mean(through, axis=1, keepdims=True)
        - normed * jnp.mean(through * normed, axis=1, keepdims=True)
    )
    return (outgoing, jnp.sum(incoming * normed, axis=0), jnp.sum(incoming, axis=0))


MESH = pl.DeviceIdType.MESH
CONV_PARTS = 4
TOKEN_PARTS = 4
VMEM_BYTES = 60 * 1024 * 1024


class Line:
    def __init__(self, chips, images):
        self.chips = chips
        self.images = images
        self.dp = lax.axis_index("dp")
        self.mp = lax.axis_index("mp")
        self.z = self.mp // 2
        self.c = self.mp % 2
        self.has_up = self.z < chips - 1
        self.has_down = self.z > 0
        self.up = (self.dp, self.mp + 2)
        self.down = (self.dp, self.mp - 2)
        self.sibling = (self.dp, 2 * self.z + 1 - self.c)

    def count(self, axis):
        return {"dp": self.images, "mp": 2 * self.chips, "all": 2 * self.chips * self.images}[axis]

    def index(self, axis):
        return {"dp": self.dp, "mp": self.mp, "all": self.dp * 2 * self.chips + self.mp}[axis]

    def place(self, axis, index):
        if axis == "dp":
            return (index, self.mp)
        if axis == "mp":
            return (self.dp, index)
        return (index // (2 * self.chips), index % (2 * self.chips))

    def peer(self, axis, step):
        return lax.rem(self.index(axis) + step, self.count(axis))

    def barrier(self, axes, neighbours):
        bar = pltpu.get_barrier_semaphore()
        axes = ("all",) if "all" in axes else axes
        steady = 0
        for axis in axes:
            for step in range(1, self.count(axis)):
                target = self.place(axis, self.peer(axis, step))
                pl.semaphore_signal(bar, inc=1, device_id=target, device_id_type=MESH)
            steady += self.count(axis) - 1
        cases = [(steady, None)]
        if neighbours and not ("all" in axes or "mp" in axes):
            pl.semaphore_signal(bar, inc=1, device_id=self.sibling, device_id_type=MESH)

            @pl.when(self.has_up)
            def _():
                pl.semaphore_signal(bar, inc=1, device_id=self.up, device_id_type=MESH)

            @pl.when(self.has_down)
            def _():
                pl.semaphore_signal(bar, inc=1, device_id=self.down, device_id_type=MESH)

            middle = jnp.logical_and(self.has_up, self.has_down)
            cases = [(steady + 3, middle), (steady + 2, jnp.logical_not(middle))]
        for count, when in cases:
            if when is None:
                pl.semaphore_wait(bar, count)
            else:

                @pl.when(when)
                def _():
                    pl.semaphore_wait(bar, count)


class Rider:
    def __init__(self, axis, array, cut=None, beside=False):
        self.axes = (axis,)
        self.axis = axis
        self.array = array
        self.cut = cut
        self.beside = beside

    def result(self, sizes):
        count = sizes[self.axis]
        shape = list(self.array.shape)
        if self.cut is not None:
            shape[self.cut] //= count
        self.columns = shape[-1]
        if self.beside:
            shape[-1] *= count
        else:
            shape = [count] + shape
        return jax.ShapeDtypeStruct(tuple(shape), self.array.dtype)

    def scratch(self, sizes):
        count = sizes[self.axis]
        return [pltpu.SemaphoreType.DMA((count,)), pltpu.SemaphoreType.DMA((count,))]

    def piece(self, ref, index, count):
        if self.cut is None:
            return ref
        size = self.array.shape[self.cut] // count
        where = [slice(None)] * len(self.array.shape)
        where[self.cut] = pl.ds(pl.multiple_of(index * size, size), size)
        return ref.at[tuple(where)]

    def copies(self, line, src, dst, send, recv):
        count, me = line.count(self.axis), line.index(self.axis)
        if self.beside:
            land = dst.at[:, pl.ds(pl.multiple_of(me * self.columns, self.columns), self.columns)]
        else:
            land = dst.at[me]
        made = [pltpu.make_async_copy(self.piece(src, me, count), land, send.at[0])]
        for step in range(1, count):
            peer = line.peer(self.axis, step)
            made.append(
                remote(
                    self.piece(src, peer, count),
                    land,
                    send.at[step],
                    recv.at[step],
                    line.place(self.axis, peer),
                )
            )
        return made

    def start(self, line, src, dst, send, recv):
        for copy in self.copies(line, src, dst, send, recv):
            copy.start()

    def middle(self, phase, *refs):
        pass

    def finish(self, line, src, dst, send, recv):
        for copy in self.copies(line, src, dst, send, recv):
            copy.wait()


class Settle:
    def __init__(self, array, summed, taps, placed):
        self.axes = ("dp", "mp")
        self.array = array
        self.summed = summed
        self.taps = taps
        self.placed = placed

    def result(self, sizes):
        n, m = sizes["mp"], sizes["dp"]
        self.ratio = n // m
        self.tail = tuple(self.array.shape[-2:])
        self.total = jax.ShapeDtypeStruct((n,) + self.tail, self.array.dtype)
        self.land = (m, self.ratio) + self.tail
        self.add = Rider("dp", self.array, None if self.summed else 1)
        self.outward = Rider("mp", self.total, 0)
        self.inward = Rider("dp", self.total, 0)
        if not self.placed:
            return jax.ShapeDtypeStruct(self.land, self.array.dtype)
        shape = (self.taps, self.ratio * self.tail[1] // self.taps, m * self.tail[0])
        return jax.ShapeDtypeStruct(shape, jnp.float32)

    def scratch(self, sizes):
        n, m = sizes["mp"], sizes["dp"]
        dtype = self.array.dtype
        refs = [pltpu.VMEM(self.land, dtype), pltpu.VMEM((n, 1) + self.tail, dtype)]
        if not self.summed:
            refs += [pltpu.VMEM((m, n, 1) + self.tail, dtype), pltpu.VMEM((n,) + self.tail, dtype)]
            refs += self.add.scratch(sizes)
        return refs + self.outward.scratch(sizes) + self.inward.scratch(sizes)

    def copies(self, step, line, src, dst, land, stage, *rest):
        if not self.summed:
            got, total = rest[:2]
            if step == 0:
                return self.add.copies(line, src, got, *rest[2:4])
            src, rest = total, rest[4:]
            step -= 1
        if step == 0:
            return self.outward.copies(line, src, stage, *rest[:2])
        return self.inward.copies(line, stage.at[:, 0], land, *rest[2:4])

    def start(self, *refs):
        for copy in self.copies(0, *refs):
            copy.start()

    def middle(self, phase, *refs):
        if self.summed and phase == 1:
            self.end(*refs)
            return
        for copy in self.copies(phase, *refs):
            copy.wait()
        if not self.summed and phase == 0:
            got, total = refs[5:7]

            @pl.loop(0, total.shape[0])
            def _(index):
                added_up = got[0, index, 0].astype(jnp.float32)
                for image in range(1, got.shape[0]):
                    added_up += got[image, index, 0].astype(jnp.float32)
                total[index] = added_up.astype(total.dtype)

        for copy in self.copies(phase + 1, *refs):
            copy.start()

    def finish(self, *refs):
        if not self.summed:
            self.end(*refs)

    def end(self, *refs):
        for copy in self.copies(1 if self.summed else 2, *refs):
            copy.wait()
        dst, land = refs[2:4]
        if not self.placed:
            dst[...] = land[...]
            return
        own = self.tail[1] // self.taps
        for half in range(self.ratio):
            for tap in range(self.taps):
                block = jnp.concatenate(
                    [
                        land[image, half, :, pl.ds(tap * own, own)].astype(jnp.float32)
                        for image in range(land.shape[0])
                    ],
                    axis=0,
                )
                dst[tap, pl.ds(half * own, own)] = block.T


def comm_call(kernel, inputs, out_shapes, scratch, riders, n, m, number, neighbours=True):
    chips = n // 2
    sizes = {"dp": m, "mp": n, "all": m * n}
    ride_shapes = tuple(rider.result(sizes) for rider in riders)
    ride_scratch = [rider.scratch(sizes) for rider in riders]
    any_spec = pl.BlockSpec(memory_space=pl.ANY)
    ni, nr, no = len(inputs), len(riders), len(out_shapes)

    def body(*refs):
        main_in, ride_in = refs[:ni], refs[ni : ni + nr]
        rest = refs[ni + nr :]
        main_out, ride_out = rest[:no], rest[no : no + nr]
        rest = rest[no + nr :]
        main_scratch, rest = rest[: len(scratch)], rest[len(scratch) :]
        line = Line(chips, m)
        line.barrier(sorted(set(axis for rider in riders for axis in rider.axes)), neighbours)
        riding = []
        for rider, src, dst, needs in zip(riders, ride_in, ride_out, ride_scratch):
            riding.append((rider, (line, src, dst) + tuple(rest[: len(needs)])))
            rest = rest[len(needs) :]
        for rider, refs_in in riding:
            rider.start(*refs_in)
        kernel(line, *main_in, *main_out, *main_scratch)
        for phase in range(2):
            for rider, refs_in in riding:
                rider.middle(phase, *refs_in)
        for rider, refs_in in riding:
            rider.finish(*refs_in)

    return pl.pallas_call(
        body,
        out_shape=tuple(out_shapes) + ride_shapes,
        in_specs=whole(ni) + [any_spec] * nr,
        out_specs=tuple(
            whole(no)
            + [whole(1)[0] if isinstance(rider, Settle) else any_spec for rider in riders]
        ),
        scratch_shapes=list(scratch) + [ref for needs in ride_scratch for ref in needs],
        compiler_params=comm_params(number),
    )(*inputs, *[rider.array for rider in riders])


def remote(src, dst, send, recv, target):
    return pltpu.make_async_remote_copy(
        src_ref=src,
        dst_ref=dst,
        send_sem=send,
        recv_sem=recv,
        device_id=target,
        device_id_type=MESH,
    )


def gather_sems(chips):
    return [pltpu.SemaphoreType.DMA((3, 2, chips)), pltpu.SemaphoreType.DMA((3, 2, chips))]


def line_gather(line, x_ref, slot, send, recv, on_own, on_pair):
    chips = line.chips
    z, c = line.z, line.c

    def hop(stream, step, src, block, target):
        return remote(src, slot(block), send.at[stream, 0, step], recv.at[stream, 0, step], target)

    def across(way, step, src, block):
        return remote(src, slot(block), send.at[2, way, step], recv.at[2, way, step], line.sibling)

    @pl.when(line.has_up)
    def _():
        hop(0, 1, x_ref, line.mp, line.up).start()

    @pl.when(line.has_down)
    def _():
        hop(1, 1, x_ref, line.mp, line.down).start()

    across(0, 0, x_ref, line.mp).start()
    slot(line.mp)[...] = x_ref[...]
    on_own()
    across(0, 0, x_ref, line.mp).wait_recv()
    on_pair(z)
    for step in range(1, chips):
        below, above = z - step, z + step

        @pl.when(below >= 0)
        def _():
            block = 2 * below + c
            hop(0, step, slot(block), block, line.up).wait_recv()
            if step + 1 < chips:

                @pl.when(line.has_up)
                def _():
                    hop(0, step + 1, slot(block), block, line.up).start()

            across(0, step, slot(block), block).start()

        @pl.when(above < chips)
        def _():
            block = 2 * above + c
            hop(1, step, slot(block), block, line.down).wait_recv()
            if step + 1 < chips:

                @pl.when(line.has_down)
                def _():
                    hop(1, step + 1, slot(block), block, line.down).start()

            across(1, step, slot(block), block).start()

        @pl.when(below >= 0)
        def _():
            across(0, step, slot(2 * below + c), 2 * below + c).wait_recv()
            on_pair(below)

        @pl.when(above < chips)
        def _():
            across(1, step, slot(2 * above + c), 2 * above + c).wait_recv()
            on_pair(above)

    @pl.when(line.has_up)
    def _():
        hop(0, 1, x_ref, line.mp, line.up).wait_send()

    @pl.when(line.has_down)
    def _():
        hop(1, 1, x_ref, line.mp, line.down).wait_send()

    across(0, 0, x_ref, line.mp).wait_send()
    for step in range(1, chips):
        below, above = z - step, z + step

        @pl.when(below >= 0)
        def _():
            block = 2 * below + c
            if step + 1 < chips:

                @pl.when(line.has_up)
                def _():
                    hop(0, step + 1, slot(block), block, line.up).wait_send()

            across(0, step, slot(block), block).wait_send()

        @pl.when(above < chips)
        def _():
            block = 2 * above + c
            if step + 1 < chips:

                @pl.when(line.has_down)
                def _():
                    hop(1, step + 1, slot(block), block, line.down).wait_send()

            across(1, step, slot(block), block).wait_send()


def scatter_scratch(chips, rows, cols, parts):
    block = (chips, rows, cols)
    return [
        pltpu.VMEM(block, jnp.float32),
        pltpu.VMEM(block, jnp.bfloat16),
        pltpu.VMEM(block, jnp.bfloat16),
        pltpu.VMEM((2,) + block, jnp.bfloat16),
        pltpu.SemaphoreType.DMA((2, 3, chips, parts)),
    ]


def line_scatter(line, scratch, parts, produce, finish, tile, side=()):
    chips = line.chips
    z = line.z
    kept, out_ref, in_ref, moving, sems = scratch
    count = kept.shape[1] // parts

    def span(part):
        return pl.ds(part * count, count)

    def across(chip, part):
        return remote(
            out_ref.at[chip, span(part)],
            in_ref.at[chip, span(part)],
            sems.at[0, 0, chip, part],
            sems.at[1, 0, chip, part],
            line.sibling,
        )

    def hop(way, chip, part):
        target = line.up if way == 0 else line.down
        ref = moving.at[way, chip, span(part)]
        return remote(
            ref, ref, sems.at[0, 1 + way, chip, part], sems.at[1, 1 + way, chip, part], target
        )

    items = []
    for step in range(chips - 1):
        for part in range(parts):
            items.append((0, chips - 1 - step + z, part, step >= z))
            items.append((1, step - (chips - 1 - z), part, step >= chips - 1 - z))
    for part in range(parts):
        items.append((2, z, part, None))

    def run(active, body):
        if active is None:
            body()
        else:
            pl.when(active)(body)

    def start(item):
        way, chip, part, active = item

        def body():
            produce(chip, part, count, kept.at[chip], out_ref.at[chip])
            across(chip, part).start()

        run(active, body)

    def tiles(part, body):
        @pl.loop(0, count // tile)
        def _(index):
            body(pl.ds(pl.multiple_of(part * count + index * tile, tile), tile))

    def close(item):
        way, chip, part, active = item

        def body():
            across(chip, part).wait_recv()
            if way < 2:
                later = line.has_down if way == 0 else line.has_up

                @pl.when(later)
                def _():
                    hop(way, chip, part).wait_recv()

                    def add(rows):
                        moving[way, chip, rows] = (
                            kept[chip, rows]
                            + in_ref[chip, rows].astype(jnp.float32)
                            + moving[way, chip, rows].astype(jnp.float32)
                        ).astype(jnp.bfloat16)

                    tiles(part, add)

                @pl.when(jnp.logical_not(later))
                def _():
                    def add(rows):
                        moving[way, chip, rows] = (
                            kept[chip, rows] + in_ref[chip, rows].astype(jnp.float32)
                        ).astype(jnp.bfloat16)

                    tiles(part, add)

                hop(way, chip, part).start()
            else:

                def total(rows):
                    return kept[chip, rows] + in_ref[chip, rows].astype(jnp.float32)

                def from_side(side, rows):
                    return moving[side, chip, rows].astype(jnp.float32)

                both = jnp.logical_and(line.has_down, line.has_up)

                @pl.when(both)
                def _():
                    hop(0, chip, part).wait_recv()
                    hop(1, chip, part).wait_recv()
                    tiles(
                        part,
                        lambda rows: finish(
                            part, rows, total(rows) + from_side(0, rows) + from_side(1, rows)
                        ),
                    )

                for side, present in ((0, line.has_down), (1, line.has_up)):

                    @pl.when(jnp.logical_and(present, jnp.logical_not(both)))
                    def _():
                        hop(side, chip, part).wait_recv()
                        tiles(
                            part,
                            lambda rows: finish(part, rows, total(rows) + from_side(side, rows)),
                        )

        run(active, body)

    lag = 2
    side = list(side)
    for index, item in enumerate(items):
        start(item)
        if index >= lag:
            close(items[index - lag])
            if index % 2 == 0 and side:
                side.pop(0)()
    for step in side:
        step()
    for item in items[-lag:]:
        close(item)
    for way, chip, part, active in items:

        def body():
            across(chip, part).wait_send()
            if way < 2:
                hop(way, chip, part).wait_send()

        run(active, body)


def whole(count):
    return [pl.BlockSpec(memory_space=pltpu.VMEM)] * count


def comm_params(number):
    return pltpu.CompilerParams(
        collective_id=number, has_side_effects=True, vmem_limit_bytes=VMEM_BYTES
    )


def pick(c, low, high):
    return jnp.where(c == 0, low, high), jnp.where(c == 0, high, low)


def conv_scatter_kernel(breadth, line, x_ref, w_ref, o_ref, *scratch):
    pixels, own = o_ref.shape
    tile = 512

    def produce(chip, part, count, mine, other):
        columns = pl.ds(pl.multiple_of(chip * 2 * own, 2 * own), 2 * own)

        @pl.loop(0, count // tile)
        def _(index):
            base = pl.multiple_of(part * count + index * tile, tile)
            total = jnp.zeros((tile, 2 * own), jnp.float32)
            for i in range(3):
                total += jnp.dot(
                    x_ref[pl.ds(base + i * breadth, tile)],
                    w_ref[i, :, columns],
                    preferred_element_type=jnp.float32,
                )
            first, second = pick(line.c, total[:, :own], total[:, own:])
            mine[pl.ds(base, tile)] = first
            other[pl.ds(base, tile)] = second.astype(jnp.bfloat16)

    def finish(part, rows, total):
        o_ref[rows] = total

    line_scatter(line, scratch, CONV_PARTS, produce, finish, tile)


def side_by_side(hidden):
    rows, cols, depth = hidden.shape
    padded = jnp.pad(hidden, ((1, 1), (1, 1), (0, 0)))
    return jnp.concatenate([padded[:, j : j + cols] for j in range(3)], axis=2).reshape(
        (rows + 2) * cols, 3 * depth
    )


def conv_scatter_fused(spread, kernel, cols, n, m, number, riders=()):
    own = kernel.shape[2] // n
    depth = kernel.shape[1]
    pixels = spread.shape[0] - 2 * cols
    return comm_call(
        partial(conv_scatter_kernel, cols),
        (spread, kernel.reshape(3, 3 * depth, kernel.shape[2])),
        (jax.ShapeDtypeStruct((pixels, own), jnp.float32),),
        scatter_scratch(n // 2, pixels, own, CONV_PARTS),
        riders,
        n,
        m,
        number,
    )


def conv_back_kernel(breadth, size, extra, line, g_ref, w_ref, x_ref, n_ref, v_ref, *refs):
    refs = list(refs)
    more_ref = refs.pop(0) if extra else None
    low_ref, wg_ref, stat_ref, acc_ref, held, sums, send, recv = refs
    chips = line.chips
    pixels, own = g_ref.shape
    wide = w_ref.shape[1]
    tile, long = 512, 1024
    zero = jnp.zeros((breadth, own), jnp.bfloat16)
    for block in range(2 * chips):
        held[block, pl.ds(0, breadth)] = zero
        held[block, pl.ds(breadth + pixels, breadth)] = zero

    def slot(block):
        return held.at[block, pl.ds(breadth, pixels)]

    def beside(base, count, chip):
        rows = pl.ds(base, count)
        return [held[2 * chip, rows], held[2 * chip + 1, rows]]

    def on_own():
        @pl.loop(0, pixels // tile)
        def _(index):
            acc_ref[pl.ds(pl.multiple_of(index * tile, tile), tile)] = jnp.zeros(
                (tile, wide), jnp.float32
            )

    def on_pair(chip):
        columns = pl.ds(pl.multiple_of(chip * 2 * own, 2 * own), 2 * own)

        @pl.loop(0, pixels // tile)
        def _(index):
            base = pl.multiple_of(index * tile, tile)
            shifted = []
            for i in range(3):
                shifted += beside(base + (2 - i) * breadth, tile, chip)
            acc_ref[pl.ds(base, tile)] += product(
                jnp.concatenate(shifted, axis=1),
                jnp.concatenate([w_ref[i, :, columns] for i in range(3)], axis=1),
                True,
            )

        sums[...] = jnp.zeros_like(sums)

        @pl.loop(0, pixels // long)
        def _(index):
            base = pl.multiple_of(index * long, long)
            sums[...] += lax.dot_general(
                jnp.concatenate(beside(base + breadth, long, chip), axis=1),
                jnp.concatenate(
                    [x_ref[pl.ds(base + i * breadth, long)] for i in range(3)], axis=1
                ),
                (((0,), (0,)), ((), ())),
                preferred_element_type=jnp.float32,
            )

        wg_ref[chip] = sums[...].astype(jnp.bfloat16)

    line_gather(line, g_ref, slot, send, recv, on_own, on_pair)

    gain, inverse = v_ref[0:1], v_ref[1:2]
    stat_ref[...] = jnp.zeros_like(stat_ref)
    column = lax.broadcasted_iota(jnp.int32, (tile, own), 0) % breadth

    @pl.loop(0, pixels // tile)
    def _(index):
        rows = pl.ds(pl.multiple_of(index * tile, tile), tile)
        left = jnp.where(
            column == breadth - 1, 0.0, pltpu.roll(acc_ref[rows, 0:own], tile - 1, 0)
        )
        right = jnp.where(column == 0, 0.0, pltpu.roll(acc_ref[rows, 2 * own : wide], 1, 0))
        incoming = left + acc_ref[rows, own : 2 * own] + right
        normed = n_ref[rows]
        pre_act = normed * gain
        sigmoid_part = 1.0 / (1.0 + jnp.exp(-pre_act))
        through = incoming * sigmoid_part * (1.0 + pre_act * (1.0 - sigmoid_part))
        acc_ref[rows, 0:own] = through
        stat_ref[0:1] += jnp.sum(through * normed, axis=0, keepdims=True)
        stat_ref[1:2] += jnp.sum(through, axis=0, keepdims=True)

    groups = [lax.broadcasted_iota(jnp.int32, (own, own), axis) // size for axis in range(2)]
    spread = jnp.where(groups[0] == groups[1], 1.0 / (pixels * size), 0.0)
    means = jnp.dot(stat_ref[...] * gain, spread, precision=PRECISE)
    second_mean, first_mean = means[0:1], means[1:2]

    @pl.loop(0, pixels // tile)
    def _(index):
        rows = pl.ds(pl.multiple_of(index * tile, tile), tile)
        outgoing = inverse * (
            acc_ref[rows, 0:own] * gain - first_mean - n_ref[rows] * second_mean
        )
        stat_ref[2:3] += jnp.sum(outgoing, axis=0, keepdims=True)
        if extra:
            outgoing = outgoing + more_ref[rows]
        low_ref[rows] = outgoing.astype(jnp.bfloat16)


def conv_back_fused(
    grad_low, spread, kernel, normed, inverse, gain, size, cols, n, m, number, riders, more=()
):
    pixels, own = grad_low.shape
    depth = kernel.shape[1]
    chips = n // 2
    vectors = jnp.concatenate([gain[None], inverse[None], jnp.zeros((6, own), jnp.float32)])
    return comm_call(
        partial(conv_back_kernel, cols, size, len(more) > 0),
        (grad_low, kernel.reshape(3, 3 * depth, kernel.shape[2]), spread, normed, vectors)
        + tuple(more),
        (
            jax.ShapeDtypeStruct((pixels, depth), jnp.bfloat16),
            jax.ShapeDtypeStruct((chips, 2 * own, 9 * depth), jnp.bfloat16),
            jax.ShapeDtypeStruct((8, own), jnp.float32),
        ),
        [
            pltpu.VMEM((pixels, 3 * depth), jnp.float32),
            pltpu.VMEM((n, pixels + 2 * cols, own), jnp.bfloat16),
            pltpu.VMEM((2 * own, 9 * depth), jnp.float32),
        ]
        + gather_sems(chips),
        riders,
        n,
        m,
        number,
    )


def join_columns(acc, cols):
    pixels, wide = acc.shape
    depth = wide // 3
    planes = acc.reshape(-1, cols, wide)
    none = jnp.zeros_like(planes[:, :1, :depth])
    left = jnp.concatenate([planes[:, 1:, :depth], none], axis=1)
    right = jnp.concatenate([none, planes[:, :-1, 2 * depth :]], axis=1)
    return (left + planes[:, :, depth : 2 * depth] + right).reshape(pixels, depth)


def product(x, w, turned):
    return lax.dot_general(
        x, w, (((1,), (1 if turned else 0,)), ((), ())), preferred_element_type=jnp.float32
    )


def outer_steps(grad, left, right, cut):
    def step(start):
        grad[pl.ds(start, cut)] = lax.dot_general(
            left[:, pl.ds(start, cut)],
            right[...],
            (((0,), (0,)), ((), ())),
            preferred_element_type=jnp.float32,
        ).astype(grad.dtype)

    return [partial(step, start) for start in range(0, left.shape[1], cut)]


def tokens_scatter_kernel(turned, beside, line, x_ref, w_ref, *refs):
    side = ()
    if beside:
        left, right, o_ref, grad, *scratch = refs
        side = outer_steps(grad, left, right, 128)
    else:
        o_ref, *scratch = refs
    tokens, width = o_ref.shape
    cut = width // TOKEN_PARTS
    depth = x_ref.shape[1] // w_ref.shape[0]

    def produce(chip, part, count, mine, other):
        rows = pl.ds(pl.multiple_of(chip * 2 * tokens, 2 * tokens), 2 * tokens)
        columns = pl.ds(part * cut, cut)
        total = None
        for j in range(w_ref.shape[0]):
            w = w_ref[j, columns] if turned else w_ref[j, :, columns]
            term = product(x_ref[rows, pl.ds(j * depth, depth)], w, turned)
            total = term if total is None else total + term
        first, second = pick(line.c, total[:tokens], total[tokens:])
        mine[pl.ds(part * count, count)] = first
        other[pl.ds(part * count, count)] = second.astype(jnp.bfloat16)

    def finish(part, rows, total):
        o_ref[:, pl.ds(part * cut, cut)] = total

    line_scatter(line, scratch, TOKEN_PARTS, produce, finish, tokens, side)


def outer_shapes(outer):
    if not outer:
        return ()
    return (jax.ShapeDtypeStruct((outer[0].shape[1], outer[1].shape[1]), jnp.bfloat16),)


def tokens_scatter(x, w, turned, n, m, number, riders=(), outer=()):
    tokens = x.shape[0] // n
    width = w.shape[1] if turned else w.shape[2]
    return comm_call(
        partial(tokens_scatter_kernel, turned, len(outer) > 0),
        (x, w) + tuple(outer),
        (jax.ShapeDtypeStruct((tokens, width), jnp.float32),) + outer_shapes(outer),
        scatter_scratch(n // 2, TOKEN_PARTS * tokens, width // TOKEN_PARTS, TOKEN_PARTS),
        riders,
        n,
        m,
        number,
    )


def add_outer(total, left, right, rows):
    cut = min(left.shape[1], 512)
    for start in range(0, left.shape[1], cut):
        total[pl.ds(start, cut)] += lax.dot_general(
            left[rows, pl.ds(start, cut)],
            right[rows],
            (((0,), (0,)), ((), ())),
            preferred_element_type=jnp.float32,
        )


def tokens_gather_kernel(
    turned, shape_out, outs, side, beside, cols, chained, line, x_ref, w_ref, *refs
):
    refs = list(refs)
    chain_w = refs.pop(0) if chained else None
    left = refs.pop(0) if side else None
    outer = (refs.pop(0), refs.pop(0)) if beside else None
    held = refs.pop(0)
    results = [refs.pop(0) for _ in range(outs)]
    grad = refs.pop(0) if side else None
    outer_grad = refs.pop(0) if beside else None
    chain_out = refs.pop(0) if chained else None
    total = refs.pop(0) if side else None
    send, recv = refs
    tokens = x_ref.shape[0]
    across = w_ref.shape[1 if turned else 2]
    cut = min(across, 512)

    def slot(block):
        return held.at[pl.ds(pl.multiple_of(block * tokens, tokens), tokens)]

    def store_pixels(ref, chip, value):
        depth = value.shape[1] // 4
        base = chip * 8 * tokens
        for row in range(4 * tokens // cols):
            for tap in range(4):
                start = base + (2 * row + tap // 2) * cols + tap % 2
                ref[pl.Slice(start, cols // 2, 2)] = value[
                    row * (cols // 2) : (row + 1) * (cols // 2), tap * depth : (tap + 1) * depth
                ]

    def on_pair(chip):
        rows = pl.ds(pl.multiple_of(chip * 2 * tokens, 2 * tokens), 2 * tokens)
        for j in range(w_ref.shape[0]):
            for start in range(0, across, cut):
                w = w_ref[j, pl.ds(start, cut)] if turned else w_ref[j, :, pl.ds(start, cut)]
                values = shape_out(product(held[rows], w, turned))
                for ref, value in zip(results, values):
                    if cols:
                        store_pixels(ref, chip, value)
                    else:
                        ref[rows, pl.ds(j * across + start, cut)] = value.astype(ref.dtype)
        if chained:
            for start in range(0, chain_w.shape[1], 512):
                columns = pl.ds(start, 512)
                chain_out[rows, columns] = product(
                    results[-1][rows], chain_w[:, columns], False
                ).astype(jnp.bfloat16)
        if side:
            add_outer(total, held, left, rows)

    def on_own():
        if side:
            total[...] = jnp.zeros_like(total)
        if beside:
            for step in outer_steps(outer_grad, *outer, 256):
                step()

    line_gather(line, x_ref, slot, send, recv, on_own, on_pair)
    if side:
        grad[...] = total[...].astype(grad.dtype)


def tokens_gather(
    x, w, turned, kinds, shape_out, n, m, number, riders=(), left=None, outer=(), cols=0, chain=()
):
    tokens, width = x.shape
    across = w.shape[0] * w.shape[1 if turned else 2]
    side = left is not None
    grads = ((width, left.shape[1]),) if side else ()
    shape = (tokens * n * 4, across // 4) if cols else (tokens * n, across)
    return comm_call(
        partial(
            tokens_gather_kernel,
            turned,
            shape_out,
            len(kinds),
            side,
            len(outer) > 0,
            cols,
            len(chain) > 0,
        ),
        (x, w) + tuple(chain) + ((left,) if side else ()) + tuple(outer),
        (jax.ShapeDtypeStruct((tokens * n, width), x.dtype),)
        + tuple(jax.ShapeDtypeStruct(shape, kind) for kind in kinds)
        + tuple(jax.ShapeDtypeStruct(grad, jnp.bfloat16) for grad in grads)
        + outer_shapes(outer)
        + tuple(jax.ShapeDtypeStruct((tokens * n, w2.shape[1]), jnp.bfloat16) for w2 in chain),
        [pltpu.VMEM(grad, jnp.float32) for grad in grads] + gather_sems(n // 2),
        riders,
        n,
        m,
        number,
    )


def exchange(riders, n, m, number):
    return comm_call(lambda line: None, (), (), [], riders, n, m, number, neighbours=False)


def tiled_up(vector):
    count = -(-vector.shape[0] // 1024) * 1024
    return jnp.pad(vector.astype(jnp.float32), (0, count - vector.shape[0])).reshape(-1, 128)


def attend_scatter_kernel(line, x_ref, valid_ref, w_ref, o_ref, mixed_ref, *scratch):
    tokens, width = o_ref.shape
    wide = mixed_ref.shape[1]
    cut = width // TOKEN_PARTS
    scale = 1.0 / math.sqrt(HEAD_DIM)

    def attend(rows):
        for head in range(wide // HEAD_DIM):
            where = [pl.ds(j * wide + head * HEAD_DIM, HEAD_DIM) for j in range(3)]
            scores = product(x_ref[rows, where[0]], x_ref[:, where[1]], True) * scale
            scores = jnp.where(valid_ref[0:1] > 0.5, scores, MASKED_SCORE)
            exponent = jnp.exp(scores - jnp.max(scores, axis=1, keepdims=True))
            inverse = 1.0 / jnp.sum(exponent, axis=1, keepdims=True)
            mixed_ref[rows, pl.ds(head * HEAD_DIM, HEAD_DIM)] = product(
                (exponent * inverse).astype(jnp.bfloat16), x_ref[:, where[2]], False
            ).astype(jnp.bfloat16)

    def produce(chip, part, count, mine, other):
        rows = pl.ds(pl.multiple_of(chip * 2 * tokens, 2 * tokens), 2 * tokens)
        if part == 0:
            attend(rows)
        total = product(mixed_ref[rows], w_ref[:, pl.ds(part * cut, cut)], False)
        first, second = pick(line.c, total[:tokens], total[tokens:])
        mine[pl.ds(part * count, count)] = first
        other[pl.ds(part * count, count)] = second.astype(jnp.bfloat16)

    def finish(part, rows, total):
        o_ref[:, pl.ds(part * cut, cut)] = total

    line_scatter(line, scratch, TOKEN_PARTS, produce, finish, tokens)


def attend_scatter(qkv_rows, valid, out_weight, n, m, number):
    total = qkv_rows.shape[0]
    tokens = total // n
    width = out_weight.shape[1]
    return comm_call(
        attend_scatter_kernel,
        (qkv_rows, jnp.broadcast_to(valid[None], (8, total)), out_weight),
        (
            jax.ShapeDtypeStruct((tokens, width), jnp.float32),
            jax.ShapeDtypeStruct((total, out_weight.shape[0]), jnp.bfloat16),
        ),
        scatter_scratch(n // 2, TOKEN_PARTS * tokens, width // TOKEN_PARTS, TOKEN_PARTS),
        (),
        n,
        m,
        number,
    )


def attend_gather_kernel(
    line,
    g_ref,
    w_ref,
    x_ref,
    kt_ref,
    valid_ref,
    mixed_ref,
    left,
    right,
    held,
    grad_ref,
    out_ref,
    outer_grad,
    keys_sum,
    values_sum,
    out_sum,
    send,
    recv,
):
    tokens = g_ref.shape[0]
    wide = w_ref.shape[0]
    heads = wide // HEAD_DIM
    scale = 1.0 / math.sqrt(HEAD_DIM)

    def slot(block):
        return held.at[pl.ds(pl.multiple_of(block * tokens, tokens), tokens)]

    def on_own():
        keys_sum[...] = jnp.zeros_like(keys_sum)
        values_sum[...] = jnp.zeros_like(values_sum)
        out_sum[...] = jnp.zeros_like(out_sum)
        for step in outer_steps(outer_grad, left, right, 256):
            step()

    def on_pair(chip):
        rows = pl.ds(pl.multiple_of(chip * 2 * tokens, 2 * tokens), 2 * tokens)
        for head in range(heads):
            place = pl.ds(head * HEAD_DIM, HEAD_DIM)
            where = [pl.ds(j * wide + head * HEAD_DIM, HEAD_DIM) for j in range(3)]
            grad = product(held[rows], w_ref[place], True).astype(jnp.bfloat16)
            query = x_ref[rows, where[0]]
            scores = product(x_ref[:, where[1]], query, True) * scale
            scores = jnp.where(valid_ref[:, 0:1] > 0.5, scores, MASKED_SCORE)
            exponent = jnp.exp(scores - jnp.max(scores, axis=0, keepdims=True))
            probs = exponent * (1.0 / jnp.sum(exponent, axis=0, keepdims=True))
            values_sum[:, place] += product(probs.astype(jnp.bfloat16), grad, False)
            grad_probs = product(x_ref[:, where[2]], grad, True)
            inner = jnp.sum(probs * grad_probs, axis=0, keepdims=True)
            grad_scores = (probs * (grad_probs - inner) * scale).astype(jnp.bfloat16)
            keys_sum[:, place] += product(grad_scores, query, False)
            grad_ref[rows, where[0]] = product(kt_ref[place], grad_scores, False).T.astype(
                jnp.bfloat16
            )
        add_outer(out_sum, mixed_ref, held, rows)

    line_gather(line, g_ref, slot, send, recv, on_own, on_pair)
    grad_ref[:, pl.ds(wide, wide)] = keys_sum[...].astype(jnp.bfloat16)
    grad_ref[:, pl.ds(2 * wide, wide)] = values_sum[...].astype(jnp.bfloat16)
    out_ref[...] = out_sum[...].astype(jnp.bfloat16)


def attend_gather(grad_mid, out_weight, qkv_rows, valid, mixed_low, outer, n, m, number, riders):
    tokens, width = grad_mid.shape
    total = tokens * n
    wide = out_weight.shape[0]
    return comm_call(
        attend_gather_kernel,
        (
            grad_mid,
            out_weight,
            qkv_rows,
            qkv_rows[:, wide : 2 * wide].T,
            jnp.broadcast_to(valid[:, None], (total, 128)),
            mixed_low,
        )
        + tuple(outer),
        (
            jax.ShapeDtypeStruct((total, width), jnp.bfloat16),
            jax.ShapeDtypeStruct((total, 3 * wide), jnp.bfloat16),
            jax.ShapeDtypeStruct((wide, width), jnp.bfloat16),
        )
        + outer_shapes(outer),
        [
            pltpu.VMEM((total, wide), jnp.float32),
            pltpu.VMEM((total, wide), jnp.float32),
            pltpu.VMEM((wide, width), jnp.float32),
        ]
        + gather_sems(n // 2),
        riders,
        n,
        m,
        number,
    )


def local(
    image,
    embedding,
    extents,
    gain_first,
    conv_first,
    gain_second,
    conv_second,
    shift_weight,
    down_weight,
    ada_weight,
    qkv_weight,
    out_weight,
    up_weight,
    proj_weight,
    cotangent,
):
    strip_rows, canvas_cols, channel_count = (image.shape[1], image.shape[2], image.shape[3])
    width_all = out_weight.shape[1]
    n = lax.axis_size("mp")
    m = lax.axis_size("dp")
    me_mp = lax.axis_index("mp")
    me_dp = lax.axis_index("dp")
    rows_all = strip_rows * n
    pixel_total = rows_all * canvas_cols
    own = channel_count // n
    size = channel_count // GROUPS
    token_rows = strip_rows // 2
    token_cols = canvas_cols // 2
    local_tokens = token_rows * token_cols
    token_total = local_tokens * n
    local_width = out_weight.shape[0]

    fused = own % 128 == 0 and n == 2 * m
    shift_vector = jnp.dot(embedding, shift_weight, preferred_element_type=jnp.float32)[0]
    columns = jnp.dot(embedding, ada_weight, preferred_element_type=jnp.float32)[0]
    riders = (Rider("mp", tiled_up(columns)),)
    if fused:
        modulation, pixels_low = exchange(
            riders + (Rider("mp", image[0].reshape(-1, channel_count), 1),), n, m, 12
        )
    else:
        (modulation,) = exchange(riders, n, m, 12)
        pixels_low = lax.all_to_all(image[0], "mp", 2, 0, tiled=True)
    modulation = modulation.reshape(n, -1)[:, : columns.shape[0]].reshape(-1)
    scale_attend = modulation[:width_all]
    shift_attend = modulation[width_all : 2 * width_all]
    scale_mlp = modulation[2 * width_all : 3 * width_all]
    shift_mlp = modulation[3 * width_all :]
    own_first = lax.dynamic_slice_in_dim(gain_first, me_mp * own, own)
    own_second = lax.dynamic_slice_in_dim(gain_second, me_mp * own, own)

    pixels = pixels_low.astype(jnp.float32).reshape(pixel_total, own)
    normed_first, inverse_first = group_forward(pixels, size)
    hidden_first = (
        jax.nn.silu(normed_first * own_first)
        .astype(jnp.bfloat16)
        .reshape(rows_all, canvas_cols, own)
    )
    spread_first = side_by_side(hidden_first)
    if fused:
        (conv_output,) = conv_scatter_fused(spread_first, conv_first, canvas_cols, n, m, 0)
    else:
        conv_output = conv_scatter(hidden_first, conv_first, n)
    conv_output = conv_output + shift_vector
    normed_second, inverse_second = group_forward(conv_output, size)
    hidden_second = (
        jax.nn.silu(normed_second * own_second)
        .astype(jnp.bfloat16)
        .reshape(rows_all, canvas_cols, own)
    )
    spread_second = side_by_side(hidden_second)
    if fused:
        (conv_again,) = conv_scatter_fused(spread_second, conv_second, canvas_cols, n, m, 1)
    else:
        conv_again = conv_scatter(hidden_second, conv_second, n)
    residual = pixels + conv_again
    down_patch = (
        residual.astype(jnp.bfloat16)
        .reshape(rows_all // 2, 2, token_cols, 2, own)
        .transpose(0, 2, 1, 3, 4)
        .reshape(token_total, 4 * own)
    )
    down_matrix = down_weight.reshape(4 * own, width_all)
    (stream,) = tokens_scatter(down_patch, down_matrix[None], False, n, m, 2)
    normed_attend, inverse_attend = layer_forward(stream)
    input_attend = (normed_attend * (1.0 + scale_attend) + shift_attend).astype(jnp.bfloat16)
    all_attend, qkv_rows = tokens_gather(
        input_attend, qkv_weight, False, (jnp.bfloat16,), lambda value: (value,), n, m, 3
    )
    token_index = jnp.arange(token_total, dtype=jnp.int32)
    key_valid = (token_index // token_cols < extents[0, 0]) & (
        token_index % token_cols < extents[0, 1]
    )
    valid = key_valid.astype(jnp.float32)
    attended, mixed_low = attend_scatter(qkv_rows, valid, out_weight, n, m, 4)
    stream_mid = stream + attended
    normed_mlp, inverse_mlp = layer_forward(stream_mid)
    input_mlp = (normed_mlp * (1.0 + scale_mlp) + shift_mlp).astype(jnp.bfloat16)
    all_mlp, upper_proj, activated, projected = tokens_gather(
        input_mlp,
        up_weight[None],
        False,
        (jnp.float32, jnp.bfloat16),
        lambda value: (value, jax.nn.gelu(value, approximate=True)),
        n,
        m,
        5,
        chain=(proj_weight,),
    )
    final_stream = stream_mid + scatter_rows(projected)
    output = final_stream.astype(jnp.bfloat16).reshape(1, token_rows, token_cols, width_all)

    grad_final_low = cotangent[0].reshape(local_tokens, width_all)
    grad_final = grad_final_low.astype(jnp.float32)
    all_final = gather_rows(lax.optimization_barrier((grad_final_low, qkv_rows))[0])
    grad_act = jnp.einsum("le,fe->lf", all_final, proj_weight, preferred_element_type=jnp.float32)
    gelu_pull = jax.vjp(partial(jax.nn.gelu, approximate=True), upper_proj)[1]
    grad_upper = gelu_pull(grad_act)[0].astype(jnp.bfloat16)
    grad_normed_mlp, grad_proj = tokens_scatter(
        grad_upper, up_weight[None], True, n, m, 6, (), (activated, all_final)
    )
    grad_mid_norm, grad_scale_mlp, grad_shift_mlp = layer_backward(
        grad_normed_mlp, normed_mlp, inverse_mlp, scale_mlp
    )
    grad_mid = grad_final + grad_mid_norm
    all_mid, grad_qkv, grad_out, grad_up, sums_proj = attend_gather(
        grad_mid.astype(jnp.bfloat16),
        out_weight,
        qkv_rows,
        valid,
        mixed_low,
        (all_mlp, grad_upper),
        n,
        m,
        7,
        (Rider("dp", grad_proj, 1),),
    )
    (grad_normed_attend,) = tokens_scatter(grad_qkv, qkv_weight, True, n, m, 8)
    grad_stream_norm, grad_scale_attend, grad_shift_attend = layer_backward(
        grad_normed_attend, normed_attend, inverse_attend, scale_attend
    )
    grad_stream = grad_mid + grad_stream_norm
    grad_modulation = jnp.concatenate(
        [
            tiled_up(piece)
            for piece in jnp.concatenate(
                [grad_scale_attend, grad_shift_attend, grad_scale_mlp, grad_shift_mlp]
            ).reshape(n, -1)
        ]
    )
    all_stream, grad_residual, grad_down, grad_qkv_weight, sums_up, ada_columns = tokens_gather(
        grad_stream.astype(jnp.bfloat16),
        down_matrix[None],
        True,
        (jnp.float32,),
        lambda value: (value,),
        n,
        m,
        9,
        (
            Rider("dp", grad_up, 0),
            Rider("mp", grad_modulation, 0),
        ),
        down_patch,
        (all_attend, grad_qkv),
        canvas_cols if fused else 0,
    )
    ada_columns = added(ada_columns).reshape(-1)[: columns.shape[0]]
    if not fused:
        grad_residual = (
            grad_residual.reshape(rows_all // 2, token_cols, 2, 2, own)
            .transpose(0, 2, 1, 3, 4)
            .reshape(pixel_total, own)
        )
    def back(grad_low, hidden, spread, kernel, normed, inverse, gain, number, riders, more=()):
        if fused:
            low, parts, sums, *ridden = conv_back_fused(
                grad_low,
                spread,
                kernel,
                normed,
                inverse,
                gain,
                size,
                canvas_cols,
                n,
                m,
                number,
                riders,
                more,
            )
            return low, parts, sums[0], sums[2], ridden
        grad_hidden, grad_kernel = conv_backward(grad_low, hidden, kernel, n)
        outgoing, gain_part = group_backward(grad_hidden, normed, inverse, gain, size)
        parts = grad_kernel.astype(jnp.bfloat16).reshape(9 * own, -1).T
        low = sum(more, outgoing).astype(jnp.bfloat16)
        return low, parts, gain_part, jnp.sum(outgoing, axis=0), exchange(riders, n, m, number)

    grad_conv_low, parts_second, grad_gain_second, grad_shift, rode_second = back(
        grad_residual.astype(jnp.bfloat16),
        hidden_second,
        spread_second,
        conv_second,
        normed_second,
        inverse_second,
        own_second,
        10,
        (
            Rider("dp", unsettled(grad_down, m, n), 1),
            Rider("dp", grad_qkv_weight, 0),
            Rider("dp", grad_out, 1),
            Rider("dp", jnp.concatenate([tiled_up(embedding[0]), tiled_up(ada_columns)])),
        ),
    )
    sums_down, sums_qkv, sums_out, every_small = rode_second
    image_turned, parts_first, grad_gain_first, _, rode_first = back(
        grad_conv_low,
        hidden_first,
        spread_first,
        conv_first,
        normed_first,
        inverse_first,
        own_first,
        11,
        (
            Rider("dp", unsettled(parts_second, m, n), 1),
            Rider("dp", tiled_up(grad_shift)),
            Settle(added(sums_down)[:, 0].astype(jnp.bfloat16), True, 4, fused),
        ),
        (grad_residual,),
    )
    sums_second, every_shift, pieces_down = rode_first
    embed_term = jnp.dot(
        grad_shift[None], shift_weight.astype(jnp.float32).T, precision=PRECISE
    ) + jnp.dot(ada_columns[None], ada_weight.astype(jnp.float32).T, precision=PRECISE)
    small = jnp.concatenate(
        [tiled_up(embed_term[0]), tiled_up(jnp.concatenate([grad_gain_first, grad_gain_second]))]
    )
    riders = (
        Settle(unsettled(parts_first, m, n), False, 9, fused),
        Rider("all", small),
        Settle(added(sums_second)[:, 0].astype(jnp.bfloat16), True, 9, fused),
    )
    if fused:
        pieces_first, small, pieces_second, image_turned = exchange(
            riders + (Rider("mp", image_turned, 0, True),), n, m, 13
        )
        image_grad = image_turned.reshape(image.shape)
    else:
        pieces_first, small, pieces_second = exchange(riders, n, m, 13)
        image_grad = lax.all_to_all(
            image_turned.reshape(rows_all, canvas_cols, own), "mp", 0, 2, tiled=True
        )[None]

    small = small.reshape(m, n, -1)
    embed_count = embedding.shape[1]
    embedding_grad = jnp.sum(
        lax.dynamic_index_in_dim(small, me_dp, axis=0, keepdims=False)[:, :embed_count], axis=0
    )[None]
    gain_start = -(-embed_count // 1024) * 1024
    gains = jnp.sum(small[:, :, gain_start : gain_start + 2 * own], axis=0)
    gains = gains.reshape(n, 2, own).transpose(1, 0, 2).reshape(2, -1)
    piece = channel_count // (m * n)
    gains = lax.dynamic_slice_in_dim(gains, (me_dp * n + me_mp) * piece, piece, axis=1)
    every_small = every_small.reshape(m, -1)
    embed_rows = lax.dynamic_slice_in_dim(
        every_small[:, :embed_count], me_dp * (embed_count // m), embed_count // m, axis=1
    )
    grad_shift_weight = jnp.dot(
        embed_rows.T, every_shift.reshape(m, -1)[:, :own], precision=PRECISE
    )
    grad_ada_weight = jnp.dot(
        embed_rows.T,
        every_small[:, gain_start : gain_start + columns.shape[0]],
        precision=PRECISE,
    )
    qkv_grad = jnp.stack(
        [added(sums_qkv[:, :, j * local_width : (j + 1) * local_width]) for j in range(3)]
    )
    return (
        output,
        image_grad,
        embedding_grad,
        gains[0],
        settled(pieces_first, 9),
        gains[1],
        settled(pieces_second, 9),
        grad_shift_weight,
        settled(pieces_down, 4),
        grad_ada_weight,
        qkv_grad,
        added(sums_out),
        added(sums_up),
        added(sums_proj),
    )


def solution(mesh):
    placed = (
        P("dp", "mp", None, None),
        P("dp", None),
        P("dp", None),
        P(),
        P(None, "mp", None),
        P(),
        P(None, "mp", None),
        P(None, "mp"),
        P(None, "mp", None),
        P(None, "mp"),
        P(None, None, "mp"),
        P("mp", None),
        P(None, "mp"),
        P("mp", None),
        P("dp", "mp", None, None),
    )
    return jax.shard_map(
        local,
        mesh=mesh,
        in_specs=placed,
        out_specs=(
            P("dp", "mp", None, None),
            P("dp", "mp", None, None),
            P("dp", None),
            P(("dp", "mp")),
            P(None, "dp", "mp"),
            P(("dp", "mp")),
            P(None, "dp", "mp"),
            P("dp", "mp"),
            P(None, "dp", "mp"),
            P("dp", "mp"),
            P(None, "dp", "mp"),
            P("mp", "dp"),
            P("dp", "mp"),
            P("mp", "dp"),
        ),
        check_vma=False,
    )
```

```python
from functools import partial
import math

import jax
import jax.numpy as jnp
from jax import lax
from jax.experimental import pallas as pl
from jax.experimental.pallas import tpu as pltpu
from jax.sharding import PartitionSpec as P

HEAD_DIM = 128
GROUPS = 32


GROUP_EPSILON = 1e-05
LAYER_EPSILON = 1e-06
MASKED_SCORE = -1000000000.0
PRECISE = lax.Precision.HIGHEST


def group_spread(per_channel, size):
    grouped = jnp.sum(per_channel.reshape(-1, size), axis=1)
    return jnp.repeat(grouped, size)


def group_forward(values, size):
    counted = values.shape[0] * size
    average = group_spread(jnp.sum(values, axis=0), size) / counted
    centre = values - average
    inverse = lax.rsqrt(
        group_spread(jnp.sum(centre * centre, axis=0), size) / counted + GROUP_EPSILON
    )
    return (centre * inverse, inverse)


def group_backward(incoming, normed, inverse, gain_vec, size):
    pre_act = normed * gain_vec
    sigmoid_part = jax.nn.sigmoid(pre_act)
    through = incoming * sigmoid_part * (1.0 + pre_act * (1.0 - sigmoid_part))
    counted = normed.shape[0] * size
    gain_part = jnp.sum(through * normed, axis=0)
    plain_part = jnp.sum(through, axis=0)
    first_mean = group_spread(plain_part * gain_vec, size) / counted
    second_mean = group_spread(gain_part * gain_vec, size) / counted
    outgoing = inverse * (through * gain_vec - first_mean - normed * second_mean)
    return (outgoing, gain_part)


def windows(planes, flipped):
    row_count, col_count, depth = planes.shape
    padded = jnp.pad(planes, ((1, 1), (1, 1), (0, 0)))
    pieces = []
    for tap_index in range(9):
        row_off, col_off = divmod(tap_index, 3)
        if flipped:
            row_off, col_off = (2 - row_off, 2 - col_off)
        pieces.append(padded[row_off : row_off + row_count, col_off : col_off + col_count])
    return jnp.stack(pieces, axis=2).reshape(row_count * col_count, 9, depth)


def gather_rows(rows):
    return lax.all_gather(rows, "mp", axis=0, tiled=True)


def scatter_rows(rows):
    return lax.psum_scatter(
        rows.astype(jnp.bfloat16), "mp", scatter_dimension=0, tiled=True
    ).astype(jnp.float32)


def conv_scatter(hidden, kernel, n):
    patch = windows(hidden, False)
    depth = kernel.shape[2] // n
    total = jnp.einsum("ptc,tcd->pd", patch, kernel, preferred_element_type=jnp.float32)
    parts = total.astype(jnp.bfloat16).reshape(-1, n, depth).transpose(1, 0, 2)
    return lax.psum_scatter(parts, "mp", scatter_dimension=0, tiled=False).astype(jnp.float32)


def conv_backward(grad_low, hidden, kernel, n):
    row_count, col_count, depth = hidden.shape
    gathered = lax.all_gather(grad_low, "mp", axis=1, tiled=True)
    padded = jnp.pad(gathered, ((col_count, col_count), (0, 0)))
    taps = kernel.reshape(3, 3 * depth, kernel.shape[2])
    acc = sum(
        jnp.einsum(
            "pd,td->pt",
            padded[(2 - i) * col_count : (2 - i) * col_count + row_count * col_count],
            taps[i],
            preferred_element_type=jnp.float32,
        )
        for i in range(3)
    )
    grad_kernel = jnp.einsum(
        "ptc,pd->tcd", windows(hidden, False), gathered, preferred_element_type=jnp.float32
    )
    return (join_columns(acc, col_count), grad_kernel)


def unsettled(parts, m, n):
    return parts.reshape(n, m, -1, parts.shape[-1])


def settled(pieces, taps):
    if pieces.ndim == 3:
        return pieces
    m, count, outs, _ = pieces.shape
    return (
        pieces.astype(jnp.float32)
        .reshape(m, count, outs, taps, -1)
        .transpose(3, 1, 4, 0, 2)
        .reshape(taps, -1, m * outs)
    )


def added(received):
    return jnp.sum(received.astype(jnp.float32), axis=0)


def layer_forward(stream):
    centre = stream - jnp.mean(stream, axis=1, keepdims=True)
    inverse = lax.rsqrt(jnp.mean(centre * centre, axis=1, keepdims=True) + LAYER_EPSILON)
    return (centre * inverse, inverse)


def layer_backward(incoming, normed, inverse, scale_vec):
    through = incoming * (1.0 + scale_vec)
    outgoing = inverse * (
        through
        - jnp.mean(through, axis=1, keepdims=True)
        - normed * jnp.mean(through * normed, axis=1, keepdims=True)
    )
    return (outgoing, jnp.sum(incoming * normed, axis=0), jnp.sum(incoming, axis=0))


MESH = pl.DeviceIdType.MESH
CONV_PARTS = 4
TOKEN_PARTS = 4
VMEM_BYTES = 60 * 1024 * 1024


class Line:
    def __init__(self, chips, images):
        self.chips = chips
        self.images = images
        self.dp = lax.axis_index("dp")
        self.mp = lax.axis_index("mp")
        self.z = self.mp // 2
        self.c = self.mp % 2
        self.has_up = self.z < chips - 1
        self.has_down = self.z > 0
        self.up = (self.dp, self.mp + 2)
        self.down = (self.dp, self.mp - 2)
        self.sibling = (self.dp, 2 * self.z + 1 - self.c)
        self.ready = lambda: None
        self.late = lambda: None

    def count(self, axis):
        return {"dp": self.images, "mp": 2 * self.chips, "all": 2 * self.chips * self.images}[axis]

    def index(self, axis):
        return {"dp": self.dp, "mp": self.mp, "all": self.dp * 2 * self.chips + self.mp}[axis]

    def place(self, axis, index):
        if axis == "dp":
            return (index, self.mp)
        if axis == "mp":
            return (self.dp, index)
        return (index // (2 * self.chips), index % (2 * self.chips))

    def peer(self, axis, step):
        return lax.rem(self.index(axis) + step, self.count(axis))

    def barrier(self, axes, neighbours):
        bar = pltpu.get_barrier_semaphore()
        axes = ("all",) if "all" in axes else axes
        steady = 0
        for axis in axes:
            for step in range(1, self.count(axis)):
                target = self.place(axis, self.peer(axis, step))
                pl.semaphore_signal(bar, inc=1, device_id=target, device_id_type=MESH)
            steady += self.count(axis) - 1
        cases = [(steady, None)]
        if neighbours and not ("all" in axes or "mp" in axes):
            pl.semaphore_signal(bar, inc=1, device_id=self.sibling, device_id_type=MESH)

            @pl.when(self.has_up)
            def _():
                pl.semaphore_signal(bar, inc=1, device_id=self.up, device_id_type=MESH)

            @pl.when(self.has_down)
            def _():
                pl.semaphore_signal(bar, inc=1, device_id=self.down, device_id_type=MESH)

            middle = jnp.logical_and(self.has_up, self.has_down)
            cases = [(steady + 3, middle), (steady + 2, jnp.logical_not(middle))]
        for count, when in cases:
            if when is None:
                pl.semaphore_wait(bar, count)
            else:

                @pl.when(when)
                def _():
                    pl.semaphore_wait(bar, count)


class Rider:
    def __init__(self, axis, array, cut=None, beside=False):
        self.axes = (axis,)
        self.axis = axis
        self.array = array
        self.cut = cut
        self.beside = beside

    def result(self, sizes):
        count = sizes[self.axis]
        shape = list(self.array.shape)
        if self.cut is not None:
            shape[self.cut] //= count
        self.columns = shape[-1]
        if self.beside:
            shape[-1] *= count
        else:
            shape = [count] + shape
        return jax.ShapeDtypeStruct(tuple(shape), self.array.dtype)

    def scratch(self, sizes):
        count = sizes[self.axis]
        return [pltpu.SemaphoreType.DMA((count,)), pltpu.SemaphoreType.DMA((count,))]

    def piece(self, ref, index, count):
        if self.cut is None:
            return ref
        size = self.array.shape[self.cut] // count
        where = [slice(None)] * len(self.array.shape)
        where[self.cut] = pl.ds(pl.multiple_of(index * size, size), size)
        return ref.at[tuple(where)]

    def copies(self, line, src, dst, send, recv):
        count, me = line.count(self.axis), line.index(self.axis)
        if self.beside:
            land = dst.at[:, pl.ds(pl.multiple_of(me * self.columns, self.columns), self.columns)]
        else:
            land = dst.at[me]
        made = [pltpu.make_async_copy(self.piece(src, me, count), land, send.at[0])]
        for step in range(1, count):
            peer = line.peer(self.axis, step)
            made.append(
                remote(
                    self.piece(src, peer, count),
                    land,
                    send.at[step],
                    recv.at[step],
                    line.place(self.axis, peer),
                )
            )
        return made

    def start(self, line, src, dst, send, recv):
        for copy in self.copies(line, src, dst, send, recv):
            copy.start()

    def middle(self, phase, *refs):
        pass

    def finish(self, line, src, dst, send, recv):
        for copy in self.copies(line, src, dst, send, recv):
            copy.wait()


class Settle:
    def __init__(self, array, summed, taps, placed):
        self.axes = ("dp", "mp")
        self.array = array
        self.summed = summed
        self.taps = taps
        self.placed = placed

    def result(self, sizes):
        n, m = sizes["mp"], sizes["dp"]
        self.ratio = n // m
        self.tail = tuple(self.array.shape[-2:])
        self.total = jax.ShapeDtypeStruct((n,) + self.tail, self.array.dtype)
        self.land = (m, self.ratio) + self.tail
        self.add = Rider("dp", self.array, None if self.summed else 1)
        self.outward = Rider("mp", self.total, 0)
        self.inward = Rider("dp", self.total, 0)
        if not self.placed:
            return jax.ShapeDtypeStruct(self.land, self.array.dtype)
        shape = (self.taps, self.ratio * self.tail[1] // self.taps, m * self.tail[0])
        return jax.ShapeDtypeStruct(shape, jnp.float32)

    def scratch(self, sizes):
        n, m = sizes["mp"], sizes["dp"]
        dtype = self.array.dtype
        refs = [pltpu.VMEM(self.land, dtype), pltpu.VMEM((n, 1) + self.tail, dtype)]
        if not self.summed:
            refs += [pltpu.VMEM((m, n, 1) + self.tail, dtype), pltpu.VMEM((n,) + self.tail, dtype)]
            refs += self.add.scratch(sizes)
        return refs + self.outward.scratch(sizes) + self.inward.scratch(sizes)

    def copies(self, step, line, src, dst, land, stage, *rest):
        if not self.summed:
            got, total = rest[:2]
            if step == 0:
                return self.add.copies(line, src, got, *rest[2:4])
            src, rest = total, rest[4:]
            step -= 1
        if step == 0:
            return self.outward.copies(line, src, stage, *rest[:2])
        return self.inward.copies(line, stage.at[:, 0], land, *rest[2:4])

    def start(self, *refs):
        for copy in self.copies(0, *refs):
            copy.start()

    def middle(self, phase, *refs):
        if self.summed and phase == 1:
            self.end(*refs)
            return
        for copy in self.copies(phase, *refs):
            copy.wait()
        if not self.summed and phase == 0:
            got, total = refs[5:7]

            @pl.loop(0, total.shape[0])
            def _(index):
                added_up = got[0, index, 0].astype(jnp.float32)
                for image in range(1, got.shape[0]):
                    added_up += got[image, index, 0].astype(jnp.float32)
                total[index] = added_up.astype(total.dtype)

        for copy in self.copies(phase + 1, *refs):
            copy.start()

    def finish(self, *refs):
        if not self.summed:
            self.end(*refs)

    def end(self, *refs):
        for copy in self.copies(1 if self.summed else 2, *refs):
            copy.wait()
        dst, land = refs[2:4]
        if not self.placed:
            dst[...] = land[...]
            return
        own = self.tail[1] // self.taps
        for half in range(self.ratio):
            for tap in range(self.taps):
                block = jnp.concatenate(
                    [
                        land[image, half, :, pl.ds(tap * own, own)].astype(jnp.float32)
                        for image in range(land.shape[0])
                    ],
                    axis=0,
                )
                dst[tap, pl.ds(half * own, own)] = block.T


def comm_call(kernel, inputs, out_shapes, scratch, riders, n, m, number, neighbours=True):
    chips = n // 2
    sizes = {"dp": m, "mp": n, "all": m * n}
    ride_shapes = tuple(rider.result(sizes) for rider in riders)
    ride_scratch = [rider.scratch(sizes) for rider in riders]
    any_spec = pl.BlockSpec(memory_space=pl.ANY)
    ni, nr, no = len(inputs), len(riders), len(out_shapes)
    large = [index for index in range(ni) if inputs[index].size * inputs[index].dtype.itemsize > 2**20]

    def body(*refs):
        main_in, ride_in = list(refs[:ni]), refs[ni : ni + nr]
        rest = refs[ni + nr :]
        main_out, ride_out = rest[:no], rest[no : no + nr]
        rest = rest[no + nr :]
        main_scratch, rest = rest[: len(scratch)], rest[len(scratch) :]
        line = Line(chips, m)
        loads = []
        if large:
            load_sems, rest = rest[0], rest[1:]
            for place, index in enumerate(large):
                loads.append(
                    pltpu.make_async_copy(main_in[index], rest[place], load_sems.at[place])
                )
                main_in[index] = rest[place]
            rest = rest[len(large) :]
        for load in loads:
            load.start()

        def ready():
            for load in loads:
                load.wait()

        line.ready = ready
        line.barrier(sorted(set(axis for rider in riders for axis in rider.axes)), neighbours)
        riding = []
        for rider, src, dst, needs in zip(riders, ride_in, ride_out, ride_scratch):
            riding.append((rider, (line, src, dst) + tuple(rest[: len(needs)])))
            rest = rest[len(needs) :]
        for rider, refs_in in riding:
            rider.start(*refs_in)
        phases = [0, 1]

        def late():
            phases.pop(0)
            for rider, refs_in in riding:
                rider.middle(0, *refs_in)

        line.late = late
        kernel(line, *main_in, *main_out, *main_scratch)
        for phase in phases:
            for rider, refs_in in riding:
                rider.middle(phase, *refs_in)
        for rider, refs_in in riding:
            rider.finish(*refs_in)

    return pl.pallas_call(
        body,
        out_shape=tuple(out_shapes) + ride_shapes,
        in_specs=[any_spec if index in large else whole(1)[0] for index in range(ni)]
        + [any_spec] * nr,
        out_specs=tuple(
            whole(no)
            + [whole(1)[0] if isinstance(rider, Settle) else any_spec for rider in riders]
        ),
        scratch_shapes=list(scratch)
        + ([pltpu.SemaphoreType.DMA((len(large),))] if large else [])
        + [pltpu.VMEM(inputs[index].shape, inputs[index].dtype) for index in large]
        + [ref for needs in ride_scratch for ref in needs],
        compiler_params=comm_params(number),
    )(*inputs, *[rider.array for rider in riders])


def remote(src, dst, send, recv, target):
    return pltpu.make_async_remote_copy(
        src_ref=src,
        dst_ref=dst,
        send_sem=send,
        recv_sem=recv,
        device_id=target,
        device_id_type=MESH,
    )


def gather_sems(chips):
    return [pltpu.SemaphoreType.DMA((3, 2, chips)), pltpu.SemaphoreType.DMA((3, 2, chips))]


def line_gather(line, x_ref, slot, send, recv, on_own, on_pair):
    chips = line.chips
    z, c = line.z, line.c

    def hop(stream, step, src, block, target):
        return remote(src, slot(block), send.at[stream, 0, step], recv.at[stream, 0, step], target)

    def across(way, step, src, block):
        return remote(src, slot(block), send.at[2, way, step], recv.at[2, way, step], line.sibling)

    @pl.when(line.has_up)
    def _():
        hop(0, 1, x_ref, line.mp, line.up).start()

    @pl.when(line.has_down)
    def _():
        hop(1, 1, x_ref, line.mp, line.down).start()

    across(0, 0, x_ref, line.mp).start()
    slot(line.mp)[...] = x_ref[...]
    line.ready()
    on_own()
    across(0, 0, x_ref, line.mp).wait_recv()
    on_pair(z)
    for step in range(1, chips):
        below, above = z - step, z + step
        if step == chips - 1:
            line.late()

        @pl.when(below >= 0)
        def _():
            block = 2 * below + c
            hop(0, step, slot(block), block, line.up).wait_recv()
            if step + 1 < chips:

                @pl.when(line.has_up)
                def _():
                    hop(0, step + 1, slot(block), block, line.up).start()

            across(0, step, slot(block), block).start()

        @pl.when(above < chips)
        def _():
            block = 2 * above + c
            hop(1, step, slot(block), block, line.down).wait_recv()
            if step + 1 < chips:

                @pl.when(line.has_down)
                def _():
                    hop(1, step + 1, slot(block), block, line.down).start()

            across(1, step, slot(block), block).start()

        @pl.when(below >= 0)
        def _():
            across(0, step, slot(2 * below + c), 2 * below + c).wait_recv()
            on_pair(below)

        @pl.when(above < chips)
        def _():
            across(1, step, slot(2 * above + c), 2 * above + c).wait_recv()
            on_pair(above)

    @pl.when(line.has_up)
    def _():
        hop(0, 1, x_ref, line.mp, line.up).wait_send()

    @pl.when(line.has_down)
    def _():
        hop(1, 1, x_ref, line.mp, line.down).wait_send()

    across(0, 0, x_ref, line.mp).wait_send()
    for step in range(1, chips):
        below, above = z - step, z + step

        @pl.when(below >= 0)
        def _():
            block = 2 * below + c
            if step + 1 < chips:

                @pl.when(line.has_up)
                def _():
                    hop(0, step + 1, slot(block), block, line.up).wait_send()

            across(0, step, slot(block), block).wait_send()

        @pl.when(above < chips)
        def _():
            block = 2 * above + c
            if step + 1 < chips:

                @pl.when(line.has_down)
                def _():
                    hop(1, step + 1, slot(block), block, line.down).wait_send()

            across(1, step, slot(block), block).wait_send()


def scatter_scratch(chips, rows, cols, parts):
    block = (chips, rows, cols)
    return [
        pltpu.VMEM(block, jnp.float32),
        pltpu.VMEM(block, jnp.bfloat16),
        pltpu.VMEM(block, jnp.bfloat16),
        pltpu.VMEM((2,) + block, jnp.bfloat16),
        pltpu.SemaphoreType.DMA((2, 3, chips, parts)),
    ]


def line_scatter(line, scratch, parts, produce, finish, tile, side=()):
    chips = line.chips
    z = line.z
    kept, out_ref, in_ref, moving, sems = scratch
    count = kept.shape[1] // parts
    line.ready()

    def span(part):
        return pl.ds(part * count, count)

    def across(chip, part):
        return remote(
            out_ref.at[chip, span(part)],
            in_ref.at[chip, span(part)],
            sems.at[0, 0, chip, part],
            sems.at[1, 0, chip, part],
            line.sibling,
        )

    def hop(way, chip, part):
        target = line.up if way == 0 else line.down
        ref = moving.at[way, chip, span(part)]
        return remote(
            ref, ref, sems.at[0, 1 + way, chip, part], sems.at[1, 1 + way, chip, part], target
        )

    items = []
    for step in range(chips - 1):
        for part in range(parts):
            items.append((0, chips - 1 - step + z, part, step >= z))
            items.append((1, step - (chips - 1 - z), part, step >= chips - 1 - z))
    for part in range(parts):
        items.append((2, z, part, None))

    def run(active, body):
        if active is None:
            body()
        else:
            pl.when(active)(body)

    def start(item):
        way, chip, part, active = item

        def body():
            produce(chip, part, count, kept.at[chip], out_ref.at[chip])
            across(chip, part).start()

        run(active, body)

    def tiles(part, body):
        @pl.loop(0, count // tile)
        def _(index):
            body(pl.ds(pl.multiple_of(part * count + index * tile, tile), tile))

    def close(item):
        way, chip, part, active = item

        def body():
            across(chip, part).wait_recv()
            if way < 2:
                later = line.has_down if way == 0 else line.has_up

                @pl.when(later)
                def _():
                    hop(way, chip, part).wait_recv()

                    def add(rows):
                        moving[way, chip, rows] = (
                            kept[chip, rows]
                            + in_ref[chip, rows].astype(jnp.float32)
                            + moving[way, chip, rows].astype(jnp.float32)
                        ).astype(jnp.bfloat16)

                    tiles(part, add)

                @pl.when(jnp.logical_not(later))
                def _():
                    def add(rows):
                        moving[way, chip, rows] = (
                            kept[chip, rows] + in_ref[chip, rows].astype(jnp.float32)
                        ).astype(jnp.bfloat16)

                    tiles(part, add)

                hop(way, chip, part).start()
            else:

                def total(rows):
                    return kept[chip, rows] + in_ref[chip, rows].astype(jnp.float32)

                def from_side(side, rows):
                    return moving[side, chip, rows].astype(jnp.float32)

                both = jnp.logical_and(line.has_down, line.has_up)

                @pl.when(both)
                def _():
                    hop(0, chip, part).wait_recv()
                    hop(1, chip, part).wait_recv()
                    tiles(
                        part,
                        lambda rows: finish(
                            part, rows, total(rows) + from_side(0, rows) + from_side(1, rows)
                        ),
                    )

                for side, present in ((0, line.has_down), (1, line.has_up)):

                    @pl.when(jnp.logical_and(present, jnp.logical_not(both)))
                    def _():
                        hop(side, chip, part).wait_recv()
                        tiles(
                            part,
                            lambda rows: finish(part, rows, total(rows) + from_side(side, rows)),
                        )

        run(active, body)

    lag = 2
    side = list(side)
    for index, item in enumerate(items):
        start(item)
        if index >= lag:
            close(items[index - lag])
            if index % 2 == 0 and side:
                side.pop(0)()
    for step in side:
        step()
    for item in items[-lag:]:
        close(item)
    for way, chip, part, active in items:

        def body():
            across(chip, part).wait_send()
            if way < 2:
                hop(way, chip, part).wait_send()

        run(active, body)


def whole(count):
    return [pl.BlockSpec(memory_space=pltpu.VMEM)] * count


def comm_params(number):
    return pltpu.CompilerParams(
        collective_id=number, has_side_effects=True, vmem_limit_bytes=VMEM_BYTES
    )


def pick(c, low, high):
    return jnp.where(c == 0, low, high), jnp.where(c == 0, high, low)


def conv_scatter_kernel(breadth, line, x_ref, w_ref, o_ref, *scratch):
    pixels, own = o_ref.shape
    tile = 512

    def produce(chip, part, count, mine, other):
        columns = pl.ds(pl.multiple_of(chip * 2 * own, 2 * own), 2 * own)

        @pl.loop(0, count // tile)
        def _(index):
            base = pl.multiple_of(part * count + index * tile, tile)
            total = jnp.zeros((tile, 2 * own), jnp.float32)
            for i in range(3):
                total += jnp.dot(
                    x_ref[pl.ds(base + i * breadth, tile)],
                    w_ref[i, :, columns],
                    preferred_element_type=jnp.float32,
                )
            first, second = pick(line.c, total[:, :own], total[:, own:])
            mine[pl.ds(base, tile)] = first
            other[pl.ds(base, tile)] = second.astype(jnp.bfloat16)

    def finish(part, rows, total):
        o_ref[rows] = total

    line_scatter(line, scratch, CONV_PARTS, produce, finish, tile)


def side_by_side(hidden):
    rows, cols, depth = hidden.shape
    padded = jnp.pad(hidden, ((1, 1), (1, 1), (0, 0)))
    return jnp.concatenate([padded[:, j : j + cols] for j in range(3)], axis=2).reshape(
        (rows + 2) * cols, 3 * depth
    )


def conv_scatter_fused(spread, kernel, cols, n, m, number, riders=()):
    own = kernel.shape[2] // n
    depth = kernel.shape[1]
    pixels = spread.shape[0] - 2 * cols
    return comm_call(
        partial(conv_scatter_kernel, cols),
        (spread, kernel.reshape(3, 3 * depth, kernel.shape[2])),
        (jax.ShapeDtypeStruct((pixels, own), jnp.float32),),
        scatter_scratch(n // 2, pixels, own, CONV_PARTS),
        riders,
        n,
        m,
        number,
    )


def conv_back_kernel(breadth, size, extra, line, g_ref, w_ref, x_ref, n_ref, v_ref, *refs):
    refs = list(refs)
    more_ref = refs.pop(0) if extra else None
    low_ref, wg_ref, stat_ref, acc_ref, held, sums, send, recv = refs
    chips = line.chips
    pixels, own = g_ref.shape
    wide = w_ref.shape[1]
    tile, long = 512, 1024
    zero = jnp.zeros((breadth, own), jnp.bfloat16)
    for block in range(2 * chips):
        held[block, pl.ds(0, breadth)] = zero
        held[block, pl.ds(breadth + pixels, breadth)] = zero

    def slot(block):
        return held.at[block, pl.ds(breadth, pixels)]

    def beside(base, count, chip):
        rows = pl.ds(base, count)
        return [held[2 * chip, rows], held[2 * chip + 1, rows]]

    def on_own():
        @pl.loop(0, pixels // tile)
        def _(index):
            acc_ref[pl.ds(pl.multiple_of(index * tile, tile), tile)] = jnp.zeros(
                (tile, wide), jnp.float32
            )

    def on_pair(chip):
        columns = pl.ds(pl.multiple_of(chip * 2 * own, 2 * own), 2 * own)

        @pl.loop(0, pixels // tile)
        def _(index):
            base = pl.multiple_of(index * tile, tile)
            shifted = []
            for i in range(3):
                shifted += beside(base + (2 - i) * breadth, tile, chip)
            acc_ref[pl.ds(base, tile)] += product(
                jnp.concatenate(shifted, axis=1),
                jnp.concatenate([w_ref[i, :, columns] for i in range(3)], axis=1),
                True,
            )

        sums[...] = jnp.zeros_like(sums)

        @pl.loop(0, pixels // long)
        def _(index):
            base = pl.multiple_of(index * long, long)
            sums[...] += lax.dot_general(
                jnp.concatenate(beside(base + breadth, long, chip), axis=1),
                jnp.concatenate(
                    [x_ref[pl.ds(base + i * breadth, long)] for i in range(3)], axis=1
                ),
                (((0,), (0,)), ((), ())),
                preferred_element_type=jnp.float32,
            )

        wg_ref[chip] = sums[...].astype(jnp.bfloat16)

    line_gather(line, g_ref, slot, send, recv, on_own, on_pair)

    gain, inverse = v_ref[0:1], v_ref[1:2]
    stat_ref[...] = jnp.zeros_like(stat_ref)
    column = lax.broadcasted_iota(jnp.int32, (tile, own), 0) % breadth

    @pl.loop(0, pixels // tile)
    def _(index):
        rows = pl.ds(pl.multiple_of(index * tile, tile), tile)
        left = jnp.where(
            column == breadth - 1, 0.0, pltpu.roll(acc_ref[rows, 0:own], tile - 1, 0)
        )
        right = jnp.where(column == 0, 0.0, pltpu.roll(acc_ref[rows, 2 * own : wide], 1, 0))
        incoming = left + acc_ref[rows, own : 2 * own] + right
        normed = n_ref[rows]
        pre_act = normed * gain
        sigmoid_part = 1.0 / (1.0 + jnp.exp(-pre_act))
        through = incoming * sigmoid_part * (1.0 + pre_act * (1.0 - sigmoid_part))
        acc_ref[rows, 0:own] = through
        stat_ref[0:1] += jnp.sum(through * normed, axis=0, keepdims=True)
        stat_ref[1:2] += jnp.sum(through, axis=0, keepdims=True)

    groups = [lax.broadcasted_iota(jnp.int32, (own, own), axis) // size for axis in range(2)]
    spread = jnp.where(groups[0] == groups[1], 1.0 / (pixels * size), 0.0)
    means = jnp.dot(stat_ref[...] * gain, spread, precision=PRECISE)
    second_mean, first_mean = means[0:1], means[1:2]

    @pl.loop(0, pixels // tile)
    def _(index):
        rows = pl.ds(pl.multiple_of(index * tile, tile), tile)
        outgoing = inverse * (
            acc_ref[rows, 0:own] * gain - first_mean - n_ref[rows] * second_mean
        )
        stat_ref[2:3] += jnp.sum(outgoing, axis=0, keepdims=True)
        if extra:
            outgoing = outgoing + more_ref[rows]
        low_ref[rows] = outgoing.astype(jnp.bfloat16)


def conv_back_fused(
    grad_low, spread, kernel, normed, inverse, gain, size, cols, n, m, number, riders, more=()
):
    pixels, own = grad_low.shape
    depth = kernel.shape[1]
    chips = n // 2
    vectors = jnp.concatenate([gain[None], inverse[None], jnp.zeros((6, own), jnp.float32)])
    return comm_call(
        partial(conv_back_kernel, cols, size, len(more) > 0),
        (grad_low, kernel.reshape(3, 3 * depth, kernel.shape[2]), spread, normed, vectors)
        + tuple(more),
        (
            jax.ShapeDtypeStruct((pixels, depth), jnp.bfloat16),
            jax.ShapeDtypeStruct((chips, 2 * own, 9 * depth), jnp.bfloat16),
            jax.ShapeDtypeStruct((8, own), jnp.float32),
        ),
        [
            pltpu.VMEM((pixels, 3 * depth), jnp.float32),
            pltpu.VMEM((n, pixels + 2 * cols, own), jnp.bfloat16),
            pltpu.VMEM((2 * own, 9 * depth), jnp.float32),
        ]
        + gather_sems(chips),
        riders,
        n,
        m,
        number,
    )


def join_columns(acc, cols):
    pixels, wide = acc.shape
    depth = wide // 3
    planes = acc.reshape(-1, cols, wide)
    none = jnp.zeros_like(planes[:, :1, :depth])
    left = jnp.concatenate([planes[:, 1:, :depth], none], axis=1)
    right = jnp.concatenate([none, planes[:, :-1, 2 * depth :]], axis=1)
    return (left + planes[:, :, depth : 2 * depth] + right).reshape(pixels, depth)


def product(x, w, turned):
    return lax.dot_general(
        x, w, (((1,), (1 if turned else 0,)), ((), ())), preferred_element_type=jnp.float32
    )


def outer_steps(grad, left, right, cut):
    def step(start):
        grad[pl.ds(start, cut)] = lax.dot_general(
            left[:, pl.ds(start, cut)],
            right[...],
            (((0,), (0,)), ((), ())),
            preferred_element_type=jnp.float32,
        ).astype(grad.dtype)

    return [partial(step, start) for start in range(0, left.shape[1], cut)]


def tokens_scatter_kernel(turned, beside, line, x_ref, w_ref, *refs):
    side = ()
    if beside:
        left, right, o_ref, grad, *scratch = refs
        side = outer_steps(grad, left, right, 128)
    else:
        o_ref, *scratch = refs
    tokens, width = o_ref.shape
    cut = width // TOKEN_PARTS
    depth = x_ref.shape[1] // w_ref.shape[0]

    def produce(chip, part, count, mine, other):
        rows = pl.ds(pl.multiple_of(chip * 2 * tokens, 2 * tokens), 2 * tokens)
        columns = pl.ds(part * cut, cut)
        total = None
        for j in range(w_ref.shape[0]):
            w = w_ref[j, columns] if turned else w_ref[j, :, columns]
            term = product(x_ref[rows, pl.ds(j * depth, depth)], w, turned)
            total = term if total is None else total + term
        first, second = pick(line.c, total[:tokens], total[tokens:])
        mine[pl.ds(part * count, count)] = first
        other[pl.ds(part * count, count)] = second.astype(jnp.bfloat16)

    def finish(part, rows, total):
        o_ref[:, pl.ds(part * cut, cut)] = total

    line_scatter(line, scratch, TOKEN_PARTS, produce, finish, tokens, side)


def outer_shapes(outer):
    if not outer:
        return ()
    return (jax.ShapeDtypeStruct((outer[0].shape[1], outer[1].shape[1]), jnp.bfloat16),)


def tokens_scatter(x, w, turned, n, m, number, riders=(), outer=()):
    tokens = x.shape[0] // n
    width = w.shape[1] if turned else w.shape[2]
    return comm_call(
        partial(tokens_scatter_kernel, turned, len(outer) > 0),
        (x, w) + tuple(outer),
        (jax.ShapeDtypeStruct((tokens, width), jnp.float32),) + outer_shapes(outer),
        scatter_scratch(n // 2, TOKEN_PARTS * tokens, width // TOKEN_PARTS, TOKEN_PARTS),
        riders,
        n,
        m,
        number,
    )


def add_outer(total, left, right, rows):
    cut = min(left.shape[1], 512)
    for start in range(0, left.shape[1], cut):
        total[pl.ds(start, cut)] += lax.dot_general(
            left[rows, pl.ds(start, cut)],
            right[rows],
            (((0,), (0,)), ((), ())),
            preferred_element_type=jnp.float32,
        )


def tokens_gather_kernel(
    turned, shape_out, outs, keep, side, beside, cols, chained, line, x_ref, w_ref, *refs
):
    refs = list(refs)
    chain_w = refs.pop(0) if chained else None
    left = refs.pop(0) if side else None
    outer = (refs.pop(0), refs.pop(0)) if beside else None
    held = refs.pop(0) if keep else None
    results = [refs.pop(0) for _ in range(outs)]
    grad = refs.pop(0) if side else None
    outer_grad = refs.pop(0) if beside else None
    chain_out = refs.pop(0) if chained else None
    total = refs.pop(0) if side else None
    if not keep:
        held = refs.pop(0)
    send, recv = refs
    tokens = x_ref.shape[0]
    across = w_ref.shape[1 if turned else 2]
    cut = min(across, 512)

    def slot(block):
        return held.at[pl.ds(pl.multiple_of(block * tokens, tokens), tokens)]

    def store_pixels(ref, chip, value):
        depth = value.shape[1] // 4
        base = chip * 8 * tokens
        for row in range(4 * tokens // cols):
            for tap in range(4):
                start = base + (2 * row + tap // 2) * cols + tap % 2
                ref[pl.Slice(start, cols // 2, 2)] = value[
                    row * (cols // 2) : (row + 1) * (cols // 2), tap * depth : (tap + 1) * depth
                ]

    def on_pair(chip):
        rows = pl.ds(pl.multiple_of(chip * 2 * tokens, 2 * tokens), 2 * tokens)
        for j in range(w_ref.shape[0]):
            for start in range(0, across, cut):
                w = w_ref[j, pl.ds(start, cut)] if turned else w_ref[j, :, pl.ds(start, cut)]
                values = shape_out(product(held[rows], w, turned))
                for ref, value in zip(results, values):
                    if cols:
                        store_pixels(ref, chip, value)
                    else:
                        ref[rows, pl.ds(j * across + start, cut)] = value.astype(ref.dtype)
        if chained:
            for start in range(0, chain_w.shape[1], 512):
                columns = pl.ds(start, 512)
                chain_out[rows, columns] = product(
                    results[-1][rows], chain_w[:, columns], False
                ).astype(jnp.bfloat16)
        if side:
            add_outer(total, held, left, rows)

    def on_own():
        if side:
            total[...] = jnp.zeros_like(total)
        if beside:
            for step in outer_steps(outer_grad, *outer, 256):
                step()

    line_gather(line, x_ref, slot, send, recv, on_own, on_pair)
    if side:
        grad[...] = total[...].astype(grad.dtype)


def tokens_gather(
    x,
    w,
    turned,
    kinds,
    shape_out,
    n,
    m,
    number,
    riders=(),
    left=None,
    outer=(),
    cols=0,
    chain=(),
    keep=True,
):
    tokens, width = x.shape
    across = w.shape[0] * w.shape[1 if turned else 2]
    side = left is not None
    grads = ((width, left.shape[1]),) if side else ()
    shape = (tokens * n * 4, across // 4) if cols else (tokens * n, across)
    return comm_call(
        partial(
            tokens_gather_kernel,
            turned,
            shape_out,
            len(kinds),
            keep,
            side,
            len(outer) > 0,
            cols,
            len(chain) > 0,
        ),
        (x, w) + tuple(chain) + ((left,) if side else ()) + tuple(outer),
        tuple(jax.ShapeDtypeStruct((tokens * n, width), x.dtype) for _ in range(int(keep)))
        + tuple(jax.ShapeDtypeStruct(shape, kind) for kind in kinds)
        + tuple(jax.ShapeDtypeStruct(grad, jnp.bfloat16) for grad in grads)
        + outer_shapes(outer)
        + tuple(jax.ShapeDtypeStruct((tokens * n, w2.shape[1]), jnp.bfloat16) for w2 in chain),
        [pltpu.VMEM(grad, jnp.float32) for grad in grads]
        + [pltpu.VMEM((tokens * n, width), x.dtype) for _ in range(int(not keep))]
        + gather_sems(n // 2),
        riders,
        n,
        m,
        number,
    )


def exchange(riders, n, m, number):
    return comm_call(lambda line: None, (), (), [], riders, n, m, number, neighbours=False)


def tiled_up(vector):
    count = -(-vector.shape[0] // 1024) * 1024
    return jnp.pad(vector.astype(jnp.float32), (0, count - vector.shape[0])).reshape(-1, 128)


def attend_scatter_kernel(line, x_ref, valid_ref, w_ref, o_ref, mixed_ref, *scratch):
    tokens, width = o_ref.shape
    wide = mixed_ref.shape[1]
    cut = width // TOKEN_PARTS
    scale = 1.0 / math.sqrt(HEAD_DIM)

    def attend(rows):
        for head in range(wide // HEAD_DIM):
            where = [pl.ds(j * wide + head * HEAD_DIM, HEAD_DIM) for j in range(3)]
            scores = product(x_ref[rows, where[0]], x_ref[:, where[1]], True) * scale
            scores = jnp.where(valid_ref[0:1] > 0.5, scores, MASKED_SCORE)
            exponent = jnp.exp(scores - jnp.max(scores, axis=1, keepdims=True))
            inverse = 1.0 / jnp.sum(exponent, axis=1, keepdims=True)
            mixed_ref[rows, pl.ds(head * HEAD_DIM, HEAD_DIM)] = product(
                (exponent * inverse).astype(jnp.bfloat16), x_ref[:, where[2]], False
            ).astype(jnp.bfloat16)

    def produce(chip, part, count, mine, other):
        rows = pl.ds(pl.multiple_of(chip * 2 * tokens, 2 * tokens), 2 * tokens)
        if part == 0:
            attend(rows)
        total = product(mixed_ref[rows], w_ref[:, pl.ds(part * cut, cut)], False)
        first, second = pick(line.c, total[:tokens], total[tokens:])
        mine[pl.ds(part * count, count)] = first
        other[pl.ds(part * count, count)] = second.astype(jnp.bfloat16)

    def finish(part, rows, total):
        o_ref[:, pl.ds(part * cut, cut)] = total

    line_scatter(line, scratch, TOKEN_PARTS, produce, finish, tokens)


def attend_scatter(qkv_rows, valid, out_weight, n, m, number):
    total = qkv_rows.shape[0]
    tokens = total // n
    width = out_weight.shape[1]
    return comm_call(
        attend_scatter_kernel,
        (qkv_rows, jnp.broadcast_to(valid[None], (8, total)), out_weight),
        (
            jax.ShapeDtypeStruct((tokens, width), jnp.float32),
            jax.ShapeDtypeStruct((total, out_weight.shape[0]), jnp.bfloat16),
        ),
        scatter_scratch(n // 2, TOKEN_PARTS * tokens, width // TOKEN_PARTS, TOKEN_PARTS),
        (),
        n,
        m,
        number,
    )


def attend_gather_kernel(
    line,
    g_ref,
    w_ref,
    x_ref,
    kt_ref,
    valid_ref,
    mixed_ref,
    left,
    right,
    grad_ref,
    out_ref,
    outer_grad,
    held,
    keys_sum,
    values_sum,
    out_sum,
    send,
    recv,
):
    tokens = g_ref.shape[0]
    wide = w_ref.shape[0]
    heads = wide // HEAD_DIM
    scale = 1.0 / math.sqrt(HEAD_DIM)

    def slot(block):
        return held.at[pl.ds(pl.multiple_of(block * tokens, tokens), tokens)]

    def on_own():
        keys_sum[...] = jnp.zeros_like(keys_sum)
        values_sum[...] = jnp.zeros_like(values_sum)
        out_sum[...] = jnp.zeros_like(out_sum)
        for step in outer_steps(outer_grad, left, right, 256):
            step()

    def on_pair(chip):
        rows = pl.ds(pl.multiple_of(chip * 2 * tokens, 2 * tokens), 2 * tokens)
        for head in range(heads):
            place = pl.ds(head * HEAD_DIM, HEAD_DIM)
            where = [pl.ds(j * wide + head * HEAD_DIM, HEAD_DIM) for j in range(3)]
            grad = product(held[rows], w_ref[place], True).astype(jnp.bfloat16)
            query = x_ref[rows, where[0]]
            scores = product(x_ref[:, where[1]], query, True) * scale
            scores = jnp.where(valid_ref[:, 0:1] > 0.5, scores, MASKED_SCORE)
            exponent = jnp.exp(scores - jnp.max(scores, axis=0, keepdims=True))
            probs = exponent * (1.0 / jnp.sum(exponent, axis=0, keepdims=True))
            values_sum[:, place] += product(probs.astype(jnp.bfloat16), grad, False)
            grad_probs = product(x_ref[:, where[2]], grad, True)
            inner = jnp.sum(probs * grad_probs, axis=0, keepdims=True)
            grad_scores = (probs * (grad_probs - inner) * scale).astype(jnp.bfloat16)
            keys_sum[:, place] += product(grad_scores, query, False)
            grad_ref[rows, where[0]] = product(kt_ref[place], grad_scores, False).T.astype(
                jnp.bfloat16
            )
        add_outer(out_sum, mixed_ref, held, rows)

    line_gather(line, g_ref, slot, send, recv, on_own, on_pair)
    grad_ref[:, pl.ds(wide, wide)] = keys_sum[...].astype(jnp.bfloat16)
    grad_ref[:, pl.ds(2 * wide, wide)] = values_sum[...].astype(jnp.bfloat16)
    out_ref[...] = out_sum[...].astype(jnp.bfloat16)


def attend_gather(grad_mid, out_weight, qkv_rows, valid, mixed_low, outer, n, m, number, riders):
    tokens, width = grad_mid.shape
    total = tokens * n
    wide = out_weight.shape[0]
    return comm_call(
        attend_gather_kernel,
        (
            grad_mid,
            out_weight,
            qkv_rows,
            qkv_rows[:, wide : 2 * wide].T,
            jnp.broadcast_to(valid[:, None], (total, 128)),
            mixed_low,
        )
        + tuple(outer),
        (
            jax.ShapeDtypeStruct((total, 3 * wide), jnp.bfloat16),
            jax.ShapeDtypeStruct((wide, width), jnp.bfloat16),
        )
        + outer_shapes(outer),
        [
            pltpu.VMEM((total, width), jnp.bfloat16),
            pltpu.VMEM((total, wide), jnp.float32),
            pltpu.VMEM((total, wide), jnp.float32),
            pltpu.VMEM((wide, width), jnp.float32),
        ]
        + gather_sems(n // 2),
        riders,
        n,
        m,
        number,
    )


def gelu_both(value):
    factor = math.sqrt(2.0 / math.pi)
    square = value * value
    bent = jnp.tanh(factor * value * (1.0 + 0.044715 * square))
    half = 0.5 * (1.0 + bent)
    slope = half + 0.5 * value * (1.0 - bent * bent) * factor * (1.0 + 3 * 0.044715 * square)
    return slope, value * half


def local(
    image,
    embedding,
    extents,
    gain_first,
    conv_first,
    gain_second,
    conv_second,
    shift_weight,
    down_weight,
    ada_weight,
    qkv_weight,
    out_weight,
    up_weight,
    proj_weight,
    cotangent,
):
    strip_rows, canvas_cols, channel_count = (image.shape[1], image.shape[2], image.shape[3])
    width_all = out_weight.shape[1]
    n = lax.axis_size("mp")
    m = lax.axis_size("dp")
    me_mp = lax.axis_index("mp")
    me_dp = lax.axis_index("dp")
    rows_all = strip_rows * n
    pixel_total = rows_all * canvas_cols
    own = channel_count // n
    size = channel_count // GROUPS
    token_rows = strip_rows // 2
    token_cols = canvas_cols // 2
    local_tokens = token_rows * token_cols
    token_total = local_tokens * n
    local_width = out_weight.shape[0]

    fused = own % 128 == 0 and n == 2 * m
    shift_vector = jnp.dot(embedding, shift_weight, preferred_element_type=jnp.float32)[0]
    columns = jnp.dot(embedding, ada_weight, preferred_element_type=jnp.float32)[0]
    riders = (Rider("mp", tiled_up(columns)),)
    if fused:
        modulation, pixels_low = exchange(
            riders + (Rider("mp", image[0].reshape(-1, channel_count), 1),), n, m, 12
        )
    else:
        (modulation,) = exchange(riders, n, m, 12)
        pixels_low = lax.all_to_all(image[0], "mp", 2, 0, tiled=True)
    modulation = modulation.reshape(n, -1)[:, : columns.shape[0]].reshape(-1)
    scale_attend = modulation[:width_all]
    shift_attend = modulation[width_all : 2 * width_all]
    scale_mlp = modulation[2 * width_all : 3 * width_all]
    shift_mlp = modulation[3 * width_all :]
    own_first = lax.dynamic_slice_in_dim(gain_first, me_mp * own, own)
    own_second = lax.dynamic_slice_in_dim(gain_second, me_mp * own, own)

    pixels = pixels_low.astype(jnp.float32).reshape(pixel_total, own)
    normed_first, inverse_first = group_forward(pixels, size)
    hidden_first = (
        jax.nn.silu(normed_first * own_first)
        .astype(jnp.bfloat16)
        .reshape(rows_all, canvas_cols, own)
    )
    spread_first = side_by_side(hidden_first)
    if fused:
        (conv_output,) = conv_scatter_fused(spread_first, conv_first, canvas_cols, n, m, 0)
    else:
        conv_output = conv_scatter(hidden_first, conv_first, n)
    conv_output = conv_output + shift_vector
    normed_second, inverse_second = group_forward(conv_output, size)
    hidden_second = (
        jax.nn.silu(normed_second * own_second)
        .astype(jnp.bfloat16)
        .reshape(rows_all, canvas_cols, own)
    )
    spread_second = side_by_side(hidden_second)
    if fused:
        (conv_again,) = conv_scatter_fused(spread_second, conv_second, canvas_cols, n, m, 1)
    else:
        conv_again = conv_scatter(hidden_second, conv_second, n)
    residual = pixels + conv_again
    down_patch = (
        residual.astype(jnp.bfloat16)
        .reshape(rows_all // 2, 2, token_cols, 2, own)
        .transpose(0, 2, 1, 3, 4)
        .reshape(token_total, 4 * own)
    )
    down_matrix = down_weight.reshape(4 * own, width_all)
    (stream,) = tokens_scatter(down_patch, down_matrix[None], False, n, m, 2)
    normed_attend, inverse_attend = layer_forward(stream)
    input_attend = (normed_attend * (1.0 + scale_attend) + shift_attend).astype(jnp.bfloat16)
    all_attend, qkv_rows = tokens_gather(
        input_attend, qkv_weight, False, (jnp.bfloat16,), lambda value: (value,), n, m, 3
    )
    token_index = jnp.arange(token_total, dtype=jnp.int32)
    key_valid = (token_index // token_cols < extents[0, 0]) & (
        token_index % token_cols < extents[0, 1]
    )
    valid = key_valid.astype(jnp.float32)
    attended, mixed_low = attend_scatter(qkv_rows, valid, out_weight, n, m, 4)
    stream_mid = stream + attended
    normed_mlp, inverse_mlp = layer_forward(stream_mid)
    input_mlp = (normed_mlp * (1.0 + scale_mlp) + shift_mlp).astype(jnp.bfloat16)
    all_mlp, slope, activated, projected = tokens_gather(
        input_mlp,
        up_weight[None],
        False,
        (jnp.bfloat16, jnp.bfloat16),
        gelu_both,
        n,
        m,
        5,
        chain=(proj_weight,),
    )
    final_stream = stream_mid + scatter_rows(projected)
    output = final_stream.astype(jnp.bfloat16).reshape(1, token_rows, token_cols, width_all)

    grad_final_low = cotangent[0].reshape(local_tokens, width_all)
    grad_final = grad_final_low.astype(jnp.float32)
    all_final = gather_rows(lax.optimization_barrier((grad_final_low, qkv_rows))[0])
    grad_act = jnp.einsum("le,fe->lf", all_final, proj_weight, preferred_element_type=jnp.float32)
    grad_upper = (grad_act * slope.astype(jnp.float32)).astype(jnp.bfloat16)
    grad_normed_mlp, grad_proj = tokens_scatter(
        grad_upper, up_weight[None], True, n, m, 6, (), (activated, all_final)
    )
    grad_mid_norm, grad_scale_mlp, grad_shift_mlp = layer_backward(
        grad_normed_mlp, normed_mlp, inverse_mlp, scale_mlp
    )
    grad_mid = grad_final + grad_mid_norm
    grad_qkv, grad_out, grad_up, sums_proj = attend_gather(
        grad_mid.astype(jnp.bfloat16),
        out_weight,
        qkv_rows,
        valid,
        mixed_low,
        (all_mlp, grad_upper),
        n,
        m,
        7,
        (Rider("dp", grad_proj, 1),),
    )
    (grad_normed_attend,) = tokens_scatter(grad_qkv, qkv_weight, True, n, m, 8)
    grad_stream_norm, grad_scale_attend, grad_shift_attend = layer_backward(
        grad_normed_attend, normed_attend, inverse_attend, scale_attend
    )
    grad_stream = grad_mid + grad_stream_norm
    grad_modulation = jnp.concatenate(
        [
            tiled_up(piece)
            for piece in jnp.concatenate(
                [grad_scale_attend, grad_shift_attend, grad_scale_mlp, grad_shift_mlp]
            ).reshape(n, -1)
        ]
    )
    grad_residual, grad_down, grad_qkv_weight, sums_up, ada_columns = tokens_gather(
        grad_stream.astype(jnp.bfloat16),
        down_matrix[None],
        True,
        (jnp.float32,),
        lambda value: (value,),
        n,
        m,
        9,
        (
            Rider("dp", grad_up, 0),
            Rider("mp", grad_modulation, 0),
        ),
        down_patch,
        (all_attend, grad_qkv),
        canvas_cols if fused else 0,
        keep=False,
    )
    ada_columns = added(ada_columns).reshape(-1)[: columns.shape[0]]
    if not fused:
        grad_residual = (
            grad_residual.reshape(rows_all // 2, token_cols, 2, 2, own)
            .transpose(0, 2, 1, 3, 4)
            .reshape(pixel_total, own)
        )
    def back(grad_low, hidden, spread, kernel, normed, inverse, gain, number, riders, more=()):
        if fused:
            low, parts, sums, *ridden = conv_back_fused(
                grad_low,
                spread,
                kernel,
                normed,
                inverse,
                gain,
                size,
                canvas_cols,
                n,
                m,
                number,
                riders,
                more,
            )
            return low, parts, sums[0], sums[2], ridden
        grad_hidden, grad_kernel = conv_backward(grad_low, hidden, kernel, n)
        outgoing, gain_part = group_backward(grad_hidden, normed, inverse, gain, size)
        parts = grad_kernel.astype(jnp.bfloat16).reshape(9 * own, -1).T
        low = sum(more, outgoing).astype(jnp.bfloat16)
        return low, parts, gain_part, jnp.sum(outgoing, axis=0), exchange(riders, n, m, number)

    grad_conv_low, parts_second, grad_gain_second, grad_shift, rode_second = back(
        grad_residual.astype(jnp.bfloat16),
        hidden_second,
        spread_second,
        conv_second,
        normed_second,
        inverse_second,
        own_second,
        10,
        (
            Rider("dp", unsettled(grad_down, m, n), 1),
            Rider("dp", grad_qkv_weight, 0),
            Rider("dp", grad_out, 1),
            Rider("dp", jnp.concatenate([tiled_up(embedding[0]), tiled_up(ada_columns)])),
        ),
    )
    sums_down, sums_qkv, sums_out, every_small = rode_second
    image_turned, parts_first, grad_gain_first, _, rode_first = back(
        grad_conv_low,
        hidden_first,
        spread_first,
        conv_first,
        normed_first,
        inverse_first,
        own_first,
        11,
        (
            Rider("dp", unsettled(parts_second, m, n), 1),
            Rider("dp", tiled_up(grad_shift)),
            Settle(added(sums_down)[:, 0].astype(jnp.bfloat16), True, 4, fused),
        ),
        (grad_residual,),
    )
    sums_second, every_shift, pieces_down = rode_first
    embed_term = jnp.dot(
        grad_shift[None], shift_weight.astype(jnp.float32).T, precision=PRECISE
    ) + jnp.dot(ada_columns[None], ada_weight.astype(jnp.float32).T, precision=PRECISE)
    small = jnp.concatenate(
        [tiled_up(embed_term[0]), tiled_up(jnp.concatenate([grad_gain_first, grad_gain_second]))]
    )
    riders = (
        Settle(unsettled(parts_first, m, n), False, 9, fused),
        Rider("all", small),
        Settle(added(sums_second)[:, 0].astype(jnp.bfloat16), True, 9, fused),
    )
    if fused:
        pieces_first, small, pieces_second, image_turned = exchange(
            riders + (Rider("mp", image_turned, 0, True),), n, m, 13
        )
        image_grad = image_turned.reshape(image.shape)
    else:
        pieces_first, small, pieces_second = exchange(riders, n, m, 13)
        image_grad = lax.all_to_all(
            image_turned.reshape(rows_all, canvas_cols, own), "mp", 0, 2, tiled=True
        )[None]

    small = small.reshape(m, n, -1)
    embed_count = embedding.shape[1]
    embedding_grad = jnp.sum(
        lax.dynamic_index_in_dim(small, me_dp, axis=0, keepdims=False)[:, :embed_count], axis=0
    )[None]
    gain_start = -(-embed_count // 1024) * 1024
    gains = jnp.sum(small[:, :, gain_start : gain_start + 2 * own], axis=0)
    gains = gains.reshape(n, 2, own).transpose(1, 0, 2).reshape(2, -1)
    piece = channel_count // (m * n)
    gains = lax.dynamic_slice_in_dim(gains, (me_dp * n + me_mp) * piece, piece, axis=1)
    every_small = every_small.reshape(m, -1)
    embed_rows = lax.dynamic_slice_in_dim(
        every_small[:, :embed_count], me_dp * (embed_count // m), embed_count // m, axis=1
    )
    grad_shift_weight = jnp.dot(
        embed_rows.T, every_shift.reshape(m, -1)[:, :own], precision=PRECISE
    )
    grad_ada_weight = jnp.dot(
        embed_rows.T,
        every_small[:, gain_start : gain_start + columns.shape[0]],
        precision=PRECISE,
    )
    qkv_grad = jnp.stack(
        [added(sums_qkv[:, :, j * local_width : (j + 1) * local_width]) for j in range(3)]
    )
    return (
        output,
        image_grad,
        embedding_grad,
        gains[0],
        settled(pieces_first, 9),
        gains[1],
        settled(pieces_second, 9),
        grad_shift_weight,
        settled(pieces_down, 4),
        grad_ada_weight,
        qkv_grad,
        added(sums_out),
        added(sums_up),
        added(sums_proj),
    )


def solution(mesh):
    placed = (
        P("dp", "mp", None, None),
        P("dp", None),
        P("dp", None),
        P(),
        P(None, "mp", None),
        P(),
        P(None, "mp", None),
        P(None, "mp"),
        P(None, "mp", None),
        P(None, "mp"),
        P(None, None, "mp"),
        P("mp", None),
        P(None, "mp"),
        P("mp", None),
        P("dp", "mp", None, None),
    )
    return jax.shard_map(
        local,
        mesh=mesh,
        in_specs=placed,
        out_specs=(
            P("dp", "mp", None, None),
            P("dp", "mp", None, None),
            P("dp", None),
            P(("dp", "mp")),
            P(None, "dp", "mp"),
            P(("dp", "mp")),
            P(None, "dp", "mp"),
            P("dp", "mp"),
            P(None, "dp", "mp"),
            P("dp", "mp"),
            P(None, "dp", "mp"),
            P("mp", "dp"),
            P("dp", "mp"),
            P("mp", "dp"),
        ),
        check_vma=False,
    )
```

```python
from functools import partial
import math

import jax
import jax.numpy as jnp
from jax import lax
from jax.experimental import pallas as pl
from jax.experimental.pallas import tpu as pltpu
from jax.sharding import PartitionSpec as P

HEAD_DIM = 128
GROUPS = 32


GROUP_EPSILON = 1e-05
LAYER_EPSILON = 1e-06
MASKED_SCORE = -1000000000.0
PRECISE = lax.Precision.HIGHEST


def group_spread(per_channel, size):
    grouped = jnp.sum(per_channel.reshape(-1, size), axis=1)
    return jnp.repeat(grouped, size)


def group_forward(values, size):
    counted = values.shape[0] * size
    average = group_spread(jnp.sum(values, axis=0), size) / counted
    centre = values - average
    inverse = lax.rsqrt(
        group_spread(jnp.sum(centre * centre, axis=0), size) / counted + GROUP_EPSILON
    )
    return (centre * inverse, inverse)


def group_backward(incoming, normed, inverse, gain_vec, size):
    pre_act = normed * gain_vec
    sigmoid_part = jax.nn.sigmoid(pre_act)
    through = incoming * sigmoid_part * (1.0 + pre_act * (1.0 - sigmoid_part))
    counted = normed.shape[0] * size
    gain_part = jnp.sum(through * normed, axis=0)
    plain_part = jnp.sum(through, axis=0)
    first_mean = group_spread(plain_part * gain_vec, size) / counted
    second_mean = group_spread(gain_part * gain_vec, size) / counted
    outgoing = inverse * (through * gain_vec - first_mean - normed * second_mean)
    return (outgoing, gain_part)


def windows(planes, flipped):
    row_count, col_count, depth = planes.shape
    padded = jnp.pad(planes, ((1, 1), (1, 1), (0, 0)))
    pieces = []
    for tap_index in range(9):
        row_off, col_off = divmod(tap_index, 3)
        if flipped:
            row_off, col_off = (2 - row_off, 2 - col_off)
        pieces.append(padded[row_off : row_off + row_count, col_off : col_off + col_count])
    return jnp.stack(pieces, axis=2).reshape(row_count * col_count, 9, depth)


def gather_rows(rows):
    return lax.all_gather(rows, "mp", axis=0, tiled=True)


def scatter_rows(rows):
    return lax.psum_scatter(
        rows.astype(jnp.bfloat16), "mp", scatter_dimension=0, tiled=True
    ).astype(jnp.float32)


def conv_scatter(hidden, kernel, n):
    patch = windows(hidden, False)
    depth = kernel.shape[2] // n
    total = jnp.einsum("ptc,tcd->pd", patch, kernel, preferred_element_type=jnp.float32)
    parts = total.astype(jnp.bfloat16).reshape(-1, n, depth).transpose(1, 0, 2)
    return lax.psum_scatter(parts, "mp", scatter_dimension=0, tiled=False).astype(jnp.float32)


def conv_backward(grad_low, hidden, kernel, n):
    row_count, col_count, depth = hidden.shape
    gathered = lax.all_gather(grad_low, "mp", axis=1, tiled=True)
    padded = jnp.pad(gathered, ((col_count, col_count), (0, 0)))
    taps = kernel.reshape(3, 3 * depth, kernel.shape[2])
    acc = sum(
        jnp.einsum(
            "pd,td->pt",
            padded[(2 - i) * col_count : (2 - i) * col_count + row_count * col_count],
            taps[i],
            preferred_element_type=jnp.float32,
        )
        for i in range(3)
    )
    grad_kernel = jnp.einsum(
        "ptc,pd->tcd", windows(hidden, False), gathered, preferred_element_type=jnp.float32
    )
    return (join_columns(acc, col_count), grad_kernel)


def unsettled(parts, m, n):
    return parts.reshape(n, m, -1, parts.shape[-1])


def settled(pieces, taps):
    if pieces.ndim == 3:
        return pieces
    m, count, outs, _ = pieces.shape
    return (
        pieces.astype(jnp.float32)
        .reshape(m, count, outs, taps, -1)
        .transpose(3, 1, 4, 0, 2)
        .reshape(taps, -1, m * outs)
    )


def added(received):
    return jnp.sum(received.astype(jnp.float32), axis=0)


def layer_forward(stream):
    centre = stream - jnp.mean(stream, axis=1, keepdims=True)
    inverse = lax.rsqrt(jnp.mean(centre * centre, axis=1, keepdims=True) + LAYER_EPSILON)
    return (centre * inverse, inverse)


def layer_backward(incoming, normed, inverse, scale_vec):
    through = incoming * (1.0 + scale_vec)
    outgoing = inverse * (
        through
        - jnp.mean(through, axis=1, keepdims=True)
        - normed * jnp.mean(through * normed, axis=1, keepdims=True)
    )
    return (outgoing, jnp.sum(incoming * normed, axis=0), jnp.sum(incoming, axis=0))


MESH = pl.DeviceIdType.MESH
CONV_PARTS = 4
TOKEN_PARTS = 4
VMEM_BYTES = 60 * 1024 * 1024


class Line:
    def __init__(self, chips, images):
        self.chips = chips
        self.images = images
        self.dp = lax.axis_index("dp")
        self.mp = lax.axis_index("mp")
        self.z = self.mp // 2
        self.c = self.mp % 2
        self.has_up = self.z < chips - 1
        self.has_down = self.z > 0
        self.up = (self.dp, self.mp + 2)
        self.down = (self.dp, self.mp - 2)
        self.sibling = (self.dp, 2 * self.z + 1 - self.c)
        self.ready = lambda: None
        self.late = lambda: None

    def count(self, axis):
        return {"dp": self.images, "mp": 2 * self.chips, "all": 2 * self.chips * self.images}[axis]

    def index(self, axis):
        return {"dp": self.dp, "mp": self.mp, "all": self.dp * 2 * self.chips + self.mp}[axis]

    def place(self, axis, index):
        if axis == "dp":
            return (index, self.mp)
        if axis == "mp":
            return (self.dp, index)
        return (index // (2 * self.chips), index % (2 * self.chips))

    def peer(self, axis, step):
        return lax.rem(self.index(axis) + step, self.count(axis))

    def barrier(self, axes, neighbours):
        bar = pltpu.get_barrier_semaphore()
        axes = ("all",) if "all" in axes else axes
        steady = 0
        for axis in axes:
            for step in range(1, self.count(axis)):
                target = self.place(axis, self.peer(axis, step))
                pl.semaphore_signal(bar, inc=1, device_id=target, device_id_type=MESH)
            steady += self.count(axis) - 1
        cases = [(steady, None)]
        if neighbours and not ("all" in axes or "mp" in axes):
            pl.semaphore_signal(bar, inc=1, device_id=self.sibling, device_id_type=MESH)

            @pl.when(self.has_up)
            def _():
                pl.semaphore_signal(bar, inc=1, device_id=self.up, device_id_type=MESH)

            @pl.when(self.has_down)
            def _():
                pl.semaphore_signal(bar, inc=1, device_id=self.down, device_id_type=MESH)

            middle = jnp.logical_and(self.has_up, self.has_down)
            cases = [(steady + 3, middle), (steady + 2, jnp.logical_not(middle))]
        for count, when in cases:
            if when is None:
                pl.semaphore_wait(bar, count)
            else:

                @pl.when(when)
                def _():
                    pl.semaphore_wait(bar, count)


class Rider:
    def __init__(self, axis, array, cut=None, beside=False, part=(0, 1), inside=False):
        self.axes = (axis,)
        self.part = part
        self.inside = inside
        self.axis = axis
        self.array = array
        self.cut = cut
        self.beside = beside

    def result(self, sizes):
        count = sizes[self.axis]
        shape = list(self.array.shape)
        if self.cut is not None:
            shape[self.cut] //= count
        shape[0] //= self.part[1]
        self.columns = shape[-1]
        if self.beside:
            shape[-1] *= count
        else:
            shape = [count] + shape
        return jax.ShapeDtypeStruct(tuple(shape), self.array.dtype)

    def scratch(self, sizes):
        count = sizes[self.axis]
        return [pltpu.SemaphoreType.DMA((count,)), pltpu.SemaphoreType.DMA((count,))]

    def piece(self, ref, index, count):
        if self.cut is None:
            return ref
        size = self.array.shape[self.cut] // count
        where = [slice(None)] * len(self.array.shape)
        where[self.cut] = pl.ds(pl.multiple_of(index * size, size), size)
        if self.part[1] > 1:
            rows = self.array.shape[0] // self.part[1]
            where[0] = pl.ds(self.part[0] * rows, rows)
        return ref.at[tuple(where)]

    def copies(self, line, src, dst, send, recv):
        count, me = line.count(self.axis), line.index(self.axis)
        if self.beside:
            land = dst.at[:, pl.ds(pl.multiple_of(me * self.columns, self.columns), self.columns)]
        else:
            land = dst.at[me]
        made = [pltpu.make_async_copy(self.piece(src, me, count), land, send.at[0])]
        for step in range(1, count):
            peer = line.peer(self.axis, step)
            made.append(
                remote(
                    self.piece(src, peer, count),
                    land,
                    send.at[step],
                    recv.at[step],
                    line.place(self.axis, peer),
                )
            )
        return made

    def start(self, line, src, dst, send, recv):
        for copy in self.copies(line, src, dst, send, recv):
            copy.start()

    def middle(self, phase, *refs):
        pass

    def finish(self, line, src, dst, send, recv):
        for copy in self.copies(line, src, dst, send, recv):
            copy.wait()


class Settle:
    def __init__(self, array, summed, taps, placed):
        self.axes = ("dp", "mp")
        self.inside = True
        self.array = array
        self.summed = summed
        self.taps = taps
        self.placed = placed

    def result(self, sizes):
        n, m = sizes["mp"], sizes["dp"]
        self.ratio = n // m
        self.tail = tuple(self.array.shape[-2:])
        self.total = jax.ShapeDtypeStruct((n,) + self.tail, self.array.dtype)
        self.land = (m, self.ratio) + self.tail
        self.add = Rider("dp", self.array, None if self.summed else 1)
        self.outward = Rider("mp", self.total, 0)
        self.inward = Rider("dp", self.total, 0)
        if not self.placed:
            return jax.ShapeDtypeStruct(self.land, self.array.dtype)
        shape = (self.taps, self.ratio * self.tail[1] // self.taps, m * self.tail[0])
        return jax.ShapeDtypeStruct(shape, jnp.float32)

    def scratch(self, sizes):
        n, m = sizes["mp"], sizes["dp"]
        dtype = self.array.dtype
        refs = [pltpu.VMEM(self.land, dtype), pltpu.VMEM((n, 1) + self.tail, dtype)]
        if not self.summed:
            refs += [pltpu.VMEM((m, n, 1) + self.tail, dtype), pltpu.VMEM((n,) + self.tail, dtype)]
            refs += self.add.scratch(sizes)
        return refs + self.outward.scratch(sizes) + self.inward.scratch(sizes)

    def copies(self, step, line, src, dst, land, stage, *rest):
        if not self.summed:
            got, total = rest[:2]
            if step == 0:
                return self.add.copies(line, src, got, *rest[2:4])
            src, rest = total, rest[4:]
            step -= 1
        if step == 0:
            return self.outward.copies(line, src, stage, *rest[:2])
        return self.inward.copies(line, stage.at[:, 0], land, *rest[2:4])

    def start(self, *refs):
        for copy in self.copies(0, *refs):
            copy.start()

    def middle(self, phase, *refs):
        if self.summed and phase == 1:
            self.end(*refs)
            return
        for copy in self.copies(phase, *refs):
            copy.wait()
        if not self.summed and phase == 0:
            got, total = refs[5:7]

            @pl.loop(0, total.shape[0])
            def _(index):
                added_up = got[0, index, 0].astype(jnp.float32)
                for image in range(1, got.shape[0]):
                    added_up += got[image, index, 0].astype(jnp.float32)
                total[index] = added_up.astype(total.dtype)

        for copy in self.copies(phase + 1, *refs):
            copy.start()

    def finish(self, *refs):
        if not self.summed:
            self.end(*refs)

    def end(self, *refs):
        for copy in self.copies(1 if self.summed else 2, *refs):
            copy.wait()
        dst, land = refs[2:4]
        if not self.placed:
            dst[...] = land[...]
            return
        own = self.tail[1] // self.taps
        for half in range(self.ratio):
            for tap in range(self.taps):
                block = jnp.concatenate(
                    [
                        land[image, half, :, pl.ds(tap * own, own)].astype(jnp.float32)
                        for image in range(land.shape[0])
                    ],
                    axis=0,
                )
                dst[tap, pl.ds(half * own, own)] = block.T


def comm_call(
    kernel, inputs, out_shapes, scratch, riders, n, m, number, neighbours=True, after=None
):
    chips = n // 2
    sizes = {"dp": m, "mp": n, "all": m * n}
    ride_shapes = tuple(rider.result(sizes) for rider in riders)
    ride_scratch = [rider.scratch(sizes) for rider in riders]
    any_spec = pl.BlockSpec(memory_space=pl.ANY)
    ni, nr, no = len(inputs), len(riders), len(out_shapes)
    large = [index for index in range(ni) if inputs[index].size * inputs[index].dtype.itemsize > 2**20]

    def body(*refs):
        main_in, ride_in = list(refs[:ni]), refs[ni : ni + nr]
        rest = refs[ni + nr :]
        main_out, ride_out = rest[:no], rest[no : no + nr]
        rest = rest[no + nr :]
        main_scratch, rest = rest[: len(scratch)], rest[len(scratch) :]
        line = Line(chips, m)
        loads = []
        if large:
            load_sems, rest = rest[0], rest[1:]
            for place, index in enumerate(large):
                loads.append(
                    pltpu.make_async_copy(main_in[index], rest[place], load_sems.at[place])
                )
                main_in[index] = rest[place]
            rest = rest[len(large) :]
        for load in loads:
            load.start()

        def ready():
            for load in loads:
                load.wait()

        line.ready = ready
        line.barrier(sorted(set(axis for rider in riders for axis in rider.axes)), neighbours)
        riding = []
        for rider, src, dst, needs in zip(riders, ride_in, ride_out, ride_scratch):
            riding.append((rider, (line, src, dst) + tuple(rest[: len(needs)])))
            rest = rest[len(needs) :]
        for rider, refs_in in riding:
            rider.start(*refs_in)
        phases = [0, 1]

        def late():
            phases.pop(0)
            for rider, refs_in in riding:
                rider.middle(0, *refs_in)

        line.late = late
        kernel(line, *main_in, *main_out, *main_scratch)
        for phase in phases:
            for rider, refs_in in riding:
                rider.middle(phase, *refs_in)
        for rider, refs_in in riding:
            rider.finish(*refs_in)
        if after is not None:
            after(main_in, main_out, ride_out)

    return pl.pallas_call(
        body,
        out_shape=tuple(out_shapes) + ride_shapes,
        in_specs=[any_spec if index in large else whole(1)[0] for index in range(ni)]
        + [any_spec] * nr,
        out_specs=tuple(
            whole(no)
            + [whole(1)[0] if rider.inside else any_spec for rider in riders]
        ),
        scratch_shapes=list(scratch)
        + ([pltpu.SemaphoreType.DMA((len(large),))] if large else [])
        + [pltpu.VMEM(inputs[index].shape, inputs[index].dtype) for index in large]
        + [ref for needs in ride_scratch for ref in needs],
        compiler_params=comm_params(number),
    )(*inputs, *[rider.array for rider in riders])


def remote(src, dst, send, recv, target):
    return pltpu.make_async_remote_copy(
        src_ref=src,
        dst_ref=dst,
        send_sem=send,
        recv_sem=recv,
        device_id=target,
        device_id_type=MESH,
    )


def gather_sems(chips):
    return [pltpu.SemaphoreType.DMA((3, 2, chips)), pltpu.SemaphoreType.DMA((3, 2, chips))]


def line_gather(line, x_ref, slot, send, recv, on_own, on_pair):
    chips = line.chips
    z, c = line.z, line.c

    def hop(stream, step, src, block, target):
        return remote(src, slot(block), send.at[stream, 0, step], recv.at[stream, 0, step], target)

    def across(way, step, src, block):
        return remote(src, slot(block), send.at[2, way, step], recv.at[2, way, step], line.sibling)

    @pl.when(line.has_up)
    def _():
        hop(0, 1, x_ref, line.mp, line.up).start()

    @pl.when(line.has_down)
    def _():
        hop(1, 1, x_ref, line.mp, line.down).start()

    across(0, 0, x_ref, line.mp).start()
    slot(line.mp)[...] = x_ref[...]
    line.ready()
    on_own()
    across(0, 0, x_ref, line.mp).wait_recv()
    on_pair(z)
    for step in range(1, chips):
        below, above = z - step, z + step
        if step == chips - 1:
            line.late()

        @pl.when(below >= 0)
        def _():
            block = 2 * below + c
            hop(0, step, slot(block), block, line.up).wait_recv()
            if step + 1 < chips:

                @pl.when(line.has_up)
                def _():
                    hop(0, step + 1, slot(block), block, line.up).start()

            across(0, step, slot(block), block).start()

        @pl.when(above < chips)
        def _():
            block = 2 * above + c
            hop(1, step, slot(block), block, line.down).wait_recv()
            if step + 1 < chips:

                @pl.when(line.has_down)
                def _():
                    hop(1, step + 1, slot(block), block, line.down).start()

            across(1, step, slot(block), block).start()

        @pl.when(below >= 0)
        def _():
            across(0, step, slot(2 * below + c), 2 * below + c).wait_recv()
            on_pair(below)

        @pl.when(above < chips)
        def _():
            across(1, step, slot(2 * above + c), 2 * above + c).wait_recv()
            on_pair(above)

    @pl.when(line.has_up)
    def _():
        hop(0, 1, x_ref, line.mp, line.up).wait_send()

    @pl.when(line.has_down)
    def _():
        hop(1, 1, x_ref, line.mp, line.down).wait_send()

    across(0, 0, x_ref, line.mp).wait_send()
    for step in range(1, chips):
        below, above = z - step, z + step

        @pl.when(below >= 0)
        def _():
            block = 2 * below + c
            if step + 1 < chips:

                @pl.when(line.has_up)
                def _():
                    hop(0, step + 1, slot(block), block, line.up).wait_send()

            across(0, step, slot(block), block).wait_send()

        @pl.when(above < chips)
        def _():
            block = 2 * above + c
            if step + 1 < chips:

                @pl.when(line.has_down)
                def _():
                    hop(1, step + 1, slot(block), block, line.down).wait_send()

            across(1, step, slot(block), block).wait_send()


def scatter_scratch(chips, rows, cols, parts):
    block = (chips, rows, cols)
    return [
        pltpu.VMEM(block, jnp.float32),
        pltpu.VMEM(block, jnp.bfloat16),
        pltpu.VMEM(block, jnp.bfloat16),
        pltpu.VMEM((2,) + block, jnp.bfloat16),
        pltpu.SemaphoreType.DMA((2, 3, chips, parts)),
    ]


def line_scatter(line, scratch, parts, produce, finish, tile, side=()):
    chips = line.chips
    z = line.z
    kept, out_ref, in_ref, moving, sems = scratch
    count = kept.shape[1] // parts
    line.ready()

    def span(part):
        return pl.ds(part * count, count)

    def across(chip, part):
        return remote(
            out_ref.at[chip, span(part)],
            in_ref.at[chip, span(part)],
            sems.at[0, 0, chip, part],
            sems.at[1, 0, chip, part],
            line.sibling,
        )

    def hop(way, chip, part):
        target = line.up if way == 0 else line.down
        ref = moving.at[way, chip, span(part)]
        return remote(
            ref, ref, sems.at[0, 1 + way, chip, part], sems.at[1, 1 + way, chip, part], target
        )

    items = []
    for step in range(chips - 1):
        for part in range(parts):
            items.append((0, chips - 1 - step + z, part, step >= z))
            items.append((1, step - (chips - 1 - z), part, step >= chips - 1 - z))
    for part in range(parts):
        items.append((2, z, part, None))

    def run(active, body):
        if active is None:
            body()
        else:
            pl.when(active)(body)

    def start(item):
        way, chip, part, active = item

        def body():
            produce(chip, part, count, kept.at[chip], out_ref.at[chip])
            across(chip, part).start()

        run(active, body)

    def tiles(part, body):
        @pl.loop(0, count // tile)
        def _(index):
            body(pl.ds(pl.multiple_of(part * count + index * tile, tile), tile))

    def close(item):
        way, chip, part, active = item

        def body():
            across(chip, part).wait_recv()
            if way < 2:
                later = line.has_down if way == 0 else line.has_up

                @pl.when(later)
                def _():
                    hop(way, chip, part).wait_recv()

                    def add(rows):
                        moving[way, chip, rows] = (
                            kept[chip, rows]
                            + in_ref[chip, rows].astype(jnp.float32)
                            + moving[way, chip, rows].astype(jnp.float32)
                        ).astype(jnp.bfloat16)

                    tiles(part, add)

                @pl.when(jnp.logical_not(later))
                def _():
                    def add(rows):
                        moving[way, chip, rows] = (
                            kept[chip, rows] + in_ref[chip, rows].astype(jnp.float32)
                        ).astype(jnp.bfloat16)

                    tiles(part, add)

                hop(way, chip, part).start()
            else:

                def total(rows):
                    return kept[chip, rows] + in_ref[chip, rows].astype(jnp.float32)

                def from_side(side, rows):
                    return moving[side, chip, rows].astype(jnp.float32)

                both = jnp.logical_and(line.has_down, line.has_up)

                @pl.when(both)
                def _():
                    hop(0, chip, part).wait_recv()
                    hop(1, chip, part).wait_recv()
                    tiles(
                        part,
                        lambda rows: finish(
                            part, rows, total(rows) + from_side(0, rows) + from_side(1, rows)
                        ),
                    )

                for side, present in ((0, line.has_down), (1, line.has_up)):

                    @pl.when(jnp.logical_and(present, jnp.logical_not(both)))
                    def _():
                        hop(side, chip, part).wait_recv()
                        tiles(
                            part,
                            lambda rows: finish(part, rows, total(rows) + from_side(side, rows)),
                        )

        run(active, body)

    lag = 2
    side = list(side)
    for index, item in enumerate(items):
        start(item)
        if index >= lag:
            close(items[index - lag])
            if index % 2 == 0 and side:
                side.pop(0)()
    for step in side:
        step()
    for item in items[-lag:]:
        close(item)
    for way, chip, part, active in items:

        def body():
            across(chip, part).wait_send()
            if way < 2:
                hop(way, chip, part).wait_send()

        run(active, body)


def whole(count):
    return [pl.BlockSpec(memory_space=pltpu.VMEM)] * count


def comm_params(number):
    return pltpu.CompilerParams(
        collective_id=number, has_side_effects=True, vmem_limit_bytes=VMEM_BYTES
    )


def pick(c, low, high):
    return jnp.where(c == 0, low, high), jnp.where(c == 0, high, low)


def group_matrix(own, size, count):
    groups = [lax.broadcasted_iota(jnp.int32, (own, own), axis) // size for axis in range(2)]
    return jnp.where(groups[0] == groups[1], 1.0 / (count * size), 0.0)


def norm_spread(values, gain, spread_ref, stat_ref, size, breadth):
    pixels, own = values.shape
    tile = 512
    matrix = group_matrix(own, size, pixels)
    stat_ref[...] = jnp.zeros_like(stat_ref)
    column = lax.broadcasted_iota(jnp.int32, (tile, own), 0) % breadth

    def tiles(body):
        @pl.loop(0, pixels // tile)
        def _(index):
            base = pl.multiple_of(index * tile, tile)
            body(base, pl.ds(base, tile))

    def add(base, rows):
        stat_ref[0:1] += jnp.sum(values[rows], axis=0, keepdims=True)

    tiles(add)
    average = jnp.dot(stat_ref[...], matrix, precision=PRECISE)[0:1]

    def square(base, rows):
        centre = values[rows] - average
        stat_ref[1:2] += jnp.sum(centre * centre, axis=0, keepdims=True)

    tiles(square)
    inverse = lax.rsqrt(jnp.dot(stat_ref[...], matrix, precision=PRECISE)[1:2] + GROUP_EPSILON)
    stat_ref[2:3] = inverse

    def write(base, rows):
        normed = (values[rows] - average) * inverse
        values[rows] = normed
        pre_act = normed * gain
        hidden = pre_act / (1.0 + jnp.exp(-pre_act))
        below = pl.ds(base + breadth, tile)
        left = jnp.where(column == 0, 0.0, pltpu.roll(hidden, 1, 0))
        right = jnp.where(column == breadth - 1, 0.0, pltpu.roll(hidden, tile - 1, 0))
        for place, value in enumerate((left, hidden, right)):
            spread_ref[below, place * own : (place + 1) * own] = value.astype(jnp.bfloat16)

    tiles(write)
    nothing = jnp.zeros((breadth, 3 * own), jnp.bfloat16)
    spread_ref[pl.ds(0, breadth)] = nothing
    spread_ref[pl.ds(breadth + pixels, breadth)] = nothing


def norm_shapes(pixels, own, cols):
    return (
        jax.ShapeDtypeStruct((pixels, own), jnp.float32),
        jax.ShapeDtypeStruct((pixels + 2 * cols, 3 * own), jnp.bfloat16),
        jax.ShapeDtypeStruct((8, own), jnp.float32),
    )


def conv_scatter_kernel(breadth, size, line, x_ref, w_ref, *refs):
    normed = size > 0
    v_ref, refs = (refs[0], refs[1:]) if normed else (None, refs)
    o_ref, refs = refs[0], refs[1:]
    spread_ref, stat_ref, *scratch = refs if normed else (None, None) + tuple(refs)
    pixels, own = o_ref.shape
    tile = 512

    def produce(chip, part, count, mine, other):
        columns = pl.ds(pl.multiple_of(chip * 2 * own, 2 * own), 2 * own)

        @pl.loop(0, count // tile)
        def _(index):
            base = pl.multiple_of(part * count + index * tile, tile)
            total = jnp.zeros((tile, 2 * own), jnp.float32)
            for i in range(3):
                total += jnp.dot(
                    x_ref[pl.ds(base + i * breadth, tile)],
                    w_ref[i, :, columns],
                    preferred_element_type=jnp.float32,
                )
            first, second = pick(line.c, total[:, :own], total[:, own:])
            mine[pl.ds(base, tile)] = first
            other[pl.ds(base, tile)] = second.astype(jnp.bfloat16)

    def finish(part, rows, total):
        o_ref[rows] = total + v_ref[0:1] if normed else total

    line_scatter(line, scratch, CONV_PARTS, produce, finish, tile)
    if normed:
        norm_spread(o_ref, v_ref[1:2], spread_ref, stat_ref, size, breadth)


def side_by_side(hidden):
    rows, cols, depth = hidden.shape
    padded = jnp.pad(hidden, ((1, 1), (1, 1), (0, 0)))
    return jnp.concatenate([padded[:, j : j + cols] for j in range(3)], axis=2).reshape(
        (rows + 2) * cols, 3 * depth
    )


def rows_of(*vectors):
    rows = jnp.stack(vectors)
    return jnp.pad(rows, ((0, 8 - rows.shape[0]), (0, 0)))


def conv_scatter_fused(spread, kernel, cols, n, m, number, shift=None, gain=None, size=0):
    own = kernel.shape[2] // n
    depth = kernel.shape[1]
    pixels = spread.shape[0] - 2 * cols
    return comm_call(
        partial(conv_scatter_kernel, cols, size),
        (spread, kernel.reshape(3, 3 * depth, kernel.shape[2]))
        + ((rows_of(shift, gain),) if size else ()),
        norm_shapes(pixels, own, cols)[: 3 if size else 1],
        scatter_scratch(n // 2, pixels, own, CONV_PARTS),
        (),
        n,
        m,
        number,
    )


def conv_back_kernel(breadth, size, extra, line, g_ref, w_ref, x_ref, n_ref, v_ref, *refs):
    refs = list(refs)
    more_ref = refs.pop(0) if extra else None
    low_ref, wg_ref, stat_ref, acc_ref, held, sums, send, recv = refs
    chips = line.chips
    pixels, own = g_ref.shape
    wide = w_ref.shape[1]
    tile, long = 512, 1024
    zero = jnp.zeros((breadth, own), jnp.bfloat16)
    for block in range(2 * chips):
        held[block, pl.ds(0, breadth)] = zero
        held[block, pl.ds(breadth + pixels, breadth)] = zero

    def slot(block):
        return held.at[block, pl.ds(breadth, pixels)]

    def beside(base, count, chip):
        rows = pl.ds(base, count)
        return [held[2 * chip, rows], held[2 * chip + 1, rows]]

    def on_own():
        @pl.loop(0, pixels // tile)
        def _(index):
            acc_ref[pl.ds(pl.multiple_of(index * tile, tile), tile)] = jnp.zeros(
                (tile, wide), jnp.float32
            )

    def on_pair(chip):
        columns = pl.ds(pl.multiple_of(chip * 2 * own, 2 * own), 2 * own)

        @pl.loop(0, pixels // tile)
        def _(index):
            base = pl.multiple_of(index * tile, tile)
            shifted = []
            for i in range(3):
                shifted += beside(base + (2 - i) * breadth, tile, chip)
            acc_ref[pl.ds(base, tile)] += product(
                jnp.concatenate(shifted, axis=1),
                jnp.concatenate([w_ref[i, :, columns] for i in range(3)], axis=1),
                True,
            )

        sums[...] = jnp.zeros_like(sums)

        @pl.loop(0, pixels // long)
        def _(index):
            base = pl.multiple_of(index * long, long)
            sums[...] += lax.dot_general(
                jnp.concatenate(beside(base + breadth, long, chip), axis=1),
                jnp.concatenate(
                    [x_ref[pl.ds(base + i * breadth, long)] for i in range(3)], axis=1
                ),
                (((0,), (0,)), ((), ())),
                preferred_element_type=jnp.float32,
            )

        wg_ref[chip] = sums[...].astype(jnp.bfloat16)

    line_gather(line, g_ref, slot, send, recv, on_own, on_pair)

    gain, inverse = v_ref[0:1], v_ref[1:2]
    stat_ref[...] = jnp.zeros_like(stat_ref)
    column = lax.broadcasted_iota(jnp.int32, (tile, own), 0) % breadth

    @pl.loop(0, pixels // tile)
    def _(index):
        rows = pl.ds(pl.multiple_of(index * tile, tile), tile)
        left = jnp.where(
            column == breadth - 1, 0.0, pltpu.roll(acc_ref[rows, 0:own], tile - 1, 0)
        )
        right = jnp.where(column == 0, 0.0, pltpu.roll(acc_ref[rows, 2 * own : wide], 1, 0))
        incoming = left + acc_ref[rows, own : 2 * own] + right
        normed = n_ref[rows]
        pre_act = normed * gain
        sigmoid_part = 1.0 / (1.0 + jnp.exp(-pre_act))
        through = incoming * sigmoid_part * (1.0 + pre_act * (1.0 - sigmoid_part))
        acc_ref[rows, 0:own] = through
        stat_ref[0:1] += jnp.sum(through * normed, axis=0, keepdims=True)
        stat_ref[1:2] += jnp.sum(through, axis=0, keepdims=True)

    means = jnp.dot(stat_ref[...] * gain, group_matrix(own, size, pixels), precision=PRECISE)
    second_mean, first_mean = means[0:1], means[1:2]

    @pl.loop(0, pixels // tile)
    def _(index):
        rows = pl.ds(pl.multiple_of(index * tile, tile), tile)
        outgoing = inverse * (
            acc_ref[rows, 0:own] * gain - first_mean - n_ref[rows] * second_mean
        )
        stat_ref[2:3] += jnp.sum(outgoing, axis=0, keepdims=True)
        if extra:
            outgoing = outgoing + more_ref[rows]
        low_ref[rows] = outgoing.astype(jnp.bfloat16)


def conv_back_fused(
    grad_low, spread, kernel, normed, inverse, gain, size, cols, n, m, number, riders, more=()
):
    pixels, own = grad_low.shape
    depth = kernel.shape[1]
    chips = n // 2
    vectors = rows_of(gain, inverse)
    return comm_call(
        partial(conv_back_kernel, cols, size, len(more) > 0),
        (grad_low, kernel.reshape(3, 3 * depth, kernel.shape[2]), spread, normed, vectors)
        + tuple(more),
        (
            jax.ShapeDtypeStruct((pixels, depth), jnp.bfloat16),
            jax.ShapeDtypeStruct((chips, 2 * own, 9 * depth), jnp.bfloat16),
            jax.ShapeDtypeStruct((8, own), jnp.float32),
        ),
        [
            pltpu.VMEM((pixels, 3 * depth), jnp.float32),
            pltpu.VMEM((n, pixels + 2 * cols, own), jnp.bfloat16),
            pltpu.VMEM((2 * own, 9 * depth), jnp.float32),
        ]
        + gather_sems(chips),
        riders,
        n,
        m,
        number,
    )


def join_columns(acc, cols):
    pixels, wide = acc.shape
    depth = wide // 3
    planes = acc.reshape(-1, cols, wide)
    none = jnp.zeros_like(planes[:, :1, :depth])
    left = jnp.concatenate([planes[:, 1:, :depth], none], axis=1)
    right = jnp.concatenate([none, planes[:, :-1, 2 * depth :]], axis=1)
    return (left + planes[:, :, depth : 2 * depth] + right).reshape(pixels, depth)


def product(x, w, turned):
    return lax.dot_general(
        x, w, (((1,), (1 if turned else 0,)), ((), ())), preferred_element_type=jnp.float32
    )


def outer_steps(grad, left, right, cut):
    def step(start):
        grad[pl.ds(start, cut)] = lax.dot_general(
            left[:, pl.ds(start, cut)],
            right[...],
            (((0,), (0,)), ((), ())),
            preferred_element_type=jnp.float32,
        ).astype(grad.dtype)

    return [partial(step, start) for start in range(0, left.shape[1], cut)]


def tokens_scatter_kernel(turned, beside, line, x_ref, w_ref, *refs):
    side = ()
    if beside:
        left, right, o_ref, grad, *scratch = refs
        side = outer_steps(grad, left, right, 128)
    else:
        o_ref, *scratch = refs
    tokens, width = o_ref.shape
    cut = width // TOKEN_PARTS
    depth = x_ref.shape[1] // w_ref.shape[0]

    def produce(chip, part, count, mine, other):
        rows = pl.ds(pl.multiple_of(chip * 2 * tokens, 2 * tokens), 2 * tokens)
        columns = pl.ds(part * cut, cut)
        total = None
        for j in range(w_ref.shape[0]):
            w = w_ref[j, columns] if turned else w_ref[j, :, columns]
            term = product(x_ref[rows, pl.ds(j * depth, depth)], w, turned)
            total = term if total is None else total + term
        first, second = pick(line.c, total[:tokens], total[tokens:])
        mine[pl.ds(part * count, count)] = first
        other[pl.ds(part * count, count)] = second.astype(jnp.bfloat16)

    def finish(part, rows, total):
        o_ref[:, pl.ds(part * cut, cut)] = total

    line_scatter(line, scratch, TOKEN_PARTS, produce, finish, tokens, side)


def outer_shapes(outer):
    if not outer:
        return ()
    return (jax.ShapeDtypeStruct((outer[0].shape[1], outer[1].shape[1]), jnp.bfloat16),)


def tokens_scatter(x, w, turned, n, m, number, riders=(), outer=()):
    tokens = x.shape[0] // n
    width = w.shape[1] if turned else w.shape[2]
    return comm_call(
        partial(tokens_scatter_kernel, turned, len(outer) > 0),
        (x, w) + tuple(outer),
        (jax.ShapeDtypeStruct((tokens, width), jnp.float32),) + outer_shapes(outer),
        scatter_scratch(n // 2, TOKEN_PARTS * tokens, width // TOKEN_PARTS, TOKEN_PARTS),
        riders,
        n,
        m,
        number,
    )


def add_outer(total, left, right, rows):
    cut = min(left.shape[1], 512)
    for start in range(0, left.shape[1], cut):
        total[pl.ds(start, cut)] += lax.dot_general(
            left[rows, pl.ds(start, cut)],
            right[rows],
            (((0,), (0,)), ((), ())),
            preferred_element_type=jnp.float32,
        )


def tokens_gather_kernel(
    turned, shape_out, outs, keep, side, beside, cols, chained, line, x_ref, w_ref, *refs
):
    refs = list(refs)
    chain_w = refs.pop(0) if chained else None
    left = refs.pop(0) if side else None
    outer = (refs.pop(0), refs.pop(0)) if beside else None
    held = refs.pop(0) if keep else None
    results = [refs.pop(0) for _ in range(outs)]
    grad = refs.pop(0) if side else None
    outer_grad = refs.pop(0) if beside else None
    chain_out = refs.pop(0) if chained else None
    total = refs.pop(0) if side else None
    if not keep:
        held = refs.pop(0)
    send, recv = refs
    tokens = x_ref.shape[0]
    across = w_ref.shape[1 if turned else 2]
    cut = min(across, 512)

    def slot(block):
        return held.at[pl.ds(pl.multiple_of(block * tokens, tokens), tokens)]

    def store_pixels(ref, chip, value):
        depth = value.shape[1] // 4
        base = chip * 8 * tokens
        for row in range(4 * tokens // cols):
            for tap in range(4):
                start = base + (2 * row + tap // 2) * cols + tap % 2
                ref[pl.Slice(start, cols // 2, 2)] = value[
                    row * (cols // 2) : (row + 1) * (cols // 2), tap * depth : (tap + 1) * depth
                ]

    def on_pair(chip):
        rows = pl.ds(pl.multiple_of(chip * 2 * tokens, 2 * tokens), 2 * tokens)
        for j in range(w_ref.shape[0]):
            for start in range(0, across, cut):
                w = w_ref[j, pl.ds(start, cut)] if turned else w_ref[j, :, pl.ds(start, cut)]
                values = shape_out(product(held[rows], w, turned))
                for ref, value in zip(results, values):
                    if cols:
                        store_pixels(ref, chip, value)
                    else:
                        ref[rows, pl.ds(j * across + start, cut)] = value.astype(ref.dtype)
        if chained:
            for start in range(0, chain_w.shape[1], 512):
                columns = pl.ds(start, 512)
                chain_out[rows, columns] = product(
                    results[-1][rows], chain_w[:, columns], False
                ).astype(jnp.bfloat16)
        if side:
            add_outer(total, held, left, rows)

    def on_own():
        if side:
            total[...] = jnp.zeros_like(total)
        if beside:
            for step in outer_steps(outer_grad, *outer, 256):
                step()

    line_gather(line, x_ref, slot, send, recv, on_own, on_pair)
    if side:
        grad[...] = total[...].astype(grad.dtype)


def tokens_gather(
    x,
    w,
    turned,
    kinds,
    shape_out,
    n,
    m,
    number,
    riders=(),
    left=None,
    outer=(),
    cols=0,
    chain=(),
    keep=True,
):
    tokens, width = x.shape
    across = w.shape[0] * w.shape[1 if turned else 2]
    side = left is not None
    grads = ((width, left.shape[1]),) if side else ()
    shape = (tokens * n * 4, across // 4) if cols else (tokens * n, across)
    return comm_call(
        partial(
            tokens_gather_kernel,
            turned,
            shape_out,
            len(kinds),
            keep,
            side,
            len(outer) > 0,
            cols,
            len(chain) > 0,
        ),
        (x, w) + tuple(chain) + ((left,) if side else ()) + tuple(outer),
        tuple(jax.ShapeDtypeStruct((tokens * n, width), x.dtype) for _ in range(int(keep)))
        + tuple(jax.ShapeDtypeStruct(shape, kind) for kind in kinds)
        + tuple(jax.ShapeDtypeStruct(grad, jnp.bfloat16) for grad in grads)
        + outer_shapes(outer)
        + tuple(jax.ShapeDtypeStruct((tokens * n, w2.shape[1]), jnp.bfloat16) for w2 in chain),
        [pltpu.VMEM(grad, jnp.float32) for grad in grads]
        + [pltpu.VMEM((tokens * n, width), x.dtype) for _ in range(int(not keep))]
        + gather_sems(n // 2),
        riders,
        n,
        m,
        number,
    )


def exchange(riders, n, m, number):
    return comm_call(lambda line: None, (), (), [], riders, n, m, number, neighbours=False)


def exchange_norm(image_rows, gain, size, cols, riders, n, m, number):
    own = image_rows.shape[1] // n
    count = image_rows.shape[0]

    def after(main_in, main_out, ride_out):
        normed, spread_ref, stat_ref = main_out

        @pl.loop(0, n)
        def _(index):
            normed[pl.ds(pl.multiple_of(index * count, count), count)] = ride_out[0][index].astype(
                jnp.float32
            )

        norm_spread(normed, main_in[0][0:1], spread_ref, stat_ref, size, cols)

    return comm_call(
        lambda line, *refs: None,
        (rows_of(gain),),
        norm_shapes(count * n, own, cols),
        [],
        (Rider("mp", image_rows, 1, inside=True),) + tuple(riders),
        n,
        m,
        number,
        neighbours=False,
        after=after,
    )


def tiled_up(vector):
    count = -(-vector.shape[0] // 1024) * 1024
    return jnp.pad(vector.astype(jnp.float32), (0, count - vector.shape[0])).reshape(-1, 128)


def attend_scatter_kernel(line, x_ref, valid_ref, w_ref, o_ref, mixed_ref, *scratch):
    tokens, width = o_ref.shape
    wide = mixed_ref.shape[1]
    cut = width // TOKEN_PARTS
    scale = 1.0 / math.sqrt(HEAD_DIM)

    def attend(rows):
        for head in range(wide // HEAD_DIM):
            where = [pl.ds(j * wide + head * HEAD_DIM, HEAD_DIM) for j in range(3)]
            scores = product(x_ref[rows, where[0]], x_ref[:, where[1]], True) * scale
            scores = jnp.where(valid_ref[0:1] > 0.5, scores, MASKED_SCORE)
            exponent = jnp.exp(scores - jnp.max(scores, axis=1, keepdims=True))
            inverse = 1.0 / jnp.sum(exponent, axis=1, keepdims=True)
            mixed_ref[rows, pl.ds(head * HEAD_DIM, HEAD_DIM)] = product(
                (exponent * inverse).astype(jnp.bfloat16), x_ref[:, where[2]], False
            ).astype(jnp.bfloat16)

    def produce(chip, part, count, mine, other):
        rows = pl.ds(pl.multiple_of(chip * 2 * tokens, 2 * tokens), 2 * tokens)
        if part == 0:
            attend(rows)
        total = product(mixed_ref[rows], w_ref[:, pl.ds(part * cut, cut)], False)
        first, second = pick(line.c, total[:tokens], total[tokens:])
        mine[pl.ds(part * count, count)] = first
        other[pl.ds(part * count, count)] = second.astype(jnp.bfloat16)

    def finish(part, rows, total):
        o_ref[:, pl.ds(part * cut, cut)] = total

    line_scatter(line, scratch, TOKEN_PARTS, produce, finish, tokens)


def attend_scatter(qkv_rows, valid, out_weight, n, m, number):
    total = qkv_rows.shape[0]
    tokens = total // n
    width = out_weight.shape[1]
    return comm_call(
        attend_scatter_kernel,
        (qkv_rows, jnp.broadcast_to(valid[None], (8, total)), out_weight),
        (
            jax.ShapeDtypeStruct((tokens, width), jnp.float32),
            jax.ShapeDtypeStruct((total, out_weight.shape[0]), jnp.bfloat16),
        ),
        scatter_scratch(n // 2, TOKEN_PARTS * tokens, width // TOKEN_PARTS, TOKEN_PARTS),
        (),
        n,
        m,
        number,
    )


def attend_gather_kernel(
    line,
    g_ref,
    w_ref,
    x_ref,
    valid_ref,
    mixed_ref,
    left,
    right,
    grad_ref,
    out_ref,
    outer_grad,
    held,
    keys_sum,
    values_sum,
    out_sum,
    send,
    recv,
):
    tokens = g_ref.shape[0]
    wide = w_ref.shape[0]
    heads = wide // HEAD_DIM
    scale = 1.0 / math.sqrt(HEAD_DIM)

    def slot(block):
        return held.at[pl.ds(pl.multiple_of(block * tokens, tokens), tokens)]

    def on_own():
        keys_sum[...] = jnp.zeros_like(keys_sum)
        values_sum[...] = jnp.zeros_like(values_sum)
        out_sum[...] = jnp.zeros_like(out_sum)
        for step in outer_steps(outer_grad, left, right, 256):
            step()

    def on_pair(chip):
        rows = pl.ds(pl.multiple_of(chip * 2 * tokens, 2 * tokens), 2 * tokens)
        for head in range(heads):
            place = pl.ds(head * HEAD_DIM, HEAD_DIM)
            where = [pl.ds(j * wide + head * HEAD_DIM, HEAD_DIM) for j in range(3)]
            grad = product(held[rows], w_ref[place], True).astype(jnp.bfloat16)
            query = x_ref[rows, where[0]]
            scores = product(x_ref[:, where[1]], query, True) * scale
            scores = jnp.where(valid_ref[:, 0:1] > 0.5, scores, MASKED_SCORE)
            exponent = jnp.exp(scores - jnp.max(scores, axis=0, keepdims=True))
            probs = exponent * (1.0 / jnp.sum(exponent, axis=0, keepdims=True))
            values_sum[:, place] += product(probs.astype(jnp.bfloat16), grad, False)
            grad_probs = product(x_ref[:, where[2]], grad, True)
            inner = jnp.sum(probs * grad_probs, axis=0, keepdims=True)
            grad_scores = (probs * (grad_probs - inner) * scale).astype(jnp.bfloat16)
            keys_sum[:, place] += product(grad_scores, query, False)
            grad_ref[rows, where[0]] = lax.dot_general(
                grad_scores,
                x_ref[:, where[1]],
                (((0,), (0,)), ((), ())),
                preferred_element_type=jnp.float32,
            ).astype(jnp.bfloat16)
        add_outer(out_sum, mixed_ref, held, rows)

    line_gather(line, g_ref, slot, send, recv, on_own, on_pair)
    grad_ref[:, pl.ds(wide, wide)] = keys_sum[...].astype(jnp.bfloat16)
    grad_ref[:, pl.ds(2 * wide, wide)] = values_sum[...].astype(jnp.bfloat16)
    out_ref[...] = out_sum[...].astype(jnp.bfloat16)


def attend_gather(grad_mid, out_weight, qkv_rows, valid, mixed_low, outer, n, m, number, riders):
    tokens, width = grad_mid.shape
    total = tokens * n
    wide = out_weight.shape[0]
    return comm_call(
        attend_gather_kernel,
        (
            grad_mid,
            out_weight,
            qkv_rows,
            jnp.broadcast_to(valid[:, None], (total, 128)),
            mixed_low,
        )
        + tuple(outer),
        (
            jax.ShapeDtypeStruct((total, 3 * wide), jnp.bfloat16),
            jax.ShapeDtypeStruct((wide, width), jnp.bfloat16),
        )
        + outer_shapes(outer),
        [
            pltpu.VMEM((total, width), jnp.bfloat16),
            pltpu.VMEM((total, wide), jnp.float32),
            pltpu.VMEM((total, wide), jnp.float32),
            pltpu.VMEM((wide, width), jnp.float32),
        ]
        + gather_sems(n // 2),
        riders,
        n,
        m,
        number,
    )


def gelu_both(value):
    factor = math.sqrt(2.0 / math.pi)
    square = value * value
    bent = jnp.tanh(factor * value * (1.0 + 0.044715 * square))
    half = 0.5 * (1.0 + bent)
    slope = half + 0.5 * value * (1.0 - bent * bent) * factor * (1.0 + 3 * 0.044715 * square)
    return slope, value * half


def local(
    image,
    embedding,
    extents,
    gain_first,
    conv_first,
    gain_second,
    conv_second,
    shift_weight,
    down_weight,
    ada_weight,
    qkv_weight,
    out_weight,
    up_weight,
    proj_weight,
    cotangent,
):
    strip_rows, canvas_cols, channel_count = (image.shape[1], image.shape[2], image.shape[3])
    width_all = out_weight.shape[1]
    n = lax.axis_size("mp")
    m = lax.axis_size("dp")
    me_mp = lax.axis_index("mp")
    me_dp = lax.axis_index("dp")
    rows_all = strip_rows * n
    pixel_total = rows_all * canvas_cols
    own = channel_count // n
    size = channel_count // GROUPS
    token_rows = strip_rows // 2
    token_cols = canvas_cols // 2
    local_tokens = token_rows * token_cols
    token_total = local_tokens * n
    local_width = out_weight.shape[0]

    fused = own % 128 == 0 and n == 2 * m
    shift_vector = jnp.dot(embedding, shift_weight, preferred_element_type=jnp.float32)[0]
    columns = jnp.dot(embedding, ada_weight, preferred_element_type=jnp.float32)[0]
    own_first = lax.dynamic_slice_in_dim(gain_first, me_mp * own, own)
    own_second = lax.dynamic_slice_in_dim(gain_second, me_mp * own, own)
    riders = (Rider("mp", tiled_up(columns)),)
    if fused:
        normed_first, spread_first, stats, pixels_low, modulation = exchange_norm(
            image[0].reshape(-1, channel_count), own_first, size, canvas_cols, riders, n, m, 12
        )
        inverse_first = stats[2]
    else:
        (modulation,) = exchange(riders, n, m, 12)
        pixels_low = lax.all_to_all(image[0], "mp", 2, 0, tiled=True)
    modulation = modulation.reshape(n, -1)[:, : columns.shape[0]].reshape(-1)
    scale_attend = modulation[:width_all]
    shift_attend = modulation[width_all : 2 * width_all]
    scale_mlp = modulation[2 * width_all : 3 * width_all]
    shift_mlp = modulation[3 * width_all :]

    pixels = pixels_low.astype(jnp.float32).reshape(pixel_total, own)
    if fused:
        hidden_first = hidden_second = None
        normed_second, spread_second, stats = conv_scatter_fused(
            spread_first, conv_first, canvas_cols, n, m, 0, shift_vector, own_second, size
        )
        inverse_second = stats[2]
        (conv_again,) = conv_scatter_fused(spread_second, conv_second, canvas_cols, n, m, 1)
    else:
        spread_first = spread_second = None
        normed_first, inverse_first = group_forward(pixels, size)
        hidden_first = (
            jax.nn.silu(normed_first * own_first)
            .astype(jnp.bfloat16)
            .reshape(rows_all, canvas_cols, own)
        )
        conv_output = conv_scatter(hidden_first, conv_first, n) + shift_vector
        normed_second, inverse_second = group_forward(conv_output, size)
        hidden_second = (
            jax.nn.silu(normed_second * own_second)
            .astype(jnp.bfloat16)
            .reshape(rows_all, canvas_cols, own)
        )
        conv_again = conv_scatter(hidden_second, conv_second, n)
    residual = pixels + conv_again
    down_patch = (
        residual.astype(jnp.bfloat16)
        .reshape(rows_all // 2, 2, token_cols, 2, own)
        .transpose(0, 2, 1, 3, 4)
        .reshape(token_total, 4 * own)
    )
    down_matrix = down_weight.reshape(4 * own, width_all)
    (stream,) = tokens_scatter(down_patch, down_matrix[None], False, n, m, 2)
    normed_attend, inverse_attend = layer_forward(stream)
    input_attend = (normed_attend * (1.0 + scale_attend) + shift_attend).astype(jnp.bfloat16)
    all_attend, qkv_rows = tokens_gather(
        input_attend, qkv_weight, False, (jnp.bfloat16,), lambda value: (value,), n, m, 3
    )
    token_index = jnp.arange(token_total, dtype=jnp.int32)
    key_valid = (token_index // token_cols < extents[0, 0]) & (
        token_index % token_cols < extents[0, 1]
    )
    valid = key_valid.astype(jnp.float32)
    attended, mixed_low = attend_scatter(qkv_rows, valid, out_weight, n, m, 4)
    stream_mid = stream + attended
    normed_mlp, inverse_mlp = layer_forward(stream_mid)
    input_mlp = (normed_mlp * (1.0 + scale_mlp) + shift_mlp).astype(jnp.bfloat16)
    all_mlp, slope, activated, projected = tokens_gather(
        input_mlp,
        up_weight[None],
        False,
        (jnp.bfloat16, jnp.bfloat16),
        gelu_both,
        n,
        m,
        5,
        chain=(proj_weight,),
    )
    final_stream = stream_mid + scatter_rows(projected)
    output = final_stream.astype(jnp.bfloat16).reshape(1, token_rows, token_cols, width_all)

    grad_final_low = cotangent[0].reshape(local_tokens, width_all)
    grad_final = grad_final_low.astype(jnp.float32)
    all_final = gather_rows(lax.optimization_barrier((grad_final_low, qkv_rows))[0])
    grad_act = jnp.einsum("le,fe->lf", all_final, proj_weight, preferred_element_type=jnp.float32)
    grad_upper = (grad_act * slope.astype(jnp.float32)).astype(jnp.bfloat16)
    grad_normed_mlp, grad_proj = tokens_scatter(
        grad_upper, up_weight[None], True, n, m, 6, (), (activated, all_final)
    )
    grad_mid_norm, grad_scale_mlp, grad_shift_mlp = layer_backward(
        grad_normed_mlp, normed_mlp, inverse_mlp, scale_mlp
    )
    grad_mid = grad_final + grad_mid_norm
    grad_qkv, grad_out, grad_up = attend_gather(
        grad_mid.astype(jnp.bfloat16),
        out_weight,
        qkv_rows,
        valid,
        mixed_low,
        (all_mlp, grad_upper),
        n,
        m,
        7,
        (),
    )
    grad_normed_attend, sums_proj, sums_out = tokens_scatter(
        grad_qkv,
        qkv_weight,
        True,
        n,
        m,
        8,
        (Rider("dp", grad_proj, 1, part=(0, 2)), Rider("dp", grad_out, 1)),
    )
    grad_stream_norm, grad_scale_attend, grad_shift_attend = layer_backward(
        grad_normed_attend, normed_attend, inverse_attend, scale_attend
    )
    grad_stream = grad_mid + grad_stream_norm
    grad_modulation = jnp.concatenate(
        [
            tiled_up(piece)
            for piece in jnp.concatenate(
                [grad_scale_attend, grad_shift_attend, grad_scale_mlp, grad_shift_mlp]
            ).reshape(n, -1)
        ]
    )
    grad_residual, grad_down, grad_qkv_weight, sums_more, ada_columns = tokens_gather(
        grad_stream.astype(jnp.bfloat16),
        down_matrix[None],
        True,
        (jnp.float32,),
        lambda value: (value,),
        n,
        m,
        9,
        (
            Rider("dp", grad_proj, 1, part=(1, 2)),
            Rider("mp", grad_modulation, 0),
        ),
        down_patch,
        (all_attend, grad_qkv),
        canvas_cols if fused else 0,
        keep=False,
    )
    ada_columns = added(ada_columns).reshape(-1)[: columns.shape[0]]
    if not fused:
        grad_residual = (
            grad_residual.reshape(rows_all // 2, token_cols, 2, 2, own)
            .transpose(0, 2, 1, 3, 4)
            .reshape(pixel_total, own)
        )
    def back(grad_low, hidden, spread, kernel, normed, inverse, gain, number, riders, more=()):
        if fused:
            low, parts, sums, *ridden = conv_back_fused(
                grad_low,
                spread,
                kernel,
                normed,
                inverse,
                gain,
                size,
                canvas_cols,
                n,
                m,
                number,
                riders,
                more,
            )
            return low, parts, sums[0], sums[2], ridden
        grad_hidden, grad_kernel = conv_backward(grad_low, hidden, kernel, n)
        outgoing, gain_part = group_backward(grad_hidden, normed, inverse, gain, size)
        parts = grad_kernel.astype(jnp.bfloat16).reshape(9 * own, -1).T
        low = sum(more, outgoing).astype(jnp.bfloat16)
        return low, parts, gain_part, jnp.sum(outgoing, axis=0), exchange(riders, n, m, number)

    grad_conv_low, parts_second, grad_gain_second, grad_shift, rode_second = back(
        grad_residual.astype(jnp.bfloat16),
        hidden_second,
        spread_second,
        conv_second,
        normed_second,
        inverse_second,
        own_second,
        10,
        (
            Rider("dp", unsettled(grad_down, m, n), 1),
            Rider("dp", grad_qkv_weight, 0),
            Rider("dp", jnp.concatenate([tiled_up(embedding[0]), tiled_up(ada_columns)])),
        ),
    )
    sums_down, sums_qkv, every_small = rode_second
    image_turned, parts_first, grad_gain_first, _, rode_first = back(
        grad_conv_low,
        hidden_first,
        spread_first,
        conv_first,
        normed_first,
        inverse_first,
        own_first,
        11,
        (
            Rider("dp", unsettled(parts_second, m, n), 1),
            Rider("dp", tiled_up(grad_shift)),
            Settle(added(sums_down)[:, 0].astype(jnp.bfloat16), True, 4, fused),
            Rider("dp", grad_up, 0),
        ),
        (grad_residual,),
    )
    sums_second, every_shift, pieces_down, sums_up = rode_first
    embed_term = jnp.dot(
        grad_shift[None], shift_weight.astype(jnp.float32).T, precision=PRECISE
    ) + jnp.dot(ada_columns[None], ada_weight.astype(jnp.float32).T, precision=PRECISE)
    small = jnp.concatenate(
        [tiled_up(embed_term[0]), tiled_up(jnp.concatenate([grad_gain_first, grad_gain_second]))]
    )
    riders = (
        Settle(unsettled(parts_first, m, n), False, 9, fused),
        Rider("all", small),
        Settle(added(sums_second)[:, 0].astype(jnp.bfloat16), True, 9, fused),
    )
    if fused:
        pieces_first, small, pieces_second, image_turned = exchange(
            riders + (Rider("mp", image_turned, 0, True),), n, m, 13
        )
        image_grad = image_turned.reshape(image.shape)
    else:
        pieces_first, small, pieces_second = exchange(riders, n, m, 13)
        image_grad = lax.all_to_all(
            image_turned.reshape(rows_all, canvas_cols, own), "mp", 0, 2, tiled=True
        )[None]

    small = small.reshape(m, n, -1)
    embed_count = embedding.shape[1]
    embedding_grad = jnp.sum(
        lax.dynamic_index_in_dim(small, me_dp, axis=0, keepdims=False)[:, :embed_count], axis=0
    )[None]
    gain_start = -(-embed_count // 1024) * 1024
    gains = jnp.sum(small[:, :, gain_start : gain_start + 2 * own], axis=0)
    gains = gains.reshape(n, 2, own).transpose(1, 0, 2).reshape(2, -1)
    piece = channel_count // (m * n)
    gains = lax.dynamic_slice_in_dim(gains, (me_dp * n + me_mp) * piece, piece, axis=1)
    every_small = every_small.reshape(m, -1)
    embed_rows = lax.dynamic_slice_in_dim(
        every_small[:, :embed_count], me_dp * (embed_count // m), embed_count // m, axis=1
    )
    grad_shift_weight = jnp.dot(
        embed_rows.T, every_shift.reshape(m, -1)[:, :own], precision=PRECISE
    )
    grad_ada_weight = jnp.dot(
        embed_rows.T,
        every_small[:, gain_start : gain_start + columns.shape[0]],
        precision=PRECISE,
    )
    qkv_grad = jnp.stack(
        [added(sums_qkv[:, :, j * local_width : (j + 1) * local_width]) for j in range(3)]
    )
    return (
        output,
        image_grad,
        embedding_grad,
        gains[0],
        settled(pieces_first, 9),
        gains[1],
        settled(pieces_second, 9),
        grad_shift_weight,
        settled(pieces_down, 4),
        grad_ada_weight,
        qkv_grad,
        added(sums_out),
        added(sums_up),
        jnp.concatenate([added(sums_proj), added(sums_more)]),
    )


def solution(mesh):
    placed = (
        P("dp", "mp", None, None),
        P("dp", None),
        P("dp", None),
        P(),
        P(None, "mp", None),
        P(),
        P(None, "mp", None),
        P(None, "mp"),
        P(None, "mp", None),
        P(None, "mp"),
        P(None, None, "mp"),
        P("mp", None),
        P(None, "mp"),
        P("mp", None),
        P("dp", "mp", None, None),
    )
    return jax.shard_map(
        local,
        mesh=mesh,
        in_specs=placed,
        out_specs=(
            P("dp", "mp", None, None),
            P("dp", "mp", None, None),
            P("dp", None),
            P(("dp", "mp")),
            P(None, "dp", "mp"),
            P(("dp", "mp")),
            P(None, "dp", "mp"),
            P("dp", "mp"),
            P(None, "dp", "mp"),
            P("dp", "mp"),
            P(None, "dp", "mp"),
            P("mp", "dp"),
            P("dp", "mp"),
            P("mp", "dp"),
        ),
        check_vma=False,
    )
```

```python
from functools import partial
import math

import jax
import jax.numpy as jnp
from jax import lax
from jax.experimental import pallas as pl
from jax.experimental.pallas import tpu as pltpu
from jax.sharding import PartitionSpec as P

HEAD_DIM = 128
GROUPS = 32


GROUP_EPSILON = 1e-05
LAYER_EPSILON = 1e-06
MASKED_SCORE = -1000000000.0
PRECISE = lax.Precision.HIGHEST


def group_spread(per_channel, size):
    grouped = jnp.sum(per_channel.reshape(-1, size), axis=1)
    return jnp.repeat(grouped, size)


def group_forward(values, size):
    counted = values.shape[0] * size
    average = group_spread(jnp.sum(values, axis=0), size) / counted
    centre = values - average
    inverse = lax.rsqrt(
        group_spread(jnp.sum(centre * centre, axis=0), size) / counted + GROUP_EPSILON
    )
    return (centre * inverse, inverse)


def group_backward(incoming, normed, inverse, gain_vec, size):
    pre_act = normed * gain_vec
    sigmoid_part = jax.nn.sigmoid(pre_act)
    through = incoming * sigmoid_part * (1.0 + pre_act * (1.0 - sigmoid_part))
    counted = normed.shape[0] * size
    gain_part = jnp.sum(through * normed, axis=0)
    plain_part = jnp.sum(through, axis=0)
    first_mean = group_spread(plain_part * gain_vec, size) / counted
    second_mean = group_spread(gain_part * gain_vec, size) / counted
    outgoing = inverse * (through * gain_vec - first_mean - normed * second_mean)
    return (outgoing, gain_part)


def windows(planes, flipped):
    row_count, col_count, depth = planes.shape
    padded = jnp.pad(planes, ((1, 1), (1, 1), (0, 0)))
    pieces = []
    for tap_index in range(9):
        row_off, col_off = divmod(tap_index, 3)
        if flipped:
            row_off, col_off = (2 - row_off, 2 - col_off)
        pieces.append(padded[row_off : row_off + row_count, col_off : col_off + col_count])
    return jnp.stack(pieces, axis=2).reshape(row_count * col_count, 9, depth)


def gather_rows(rows):
    return lax.all_gather(rows, "mp", axis=0, tiled=True)


def scatter_rows(rows):
    return lax.psum_scatter(
        rows.astype(jnp.bfloat16), "mp", scatter_dimension=0, tiled=True
    ).astype(jnp.float32)


def conv_scatter(hidden, kernel, n):
    patch = windows(hidden, False)
    depth = kernel.shape[2] // n
    total = jnp.einsum("ptc,tcd->pd", patch, kernel, preferred_element_type=jnp.float32)
    parts = total.astype(jnp.bfloat16).reshape(-1, n, depth).transpose(1, 0, 2)
    return lax.psum_scatter(parts, "mp", scatter_dimension=0, tiled=False).astype(jnp.float32)


def conv_backward(grad_low, hidden, kernel, n):
    row_count, col_count, depth = hidden.shape
    gathered = lax.all_gather(grad_low, "mp", axis=1, tiled=True)
    padded = jnp.pad(gathered, ((col_count, col_count), (0, 0)))
    taps = kernel.reshape(3, 3 * depth, kernel.shape[2])
    acc = sum(
        jnp.einsum(
            "pd,td->pt",
            padded[(2 - i) * col_count : (2 - i) * col_count + row_count * col_count],
            taps[i],
            preferred_element_type=jnp.float32,
        )
        for i in range(3)
    )
    grad_kernel = jnp.einsum(
        "ptc,pd->tcd", windows(hidden, False), gathered, preferred_element_type=jnp.float32
    )
    return (join_columns(acc, col_count), grad_kernel)


def unsettled(parts, m, n):
    return parts.reshape(n, m, -1, parts.shape[-1])


def settled(pieces, taps):
    if pieces.ndim == 3:
        return pieces
    m, count, outs, _ = pieces.shape
    return (
        pieces.astype(jnp.float32)
        .reshape(m, count, outs, taps, -1)
        .transpose(3, 1, 4, 0, 2)
        .reshape(taps, -1, m * outs)
    )


def added(received):
    return jnp.sum(received.astype(jnp.float32), axis=0)


MESH = pl.DeviceIdType.MESH
CONV_PARTS = 4
TOKEN_PARTS = 4
VMEM_BYTES = 60 * 1024 * 1024


class Line:
    def __init__(self, chips, images):
        self.chips = chips
        self.images = images
        self.dp = lax.axis_index("dp")
        self.mp = lax.axis_index("mp")
        self.z = self.mp // 2
        self.c = self.mp % 2
        self.has_up = self.z < chips - 1
        self.has_down = self.z > 0
        self.up = (self.dp, self.mp + 2)
        self.down = (self.dp, self.mp - 2)
        self.sibling = (self.dp, 2 * self.z + 1 - self.c)
        self.ready = lambda: None
        self.late = lambda: None

    def count(self, axis):
        return {"dp": self.images, "mp": 2 * self.chips, "all": 2 * self.chips * self.images}[axis]

    def index(self, axis):
        return {"dp": self.dp, "mp": self.mp, "all": self.dp * 2 * self.chips + self.mp}[axis]

    def place(self, axis, index):
        if axis == "dp":
            return (index, self.mp)
        if axis == "mp":
            return (self.dp, index)
        return (index // (2 * self.chips), index % (2 * self.chips))

    def peer(self, axis, step):
        return lax.rem(self.index(axis) + step, self.count(axis))

    def barrier(self, axes, neighbours):
        bar = pltpu.get_barrier_semaphore()
        axes = ("all",) if "all" in axes else axes
        steady = 0
        for axis in axes:
            for step in range(1, self.count(axis)):
                target = self.place(axis, self.peer(axis, step))
                pl.semaphore_signal(bar, inc=1, device_id=target, device_id_type=MESH)
            steady += self.count(axis) - 1
        cases = [(steady, None)]
        if neighbours and not ("all" in axes or "mp" in axes):
            pl.semaphore_signal(bar, inc=1, device_id=self.sibling, device_id_type=MESH)

            @pl.when(self.has_up)
            def _():
                pl.semaphore_signal(bar, inc=1, device_id=self.up, device_id_type=MESH)

            @pl.when(self.has_down)
            def _():
                pl.semaphore_signal(bar, inc=1, device_id=self.down, device_id_type=MESH)

            middle = jnp.logical_and(self.has_up, self.has_down)
            cases = [(steady + 3, middle), (steady + 2, jnp.logical_not(middle))]
        for count, when in cases:
            if when is None:
                pl.semaphore_wait(bar, count)
            else:

                @pl.when(when)
                def _():
                    pl.semaphore_wait(bar, count)


class Rider:
    def __init__(self, axis, array, cut=None, beside=False, part=(0, 1), inside=False):
        self.axes = (axis,)
        self.part = part
        self.inside = inside
        self.axis = axis
        self.array = array
        self.cut = cut
        self.beside = beside

    def result(self, sizes):
        count = sizes[self.axis]
        shape = list(self.array.shape)
        if self.cut is not None:
            shape[self.cut] //= count
        shape[0] //= self.part[1]
        self.columns = shape[-1]
        if self.beside:
            shape[-1] *= count
        else:
            shape = [count] + shape
        return jax.ShapeDtypeStruct(tuple(shape), self.array.dtype)

    def scratch(self, sizes):
        count = sizes[self.axis]
        return [pltpu.SemaphoreType.DMA((count,)), pltpu.SemaphoreType.DMA((count,))]

    def piece(self, ref, index, count):
        if self.cut is None:
            return ref
        size = self.array.shape[self.cut] // count
        where = [slice(None)] * len(self.array.shape)
        where[self.cut] = pl.ds(pl.multiple_of(index * size, size), size)
        if self.part[1] > 1:
            rows = self.array.shape[0] // self.part[1]
            where[0] = pl.ds(self.part[0] * rows, rows)
        return ref.at[tuple(where)]

    def copies(self, line, src, dst, send, recv):
        count, me = line.count(self.axis), line.index(self.axis)
        if self.beside:
            land = dst.at[:, pl.ds(pl.multiple_of(me * self.columns, self.columns), self.columns)]
        else:
            land = dst.at[me]
        made = [pltpu.make_async_copy(self.piece(src, me, count), land, send.at[0])]
        for step in range(1, count):
            peer = line.peer(self.axis, step)
            made.append(
                remote(
                    self.piece(src, peer, count),
                    land,
                    send.at[step],
                    recv.at[step],
                    line.place(self.axis, peer),
                )
            )
        return made

    def start(self, line, src, dst, send, recv):
        for copy in self.copies(line, src, dst, send, recv):
            copy.start()

    def middle(self, phase, *refs):
        pass

    def finish(self, line, src, dst, send, recv):
        for copy in self.copies(line, src, dst, send, recv):
            copy.wait()


class Settle:
    def __init__(self, array, summed, taps, placed):
        self.axes = ("dp", "mp")
        self.inside = True
        self.array = array
        self.summed = summed
        self.taps = taps
        self.placed = placed

    def result(self, sizes):
        n, m = sizes["mp"], sizes["dp"]
        self.ratio = n // m
        self.tail = tuple(self.array.shape[-2:])
        self.total = jax.ShapeDtypeStruct((n,) + self.tail, self.array.dtype)
        self.land = (m, self.ratio) + self.tail
        self.add = Rider("dp", self.array, None if self.summed else 1)
        self.outward = Rider("mp", self.total, 0)
        self.inward = Rider("dp", self.total, 0)
        if not self.placed:
            return jax.ShapeDtypeStruct(self.land, self.array.dtype)
        shape = (self.taps, self.ratio * self.tail[1] // self.taps, m * self.tail[0])
        return jax.ShapeDtypeStruct(shape, jnp.float32)

    def scratch(self, sizes):
        n, m = sizes["mp"], sizes["dp"]
        dtype = self.array.dtype
        refs = [pltpu.VMEM(self.land, dtype), pltpu.VMEM((n, 1) + self.tail, dtype)]
        if not self.summed:
            refs += [pltpu.VMEM((m, n, 1) + self.tail, dtype), pltpu.VMEM((n,) + self.tail, dtype)]
            refs += self.add.scratch(sizes)
        return refs + self.outward.scratch(sizes) + self.inward.scratch(sizes)

    def copies(self, step, line, src, dst, land, stage, *rest):
        if not self.summed:
            got, total = rest[:2]
            if step == 0:
                return self.add.copies(line, src, got, *rest[2:4])
            src, rest = total, rest[4:]
            step -= 1
        if step == 0:
            return self.outward.copies(line, src, stage, *rest[:2])
        return self.inward.copies(line, stage.at[:, 0], land, *rest[2:4])

    def start(self, *refs):
        for copy in self.copies(0, *refs):
            copy.start()

    def middle(self, phase, *refs):
        if self.summed and phase == 1:
            self.end(*refs)
            return
        for copy in self.copies(phase, *refs):
            copy.wait()
        if not self.summed and phase == 0:
            got, total = refs[5:7]

            @pl.loop(0, total.shape[0])
            def _(index):
                added_up = got[0, index, 0].astype(jnp.float32)
                for image in range(1, got.shape[0]):
                    added_up += got[image, index, 0].astype(jnp.float32)
                total[index] = added_up.astype(total.dtype)

        for copy in self.copies(phase + 1, *refs):
            copy.start()

    def finish(self, *refs):
        if not self.summed:
            self.end(*refs)

    def end(self, *refs):
        for copy in self.copies(1 if self.summed else 2, *refs):
            copy.wait()
        dst, land = refs[2:4]
        if not self.placed:
            dst[...] = land[...]
            return
        own = self.tail[1] // self.taps
        for half in range(self.ratio):
            for tap in range(self.taps):
                block = jnp.concatenate(
                    [
                        land[image, half, :, pl.ds(tap * own, own)].astype(jnp.float32)
                        for image in range(land.shape[0])
                    ],
                    axis=0,
                )
                dst[tap, pl.ds(half * own, own)] = block.T


def comm_call(
    kernel, inputs, out_shapes, scratch, riders, n, m, number, neighbours=True, after=None
):
    chips = n // 2
    sizes = {"dp": m, "mp": n, "all": m * n}
    ride_shapes = tuple(rider.result(sizes) for rider in riders)
    ride_scratch = [rider.scratch(sizes) for rider in riders]
    any_spec = pl.BlockSpec(memory_space=pl.ANY)
    ni, nr, no = len(inputs), len(riders), len(out_shapes)
    large = [index for index in range(ni) if inputs[index].size * inputs[index].dtype.itemsize > 2**20]

    def body(*refs):
        main_in, ride_in = list(refs[:ni]), refs[ni : ni + nr]
        rest = refs[ni + nr :]
        main_out, ride_out = rest[:no], rest[no : no + nr]
        rest = rest[no + nr :]
        main_scratch, rest = rest[: len(scratch)], rest[len(scratch) :]
        line = Line(chips, m)
        loads = []
        if large:
            load_sems, rest = rest[0], rest[1:]
            for place, index in enumerate(large):
                loads.append(
                    pltpu.make_async_copy(main_in[index], rest[place], load_sems.at[place])
                )
                main_in[index] = rest[place]
            rest = rest[len(large) :]
        for load in loads:
            load.start()

        def ready():
            for load in loads:
                load.wait()

        line.ready = ready
        line.barrier(sorted(set(axis for rider in riders for axis in rider.axes)), neighbours)
        riding = []
        for rider, src, dst, needs in zip(riders, ride_in, ride_out, ride_scratch):
            riding.append((rider, (line, src, dst) + tuple(rest[: len(needs)])))
            rest = rest[len(needs) :]
        for rider, refs_in in riding:
            rider.start(*refs_in)
        phases = [0, 1]

        def late():
            phases.pop(0)
            for rider, refs_in in riding:
                rider.middle(0, *refs_in)

        line.late = late
        kernel(line, *main_in, *main_out, *main_scratch)
        for phase in phases:
            for rider, refs_in in riding:
                rider.middle(phase, *refs_in)
        for rider, refs_in in riding:
            rider.finish(*refs_in)
        if after is not None:
            after(main_in, main_out, ride_out)

    return pl.pallas_call(
        body,
        out_shape=tuple(out_shapes) + ride_shapes,
        in_specs=[any_spec if index in large else whole(1)[0] for index in range(ni)]
        + [any_spec] * nr,
        out_specs=tuple(
            whole(no)
            + [whole(1)[0] if rider.inside else any_spec for rider in riders]
        ),
        scratch_shapes=list(scratch)
        + ([pltpu.SemaphoreType.DMA((len(large),))] if large else [])
        + [pltpu.VMEM(inputs[index].shape, inputs[index].dtype) for index in large]
        + [ref for needs in ride_scratch for ref in needs],
        compiler_params=comm_params(number),
    )(*inputs, *[rider.array for rider in riders])


def remote(src, dst, send, recv, target):
    return pltpu.make_async_remote_copy(
        src_ref=src,
        dst_ref=dst,
        send_sem=send,
        recv_sem=recv,
        device_id=target,
        device_id_type=MESH,
    )


def gather_sems(chips):
    return [pltpu.SemaphoreType.DMA((3, 2, chips)), pltpu.SemaphoreType.DMA((3, 2, chips))]


def line_gather(line, x_ref, slot, send, recv, on_own, on_pair):
    chips = line.chips
    z, c = line.z, line.c

    def hop(stream, step, src, block, target):
        return remote(src, slot(block), send.at[stream, 0, step], recv.at[stream, 0, step], target)

    def across(way, step, src, block):
        return remote(src, slot(block), send.at[2, way, step], recv.at[2, way, step], line.sibling)

    @pl.when(line.has_up)
    def _():
        hop(0, 1, x_ref, line.mp, line.up).start()

    @pl.when(line.has_down)
    def _():
        hop(1, 1, x_ref, line.mp, line.down).start()

    across(0, 0, x_ref, line.mp).start()
    slot(line.mp)[...] = x_ref[...]
    line.ready()
    on_own()
    across(0, 0, x_ref, line.mp).wait_recv()
    on_pair(z)
    for step in range(1, chips):
        below, above = z - step, z + step
        if step == chips - 1:
            line.late()

        @pl.when(below >= 0)
        def _():
            block = 2 * below + c
            hop(0, step, slot(block), block, line.up).wait_recv()
            if step + 1 < chips:

                @pl.when(line.has_up)
                def _():
                    hop(0, step + 1, slot(block), block, line.up).start()

            across(0, step, slot(block), block).start()

        @pl.when(above < chips)
        def _():
            block = 2 * above + c
            hop(1, step, slot(block), block, line.down).wait_recv()
            if step + 1 < chips:

                @pl.when(line.has_down)
                def _():
                    hop(1, step + 1, slot(block), block, line.down).start()

            across(1, step, slot(block), block).start()

        @pl.when(below >= 0)
        def _():
            across(0, step, slot(2 * below + c), 2 * below + c).wait_recv()
            on_pair(below)

        @pl.when(above < chips)
        def _():
            across(1, step, slot(2 * above + c), 2 * above + c).wait_recv()
            on_pair(above)

    @pl.when(line.has_up)
    def _():
        hop(0, 1, x_ref, line.mp, line.up).wait_send()

    @pl.when(line.has_down)
    def _():
        hop(1, 1, x_ref, line.mp, line.down).wait_send()

    across(0, 0, x_ref, line.mp).wait_send()
    for step in range(1, chips):
        below, above = z - step, z + step

        @pl.when(below >= 0)
        def _():
            block = 2 * below + c
            if step + 1 < chips:

                @pl.when(line.has_up)
                def _():
                    hop(0, step + 1, slot(block), block, line.up).wait_send()

            across(0, step, slot(block), block).wait_send()

        @pl.when(above < chips)
        def _():
            block = 2 * above + c
            if step + 1 < chips:

                @pl.when(line.has_down)
                def _():
                    hop(1, step + 1, slot(block), block, line.down).wait_send()

            across(1, step, slot(block), block).wait_send()


def scatter_scratch(chips, rows, cols, parts):
    block = (chips, rows, cols)
    return [
        pltpu.VMEM(block, jnp.float32),
        pltpu.VMEM(block, jnp.bfloat16),
        pltpu.VMEM(block, jnp.bfloat16),
        pltpu.VMEM((2,) + block, jnp.bfloat16),
        pltpu.SemaphoreType.DMA((2, 3, chips, parts)),
    ]


def line_scatter(line, scratch, parts, produce, finish, tile, side=()):
    chips = line.chips
    z = line.z
    kept, out_ref, in_ref, moving, sems = scratch
    count = kept.shape[1] // parts
    line.ready()

    def span(part):
        return pl.ds(part * count, count)

    def across(chip, part):
        return remote(
            out_ref.at[chip, span(part)],
            in_ref.at[chip, span(part)],
            sems.at[0, 0, chip, part],
            sems.at[1, 0, chip, part],
            line.sibling,
        )

    def hop(way, chip, part):
        target = line.up if way == 0 else line.down
        ref = moving.at[way, chip, span(part)]
        return remote(
            ref, ref, sems.at[0, 1 + way, chip, part], sems.at[1, 1 + way, chip, part], target
        )

    items = []
    for step in range(chips - 1):
        for part in range(parts):
            items.append((0, chips - 1 - step + z, part, step >= z))
            items.append((1, step - (chips - 1 - z), part, step >= chips - 1 - z))
    for part in range(parts):
        items.append((2, z, part, None))

    def run(active, body):
        if active is None:
            body()
        else:
            pl.when(active)(body)

    def start(item):
        way, chip, part, active = item

        def body():
            produce(chip, part, count, kept.at[chip], out_ref.at[chip])
            across(chip, part).start()

        run(active, body)

    def tiles(part, body):
        @pl.loop(0, count // tile)
        def _(index):
            body(pl.ds(pl.multiple_of(part * count + index * tile, tile), tile))

    def close(item):
        way, chip, part, active = item

        def body():
            across(chip, part).wait_recv()
            if way < 2:
                later = line.has_down if way == 0 else line.has_up

                @pl.when(later)
                def _():
                    hop(way, chip, part).wait_recv()

                    def add(rows):
                        moving[way, chip, rows] = (
                            kept[chip, rows]
                            + in_ref[chip, rows].astype(jnp.float32)
                            + moving[way, chip, rows].astype(jnp.float32)
                        ).astype(jnp.bfloat16)

                    tiles(part, add)

                @pl.when(jnp.logical_not(later))
                def _():
                    def add(rows):
                        moving[way, chip, rows] = (
                            kept[chip, rows] + in_ref[chip, rows].astype(jnp.float32)
                        ).astype(jnp.bfloat16)

                    tiles(part, add)

                hop(way, chip, part).start()
            else:

                def total(rows):
                    return kept[chip, rows] + in_ref[chip, rows].astype(jnp.float32)

                def from_side(side, rows):
                    return moving[side, chip, rows].astype(jnp.float32)

                both = jnp.logical_and(line.has_down, line.has_up)

                @pl.when(both)
                def _():
                    hop(0, chip, part).wait_recv()
                    hop(1, chip, part).wait_recv()
                    tiles(
                        part,
                        lambda rows: finish(
                            part, rows, total(rows) + from_side(0, rows) + from_side(1, rows)
                        ),
                    )

                for side, present in ((0, line.has_down), (1, line.has_up)):

                    @pl.when(jnp.logical_and(present, jnp.logical_not(both)))
                    def _():
                        hop(side, chip, part).wait_recv()
                        tiles(
                            part,
                            lambda rows: finish(part, rows, total(rows) + from_side(side, rows)),
                        )

        run(active, body)

    lag = 2
    side = list(side)
    for index, item in enumerate(items):
        start(item)
        if index >= lag:
            close(items[index - lag])
            if index % 2 == 0 and side:
                side.pop(0)()
    for step in side:
        step()
    for item in items[-lag:]:
        close(item)
    for way, chip, part, active in items:

        def body():
            across(chip, part).wait_send()
            if way < 2:
                hop(way, chip, part).wait_send()

        run(active, body)


def whole(count):
    return [pl.BlockSpec(memory_space=pltpu.VMEM)] * count


def comm_params(number):
    return pltpu.CompilerParams(
        collective_id=number, has_side_effects=True, vmem_limit_bytes=VMEM_BYTES
    )


def pick(c, low, high):
    return jnp.where(c == 0, low, high), jnp.where(c == 0, high, low)


def group_matrix(own, size, count):
    groups = [lax.broadcasted_iota(jnp.int32, (own, own), axis) // size for axis in range(2)]
    return jnp.where(groups[0] == groups[1], 1.0 / (count * size), 0.0)


def norm_spread(values, gain, spread_ref, stat_ref, size, breadth):
    pixels, own = values.shape
    tile = 512
    matrix = group_matrix(own, size, pixels)
    stat_ref[...] = jnp.zeros_like(stat_ref)
    column = lax.broadcasted_iota(jnp.int32, (tile, own), 0) % breadth

    def tiles(body):
        @pl.loop(0, pixels // tile)
        def _(index):
            base = pl.multiple_of(index * tile, tile)
            body(base, pl.ds(base, tile))

    def add(base, rows):
        stat_ref[0:1] += jnp.sum(values[rows], axis=0, keepdims=True)

    tiles(add)
    average = jnp.dot(stat_ref[...], matrix, precision=PRECISE)[0:1]

    def square(base, rows):
        centre = values[rows] - average
        stat_ref[1:2] += jnp.sum(centre * centre, axis=0, keepdims=True)

    tiles(square)
    inverse = lax.rsqrt(jnp.dot(stat_ref[...], matrix, precision=PRECISE)[1:2] + GROUP_EPSILON)
    stat_ref[2:3] = inverse

    def write(base, rows):
        normed = (values[rows] - average) * inverse
        values[rows] = normed
        pre_act = normed * gain
        hidden = pre_act / (1.0 + jnp.exp(-pre_act))
        below = pl.ds(base + breadth, tile)
        left = jnp.where(column == 0, 0.0, pltpu.roll(hidden, 1, 0))
        right = jnp.where(column == breadth - 1, 0.0, pltpu.roll(hidden, tile - 1, 0))
        for place, value in enumerate((left, hidden, right)):
            spread_ref[below, place * own : (place + 1) * own] = value.astype(jnp.bfloat16)

    tiles(write)
    nothing = jnp.zeros((breadth, 3 * own), jnp.bfloat16)
    spread_ref[pl.ds(0, breadth)] = nothing
    spread_ref[pl.ds(breadth + pixels, breadth)] = nothing


def norm_shapes(pixels, own, cols):
    return (
        jax.ShapeDtypeStruct((pixels, own), jnp.float32),
        jax.ShapeDtypeStruct((pixels + 2 * cols, 3 * own), jnp.bfloat16),
        jax.ShapeDtypeStruct((8, own), jnp.float32),
    )


def conv_scatter_kernel(breadth, size, line, x_ref, w_ref, *refs):
    normed = size > 0
    v_ref, refs = (refs[0], refs[1:]) if normed else (None, refs)
    o_ref, refs = refs[0], refs[1:]
    spread_ref, stat_ref, *scratch = refs if normed else (None, None) + tuple(refs)
    pixels, own = o_ref.shape
    tile = 512

    def produce(chip, part, count, mine, other):
        columns = pl.ds(pl.multiple_of(chip * 2 * own, 2 * own), 2 * own)

        @pl.loop(0, count // tile)
        def _(index):
            base = pl.multiple_of(part * count + index * tile, tile)
            total = jnp.zeros((tile, 2 * own), jnp.float32)
            for i in range(3):
                total += jnp.dot(
                    x_ref[pl.ds(base + i * breadth, tile)],
                    w_ref[i, :, columns],
                    preferred_element_type=jnp.float32,
                )
            first, second = pick(line.c, total[:, :own], total[:, own:])
            mine[pl.ds(base, tile)] = first
            other[pl.ds(base, tile)] = second.astype(jnp.bfloat16)

    def finish(part, rows, total):
        o_ref[rows] = total + v_ref[0:1] if normed else total

    line_scatter(line, scratch, CONV_PARTS, produce, finish, tile)
    if normed:
        norm_spread(o_ref, v_ref[1:2], spread_ref, stat_ref, size, breadth)


def side_by_side(hidden):
    rows, cols, depth = hidden.shape
    padded = jnp.pad(hidden, ((1, 1), (1, 1), (0, 0)))
    return jnp.concatenate([padded[:, j : j + cols] for j in range(3)], axis=2).reshape(
        (rows + 2) * cols, 3 * depth
    )


def rows_of(*vectors):
    rows = jnp.stack(vectors)
    return jnp.pad(rows, ((0, 8 - rows.shape[0]), (0, 0)))


def conv_scatter_fused(spread, kernel, cols, n, m, number, shift=None, gain=None, size=0):
    own = kernel.shape[2] // n
    depth = kernel.shape[1]
    pixels = spread.shape[0] - 2 * cols
    return comm_call(
        partial(conv_scatter_kernel, cols, size),
        (spread, kernel.reshape(3, 3 * depth, kernel.shape[2]))
        + ((rows_of(shift, gain),) if size else ()),
        norm_shapes(pixels, own, cols)[: 3 if size else 1],
        scatter_scratch(n // 2, pixels, own, CONV_PARTS),
        (),
        n,
        m,
        number,
    )


def conv_back_kernel(breadth, size, extra, line, g_ref, w_ref, x_ref, n_ref, v_ref, *refs):
    refs = list(refs)
    more_ref = refs.pop(0) if extra else None
    low_ref, wg_ref, stat_ref, acc_ref, held, sums, send, recv = refs
    chips = line.chips
    pixels, own = g_ref.shape
    wide = w_ref.shape[1]
    tile, long = 512, 1024
    zero = jnp.zeros((breadth, own), jnp.bfloat16)
    for block in range(2 * chips):
        held[block, pl.ds(0, breadth)] = zero
        held[block, pl.ds(breadth + pixels, breadth)] = zero

    def slot(block):
        return held.at[block, pl.ds(breadth, pixels)]

    def beside(base, count, chip):
        rows = pl.ds(base, count)
        return [held[2 * chip, rows], held[2 * chip + 1, rows]]

    def on_own():
        @pl.loop(0, pixels // tile)
        def _(index):
            acc_ref[pl.ds(pl.multiple_of(index * tile, tile), tile)] = jnp.zeros(
                (tile, wide), jnp.float32
            )

    def on_pair(chip):
        columns = pl.ds(pl.multiple_of(chip * 2 * own, 2 * own), 2 * own)

        @pl.loop(0, pixels // tile)
        def _(index):
            base = pl.multiple_of(index * tile, tile)
            shifted = []
            for i in range(3):
                shifted += beside(base + (2 - i) * breadth, tile, chip)
            acc_ref[pl.ds(base, tile)] += product(
                jnp.concatenate(shifted, axis=1),
                jnp.concatenate([w_ref[i, :, columns] for i in range(3)], axis=1),
                True,
            )

        sums[...] = jnp.zeros_like(sums)

        @pl.loop(0, pixels // long)
        def _(index):
            base = pl.multiple_of(index * long, long)
            sums[...] += lax.dot_general(
                jnp.concatenate(beside(base + breadth, long, chip), axis=1),
                jnp.concatenate(
                    [x_ref[pl.ds(base + i * breadth, long)] for i in range(3)], axis=1
                ),
                (((0,), (0,)), ((), ())),
                preferred_element_type=jnp.float32,
            )

        wg_ref[chip] = sums[...].astype(jnp.bfloat16)

    line_gather(line, g_ref, slot, send, recv, on_own, on_pair)

    gain, inverse = v_ref[0:1], v_ref[1:2]
    stat_ref[...] = jnp.zeros_like(stat_ref)
    column = lax.broadcasted_iota(jnp.int32, (tile, own), 0) % breadth

    @pl.loop(0, pixels // tile)
    def _(index):
        rows = pl.ds(pl.multiple_of(index * tile, tile), tile)
        left = jnp.where(
            column == breadth - 1, 0.0, pltpu.roll(acc_ref[rows, 0:own], tile - 1, 0)
        )
        right = jnp.where(column == 0, 0.0, pltpu.roll(acc_ref[rows, 2 * own : wide], 1, 0))
        incoming = left + acc_ref[rows, own : 2 * own] + right
        normed = n_ref[rows]
        pre_act = normed * gain
        sigmoid_part = 1.0 / (1.0 + jnp.exp(-pre_act))
        through = incoming * sigmoid_part * (1.0 + pre_act * (1.0 - sigmoid_part))
        acc_ref[rows, 0:own] = through
        stat_ref[0:1] += jnp.sum(through * normed, axis=0, keepdims=True)
        stat_ref[1:2] += jnp.sum(through, axis=0, keepdims=True)

    means = jnp.dot(stat_ref[...] * gain, group_matrix(own, size, pixels), precision=PRECISE)
    second_mean, first_mean = means[0:1], means[1:2]

    @pl.loop(0, pixels // tile)
    def _(index):
        rows = pl.ds(pl.multiple_of(index * tile, tile), tile)
        outgoing = inverse * (
            acc_ref[rows, 0:own] * gain - first_mean - n_ref[rows] * second_mean
        )
        stat_ref[2:3] += jnp.sum(outgoing, axis=0, keepdims=True)
        if extra:
            outgoing = outgoing + more_ref[rows]
        low_ref[rows] = outgoing.astype(jnp.bfloat16)


def conv_back_fused(
    grad_low, spread, kernel, normed, inverse, gain, size, cols, n, m, number, riders, more=()
):
    pixels, own = grad_low.shape
    depth = kernel.shape[1]
    chips = n // 2
    vectors = rows_of(gain, inverse)
    return comm_call(
        partial(conv_back_kernel, cols, size, len(more) > 0),
        (grad_low, kernel.reshape(3, 3 * depth, kernel.shape[2]), spread, normed, vectors)
        + tuple(more),
        (
            jax.ShapeDtypeStruct((pixels, depth), jnp.bfloat16),
            jax.ShapeDtypeStruct((chips, 2 * own, 9 * depth), jnp.bfloat16),
            jax.ShapeDtypeStruct((8, own), jnp.float32),
        ),
        [
            pltpu.VMEM((pixels, 3 * depth), jnp.float32),
            pltpu.VMEM((n, pixels + 2 * cols, own), jnp.bfloat16),
            pltpu.VMEM((2 * own, 9 * depth), jnp.float32),
        ]
        + gather_sems(chips),
        riders,
        n,
        m,
        number,
    )


def join_columns(acc, cols):
    pixels, wide = acc.shape
    depth = wide // 3
    planes = acc.reshape(-1, cols, wide)
    none = jnp.zeros_like(planes[:, :1, :depth])
    left = jnp.concatenate([planes[:, 1:, :depth], none], axis=1)
    right = jnp.concatenate([none, planes[:, :-1, 2 * depth :]], axis=1)
    return (left + planes[:, :, depth : 2 * depth] + right).reshape(pixels, depth)


def product(x, w, turned):
    return lax.dot_general(
        x, w, (((1,), (1 if turned else 0,)), ((), ())), preferred_element_type=jnp.float32
    )


def outer_steps(grad, left, right, cut):
    def step(start):
        grad[pl.ds(start, cut)] = lax.dot_general(
            left[:, pl.ds(start, cut)],
            right[...],
            (((0,), (0,)), ((), ())),
            preferred_element_type=jnp.float32,
        ).astype(grad.dtype)

    return [partial(step, start) for start in range(0, left.shape[1], cut)]


class NormAfter:
    def __init__(self, scale, shift, more=()):
        self.inputs = (rows_of(scale, shift),) + tuple(more)

    def shapes(self, tokens, width):
        return (
            jax.ShapeDtypeStruct((tokens, width), jnp.float32),
            jax.ShapeDtypeStruct((tokens, 128), jnp.float32),
            jax.ShapeDtypeStruct((tokens, width), jnp.bfloat16),
        )

    def run(self, in_refs, o_ref, out_refs):
        v_ref, normed_ref, inverse_ref, low_ref = in_refs[0], *out_refs
        tile = 16

        @pl.loop(0, o_ref.shape[0] // tile)
        def _(index):
            rows = pl.ds(pl.multiple_of(index * tile, tile), tile)
            stream = o_ref[rows]
            for ref in in_refs[1:]:
                stream = stream + ref[rows]
            o_ref[rows] = stream
            centre = stream - jnp.mean(stream, axis=1, keepdims=True)
            inverse = lax.rsqrt(jnp.mean(centre * centre, axis=1, keepdims=True) + LAYER_EPSILON)
            normed = centre * inverse
            normed_ref[rows] = normed
            inverse_ref[rows] = jnp.broadcast_to(inverse, (tile, 128))
            low_ref[rows] = (normed * (1.0 + v_ref[0:1]) + v_ref[1:2]).astype(jnp.bfloat16)


class NormBack:
    def __init__(self, scale, normed, inverse, carry):
        self.inputs = (rows_of(scale), normed, inverse, carry)

    def shapes(self, tokens, width):
        return (
            jax.ShapeDtypeStruct((tokens, width), jnp.bfloat16),
            jax.ShapeDtypeStruct((8, width), jnp.float32),
        )

    def run(self, in_refs, o_ref, out_refs):
        v_ref, normed_ref, inverse_ref, carry_ref = in_refs
        low_ref, sum_ref = out_refs
        tile = 16
        sum_ref[...] = jnp.zeros_like(sum_ref)

        @pl.loop(0, o_ref.shape[0] // tile)
        def _(index):
            rows = pl.ds(pl.multiple_of(index * tile, tile), tile)
            incoming, normed = o_ref[rows], normed_ref[rows]
            sum_ref[0:1] += jnp.sum(incoming * normed, axis=0, keepdims=True)
            sum_ref[1:2] += jnp.sum(incoming, axis=0, keepdims=True)
            through = incoming * (1.0 + v_ref[0:1])
            outgoing = inverse_ref[rows][:, 0:1] * (
                through
                - jnp.mean(through, axis=1, keepdims=True)
                - normed * jnp.mean(through * normed, axis=1, keepdims=True)
            )
            grad = carry_ref[rows].astype(jnp.float32) + outgoing
            o_ref[rows] = grad
            low_ref[rows] = grad.astype(jnp.bfloat16)


def followed(kernel, ni, no, post):
    count = len(post.inputs)

    def run(line, *refs):
        inputs, more, rest = refs[:ni], refs[ni : ni + count], refs[ni + count :]
        outputs, rest = rest[:no], rest[no:]
        made = len(post.shapes(8, 128))
        kernel(line, *inputs, *outputs, *rest[made:])
        post.run(more, outputs[0], rest[:made])

    return run


def tokens_scatter_kernel(turned, beside, line, x_ref, w_ref, *refs):
    side = ()
    if beside:
        left, right, o_ref, grad, *scratch = refs
        side = outer_steps(grad, left, right, 128)
    else:
        o_ref, *scratch = refs
    tokens, width = o_ref.shape
    cut = width // TOKEN_PARTS
    depth = x_ref.shape[1] // w_ref.shape[0]

    def produce(chip, part, count, mine, other):
        rows = pl.ds(pl.multiple_of(chip * 2 * tokens, 2 * tokens), 2 * tokens)
        columns = pl.ds(part * cut, cut)
        total = None
        for j in range(w_ref.shape[0]):
            w = w_ref[j, columns] if turned else w_ref[j, :, columns]
            term = product(x_ref[rows, pl.ds(j * depth, depth)], w, turned)
            total = term if total is None else total + term
        first, second = pick(line.c, total[:tokens], total[tokens:])
        mine[pl.ds(part * count, count)] = first
        other[pl.ds(part * count, count)] = second.astype(jnp.bfloat16)

    def finish(part, rows, total):
        o_ref[:, pl.ds(part * cut, cut)] = total

    line_scatter(line, scratch, TOKEN_PARTS, produce, finish, tokens, side)


def outer_shapes(outer):
    if not outer:
        return ()
    return (jax.ShapeDtypeStruct((outer[0].shape[1], outer[1].shape[1]), jnp.bfloat16),)


def tokens_scatter(x, w, turned, n, m, number, post, riders=(), outer=()):
    tokens = x.shape[0] // n
    width = w.shape[1] if turned else w.shape[2]
    return comm_call(
        followed(
            partial(tokens_scatter_kernel, turned, len(outer) > 0),
            2 + len(outer),
            2 if outer else 1,
            post,
        ),
        (x, w) + tuple(outer) + post.inputs,
        (jax.ShapeDtypeStruct((tokens, width), jnp.float32),)
        + outer_shapes(outer)
        + post.shapes(tokens, width),
        scatter_scratch(n // 2, TOKEN_PARTS * tokens, width // TOKEN_PARTS, TOKEN_PARTS),
        riders,
        n,
        m,
        number,
    )


def add_outer(total, left, right, rows):
    cut = min(left.shape[1], 512)
    for start in range(0, left.shape[1], cut):
        total[pl.ds(start, cut)] += lax.dot_general(
            left[rows, pl.ds(start, cut)],
            right[rows],
            (((0,), (0,)), ((), ())),
            preferred_element_type=jnp.float32,
        )


def tokens_gather_kernel(
    turned, shape_out, outs, keep, side, beside, cols, chained, line, x_ref, w_ref, *refs
):
    refs = list(refs)
    chain_w = refs.pop(0) if chained else None
    left = refs.pop(0) if side else None
    outer = (refs.pop(0), refs.pop(0)) if beside else None
    held = refs.pop(0) if keep else None
    results = [refs.pop(0) for _ in range(outs)]
    grad = refs.pop(0) if side else None
    outer_grad = refs.pop(0) if beside else None
    chain_out = refs.pop(0) if chained else None
    total = refs.pop(0) if side else None
    if not keep:
        held = refs.pop(0)
    send, recv = refs
    tokens = x_ref.shape[0]
    across = w_ref.shape[1 if turned else 2]
    cut = min(across, 512)

    def slot(block):
        return held.at[pl.ds(pl.multiple_of(block * tokens, tokens), tokens)]

    def store_pixels(ref, chip, value):
        depth = value.shape[1] // 4
        base = chip * 8 * tokens
        for row in range(4 * tokens // cols):
            for tap in range(4):
                start = base + (2 * row + tap // 2) * cols + tap % 2
                ref[pl.Slice(start, cols // 2, 2)] = value[
                    row * (cols // 2) : (row + 1) * (cols // 2), tap * depth : (tap + 1) * depth
                ]

    def on_pair(chip):
        rows = pl.ds(pl.multiple_of(chip * 2 * tokens, 2 * tokens), 2 * tokens)
        for j in range(w_ref.shape[0]):
            for start in range(0, across, cut):
                w = w_ref[j, pl.ds(start, cut)] if turned else w_ref[j, :, pl.ds(start, cut)]
                values = shape_out(product(held[rows], w, turned))
                for ref, value in zip(results, values):
                    if cols:
                        store_pixels(ref, chip, value)
                    else:
                        ref[rows, pl.ds(j * across + start, cut)] = value.astype(ref.dtype)
        if chained:
            for start in range(0, chain_w.shape[1], 512):
                columns = pl.ds(start, 512)
                chain_out[rows, columns] = product(
                    results[-1][rows], chain_w[:, columns], False
                ).astype(jnp.bfloat16)
        if side:
            add_outer(total, held, left, rows)

    def on_own():
        if side:
            total[...] = jnp.zeros_like(total)
        if beside:
            for step in outer_steps(outer_grad, *outer, 256):
                step()

    line_gather(line, x_ref, slot, send, recv, on_own, on_pair)
    if side:
        grad[...] = total[...].astype(grad.dtype)


def tokens_gather(
    x,
    w,
    turned,
    kinds,
    shape_out,
    n,
    m,
    number,
    riders=(),
    left=None,
    outer=(),
    cols=0,
    chain=(),
    keep=True,
):
    tokens, width = x.shape
    across = w.shape[0] * w.shape[1 if turned else 2]
    side = left is not None
    grads = ((width, left.shape[1]),) if side else ()
    shape = (tokens * n * 4, across // 4) if cols else (tokens * n, across)
    return comm_call(
        partial(
            tokens_gather_kernel,
            turned,
            shape_out,
            len(kinds),
            keep,
            side,
            len(outer) > 0,
            cols,
            len(chain) > 0,
        ),
        (x, w) + tuple(chain) + ((left,) if side else ()) + tuple(outer),
        tuple(jax.ShapeDtypeStruct((tokens * n, width), x.dtype) for _ in range(int(keep)))
        + tuple(jax.ShapeDtypeStruct(shape, kind) for kind in kinds)
        + tuple(jax.ShapeDtypeStruct(grad, jnp.bfloat16) for grad in grads)
        + outer_shapes(outer)
        + tuple(jax.ShapeDtypeStruct((tokens * n, w2.shape[1]), jnp.bfloat16) for w2 in chain),
        [pltpu.VMEM(grad, jnp.float32) for grad in grads]
        + [pltpu.VMEM((tokens * n, width), x.dtype) for _ in range(int(not keep))]
        + gather_sems(n // 2),
        riders,
        n,
        m,
        number,
    )


def exchange(riders, n, m, number):
    return comm_call(lambda line: None, (), (), [], riders, n, m, number, neighbours=False)


def exchange_norm(image_rows, gain, size, cols, riders, n, m, number):
    own = image_rows.shape[1] // n
    count = image_rows.shape[0]

    def after(main_in, main_out, ride_out):
        normed, spread_ref, stat_ref = main_out

        @pl.loop(0, n)
        def _(index):
            normed[pl.ds(pl.multiple_of(index * count, count), count)] = ride_out[0][index].astype(
                jnp.float32
            )

        norm_spread(normed, main_in[0][0:1], spread_ref, stat_ref, size, cols)

    return comm_call(
        lambda line, *refs: None,
        (rows_of(gain),),
        norm_shapes(count * n, own, cols),
        [],
        (Rider("mp", image_rows, 1, inside=True),) + tuple(riders),
        n,
        m,
        number,
        neighbours=False,
        after=after,
    )


def tiled_up(vector):
    count = -(-vector.shape[0] // 1024) * 1024
    return jnp.pad(vector.astype(jnp.float32), (0, count - vector.shape[0])).reshape(-1, 128)


def attend_scatter_kernel(line, x_ref, valid_ref, w_ref, o_ref, mixed_ref, *scratch):
    tokens, width = o_ref.shape
    wide = mixed_ref.shape[1]
    cut = width // TOKEN_PARTS
    scale = 1.0 / math.sqrt(HEAD_DIM)

    def attend(rows):
        for head in range(wide // HEAD_DIM):
            where = [pl.ds(j * wide + head * HEAD_DIM, HEAD_DIM) for j in range(3)]
            scores = product(x_ref[rows, where[0]], x_ref[:, where[1]], True) * scale
            scores = jnp.where(valid_ref[0:1] > 0.5, scores, MASKED_SCORE)
            exponent = jnp.exp(scores - jnp.max(scores, axis=1, keepdims=True))
            inverse = 1.0 / jnp.sum(exponent, axis=1, keepdims=True)
            mixed_ref[rows, pl.ds(head * HEAD_DIM, HEAD_DIM)] = product(
                (exponent * inverse).astype(jnp.bfloat16), x_ref[:, where[2]], False
            ).astype(jnp.bfloat16)

    def produce(chip, part, count, mine, other):
        rows = pl.ds(pl.multiple_of(chip * 2 * tokens, 2 * tokens), 2 * tokens)
        if part == 0:
            attend(rows)
        total = product(mixed_ref[rows], w_ref[:, pl.ds(part * cut, cut)], False)
        first, second = pick(line.c, total[:tokens], total[tokens:])
        mine[pl.ds(part * count, count)] = first
        other[pl.ds(part * count, count)] = second.astype(jnp.bfloat16)

    def finish(part, rows, total):
        o_ref[:, pl.ds(part * cut, cut)] = total

    line_scatter(line, scratch, TOKEN_PARTS, produce, finish, tokens)


def attend_scatter(qkv_rows, valid, out_weight, n, m, number, post):
    total = qkv_rows.shape[0]
    tokens = total // n
    width = out_weight.shape[1]
    return comm_call(
        followed(attend_scatter_kernel, 3, 2, post),
        (qkv_rows, jnp.broadcast_to(valid[None], (8, total)), out_weight) + post.inputs,
        (
            jax.ShapeDtypeStruct((tokens, width), jnp.float32),
            jax.ShapeDtypeStruct((total, out_weight.shape[0]), jnp.bfloat16),
        )
        + post.shapes(tokens, width),
        scatter_scratch(n // 2, TOKEN_PARTS * tokens, width // TOKEN_PARTS, TOKEN_PARTS),
        (),
        n,
        m,
        number,
    )


def attend_gather_kernel(
    line,
    g_ref,
    w_ref,
    x_ref,
    valid_ref,
    mixed_ref,
    left,
    right,
    grad_ref,
    out_ref,
    outer_grad,
    held,
    keys_sum,
    values_sum,
    out_sum,
    send,
    recv,
):
    tokens = g_ref.shape[0]
    wide = w_ref.shape[0]
    heads = wide // HEAD_DIM
    scale = 1.0 / math.sqrt(HEAD_DIM)

    def slot(block):
        return held.at[pl.ds(pl.multiple_of(block * tokens, tokens), tokens)]

    def on_own():
        keys_sum[...] = jnp.zeros_like(keys_sum)
        values_sum[...] = jnp.zeros_like(values_sum)
        out_sum[...] = jnp.zeros_like(out_sum)
        for step in outer_steps(outer_grad, left, right, 256):
            step()

    def on_pair(chip):
        rows = pl.ds(pl.multiple_of(chip * 2 * tokens, 2 * tokens), 2 * tokens)
        for head in range(heads):
            place = pl.ds(head * HEAD_DIM, HEAD_DIM)
            where = [pl.ds(j * wide + head * HEAD_DIM, HEAD_DIM) for j in range(3)]
            grad = product(held[rows], w_ref[place], True).astype(jnp.bfloat16)
            query = x_ref[rows, where[0]]
            scores = product(x_ref[:, where[1]], query, True) * scale
            scores = jnp.where(valid_ref[:, 0:1] > 0.5, scores, MASKED_SCORE)
            exponent = jnp.exp(scores - jnp.max(scores, axis=0, keepdims=True))
            probs = exponent * (1.0 / jnp.sum(exponent, axis=0, keepdims=True))
            values_sum[:, place] += product(probs.astype(jnp.bfloat16), grad, False)
            grad_probs = product(x_ref[:, where[2]], grad, True)
            inner = jnp.sum(probs * grad_probs, axis=0, keepdims=True)
            grad_scores = (probs * (grad_probs - inner) * scale).astype(jnp.bfloat16)
            keys_sum[:, place] += product(grad_scores, query, False)
            grad_ref[rows, where[0]] = lax.dot_general(
                grad_scores,
                x_ref[:, where[1]],
                (((0,), (0,)), ((), ())),
                preferred_element_type=jnp.float32,
            ).astype(jnp.bfloat16)
        add_outer(out_sum, mixed_ref, held, rows)

    line_gather(line, g_ref, slot, send, recv, on_own, on_pair)
    grad_ref[:, pl.ds(wide, wide)] = keys_sum[...].astype(jnp.bfloat16)
    grad_ref[:, pl.ds(2 * wide, wide)] = values_sum[...].astype(jnp.bfloat16)
    out_ref[...] = out_sum[...].astype(jnp.bfloat16)


def attend_gather(grad_mid, out_weight, qkv_rows, valid, mixed_low, outer, n, m, number, riders):
    tokens, width = grad_mid.shape
    total = tokens * n
    wide = out_weight.shape[0]
    return comm_call(
        attend_gather_kernel,
        (
            grad_mid,
            out_weight,
            qkv_rows,
            jnp.broadcast_to(valid[:, None], (total, 128)),
            mixed_low,
        )
        + tuple(outer),
        (
            jax.ShapeDtypeStruct((total, 3 * wide), jnp.bfloat16),
            jax.ShapeDtypeStruct((wide, width), jnp.bfloat16),
        )
        + outer_shapes(outer),
        [
            pltpu.VMEM((total, width), jnp.bfloat16),
            pltpu.VMEM((total, wide), jnp.float32),
            pltpu.VMEM((total, wide), jnp.float32),
            pltpu.VMEM((wide, width), jnp.float32),
        ]
        + gather_sems(n // 2),
        riders,
        n,
        m,
        number,
    )


def gelu_both(value):
    factor = math.sqrt(2.0 / math.pi)
    square = value * value
    bent = jnp.tanh(factor * value * (1.0 + 0.044715 * square))
    half = 0.5 * (1.0 + bent)
    slope = half + 0.5 * value * (1.0 - bent * bent) * factor * (1.0 + 3 * 0.044715 * square)
    return slope, value * half


def local(
    image,
    embedding,
    extents,
    gain_first,
    conv_first,
    gain_second,
    conv_second,
    shift_weight,
    down_weight,
    ada_weight,
    qkv_weight,
    out_weight,
    up_weight,
    proj_weight,
    cotangent,
):
    strip_rows, canvas_cols, channel_count = (image.shape[1], image.shape[2], image.shape[3])
    width_all = out_weight.shape[1]
    n = lax.axis_size("mp")
    m = lax.axis_size("dp")
    me_mp = lax.axis_index("mp")
    me_dp = lax.axis_index("dp")
    rows_all = strip_rows * n
    pixel_total = rows_all * canvas_cols
    own = channel_count // n
    size = channel_count // GROUPS
    token_rows = strip_rows // 2
    token_cols = canvas_cols // 2
    local_tokens = token_rows * token_cols
    token_total = local_tokens * n
    local_width = out_weight.shape[0]

    fused = own % 128 == 0 and n == 2 * m
    shift_vector = jnp.dot(embedding, shift_weight, preferred_element_type=jnp.float32)[0]
    columns = jnp.dot(embedding, ada_weight, preferred_element_type=jnp.float32)[0]
    own_first = lax.dynamic_slice_in_dim(gain_first, me_mp * own, own)
    own_second = lax.dynamic_slice_in_dim(gain_second, me_mp * own, own)
    riders = (Rider("mp", tiled_up(columns)),)
    if fused:
        normed_first, spread_first, stats, pixels_low, modulation = exchange_norm(
            image[0].reshape(-1, channel_count), own_first, size, canvas_cols, riders, n, m, 12
        )
        inverse_first = stats[2]
    else:
        (modulation,) = exchange(riders, n, m, 12)
        pixels_low = lax.all_to_all(image[0], "mp", 2, 0, tiled=True)
    modulation = modulation.reshape(n, -1)[:, : columns.shape[0]].reshape(-1)
    scale_attend = modulation[:width_all]
    shift_attend = modulation[width_all : 2 * width_all]
    scale_mlp = modulation[2 * width_all : 3 * width_all]
    shift_mlp = modulation[3 * width_all :]

    pixels = pixels_low.astype(jnp.float32).reshape(pixel_total, own)
    if fused:
        hidden_first = hidden_second = None
        normed_second, spread_second, stats = conv_scatter_fused(
            spread_first, conv_first, canvas_cols, n, m, 0, shift_vector, own_second, size
        )
        inverse_second = stats[2]
        (conv_again,) = conv_scatter_fused(spread_second, conv_second, canvas_cols, n, m, 1)
    else:
        spread_first = spread_second = None
        normed_first, inverse_first = group_forward(pixels, size)
        hidden_first = (
            jax.nn.silu(normed_first * own_first)
            .astype(jnp.bfloat16)
            .reshape(rows_all, canvas_cols, own)
        )
        conv_output = conv_scatter(hidden_first, conv_first, n) + shift_vector
        normed_second, inverse_second = group_forward(conv_output, size)
        hidden_second = (
            jax.nn.silu(normed_second * own_second)
            .astype(jnp.bfloat16)
            .reshape(rows_all, canvas_cols, own)
        )
        conv_again = conv_scatter(hidden_second, conv_second, n)
    residual = pixels + conv_again
    down_patch = (
        residual.astype(jnp.bfloat16)
        .reshape(rows_all // 2, 2, token_cols, 2, own)
        .transpose(0, 2, 1, 3, 4)
        .reshape(token_total, 4 * own)
    )
    down_matrix = down_weight.reshape(4 * own, width_all)
    stream, normed_attend, inverse_attend, input_attend = tokens_scatter(
        down_patch, down_matrix[None], False, n, m, 2, NormAfter(scale_attend, shift_attend)
    )
    all_attend, qkv_rows = tokens_gather(
        input_attend, qkv_weight, False, (jnp.bfloat16,), lambda value: (value,), n, m, 3
    )
    token_index = jnp.arange(token_total, dtype=jnp.int32)
    key_valid = (token_index // token_cols < extents[0, 0]) & (
        token_index % token_cols < extents[0, 1]
    )
    valid = key_valid.astype(jnp.float32)
    stream_mid, mixed_low, normed_mlp, inverse_mlp, input_mlp = attend_scatter(
        qkv_rows, valid, out_weight, n, m, 4, NormAfter(scale_mlp, shift_mlp, (stream,))
    )
    all_mlp, slope, activated, projected = tokens_gather(
        input_mlp,
        up_weight[None],
        False,
        (jnp.bfloat16, jnp.bfloat16),
        gelu_both,
        n,
        m,
        5,
        chain=(proj_weight,),
    )
    final_stream = stream_mid + scatter_rows(projected)
    output = final_stream.astype(jnp.bfloat16).reshape(1, token_rows, token_cols, width_all)

    grad_final_low = cotangent[0].reshape(local_tokens, width_all)
    all_final = gather_rows(lax.optimization_barrier((grad_final_low, qkv_rows))[0])
    grad_act = jnp.einsum("le,fe->lf", all_final, proj_weight, preferred_element_type=jnp.float32)
    grad_upper = (grad_act * slope.astype(jnp.float32)).astype(jnp.bfloat16)
    grad_mid, grad_proj, grad_mid_low, mlp_sums = tokens_scatter(
        grad_upper,
        up_weight[None],
        True,
        n,
        m,
        6,
        NormBack(scale_mlp, normed_mlp, inverse_mlp, grad_final_low),
        (),
        (activated, all_final),
    )
    grad_qkv, grad_out, grad_up = attend_gather(
        grad_mid_low,
        out_weight,
        qkv_rows,
        valid,
        mixed_low,
        (all_mlp, grad_upper),
        n,
        m,
        7,
        (),
    )
    _, grad_stream_low, attend_sums, sums_proj, sums_out = tokens_scatter(
        grad_qkv,
        qkv_weight,
        True,
        n,
        m,
        8,
        NormBack(scale_attend, normed_attend, inverse_attend, grad_mid),
        (Rider("dp", grad_proj, 1, part=(0, 2)), Rider("dp", grad_out, 1)),
    )
    grad_modulation = jnp.concatenate(
        [
            tiled_up(piece)
            for piece in jnp.concatenate([attend_sums[:2], mlp_sums[:2]]).reshape(n, -1)
        ]
    )
    grad_residual, grad_down, grad_qkv_weight, sums_more, ada_columns = tokens_gather(
        grad_stream_low,
        down_matrix[None],
        True,
        (jnp.float32,),
        lambda value: (value,),
        n,
        m,
        9,
        (
            Rider("dp", grad_proj, 1, part=(1, 2)),
            Rider("mp", grad_modulation, 0),
        ),
        down_patch,
        (all_attend, grad_qkv),
        canvas_cols if fused else 0,
        keep=False,
    )
    ada_columns = added(ada_columns).reshape(-1)[: columns.shape[0]]
    if not fused:
        grad_residual = (
            grad_residual.reshape(rows_all // 2, token_cols, 2, 2, own)
            .transpose(0, 2, 1, 3, 4)
            .reshape(pixel_total, own)
        )
    def back(grad_low, hidden, spread, kernel, normed, inverse, gain, number, riders, more=()):
        if fused:
            low, parts, sums, *ridden = conv_back_fused(
                grad_low,
                spread,
                kernel,
                normed,
                inverse,
                gain,
                size,
                canvas_cols,
                n,
                m,
                number,
                riders,
                more,
            )
            return low, parts, sums[0], sums[2], ridden
        grad_hidden, grad_kernel = conv_backward(grad_low, hidden, kernel, n)
        outgoing, gain_part = group_backward(grad_hidden, normed, inverse, gain, size)
        parts = grad_kernel.astype(jnp.bfloat16).reshape(9 * own, -1).T
        low = sum(more, outgoing).astype(jnp.bfloat16)
        return low, parts, gain_part, jnp.sum(outgoing, axis=0), exchange(riders, n, m, number)

    grad_conv_low, parts_second, grad_gain_second, grad_shift, rode_second = back(
        grad_residual.astype(jnp.bfloat16),
        hidden_second,
        spread_second,
        conv_second,
        normed_second,
        inverse_second,
        own_second,
        10,
        (
            Rider("dp", unsettled(grad_down, m, n), 1),
            Rider("dp", grad_qkv_weight, 0),
            Rider("dp", jnp.concatenate([tiled_up(embedding[0]), tiled_up(ada_columns)])),
        ),
    )
    sums_down, sums_qkv, every_small = rode_second
    image_turned, parts_first, grad_gain_first, _, rode_first = back(
        grad_conv_low,
        hidden_first,
        spread_first,
        conv_first,
        normed_first,
        inverse_first,
        own_first,
        11,
        (
            Rider("dp", unsettled(parts_second, m, n), 1),
            Rider("dp", tiled_up(grad_shift)),
            Settle(added(sums_down)[:, 0].astype(jnp.bfloat16), True, 4, fused),
            Rider("dp", grad_up, 0),
        ),
        (grad_residual,),
    )
    sums_second, every_shift, pieces_down, sums_up = rode_first
    embed_term = jnp.dot(
        grad_shift[None], shift_weight.astype(jnp.float32).T, precision=PRECISE
    ) + jnp.dot(ada_columns[None], ada_weight.astype(jnp.float32).T, precision=PRECISE)
    small = jnp.concatenate(
        [tiled_up(embed_term[0]), tiled_up(jnp.concatenate([grad_gain_first, grad_gain_second]))]
    )
    riders = (
        Settle(unsettled(parts_first, m, n), False, 9, fused),
        Rider("all", small),
        Settle(added(sums_second)[:, 0].astype(jnp.bfloat16), True, 9, fused),
    )
    if fused:
        pieces_first, small, pieces_second, image_turned = exchange(
            riders + (Rider("mp", image_turned, 0, True),), n, m, 13
        )
        image_grad = image_turned.reshape(image.shape)
    else:
        pieces_first, small, pieces_second = exchange(riders, n, m, 13)
        image_grad = lax.all_to_all(
            image_turned.reshape(rows_all, canvas_cols, own), "mp", 0, 2, tiled=True
        )[None]

    small = small.reshape(m, n, -1)
    embed_count = embedding.shape[1]
    embedding_grad = jnp.sum(
        lax.dynamic_index_in_dim(small, me_dp, axis=0, keepdims=False)[:, :embed_count], axis=0
    )[None]
    gain_start = -(-embed_count // 1024) * 1024
    gains = jnp.sum(small[:, :, gain_start : gain_start + 2 * own], axis=0)
    gains = gains.reshape(n, 2, own).transpose(1, 0, 2).reshape(2, -1)
    piece = channel_count // (m * n)
    gains = lax.dynamic_slice_in_dim(gains, (me_dp * n + me_mp) * piece, piece, axis=1)
    every_small = every_small.reshape(m, -1)
    embed_rows = lax.dynamic_slice_in_dim(
        every_small[:, :embed_count], me_dp * (embed_count // m), embed_count // m, axis=1
    )
    grad_shift_weight = jnp.dot(
        embed_rows.T, every_shift.reshape(m, -1)[:, :own], precision=PRECISE
    )
    grad_ada_weight = jnp.dot(
        embed_rows.T,
        every_small[:, gain_start : gain_start + columns.shape[0]],
        precision=PRECISE,
    )
    qkv_grad = jnp.stack(
        [added(sums_qkv[:, :, j * local_width : (j + 1) * local_width]) for j in range(3)]
    )
    return (
        output,
        image_grad,
        embedding_grad,
        gains[0],
        settled(pieces_first, 9),
        gains[1],
        settled(pieces_second, 9),
        grad_shift_weight,
        settled(pieces_down, 4),
        grad_ada_weight,
        qkv_grad,
        added(sums_out),
        added(sums_up),
        jnp.concatenate([added(sums_proj), added(sums_more)]),
    )


def solution(mesh):
    placed = (
        P("dp", "mp", None, None),
        P("dp", None),
        P("dp", None),
        P(),
        P(None, "mp", None),
        P(),
        P(None, "mp", None),
        P(None, "mp"),
        P(None, "mp", None),
        P(None, "mp"),
        P(None, None, "mp"),
        P("mp", None),
        P(None, "mp"),
        P("mp", None),
        P("dp", "mp", None, None),
    )
    return jax.shard_map(
        local,
        mesh=mesh,
        in_specs=placed,
        out_specs=(
            P("dp", "mp", None, None),
            P("dp", "mp", None, None),
            P("dp", None),
            P(("dp", "mp")),
            P(None, "dp", "mp"),
            P(("dp", "mp")),
            P(None, "dp", "mp"),
            P("dp", "mp"),
            P(None, "dp", "mp"),
            P("dp", "mp"),
            P(None, "dp", "mp"),
            P("mp", "dp"),
            P("dp", "mp"),
            P("mp", "dp"),
        ),
        check_vma=False,
    )
```

```python
from functools import partial
import math

import jax
import jax.numpy as jnp
from jax import lax
from jax.experimental import pallas as pl
from jax.experimental.pallas import tpu as pltpu
from jax.sharding import PartitionSpec as P

HEAD_DIM = 128
GROUPS = 32


GROUP_EPSILON = 1e-05
LAYER_EPSILON = 1e-06
MASKED_SCORE = -1000000000.0
PRECISE = lax.Precision.HIGHEST


def group_spread(per_channel, size):
    grouped = jnp.sum(per_channel.reshape(-1, size), axis=1)
    return jnp.repeat(grouped, size)


def group_forward(values, size):
    counted = values.shape[0] * size
    average = group_spread(jnp.sum(values, axis=0), size) / counted
    centre = values - average
    inverse = lax.rsqrt(
        group_spread(jnp.sum(centre * centre, axis=0), size) / counted + GROUP_EPSILON
    )
    return (centre * inverse, inverse)


def group_backward(incoming, normed, inverse, gain_vec, size):
    pre_act = normed * gain_vec
    sigmoid_part = jax.nn.sigmoid(pre_act)
    through = incoming * sigmoid_part * (1.0 + pre_act * (1.0 - sigmoid_part))
    counted = normed.shape[0] * size
    gain_part = jnp.sum(through * normed, axis=0)
    plain_part = jnp.sum(through, axis=0)
    first_mean = group_spread(plain_part * gain_vec, size) / counted
    second_mean = group_spread(gain_part * gain_vec, size) / counted
    outgoing = inverse * (through * gain_vec - first_mean - normed * second_mean)
    return (outgoing, gain_part)


def windows(planes, flipped):
    row_count, col_count, depth = planes.shape
    padded = jnp.pad(planes, ((1, 1), (1, 1), (0, 0)))
    pieces = []
    for tap_index in range(9):
        row_off, col_off = divmod(tap_index, 3)
        if flipped:
            row_off, col_off = (2 - row_off, 2 - col_off)
        pieces.append(padded[row_off : row_off + row_count, col_off : col_off + col_count])
    return jnp.stack(pieces, axis=2).reshape(row_count * col_count, 9, depth)


def gather_rows(rows):
    return lax.all_gather(rows, "mp", axis=0, tiled=True)


def scatter_rows(rows):
    return lax.psum_scatter(
        rows.astype(jnp.bfloat16), "mp", scatter_dimension=0, tiled=True
    ).astype(jnp.float32)


def conv_scatter(hidden, kernel, n):
    patch = windows(hidden, False)
    depth = kernel.shape[2] // n
    total = jnp.einsum("ptc,tcd->pd", patch, kernel, preferred_element_type=jnp.float32)
    parts = total.astype(jnp.bfloat16).reshape(-1, n, depth).transpose(1, 0, 2)
    return lax.psum_scatter(parts, "mp", scatter_dimension=0, tiled=False).astype(jnp.float32)


def conv_backward(grad_low, hidden, kernel, n):
    row_count, col_count, depth = hidden.shape
    gathered = lax.all_gather(grad_low, "mp", axis=1, tiled=True)
    padded = jnp.pad(gathered, ((col_count, col_count), (0, 0)))
    taps = kernel.reshape(3, 3 * depth, kernel.shape[2])
    acc = sum(
        jnp.einsum(
            "pd,td->pt",
            padded[(2 - i) * col_count : (2 - i) * col_count + row_count * col_count],
            taps[i],
            preferred_element_type=jnp.float32,
        )
        for i in range(3)
    )
    grad_kernel = jnp.einsum(
        "ptc,pd->tcd", windows(hidden, False), gathered, preferred_element_type=jnp.float32
    )
    return (join_columns(acc, col_count), grad_kernel)


def unsettled(parts, m, n):
    return parts.reshape(n, m, -1, parts.shape[-1])


def settled(pieces, taps):
    if pieces.ndim == 3:
        return pieces
    m, count, outs, _ = pieces.shape
    return (
        pieces.astype(jnp.float32)
        .reshape(m, count, outs, taps, -1)
        .transpose(3, 1, 4, 0, 2)
        .reshape(taps, -1, m * outs)
    )


def added(received):
    return jnp.sum(received.astype(jnp.float32), axis=0)


MESH = pl.DeviceIdType.MESH
CONV_PARTS = 4
TOKEN_PARTS = 4
VMEM_BYTES = 60 * 1024 * 1024


class Line:
    def __init__(self, chips, images):
        self.chips = chips
        self.images = images
        self.dp = lax.axis_index("dp")
        self.mp = lax.axis_index("mp")
        self.z = self.mp // 2
        self.c = self.mp % 2
        self.has_up = self.z < chips - 1
        self.has_down = self.z > 0
        self.up = (self.dp, self.mp + 2)
        self.down = (self.dp, self.mp - 2)
        self.sibling = (self.dp, 2 * self.z + 1 - self.c)
        self.ready = lambda: None
        self.early = lambda: None
        self.late = lambda: None

    def count(self, axis):
        return {"dp": self.images, "mp": 2 * self.chips, "all": 2 * self.chips * self.images}[axis]

    def index(self, axis):
        return {"dp": self.dp, "mp": self.mp, "all": self.dp * 2 * self.chips + self.mp}[axis]

    def place(self, axis, index):
        if axis == "dp":
            return (index, self.mp)
        if axis == "mp":
            return (self.dp, index)
        return (index // (2 * self.chips), index % (2 * self.chips))

    def peer(self, axis, step):
        return lax.rem(self.index(axis) + step, self.count(axis))

    def barrier(self, axes, neighbours):
        bar = pltpu.get_barrier_semaphore()
        axes = ("all",) if "all" in axes else axes
        steady = 0
        for axis in axes:
            for step in range(1, self.count(axis)):
                target = self.place(axis, self.peer(axis, step))
                pl.semaphore_signal(bar, inc=1, device_id=target, device_id_type=MESH)
            steady += self.count(axis) - 1
        cases = [(steady, None)]
        if neighbours and not ("all" in axes or "mp" in axes):
            pl.semaphore_signal(bar, inc=1, device_id=self.sibling, device_id_type=MESH)

            @pl.when(self.has_up)
            def _():
                pl.semaphore_signal(bar, inc=1, device_id=self.up, device_id_type=MESH)

            @pl.when(self.has_down)
            def _():
                pl.semaphore_signal(bar, inc=1, device_id=self.down, device_id_type=MESH)

            middle = jnp.logical_and(self.has_up, self.has_down)
            cases = [(steady + 3, middle), (steady + 2, jnp.logical_not(middle))]
        for count, when in cases:
            if when is None:
                pl.semaphore_wait(bar, count)
            else:

                @pl.when(when)
                def _():
                    pl.semaphore_wait(bar, count)


class Rider:
    def __init__(self, axis, array, cut=None, beside=False, part=(0, 1), inside=False):
        self.axes = (axis,)
        self.part = part
        self.inside = inside
        self.axis = axis
        self.array = array
        self.cut = cut
        self.beside = beside

    def result(self, sizes):
        count = sizes[self.axis]
        shape = list(self.array.shape)
        if self.cut is not None:
            shape[self.cut] //= count
        shape[0] //= self.part[1]
        self.columns = shape[-1]
        if self.beside:
            shape[-1] *= count
        else:
            shape = [count] + shape
        return jax.ShapeDtypeStruct(tuple(shape), self.array.dtype)

    def scratch(self, sizes):
        count = sizes[self.axis]
        return [pltpu.SemaphoreType.DMA((count,)), pltpu.SemaphoreType.DMA((count,))]

    def piece(self, ref, index, count):
        if self.cut is None:
            return ref
        size = self.array.shape[self.cut] // count
        where = [slice(None)] * len(self.array.shape)
        where[self.cut] = pl.ds(pl.multiple_of(index * size, size), size)
        if self.part[1] > 1:
            rows = self.array.shape[0] // self.part[1]
            where[0] = pl.ds(self.part[0] * rows, rows)
        return ref.at[tuple(where)]

    def copies(self, line, src, dst, send, recv):
        count, me = line.count(self.axis), line.index(self.axis)
        if self.beside:
            land = dst.at[:, pl.ds(pl.multiple_of(me * self.columns, self.columns), self.columns)]
        else:
            land = dst.at[me]
        made = [pltpu.make_async_copy(self.piece(src, me, count), land, send.at[0])]
        for step in range(1, count):
            peer = line.peer(self.axis, step)
            made.append(
                remote(
                    self.piece(src, peer, count),
                    land,
                    send.at[step],
                    recv.at[step],
                    line.place(self.axis, peer),
                )
            )
        return made

    def start(self, line, src, dst, send, recv):
        for copy in self.copies(line, src, dst, send, recv):
            copy.start()

    def early(self, *refs):
        pass

    def middle(self, phase, *refs):
        pass

    def finish(self, line, src, dst, send, recv):
        for copy in self.copies(line, src, dst, send, recv):
            copy.wait()


class Settle:
    def __init__(self, array, summed, taps, placed):
        self.axes = ("dp", "mp")
        self.inside = True
        self.array = array
        self.summed = summed
        self.taps = taps
        self.placed = placed

    def result(self, sizes):
        n, m = sizes["mp"], sizes["dp"]
        self.ratio = n // m
        self.tail = tuple(self.array.shape[-2:])
        self.total = jax.ShapeDtypeStruct((n,) + self.tail, self.array.dtype)
        self.land = (m, self.ratio) + self.tail
        self.add = None if self.summed else Rider("dp", self.array, 1)
        self.outward = Rider("mp", self.total, 0)
        self.inward = Rider("dp", self.total, 0)
        if not self.placed:
            return jax.ShapeDtypeStruct(self.land, self.array.dtype)
        shape = (self.taps, self.ratio * self.tail[1] // self.taps, m * self.tail[0])
        return jax.ShapeDtypeStruct(shape, jnp.float32)

    def scratch(self, sizes):
        n, m = sizes["mp"], sizes["dp"]
        dtype = self.array.dtype
        refs = [pltpu.VMEM(self.land, dtype), pltpu.VMEM((n, 1) + self.tail, dtype)]
        refs += [pltpu.VMEM((m, n, 1) + self.tail, dtype), pltpu.VMEM((n,) + self.tail, dtype)]
        refs += [pltpu.SemaphoreType.DMA((1,))] if self.summed else self.add.scratch(sizes)
        return refs + self.outward.scratch(sizes) + self.inward.scratch(sizes)

    def copies(self, step, line, src, dst, land, stage, got, total, *sems):
        if step == 0 and self.summed:
            return [pltpu.make_async_copy(src, got, sems[0].at[0])]
        if step == 0:
            return self.add.copies(line, src, got, *sems[:2])
        if step == 1:
            return self.outward.copies(line, total, stage, *sems[-4:-2])
        return self.inward.copies(line, stage.at[:, 0], land, *sems[-2:])

    def start(self, *refs):
        for copy in self.copies(0, *refs):
            copy.start()

    def add_up(self, *refs):
        for copy in self.copies(0, *refs):
            copy.wait()
        got, total = refs[5:7]

        @pl.loop(0, total.shape[0])
        def _(index):
            added_up = got[0, index, 0].astype(jnp.float32)
            for image in range(1, got.shape[0]):
                added_up += got[image, index, 0].astype(jnp.float32)
            total[index] = added_up.astype(total.dtype)

        for copy in self.copies(1, *refs):
            copy.start()

    def early(self, *refs):
        if self.summed:
            self.add_up(*refs)

    def middle(self, phase, *refs):
        if phase == 0 and not self.summed:
            self.add_up(*refs)
        elif phase == 1 and self.summed:
            self.end(*refs)
        else:
            for copy in self.copies(1, *refs):
                copy.wait()
            for copy in self.copies(2, *refs):
                copy.start()

    def finish(self, *refs):
        if not self.summed:
            self.end(*refs)

    def end(self, *refs):
        for copy in self.copies(2, *refs):
            copy.wait()
        dst, land = refs[2:4]
        if not self.placed:
            dst[...] = land[...]
            return
        own = self.tail[1] // self.taps
        for half in range(self.ratio):
            for tap in range(self.taps):
                block = jnp.concatenate(
                    [
                        land[image, half, :, pl.ds(tap * own, own)].astype(jnp.float32)
                        for image in range(land.shape[0])
                    ],
                    axis=0,
                )
                dst[tap, pl.ds(half * own, own)] = block.T


def comm_call(
    kernel, inputs, out_shapes, scratch, riders, n, m, number, neighbours=True, after=None
):
    chips = n // 2
    sizes = {"dp": m, "mp": n, "all": m * n}
    ride_shapes = tuple(rider.result(sizes) for rider in riders)
    ride_scratch = [rider.scratch(sizes) for rider in riders]
    any_spec = pl.BlockSpec(memory_space=pl.ANY)
    ni, nr, no = len(inputs), len(riders), len(out_shapes)
    large = [index for index in range(ni) if inputs[index].size * inputs[index].dtype.itemsize > 2**20]

    def body(*refs):
        main_in, ride_in = list(refs[:ni]), refs[ni : ni + nr]
        rest = refs[ni + nr :]
        main_out, ride_out = rest[:no], rest[no : no + nr]
        rest = rest[no + nr :]
        main_scratch, rest = rest[: len(scratch)], rest[len(scratch) :]
        line = Line(chips, m)
        loads = []
        if large:
            load_sems, rest = rest[0], rest[1:]
            for place, index in enumerate(large):
                loads.append(
                    pltpu.make_async_copy(main_in[index], rest[place], load_sems.at[place])
                )
                main_in[index] = rest[place]
            rest = rest[len(large) :]
        for load in loads:
            load.start()

        def ready():
            for load in loads:
                load.wait()

        line.ready = ready
        line.barrier(sorted(set(axis for rider in riders for axis in rider.axes)), neighbours)
        riding = []
        for rider, src, dst, needs in zip(riders, ride_in, ride_out, ride_scratch):
            riding.append((rider, (line, src, dst) + tuple(rest[: len(needs)])))
            rest = rest[len(needs) :]
        for rider, refs_in in riding:
            rider.start(*refs_in)
        phases = [-1, 0, 1]

        def early():
            phases.pop(0)
            for rider, refs_in in riding:
                rider.early(*refs_in)

        def late():
            phases.pop(0)
            for rider, refs_in in riding:
                rider.middle(0, *refs_in)

        line.early = early
        line.late = late
        kernel(line, *main_in, *main_out, *main_scratch)
        if -1 in phases:
            early()
        for phase in phases:
            for rider, refs_in in riding:
                rider.middle(phase, *refs_in)
        for rider, refs_in in riding:
            rider.finish(*refs_in)
        if after is not None:
            after(main_in, main_out, ride_out)

    return pl.pallas_call(
        body,
        out_shape=tuple(out_shapes) + ride_shapes,
        in_specs=[any_spec if index in large else whole(1)[0] for index in range(ni)]
        + [any_spec] * nr,
        out_specs=tuple(
            whole(no)
            + [whole(1)[0] if rider.inside else any_spec for rider in riders]
        ),
        scratch_shapes=list(scratch)
        + ([pltpu.SemaphoreType.DMA((len(large),))] if large else [])
        + [pltpu.VMEM(inputs[index].shape, inputs[index].dtype) for index in large]
        + [ref for needs in ride_scratch for ref in needs],
        compiler_params=comm_params(number),
    )(*inputs, *[rider.array for rider in riders])


def remote(src, dst, send, recv, target):
    return pltpu.make_async_remote_copy(
        src_ref=src,
        dst_ref=dst,
        send_sem=send,
        recv_sem=recv,
        device_id=target,
        device_id_type=MESH,
    )


def gather_sems(chips):
    return [pltpu.SemaphoreType.DMA((3, 2, chips)), pltpu.SemaphoreType.DMA((3, 2, chips))]


def line_gather(line, x_ref, slot, send, recv, on_own, on_pair):
    chips = line.chips
    z, c = line.z, line.c

    def hop(stream, step, src, block, target):
        return remote(src, slot(block), send.at[stream, 0, step], recv.at[stream, 0, step], target)

    def across(way, step, src, block):
        return remote(src, slot(block), send.at[2, way, step], recv.at[2, way, step], line.sibling)

    @pl.when(line.has_up)
    def _():
        hop(0, 1, x_ref, line.mp, line.up).start()

    @pl.when(line.has_down)
    def _():
        hop(1, 1, x_ref, line.mp, line.down).start()

    across(0, 0, x_ref, line.mp).start()
    slot(line.mp)[...] = x_ref[...]
    line.early()
    line.ready()
    on_own()
    across(0, 0, x_ref, line.mp).wait_recv()
    on_pair(z)
    for step in range(1, chips):
        below, above = z - step, z + step
        if step == chips - 1:
            line.late()

        @pl.when(below >= 0)
        def _():
            block = 2 * below + c
            hop(0, step, slot(block), block, line.up).wait_recv()
            if step + 1 < chips:

                @pl.when(line.has_up)
                def _():
                    hop(0, step + 1, slot(block), block, line.up).start()

            across(0, step, slot(block), block).start()

        @pl.when(above < chips)
        def _():
            block = 2 * above + c
            hop(1, step, slot(block), block, line.down).wait_recv()
            if step + 1 < chips:

                @pl.when(line.has_down)
                def _():
                    hop(1, step + 1, slot(block), block, line.down).start()

            across(1, step, slot(block), block).start()

        @pl.when(below >= 0)
        def _():
            across(0, step, slot(2 * below + c), 2 * below + c).wait_recv()
            on_pair(below)

        @pl.when(above < chips)
        def _():
            across(1, step, slot(2 * above + c), 2 * above + c).wait_recv()
            on_pair(above)

    @pl.when(line.has_up)
    def _():
        hop(0, 1, x_ref, line.mp, line.up).wait_send()

    @pl.when(line.has_down)
    def _():
        hop(1, 1, x_ref, line.mp, line.down).wait_send()

    across(0, 0, x_ref, line.mp).wait_send()
    for step in range(1, chips):
        below, above = z - step, z + step

        @pl.when(below >= 0)
        def _():
            block = 2 * below + c
            if step + 1 < chips:

                @pl.when(line.has_up)
                def _():
                    hop(0, step + 1, slot(block), block, line.up).wait_send()

            across(0, step, slot(block), block).wait_send()

        @pl.when(above < chips)
        def _():
            block = 2 * above + c
            if step + 1 < chips:

                @pl.when(line.has_down)
                def _():
                    hop(1, step + 1, slot(block), block, line.down).wait_send()

            across(1, step, slot(block), block).wait_send()


def scatter_scratch(chips, rows, cols, parts):
    block = (chips, rows, cols)
    return [
        pltpu.VMEM(block, jnp.float32),
        pltpu.VMEM(block, jnp.bfloat16),
        pltpu.VMEM(block, jnp.bfloat16),
        pltpu.VMEM((2,) + block, jnp.bfloat16),
        pltpu.SemaphoreType.DMA((2, 3, chips, parts)),
    ]


def line_scatter(line, scratch, parts, produce, finish, tile, side=()):
    chips = line.chips
    z = line.z
    kept, out_ref, in_ref, moving, sems = scratch
    count = kept.shape[1] // parts
    line.ready()

    def span(part):
        return pl.ds(part * count, count)

    def across(chip, part):
        return remote(
            out_ref.at[chip, span(part)],
            in_ref.at[chip, span(part)],
            sems.at[0, 0, chip, part],
            sems.at[1, 0, chip, part],
            line.sibling,
        )

    def hop(way, chip, part):
        target = line.up if way == 0 else line.down
        ref = moving.at[way, chip, span(part)]
        return remote(
            ref, ref, sems.at[0, 1 + way, chip, part], sems.at[1, 1 + way, chip, part], target
        )

    items = []
    for step in range(chips - 1):
        for part in range(parts):
            items.append((0, chips - 1 - step + z, part, step >= z))
            items.append((1, step - (chips - 1 - z), part, step >= chips - 1 - z))
    for part in range(parts):
        items.append((2, z, part, None))

    def run(active, body):
        if active is None:
            body()
        else:
            pl.when(active)(body)

    def start(item):
        way, chip, part, active = item

        def body():
            produce(chip, part, count, kept.at[chip], out_ref.at[chip])
            across(chip, part).start()

        run(active, body)

    def tiles(part, body):
        @pl.loop(0, count // tile)
        def _(index):
            body(pl.ds(pl.multiple_of(part * count + index * tile, tile), tile))

    def close(item):
        way, chip, part, active = item

        def body():
            across(chip, part).wait_recv()
            if way < 2:
                later = line.has_down if way == 0 else line.has_up

                @pl.when(later)
                def _():
                    hop(way, chip, part).wait_recv()

                    def add(rows):
                        moving[way, chip, rows] = (
                            kept[chip, rows]
                            + in_ref[chip, rows].astype(jnp.float32)
                            + moving[way, chip, rows].astype(jnp.float32)
                        ).astype(jnp.bfloat16)

                    tiles(part, add)

                @pl.when(jnp.logical_not(later))
                def _():
                    def add(rows):
                        moving[way, chip, rows] = (
                            kept[chip, rows] + in_ref[chip, rows].astype(jnp.float32)
                        ).astype(jnp.bfloat16)

                    tiles(part, add)

                hop(way, chip, part).start()
            else:

                def total(rows):
                    return kept[chip, rows] + in_ref[chip, rows].astype(jnp.float32)

                def from_side(side, rows):
                    return moving[side, chip, rows].astype(jnp.float32)

                both = jnp.logical_and(line.has_down, line.has_up)

                @pl.when(both)
                def _():
                    hop(0, chip, part).wait_recv()
                    hop(1, chip, part).wait_recv()
                    tiles(
                        part,
                        lambda rows: finish(
                            part, rows, total(rows) + from_side(0, rows) + from_side(1, rows)
                        ),
                    )

                for side, present in ((0, line.has_down), (1, line.has_up)):

                    @pl.when(jnp.logical_and(present, jnp.logical_not(both)))
                    def _():
                        hop(side, chip, part).wait_recv()
                        tiles(
                            part,
                            lambda rows: finish(part, rows, total(rows) + from_side(side, rows)),
                        )

        run(active, body)

    lag = 2
    side = list(side)
    for index, item in enumerate(items):
        start(item)
        if index >= lag:
            close(items[index - lag])
            if index % 2 == 0 and side:
                side.pop(0)()
    for step in side:
        step()
    for item in items[-lag:]:
        close(item)
    for way, chip, part, active in items:

        def body():
            across(chip, part).wait_send()
            if way < 2:
                hop(way, chip, part).wait_send()

        run(active, body)


def whole(count):
    return [pl.BlockSpec(memory_space=pltpu.VMEM)] * count


def comm_params(number):
    return pltpu.CompilerParams(
        collective_id=number, has_side_effects=True, vmem_limit_bytes=VMEM_BYTES
    )


def pick(c, low, high):
    return jnp.where(c == 0, low, high), jnp.where(c == 0, high, low)


def group_matrix(own, size, count):
    groups = [lax.broadcasted_iota(jnp.int32, (own, own), axis) // size for axis in range(2)]
    return jnp.where(groups[0] == groups[1], 1.0 / (count * size), 0.0)


def norm_spread(values, gain, spread_ref, stat_ref, size, breadth):
    pixels, own = values.shape
    tile = 512
    matrix = group_matrix(own, size, pixels)
    stat_ref[...] = jnp.zeros_like(stat_ref)
    column = lax.broadcasted_iota(jnp.int32, (tile, own), 0) % breadth

    def tiles(body):
        @pl.loop(0, pixels // tile)
        def _(index):
            base = pl.multiple_of(index * tile, tile)
            body(base, pl.ds(base, tile))

    def add(base, rows):
        stat_ref[0:1] += jnp.sum(values[rows], axis=0, keepdims=True)

    tiles(add)
    average = jnp.dot(stat_ref[...], matrix, precision=PRECISE)[0:1]

    def square(base, rows):
        centre = values[rows] - average
        stat_ref[1:2] += jnp.sum(centre * centre, axis=0, keepdims=True)

    tiles(square)
    inverse = lax.rsqrt(jnp.dot(stat_ref[...], matrix, precision=PRECISE)[1:2] + GROUP_EPSILON)
    stat_ref[2:3] = inverse

    def write(base, rows):
        normed = (values[rows] - average) * inverse
        values[rows] = normed
        pre_act = normed * gain
        hidden = pre_act / (1.0 + jnp.exp(-pre_act))
        below = pl.ds(base + breadth, tile)
        left = jnp.where(column == 0, 0.0, pltpu.roll(hidden, 1, 0))
        right = jnp.where(column == breadth - 1, 0.0, pltpu.roll(hidden, tile - 1, 0))
        for place, value in enumerate((left, hidden, right)):
            spread_ref[below, place * own : (place + 1) * own] = value.astype(jnp.bfloat16)

    tiles(write)
    nothing = jnp.zeros((breadth, 3 * own), jnp.bfloat16)
    spread_ref[pl.ds(0, breadth)] = nothing
    spread_ref[pl.ds(breadth + pixels, breadth)] = nothing


def norm_shapes(pixels, own, cols):
    return (
        jax.ShapeDtypeStruct((pixels, own), jnp.float32),
        jax.ShapeDtypeStruct((pixels + 2 * cols, 3 * own), jnp.bfloat16),
        jax.ShapeDtypeStruct((8, own), jnp.float32),
    )


def conv_scatter_kernel(breadth, size, line, x_ref, w_ref, *refs):
    normed = size > 0
    v_ref, refs = (refs[0], refs[1:]) if normed else (None, refs)
    o_ref, refs = refs[0], refs[1:]
    spread_ref, stat_ref, *scratch = refs if normed else (None, None) + tuple(refs)
    pixels, own = o_ref.shape
    tile = 512

    def produce(chip, part, count, mine, other):
        columns = pl.ds(pl.multiple_of(chip * 2 * own, 2 * own), 2 * own)

        @pl.loop(0, count // tile)
        def _(index):
            base = pl.multiple_of(part * count + index * tile, tile)
            total = jnp.zeros((tile, 2 * own), jnp.float32)
            for i in range(3):
                total += jnp.dot(
                    x_ref[pl.ds(base + i * breadth, tile)],
                    w_ref[i, :, columns],
                    preferred_element_type=jnp.float32,
                )
            first, second = pick(line.c, total[:, :own], total[:, own:])
            mine[pl.ds(base, tile)] = first
            other[pl.ds(base, tile)] = second.astype(jnp.bfloat16)

    def finish(part, rows, total):
        o_ref[rows] = total + v_ref[0:1] if normed else total

    line_scatter(line, scratch, CONV_PARTS, produce, finish, tile)
    if normed:
        norm_spread(o_ref, v_ref[1:2], spread_ref, stat_ref, size, breadth)


def side_by_side(hidden):
    rows, cols, depth = hidden.shape
    padded = jnp.pad(hidden, ((1, 1), (1, 1), (0, 0)))
    return jnp.concatenate([padded[:, j : j + cols] for j in range(3)], axis=2).reshape(
        (rows + 2) * cols, 3 * depth
    )


def rows_of(*vectors):
    rows = jnp.stack(vectors)
    return jnp.pad(rows, ((0, 8 - rows.shape[0]), (0, 0)))


def conv_scatter_fused(spread, kernel, cols, n, m, number, shift=None, gain=None, size=0):
    own = kernel.shape[2] // n
    depth = kernel.shape[1]
    pixels = spread.shape[0] - 2 * cols
    return comm_call(
        partial(conv_scatter_kernel, cols, size),
        (spread, kernel.reshape(3, 3 * depth, kernel.shape[2]))
        + ((rows_of(shift, gain),) if size else ()),
        norm_shapes(pixels, own, cols)[: 3 if size else 1],
        scatter_scratch(n // 2, pixels, own, CONV_PARTS),
        (),
        n,
        m,
        number,
    )


def conv_back_kernel(breadth, size, extra, line, g_ref, w_ref, x_ref, n_ref, v_ref, *refs):
    refs = list(refs)
    more_ref = refs.pop(0) if extra else None
    low_ref, wg_ref, stat_ref, acc_ref, held, sums, send, recv = refs
    chips = line.chips
    pixels, own = g_ref.shape
    wide = w_ref.shape[1]
    tile, long = 512, 1024
    zero = jnp.zeros((breadth, own), jnp.bfloat16)
    for block in range(2 * chips):
        held[block, pl.ds(0, breadth)] = zero
        held[block, pl.ds(breadth + pixels, breadth)] = zero

    def slot(block):
        return held.at[block, pl.ds(breadth, pixels)]

    def beside(base, count, chip):
        rows = pl.ds(base, count)
        return [held[2 * chip, rows], held[2 * chip + 1, rows]]

    def on_own():
        @pl.loop(0, pixels // tile)
        def _(index):
            acc_ref[pl.ds(pl.multiple_of(index * tile, tile), tile)] = jnp.zeros(
                (tile, wide), jnp.float32
            )

    def on_pair(chip):
        columns = pl.ds(pl.multiple_of(chip * 2 * own, 2 * own), 2 * own)

        @pl.loop(0, pixels // tile)
        def _(index):
            base = pl.multiple_of(index * tile, tile)
            shifted = []
            for i in range(3):
                shifted += beside(base + (2 - i) * breadth, tile, chip)
            acc_ref[pl.ds(base, tile)] += product(
                jnp.concatenate(shifted, axis=1),
                jnp.concatenate([w_ref[i, :, columns] for i in range(3)], axis=1),
                True,
            )

        sums[...] = jnp.zeros_like(sums)

        @pl.loop(0, pixels // long)
        def _(index):
            base = pl.multiple_of(index * long, long)
            sums[...] += lax.dot_general(
                jnp.concatenate(beside(base + breadth, long, chip), axis=1),
                jnp.concatenate(
                    [x_ref[pl.ds(base + i * breadth, long)] for i in range(3)], axis=1
                ),
                (((0,), (0,)), ((), ())),
                preferred_element_type=jnp.float32,
            )

        wg_ref[chip] = sums[...].astype(jnp.bfloat16)

    line_gather(line, g_ref, slot, send, recv, on_own, on_pair)

    gain, inverse = v_ref[0:1], v_ref[1:2]
    stat_ref[...] = jnp.zeros_like(stat_ref)
    column = lax.broadcasted_iota(jnp.int32, (tile, own), 0) % breadth

    @pl.loop(0, pixels // tile)
    def _(index):
        rows = pl.ds(pl.multiple_of(index * tile, tile), tile)
        left = jnp.where(
            column == breadth - 1, 0.0, pltpu.roll(acc_ref[rows, 0:own], tile - 1, 0)
        )
        right = jnp.where(column == 0, 0.0, pltpu.roll(acc_ref[rows, 2 * own : wide], 1, 0))
        incoming = left + acc_ref[rows, own : 2 * own] + right
        normed = n_ref[rows]
        pre_act = normed * gain
        sigmoid_part = 1.0 / (1.0 + jnp.exp(-pre_act))
        through = incoming * sigmoid_part * (1.0 + pre_act * (1.0 - sigmoid_part))
        acc_ref[rows, 0:own] = through
        stat_ref[0:1] += jnp.sum(through * normed, axis=0, keepdims=True)
        stat_ref[1:2] += jnp.sum(through, axis=0, keepdims=True)

    means = jnp.dot(stat_ref[...] * gain, group_matrix(own, size, pixels), precision=PRECISE)
    second_mean, first_mean = means[0:1], means[1:2]

    @pl.loop(0, pixels // tile)
    def _(index):
        rows = pl.ds(pl.multiple_of(index * tile, tile), tile)
        outgoing = inverse * (
            acc_ref[rows, 0:own] * gain - first_mean - n_ref[rows] * second_mean
        )
        stat_ref[2:3] += jnp.sum(outgoing, axis=0, keepdims=True)
        if extra:
            outgoing = outgoing + more_ref[rows]
        low_ref[rows] = outgoing.astype(jnp.bfloat16)


def conv_back_fused(
    grad_low, spread, kernel, normed, inverse, gain, size, cols, n, m, number, riders, more=()
):
    pixels, own = grad_low.shape
    depth = kernel.shape[1]
    chips = n // 2
    vectors = rows_of(gain, inverse)
    return comm_call(
        partial(conv_back_kernel, cols, size, len(more) > 0),
        (grad_low, kernel.reshape(3, 3 * depth, kernel.shape[2]), spread, normed, vectors)
        + tuple(more),
        (
            jax.ShapeDtypeStruct((pixels, depth), jnp.bfloat16),
            jax.ShapeDtypeStruct((chips, 2 * own, 9 * depth), jnp.bfloat16),
            jax.ShapeDtypeStruct((8, own), jnp.float32),
        ),
        [
            pltpu.VMEM((pixels, 3 * depth), jnp.float32),
            pltpu.VMEM((n, pixels + 2 * cols, own), jnp.bfloat16),
            pltpu.VMEM((2 * own, 9 * depth), jnp.float32),
        ]
        + gather_sems(chips),
        riders,
        n,
        m,
        number,
    )


def join_columns(acc, cols):
    pixels, wide = acc.shape
    depth = wide // 3
    planes = acc.reshape(-1, cols, wide)
    none = jnp.zeros_like(planes[:, :1, :depth])
    left = jnp.concatenate([planes[:, 1:, :depth], none], axis=1)
    right = jnp.concatenate([none, planes[:, :-1, 2 * depth :]], axis=1)
    return (left + planes[:, :, depth : 2 * depth] + right).reshape(pixels, depth)


def product(x, w, turned):
    return lax.dot_general(
        x, w, (((1,), (1 if turned else 0,)), ((), ())), preferred_element_type=jnp.float32
    )


def outer_steps(grad, left, right, cut):
    def step(start):
        grad[pl.ds(start, cut)] = lax.dot_general(
            left[:, pl.ds(start, cut)],
            right[...],
            (((0,), (0,)), ((), ())),
            preferred_element_type=jnp.float32,
        ).astype(grad.dtype)

    return [partial(step, start) for start in range(0, left.shape[1], cut)]


class NormAfter:
    def __init__(self, scale, shift, more=()):
        self.inputs = (rows_of(scale, shift),) + tuple(more)

    def shapes(self, tokens, width):
        return (
            jax.ShapeDtypeStruct((tokens, width), jnp.float32),
            jax.ShapeDtypeStruct((tokens, 128), jnp.float32),
            jax.ShapeDtypeStruct((tokens, width), jnp.bfloat16),
        )

    def run(self, in_refs, o_ref, out_refs):
        v_ref, normed_ref, inverse_ref, low_ref = in_refs[0], *out_refs
        tile = 16

        @pl.loop(0, o_ref.shape[0] // tile)
        def _(index):
            rows = pl.ds(pl.multiple_of(index * tile, tile), tile)
            stream = o_ref[rows]
            for ref in in_refs[1:]:
                stream = stream + ref[rows]
            o_ref[rows] = stream
            centre = stream - jnp.mean(stream, axis=1, keepdims=True)
            inverse = lax.rsqrt(jnp.mean(centre * centre, axis=1, keepdims=True) + LAYER_EPSILON)
            normed = centre * inverse
            normed_ref[rows] = normed
            inverse_ref[rows] = jnp.broadcast_to(inverse, (tile, 128))
            low_ref[rows] = (normed * (1.0 + v_ref[0:1]) + v_ref[1:2]).astype(jnp.bfloat16)


class NormBack:
    def __init__(self, scale, normed, inverse, carry):
        self.inputs = (rows_of(scale), normed, inverse, carry)

    def shapes(self, tokens, width):
        return (
            jax.ShapeDtypeStruct((tokens, width), jnp.bfloat16),
            jax.ShapeDtypeStruct((8, width), jnp.float32),
        )

    def run(self, in_refs, o_ref, out_refs):
        v_ref, normed_ref, inverse_ref, carry_ref = in_refs
        low_ref, sum_ref = out_refs
        tile = 16
        sum_ref[...] = jnp.zeros_like(sum_ref)

        @pl.loop(0, o_ref.shape[0] // tile)
        def _(index):
            rows = pl.ds(pl.multiple_of(index * tile, tile), tile)
            incoming, normed = o_ref[rows], normed_ref[rows]
            sum_ref[0:1] += jnp.sum(incoming * normed, axis=0, keepdims=True)
            sum_ref[1:2] += jnp.sum(incoming, axis=0, keepdims=True)
            through = incoming * (1.0 + v_ref[0:1])
            outgoing = inverse_ref[rows][:, 0:1] * (
                through
                - jnp.mean(through, axis=1, keepdims=True)
                - normed * jnp.mean(through * normed, axis=1, keepdims=True)
            )
            grad = carry_ref[rows].astype(jnp.float32) + outgoing
            o_ref[rows] = grad
            low_ref[rows] = grad.astype(jnp.bfloat16)


def followed(kernel, ni, no, post):
    count = len(post.inputs)

    def run(line, *refs):
        inputs, more, rest = refs[:ni], refs[ni : ni + count], refs[ni + count :]
        outputs, rest = rest[:no], rest[no:]
        made = len(post.shapes(8, 128))
        kernel(line, *inputs, *outputs, *rest[made:])
        post.run(more, outputs[0], rest[:made])

    return run


def tokens_scatter_kernel(turned, beside, line, x_ref, w_ref, *refs):
    side = ()
    if beside:
        left, right, o_ref, grad, *scratch = refs
        side = outer_steps(grad, left, right, 128)
    else:
        o_ref, *scratch = refs
    tokens, width = o_ref.shape
    cut = width // TOKEN_PARTS
    depth = x_ref.shape[1] // w_ref.shape[0]

    def produce(chip, part, count, mine, other):
        rows = pl.ds(pl.multiple_of(chip * 2 * tokens, 2 * tokens), 2 * tokens)
        columns = pl.ds(part * cut, cut)
        total = None
        for j in range(w_ref.shape[0]):
            w = w_ref[j, columns] if turned else w_ref[j, :, columns]
            term = product(x_ref[rows, pl.ds(j * depth, depth)], w, turned)
            total = term if total is None else total + term
        first, second = pick(line.c, total[:tokens], total[tokens:])
        mine[pl.ds(part * count, count)] = first
        other[pl.ds(part * count, count)] = second.astype(jnp.bfloat16)

    def finish(part, rows, total):
        o_ref[:, pl.ds(part * cut, cut)] = total

    line_scatter(line, scratch, TOKEN_PARTS, produce, finish, tokens, side)


def outer_shapes(outer):
    if not outer:
        return ()
    return (jax.ShapeDtypeStruct((outer[0].shape[1], outer[1].shape[1]), jnp.bfloat16),)


def tokens_scatter(x, w, turned, n, m, number, post, riders=(), outer=()):
    tokens = x.shape[0] // n
    width = w.shape[1] if turned else w.shape[2]
    return comm_call(
        followed(
            partial(tokens_scatter_kernel, turned, len(outer) > 0),
            2 + len(outer),
            2 if outer else 1,
            post,
        ),
        (x, w) + tuple(outer) + post.inputs,
        (jax.ShapeDtypeStruct((tokens, width), jnp.float32),)
        + outer_shapes(outer)
        + post.shapes(tokens, width),
        scatter_scratch(n // 2, TOKEN_PARTS * tokens, width // TOKEN_PARTS, TOKEN_PARTS),
        riders,
        n,
        m,
        number,
    )


def add_outer(total, left, right, rows):
    cut = min(left.shape[1], 512)
    for start in range(0, left.shape[1], cut):
        total[pl.ds(start, cut)] += lax.dot_general(
            left[rows, pl.ds(start, cut)],
            right[rows],
            (((0,), (0,)), ((), ())),
            preferred_element_type=jnp.float32,
        )


def tokens_gather_kernel(
    turned, shape_out, outs, keep, side, beside, cols, chained, line, x_ref, w_ref, *refs
):
    refs = list(refs)
    chain_w = refs.pop(0) if chained else None
    left = refs.pop(0) if side else None
    outer = (refs.pop(0), refs.pop(0)) if beside else None
    held = refs.pop(0) if keep else None
    results = [refs.pop(0) for _ in range(outs)]
    grad = refs.pop(0) if side else None
    outer_grad = refs.pop(0) if beside else None
    chain_out = refs.pop(0) if chained else None
    total = refs.pop(0) if side else None
    if not keep:
        held = refs.pop(0)
    send, recv = refs
    tokens = x_ref.shape[0]
    across = w_ref.shape[1 if turned else 2]
    cut = min(across, 512)

    def slot(block):
        return held.at[pl.ds(pl.multiple_of(block * tokens, tokens), tokens)]

    def store_pixels(ref, chip, value):
        depth = value.shape[1] // 4
        base = chip * 8 * tokens
        for row in range(4 * tokens // cols):
            for tap in range(4):
                start = base + (2 * row + tap // 2) * cols + tap % 2
                ref[pl.Slice(start, cols // 2, 2)] = value[
                    row * (cols // 2) : (row + 1) * (cols // 2), tap * depth : (tap + 1) * depth
                ]

    def on_pair(chip):
        rows = pl.ds(pl.multiple_of(chip * 2 * tokens, 2 * tokens), 2 * tokens)
        for j in range(w_ref.shape[0]):
            for start in range(0, across, cut):
                w = w_ref[j, pl.ds(start, cut)] if turned else w_ref[j, :, pl.ds(start, cut)]
                values = shape_out(product(held[rows], w, turned))
                for ref, value in zip(results, values):
                    if cols:
                        store_pixels(ref, chip, value)
                    else:
                        ref[rows, pl.ds(j * across + start, cut)] = value.astype(ref.dtype)
        if chained:
            for start in range(0, chain_w.shape[1], 512):
                columns = pl.ds(start, 512)
                chain_out[rows, columns] = product(
                    results[-1][rows], chain_w[:, columns], False
                ).astype(jnp.bfloat16)
        if side:
            add_outer(total, held, left, rows)

    def on_own():
        if side:
            total[...] = jnp.zeros_like(total)
        if beside:
            for step in outer_steps(outer_grad, *outer, 256):
                step()

    line_gather(line, x_ref, slot, send, recv, on_own, on_pair)
    if side:
        grad[...] = total[...].astype(grad.dtype)


def tokens_gather(
    x,
    w,
    turned,
    kinds,
    shape_out,
    n,
    m,
    number,
    riders=(),
    left=None,
    outer=(),
    cols=0,
    chain=(),
    keep=True,
):
    tokens, width = x.shape
    across = w.shape[0] * w.shape[1 if turned else 2]
    side = left is not None
    grads = ((width, left.shape[1]),) if side else ()
    shape = (tokens * n * 4, across // 4) if cols else (tokens * n, across)
    return comm_call(
        partial(
            tokens_gather_kernel,
            turned,
            shape_out,
            len(kinds),
            keep,
            side,
            len(outer) > 0,
            cols,
            len(chain) > 0,
        ),
        (x, w) + tuple(chain) + ((left,) if side else ()) + tuple(outer),
        tuple(jax.ShapeDtypeStruct((tokens * n, width), x.dtype) for _ in range(int(keep)))
        + tuple(jax.ShapeDtypeStruct(shape, kind) for kind in kinds)
        + tuple(jax.ShapeDtypeStruct(grad, jnp.bfloat16) for grad in grads)
        + outer_shapes(outer)
        + tuple(jax.ShapeDtypeStruct((tokens * n, w2.shape[1]), jnp.bfloat16) for w2 in chain),
        [pltpu.VMEM(grad, jnp.float32) for grad in grads]
        + [pltpu.VMEM((tokens * n, width), x.dtype) for _ in range(int(not keep))]
        + gather_sems(n // 2),
        riders,
        n,
        m,
        number,
    )


def exchange(riders, n, m, number):
    return comm_call(lambda line: None, (), (), [], riders, n, m, number, neighbours=False)


def exchange_norm(image_rows, gain, size, cols, riders, n, m, number):
    own = image_rows.shape[1] // n
    count = image_rows.shape[0]

    def after(main_in, main_out, ride_out):
        normed, spread_ref, stat_ref = main_out

        @pl.loop(0, n)
        def _(index):
            normed[pl.ds(pl.multiple_of(index * count, count), count)] = ride_out[0][index].astype(
                jnp.float32
            )

        norm_spread(normed, main_in[0][0:1], spread_ref, stat_ref, size, cols)

    return comm_call(
        lambda line, *refs: None,
        (rows_of(gain),),
        norm_shapes(count * n, own, cols),
        [],
        (Rider("mp", image_rows, 1, inside=True),) + tuple(riders),
        n,
        m,
        number,
        neighbours=False,
        after=after,
    )


def tiled_up(vector):
    count = -(-vector.shape[0] // 1024) * 1024
    return jnp.pad(vector.astype(jnp.float32), (0, count - vector.shape[0])).reshape(-1, 128)


def attend_scatter_kernel(line, x_ref, valid_ref, w_ref, o_ref, mixed_ref, *scratch):
    tokens, width = o_ref.shape
    wide = mixed_ref.shape[1]
    cut = width // TOKEN_PARTS
    scale = 1.0 / math.sqrt(HEAD_DIM)

    def attend(rows):
        for head in range(wide // HEAD_DIM):
            where = [pl.ds(j * wide + head * HEAD_DIM, HEAD_DIM) for j in range(3)]
            scores = product(x_ref[rows, where[0]], x_ref[:, where[1]], True) * scale
            scores = jnp.where(valid_ref[0:1] > 0.5, scores, MASKED_SCORE)
            exponent = jnp.exp(scores - jnp.max(scores, axis=1, keepdims=True))
            inverse = 1.0 / jnp.sum(exponent, axis=1, keepdims=True)
            mixed_ref[rows, pl.ds(head * HEAD_DIM, HEAD_DIM)] = product(
                (exponent * inverse).astype(jnp.bfloat16), x_ref[:, where[2]], False
            ).astype(jnp.bfloat16)

    def produce(chip, part, count, mine, other):
        rows = pl.ds(pl.multiple_of(chip * 2 * tokens, 2 * tokens), 2 * tokens)
        if part == 0:
            attend(rows)
        total = product(mixed_ref[rows], w_ref[:, pl.ds(part * cut, cut)], False)
        first, second = pick(line.c, total[:tokens], total[tokens:])
        mine[pl.ds(part * count, count)] = first
        other[pl.ds(part * count, count)] = second.astype(jnp.bfloat16)

    def finish(part, rows, total):
        o_ref[:, pl.ds(part * cut, cut)] = total

    line_scatter(line, scratch, TOKEN_PARTS, produce, finish, tokens)


def attend_scatter(qkv_rows, valid, out_weight, n, m, number, post):
    total = qkv_rows.shape[0]
    tokens = total // n
    width = out_weight.shape[1]
    return comm_call(
        followed(attend_scatter_kernel, 3, 2, post),
        (qkv_rows, jnp.broadcast_to(valid[None], (8, total)), out_weight) + post.inputs,
        (
            jax.ShapeDtypeStruct((tokens, width), jnp.float32),
            jax.ShapeDtypeStruct((total, out_weight.shape[0]), jnp.bfloat16),
        )
        + post.shapes(tokens, width),
        scatter_scratch(n // 2, TOKEN_PARTS * tokens, width // TOKEN_PARTS, TOKEN_PARTS),
        (),
        n,
        m,
        number,
    )


def attend_gather_kernel(
    line,
    g_ref,
    w_ref,
    x_ref,
    valid_ref,
    mixed_ref,
    left,
    right,
    grad_ref,
    out_ref,
    outer_grad,
    held,
    keys_sum,
    values_sum,
    out_sum,
    send,
    recv,
):
    tokens = g_ref.shape[0]
    wide = w_ref.shape[0]
    heads = wide // HEAD_DIM
    scale = 1.0 / math.sqrt(HEAD_DIM)

    def slot(block):
        return held.at[pl.ds(pl.multiple_of(block * tokens, tokens), tokens)]

    def on_own():
        keys_sum[...] = jnp.zeros_like(keys_sum)
        values_sum[...] = jnp.zeros_like(values_sum)
        out_sum[...] = jnp.zeros_like(out_sum)
        for step in outer_steps(outer_grad, left, right, 256):
            step()

    def on_pair(chip):
        rows = pl.ds(pl.multiple_of(chip * 2 * tokens, 2 * tokens), 2 * tokens)
        for head in range(heads):
            place = pl.ds(head * HEAD_DIM, HEAD_DIM)
            where = [pl.ds(j * wide + head * HEAD_DIM, HEAD_DIM) for j in range(3)]
            grad = product(held[rows], w_ref[place], True).astype(jnp.bfloat16)
            query = x_ref[rows, where[0]]
            scores = product(x_ref[:, where[1]], query, True) * scale
            scores = jnp.where(valid_ref[:, 0:1] > 0.5, scores, MASKED_SCORE)
            exponent = jnp.exp(scores - jnp.max(scores, axis=0, keepdims=True))
            probs = exponent * (1.0 / jnp.sum(exponent, axis=0, keepdims=True))
            values_sum[:, place] += product(probs.astype(jnp.bfloat16), grad, False)
            grad_probs = product(x_ref[:, where[2]], grad, True)
            inner = jnp.sum(probs * grad_probs, axis=0, keepdims=True)
            grad_scores = (probs * (grad_probs - inner) * scale).astype(jnp.bfloat16)
            keys_sum[:, place] += product(grad_scores, query, False)
            grad_ref[rows, where[0]] = lax.dot_general(
                grad_scores,
                x_ref[:, where[1]],
                (((0,), (0,)), ((), ())),
                preferred_element_type=jnp.float32,
            ).astype(jnp.bfloat16)
        add_outer(out_sum, mixed_ref, held, rows)

    line_gather(line, g_ref, slot, send, recv, on_own, on_pair)
    grad_ref[:, pl.ds(wide, wide)] = keys_sum[...].astype(jnp.bfloat16)
    grad_ref[:, pl.ds(2 * wide, wide)] = values_sum[...].astype(jnp.bfloat16)
    out_ref[...] = out_sum[...].astype(jnp.bfloat16)


def attend_gather(grad_mid, out_weight, qkv_rows, valid, mixed_low, outer, n, m, number, riders):
    tokens, width = grad_mid.shape
    total = tokens * n
    wide = out_weight.shape[0]
    return comm_call(
        attend_gather_kernel,
        (
            grad_mid,
            out_weight,
            qkv_rows,
            jnp.broadcast_to(valid[:, None], (total, 128)),
            mixed_low,
        )
        + tuple(outer),
        (
            jax.ShapeDtypeStruct((total, 3 * wide), jnp.bfloat16),
            jax.ShapeDtypeStruct((wide, width), jnp.bfloat16),
        )
        + outer_shapes(outer),
        [
            pltpu.VMEM((total, width), jnp.bfloat16),
            pltpu.VMEM((total, wide), jnp.float32),
            pltpu.VMEM((total, wide), jnp.float32),
            pltpu.VMEM((wide, width), jnp.float32),
        ]
        + gather_sems(n // 2),
        riders,
        n,
        m,
        number,
    )


def gelu_both(value):
    factor = math.sqrt(2.0 / math.pi)
    square = value * value
    bent = jnp.tanh(factor * value * (1.0 + 0.044715 * square))
    half = 0.5 * (1.0 + bent)
    slope = half + 0.5 * value * (1.0 - bent * bent) * factor * (1.0 + 3 * 0.044715 * square)
    return slope, value * half


def local(
    image,
    embedding,
    extents,
    gain_first,
    conv_first,
    gain_second,
    conv_second,
    shift_weight,
    down_weight,
    ada_weight,
    qkv_weight,
    out_weight,
    up_weight,
    proj_weight,
    cotangent,
):
    strip_rows, canvas_cols, channel_count = (image.shape[1], image.shape[2], image.shape[3])
    width_all = out_weight.shape[1]
    n = lax.axis_size("mp")
    m = lax.axis_size("dp")
    me_mp = lax.axis_index("mp")
    me_dp = lax.axis_index("dp")
    rows_all = strip_rows * n
    pixel_total = rows_all * canvas_cols
    own = channel_count // n
    size = channel_count // GROUPS
    token_rows = strip_rows // 2
    token_cols = canvas_cols // 2
    local_tokens = token_rows * token_cols
    token_total = local_tokens * n
    local_width = out_weight.shape[0]

    fused = own % 128 == 0 and n == 2 * m
    shift_vector = jnp.dot(embedding, shift_weight, preferred_element_type=jnp.float32)[0]
    columns = jnp.dot(embedding, ada_weight, preferred_element_type=jnp.float32)[0]
    own_first = lax.dynamic_slice_in_dim(gain_first, me_mp * own, own)
    own_second = lax.dynamic_slice_in_dim(gain_second, me_mp * own, own)
    riders = (Rider("mp", tiled_up(columns)),)
    if fused:
        normed_first, spread_first, stats, pixels_low, modulation = exchange_norm(
            image[0].reshape(-1, channel_count), own_first, size, canvas_cols, riders, n, m, 12
        )
        inverse_first = stats[2]
    else:
        (modulation,) = exchange(riders, n, m, 12)
        pixels_low = lax.all_to_all(image[0], "mp", 2, 0, tiled=True)
    modulation = modulation.reshape(n, -1)[:, : columns.shape[0]].reshape(-1)
    scale_attend = modulation[:width_all]
    shift_attend = modulation[width_all : 2 * width_all]
    scale_mlp = modulation[2 * width_all : 3 * width_all]
    shift_mlp = modulation[3 * width_all :]

    pixels = pixels_low.astype(jnp.float32).reshape(pixel_total, own)
    if fused:
        hidden_first = hidden_second = None
        normed_second, spread_second, stats = conv_scatter_fused(
            spread_first, conv_first, canvas_cols, n, m, 0, shift_vector, own_second, size
        )
        inverse_second = stats[2]
        (conv_again,) = conv_scatter_fused(spread_second, conv_second, canvas_cols, n, m, 1)
    else:
        spread_first = spread_second = None
        normed_first, inverse_first = group_forward(pixels, size)
        hidden_first = (
            jax.nn.silu(normed_first * own_first)
            .astype(jnp.bfloat16)
            .reshape(rows_all, canvas_cols, own)
        )
        conv_output = conv_scatter(hidden_first, conv_first, n) + shift_vector
        normed_second, inverse_second = group_forward(conv_output, size)
        hidden_second = (
            jax.nn.silu(normed_second * own_second)
            .astype(jnp.bfloat16)
            .reshape(rows_all, canvas_cols, own)
        )
        conv_again = conv_scatter(hidden_second, conv_second, n)
    residual = pixels + conv_again
    down_patch = (
        residual.astype(jnp.bfloat16)
        .reshape(rows_all // 2, 2, token_cols, 2, own)
        .transpose(0, 2, 1, 3, 4)
        .reshape(token_total, 4 * own)
    )
    down_matrix = down_weight.reshape(4 * own, width_all)
    stream, normed_attend, inverse_attend, input_attend = tokens_scatter(
        down_patch, down_matrix[None], False, n, m, 2, NormAfter(scale_attend, shift_attend)
    )
    all_attend, qkv_rows = tokens_gather(
        input_attend, qkv_weight, False, (jnp.bfloat16,), lambda value: (value,), n, m, 3
    )
    token_index = jnp.arange(token_total, dtype=jnp.int32)
    key_valid = (token_index // token_cols < extents[0, 0]) & (
        token_index % token_cols < extents[0, 1]
    )
    valid = key_valid.astype(jnp.float32)
    stream_mid, mixed_low, normed_mlp, inverse_mlp, input_mlp = attend_scatter(
        qkv_rows, valid, out_weight, n, m, 4, NormAfter(scale_mlp, shift_mlp, (stream,))
    )
    all_mlp, slope, activated, projected = tokens_gather(
        input_mlp,
        up_weight[None],
        False,
        (jnp.bfloat16, jnp.bfloat16),
        gelu_both,
        n,
        m,
        5,
        chain=(proj_weight,),
    )
    final_stream = stream_mid + scatter_rows(projected)
    output = final_stream.astype(jnp.bfloat16).reshape(1, token_rows, token_cols, width_all)

    grad_final_low = cotangent[0].reshape(local_tokens, width_all)
    all_final = gather_rows(lax.optimization_barrier((grad_final_low, qkv_rows))[0])
    grad_act = jnp.einsum("le,fe->lf", all_final, proj_weight, preferred_element_type=jnp.float32)
    grad_upper = (grad_act * slope.astype(jnp.float32)).astype(jnp.bfloat16)
    grad_mid, grad_proj, grad_mid_low, mlp_sums = tokens_scatter(
        grad_upper,
        up_weight[None],
        True,
        n,
        m,
        6,
        NormBack(scale_mlp, normed_mlp, inverse_mlp, grad_final_low),
        (),
        (activated, all_final),
    )
    grad_qkv, grad_out, grad_up = attend_gather(
        grad_mid_low,
        out_weight,
        qkv_rows,
        valid,
        mixed_low,
        (all_mlp, grad_upper),
        n,
        m,
        7,
        (),
    )
    _, grad_stream_low, attend_sums, sums_proj, sums_out = tokens_scatter(
        grad_qkv,
        qkv_weight,
        True,
        n,
        m,
        8,
        NormBack(scale_attend, normed_attend, inverse_attend, grad_mid),
        (Rider("dp", grad_proj, 1, part=(0, 2)), Rider("dp", grad_out, 1)),
    )
    grad_modulation = jnp.concatenate(
        [
            tiled_up(piece)
            for piece in jnp.concatenate([attend_sums[:2], mlp_sums[:2]]).reshape(n, -1)
        ]
    )
    grad_residual, grad_down, grad_qkv_weight, sums_more, ada_columns = tokens_gather(
        grad_stream_low,
        down_matrix[None],
        True,
        (jnp.float32,),
        lambda value: (value,),
        n,
        m,
        9,
        (
            Rider("dp", grad_proj, 1, part=(1, 2)),
            Rider("mp", grad_modulation, 0),
        ),
        down_patch,
        (all_attend, grad_qkv),
        canvas_cols if fused else 0,
        keep=False,
    )
    ada_columns = added(ada_columns).reshape(-1)[: columns.shape[0]]
    if not fused:
        grad_residual = (
            grad_residual.reshape(rows_all // 2, token_cols, 2, 2, own)
            .transpose(0, 2, 1, 3, 4)
            .reshape(pixel_total, own)
        )
    def back(grad_low, hidden, spread, kernel, normed, inverse, gain, number, riders, more=()):
        if fused:
            low, parts, sums, *ridden = conv_back_fused(
                grad_low,
                spread,
                kernel,
                normed,
                inverse,
                gain,
                size,
                canvas_cols,
                n,
                m,
                number,
                riders,
                more,
            )
            return low, parts, sums[0], sums[2], ridden
        grad_hidden, grad_kernel = conv_backward(grad_low, hidden, kernel, n)
        outgoing, gain_part = group_backward(grad_hidden, normed, inverse, gain, size)
        parts = grad_kernel.astype(jnp.bfloat16).reshape(9 * own, -1).T
        low = sum(more, outgoing).astype(jnp.bfloat16)
        return low, parts, gain_part, jnp.sum(outgoing, axis=0), exchange(riders, n, m, number)

    grad_conv_low, parts_second, grad_gain_second, grad_shift, rode_second = back(
        grad_residual.astype(jnp.bfloat16),
        hidden_second,
        spread_second,
        conv_second,
        normed_second,
        inverse_second,
        own_second,
        10,
        (
            Rider("dp", unsettled(grad_down, m, n), 1),
            Rider("dp", grad_qkv_weight, 0),
            Rider("dp", jnp.concatenate([tiled_up(embedding[0]), tiled_up(ada_columns)])),
        ),
    )
    sums_down, sums_qkv, every_small = rode_second
    image_turned, parts_first, grad_gain_first, _, rode_first = back(
        grad_conv_low,
        hidden_first,
        spread_first,
        conv_first,
        normed_first,
        inverse_first,
        own_first,
        11,
        (
            Rider("dp", unsettled(parts_second, m, n), 1),
            Rider("dp", tiled_up(grad_shift)),
            Settle(sums_down, True, 4, fused),
            Rider("dp", grad_up, 0),
        ),
        (grad_residual,),
    )
    sums_second, every_shift, pieces_down, sums_up = rode_first
    embed_term = jnp.dot(
        grad_shift[None], shift_weight.astype(jnp.float32).T, precision=PRECISE
    ) + jnp.dot(ada_columns[None], ada_weight.astype(jnp.float32).T, precision=PRECISE)
    small = jnp.concatenate(
        [tiled_up(embed_term[0]), tiled_up(jnp.concatenate([grad_gain_first, grad_gain_second]))]
    )
    riders = (
        Settle(unsettled(parts_first, m, n), False, 9, fused),
        Rider("all", small),
        Settle(sums_second, True, 9, fused),
    )
    if fused:
        pieces_first, small, pieces_second, image_turned = exchange(
            riders + (Rider("mp", image_turned, 0, True),), n, m, 13
        )
        image_grad = image_turned.reshape(image.shape)
    else:
        pieces_first, small, pieces_second = exchange(riders, n, m, 13)
        image_grad = lax.all_to_all(
            image_turned.reshape(rows_all, canvas_cols, own), "mp", 0, 2, tiled=True
        )[None]

    small = small.reshape(m, n, -1)
    embed_count = embedding.shape[1]
    embedding_grad = jnp.sum(
        lax.dynamic_index_in_dim(small, me_dp, axis=0, keepdims=False)[:, :embed_count], axis=0
    )[None]
    gain_start = -(-embed_count // 1024) * 1024
    gains = jnp.sum(small[:, :, gain_start : gain_start + 2 * own], axis=0)
    gains = gains.reshape(n, 2, own).transpose(1, 0, 2).reshape(2, -1)
    piece = channel_count // (m * n)
    gains = lax.dynamic_slice_in_dim(gains, (me_dp * n + me_mp) * piece, piece, axis=1)
    every_small = every_small.reshape(m, -1)
    embed_rows = lax.dynamic_slice_in_dim(
        every_small[:, :embed_count], me_dp * (embed_count // m), embed_count // m, axis=1
    )
    grad_shift_weight = jnp.dot(
        embed_rows.T, every_shift.reshape(m, -1)[:, :own], precision=PRECISE
    )
    grad_ada_weight = jnp.dot(
        embed_rows.T,
        every_small[:, gain_start : gain_start + columns.shape[0]],
        precision=PRECISE,
    )
    qkv_grad = jnp.stack(
        [added(sums_qkv[:, :, j * local_width : (j + 1) * local_width]) for j in range(3)]
    )
    return (
        output,
        image_grad,
        embedding_grad,
        gains[0],
        settled(pieces_first, 9),
        gains[1],
        settled(pieces_second, 9),
        grad_shift_weight,
        settled(pieces_down, 4),
        grad_ada_weight,
        qkv_grad,
        added(sums_out),
        added(sums_up),
        jnp.concatenate([added(sums_proj), added(sums_more)]),
    )


def solution(mesh):
    placed = (
        P("dp", "mp", None, None),
        P("dp", None),
        P("dp", None),
        P(),
        P(None, "mp", None),
        P(),
        P(None, "mp", None),
        P(None, "mp"),
        P(None, "mp", None),
        P(None, "mp"),
        P(None, None, "mp"),
        P("mp", None),
        P(None, "mp"),
        P("mp", None),
        P("dp", "mp", None, None),
    )
    return jax.shard_map(
        local,
        mesh=mesh,
        in_specs=placed,
        out_specs=(
            P("dp", "mp", None, None),
            P("dp", "mp", None, None),
            P("dp", None),
            P(("dp", "mp")),
            P(None, "dp", "mp"),
            P(("dp", "mp")),
            P(None, "dp", "mp"),
            P("dp", "mp"),
            P(None, "dp", "mp"),
            P("dp", "mp"),
            P(None, "dp", "mp"),
            P("mp", "dp"),
            P("dp", "mp"),
            P("mp", "dp"),
        ),
        check_vma=False,
    )
```
